32 devices in a mesh: section: 2 (over core), tm: 4 (over z), item: 4 (over y, x).
Axes of the slice: x: 2, y: 2, z: 4, core: 2. Of those that a mesh axis runs over, the one named last changes fastest.
Arguments:
- sources: bfloat16 [3, 32, 128, 4096], P(None, 'item', 'section', 'tm'), may hold values from -40 to 40
- source_counts: int32 [32], P('item'), may hold values from 2 to 3
- valid_lengths: int32 [32], P('item'), may hold values from 2048 to 4096, as said below
- w_in: bfloat16 [2, 512, 128], P('section'), may hold values from -0.5 to 0.5
- chan: float32 [2, 11, 512], P('section'), may hold values from -3 to 3
- w_out: bfloat16 [2, 256, 512], P('section'), may hold values from -0.25 to 0.25
- b_out: float32 [2, 256], P('section'), may hold values from -2 to 2
- grad_out: bfloat16 [32, 128, 4096], P('item', None, 'tm'), may hold values from -6 to 6
- grad_skip: bfloat16 [32, 128, 4096], P('item', None, 'tm'), may hold values from -6 to 6
Outputs:
- block_out: bfloat16 [2, 32, 128, 4096], P('section', 'item', None, 'tm')
- skip_out: bfloat16 [2, 32, 128, 4096], P('section', 'item', None, 'tm')
- grad_sources: float32 [3, 32, 128, 4096], P(None, 'item', 'section', 'tm')
- grad_w_in: float32 [2, 512, 128], P('section')
- grad_chan: float32 [2, 11, 512], P('section')
- grad_w_out: float32 [2, 256, 512], P('section')
- grad_b_out: float32 [2, 256], P('section')
The draws below stay inside these ranges and needn't reach their ends.
Inputs may be any that keep to these rules, and one draw needn't show every extreme that they name: `valid_lengths`: in each aligned block of 8 items one item has all 4096 frames valid.
All inputs are finite; a program needn't handle non-finite values.
Results may differ from the reference program's by a relative error of at most 0.0095.
Values may be sent and summed in bfloat16 or wider, within the bound.
A program may use at most 256 MiB of HBM per device.

```python
import jax
import jax.numpy as jnp
import numpy as np
from jax import lax

B = 128
H = 512
FIRST_DILATION = 128
NSRC = 3
CHAN_ROWS = 11
MICRO = 4
IMB = 2
FRAMES = 4096
ITEMS = 32


NORMAL_SCALES = np.array([0.4, 0.0, 0.0, 0.4, 0.6, 0.6, 0.6, 0.4, 0.0, 0.0, 0.4], np.float32)


UNIFORM_LOWS = np.array([0.0, 0.05, 0.5, 0.0, 0.0, 0.0, 0.0, 0.0, 0.05, 0.5, 0.0], np.float32)


UNIFORM_SPANS = np.array([0.0, 0.45, 1.0, 0.0, 0.0, 0.0, 0.0, 0.0, 0.45, 1.0, 0.0], np.float32)


def draw_sources(key, part):
    key = jax.random.fold_in(key, 11)
    key_base, key_chan, key_frame, key_slope = jax.random.split(key, 4)
    shape = (NSRC, ITEMS, B, FRAMES)
    position = jnp.arange(FRAMES, dtype=jnp.float32) / FRAMES
    chan_scale = jax.random.uniform(key_chan, (NSRC, 1, B, 1), jnp.float32, -0.7, 0.7)
    frame_rough = jax.random.uniform(key_frame, (1, ITEMS, 1, FRAMES), jnp.float32, -0.35, 0.35)
    base_part = jax.random.truncated_normal(key_base, -6.0, 6.0, shape, jnp.float32)
    slope_part = jax.random.uniform(key_slope, (NSRC, ITEMS, 1, 1), jnp.float32, 0.6, 1.2)
    envelope = jnp.exp(slope_part * (position[None, None, None, :] - 0.5) + chan_scale + frame_rough)
    return (base_part * envelope).astype(jnp.bfloat16)


def draw_valid_lengths(key, part):
    key = jax.random.fold_in(key, 37)
    key_length, key_full = jax.random.split(key)
    group_size = MICRO * IMB
    lengths = jax.random.randint(key_length, (ITEMS,), FRAMES // 2, FRAMES + 1, jnp.int32)
    full_pick = jax.random.randint(key_full, (ITEMS // group_size,), 0, group_size, jnp.int32)
    picked = jnp.arange(ITEMS, dtype=jnp.int32) % group_size == jnp.repeat(full_pick, group_size)
    return jnp.where(picked, FRAMES, lengths).astype(jnp.int32)


def draw_chan(key, part):
    key = jax.random.fold_in(key, 23)
    key_normal, key_uniform = jax.random.split(key)
    shape = (2, CHAN_ROWS, H)
    normal_part = jax.random.truncated_normal(key_normal, -4.0, 4.0, shape, jnp.float32)
    uniform_part = jax.random.uniform(key_uniform, shape, jnp.float32)
    return normal_part * NORMAL_SCALES[None, :, None] + UNIFORM_LOWS[None, :, None] + uniform_part * UNIFORM_SPANS[None, :, None]


def place_ends(values, rng, least, largest):
    longest = values.shape.index(max(values.shape))
    spots = []
    for shift in (0, 1):
        where = [jax.random.randint(jax.random.fold_in(rng, axis), (), 0, length) for axis, length in enumerate(values.shape)]
        where[longest] = (where[longest] + shift) % values.shape[longest]
        spots.append(tuple(where))
    return values.at[spots[0]].set(least).at[spots[1]].set(largest)


def shard_levels(own_key, dims, cuts, smallest, largest):
    factor_of = 1.0
    for dim, blocks in cuts:
        draws = jax.random.uniform(jax.random.fold_in(jax.random.fold_in(own_key, 6), dim), (blocks,), jnp.float32, smallest / len(cuts), largest / len(cuts))
        factor_of = factor_of * jnp.repeat(jnp.exp(draws), dims[dim] // blocks).reshape((-1,) + (1,) * (len(dims) - 1 - dim))
    return factor_of


def noise(key, shape, width, most, cuts=(), kind=jnp.bfloat16):
    level = shard_levels(key, shape, cuts, -0.22, 0.18) if cuts else 1.0
    values = jax.random.normal(key, shape, jnp.float32) * width * level
    return jnp.minimum(jnp.maximum(values, -most), most).astype(kind)


def setup_inputs(seed: int = 0) -> dict:
    key_list = jax.random.split(jax.random.key(seed), 10)
    return {
        "sources": draw_sources(jax.random.fold_in(key_list[9], 71), 0),
        "source_counts": place_ends(jax.random.randint(key_list[1], (ITEMS,), 2, 4), jax.random.fold_in(key_list[1], 1), 2, 3).astype(jnp.int32),
        "valid_lengths": draw_valid_lengths(jax.random.fold_in(key_list[9], 71), 0),
        "w_in": noise(key_list[3], (2, H, B), B ** -0.5, 0.5, ((0, 2),)),
        "chan": draw_chan(jax.random.fold_in(key_list[9], 71), 0),
        "w_out": noise(key_list[5], (2, 2 * B, H), H ** -0.5, 0.25, ((0, 2),)),
        "b_out": noise(key_list[6], (2, 2 * B), 0.3, 2.0, ((0, 2),), jnp.float32),
        "grad_out": noise(key_list[7], (ITEMS, B, FRAMES), 1.0, 6.0, ((0, 4), (2, 4))),
        "grad_skip": noise(key_list[8], (ITEMS, B, FRAMES), 1.0, 6.0, ((0, 4), (2, 4))),
    }


@jax.custom_vjp
def low(v):
    return lax.optimization_barrier(v.astype(jnp.bfloat16)).astype(jnp.float32)

@jax.custom_vjp
def low_back(v):
    return v

def low_keep(v):
    return (low(v), None)

def low_pass(kept, grad):
    return (grad,)

def back_keep(v):
    return (v, None)

def back_low(kept, grad):
    return (low(grad),)
low.defvjp(low_keep, low_pass)
low_back.defvjp(back_keep, back_low)
EPSILON = 1e-05
PRECISE = lax.Precision.HIGHEST

def soft_prelu(values_in, slope_row):
    return jax.nn.softplus(values_in) - slope_row * jax.nn.softplus(-values_in)

def global_norm(hidden_act, frame_valid_mask, normalizer_count, gain_row, offset_row):
    mean_val = jnp.sum(hidden_act * frame_valid_mask) / normalizer_count
    centered = (hidden_act - mean_val) * frame_valid_mask
    spread = jnp.sum(centered * centered) / normalizer_count
    normed = (hidden_act - mean_val) * lax.rsqrt(spread + EPSILON)
    return (normed * gain_row[:, None] + offset_row[:, None]) * frame_valid_mask

def temporal_conv_block(block_in, w_first, params, w_last, bias_last, dilation_rate, frame_valid_mask, normalizer_count):
    frame_count = block_in.shape[1]
    pre_act = low_back(jnp.dot(w_first, block_in, precision=PRECISE, preferred_element_type=jnp.float32) + params[0][:, None])
    hidden_act = soft_prelu(pre_act, params[1][:, None])
    first_block_output = low(global_norm(hidden_act, frame_valid_mask, normalizer_count, params[2], params[3]))
    padded_input = jnp.pad(first_block_output, ((0, 0), (dilation_rate, dilation_rate)))
    left_kernel_tap = padded_input[:, :frame_count]
    right_kernel_tap = padded_input[:, 2 * dilation_rate:2 * dilation_rate + frame_count]
    conv_out = low_back(params[4][:, None] * left_kernel_tap + params[5][:, None] * first_block_output + params[6][:, None] * right_kernel_tap + params[7][:, None])
    second_act = soft_prelu(conv_out, params[8][:, None])
    second_out = low(global_norm(second_act, frame_valid_mask, normalizer_count, params[9], params[10]))
    projected = jnp.dot(w_last, second_out, precision=PRECISE, preferred_element_type=jnp.float32) + bias_last[:, None]
    bottleneck = block_in.shape[0]
    return (block_in + projected[:bottleneck] * frame_valid_mask, projected[bottleneck:] * frame_valid_mask)

def item_forward(weights, source_item, source_count, valid_length):
    stacked_first_weights, stacked_channel_scales, stacked_last_weights, stacked_biases = weights
    frame_count = source_item.shape[2]
    frame_valid_mask = (jnp.arange(frame_count, dtype=jnp.int32) < valid_length).astype(jnp.float32)[None, :]
    chosen = (jnp.arange(source_item.shape[0], dtype=jnp.int32) < source_count).astype(jnp.float32)
    source_mixture = low(lax.optimization_barrier(jnp.sum(source_item * chosen[:, None, None], axis=0)) * frame_valid_mask)
    normalizer_count = valid_length.astype(jnp.float32) * stacked_first_weights.shape[1]
    initial_output, initial_skip = temporal_conv_block(source_mixture, stacked_first_weights[0], stacked_channel_scales[0], stacked_last_weights[0], stacked_biases[0], FIRST_DILATION, frame_valid_mask, normalizer_count)
    initial_output = low(initial_output)
    initial_skip = low(initial_skip)
    out_one, skip_one = temporal_conv_block(low_back(initial_output), stacked_first_weights[1], stacked_channel_scales[1], stacked_last_weights[1], stacked_biases[1], 1, frame_valid_mask, normalizer_count)
    return (out_one, initial_skip + skip_one, initial_output, initial_skip)

def reference(sources, source_counts, valid_lengths, w_in, chan, w_out, b_out, grad_out, grad_skip):
    weights = (w_in.astype(jnp.float32), chan, w_out.astype(jnp.float32), b_out)
    sources_wide = sources.astype(jnp.float32)

    def one_item(totals, item_num):
        source_item = sources_wide[:, item_num]
        source_count = source_counts[item_num]
        valid_length = valid_lengths[item_num]

        def forward(weights_in, source_in):
            return item_forward(weights_in, source_in, source_count, valid_length)
        results, pullback = jax.vjp(forward, weights, source_item)
        zeros_out = jnp.zeros_like(results[2])
        cotangent = (grad_out[item_num].astype(jnp.float32), grad_skip[item_num].astype(jnp.float32), zeros_out, zeros_out)
        weight_grads, source_grad = pullback(cotangent)
        totals = jax.tree.map(jnp.add, totals, weight_grads)
        return (totals, (results[2], results[0], results[3], results[1], source_grad))
    start = jax.tree.map(jnp.zeros_like, weights)
    totals, per_item = lax.scan(one_item, start, jnp.arange(ITEMS, dtype=jnp.int32))
    initial_output, out_one, initial_skip, skip_total, source_grads = per_item
    block_out = jnp.stack([initial_output, out_one]).astype(jnp.bfloat16)
    skip_out = jnp.stack([initial_skip, skip_total]).astype(jnp.bfloat16)
    grad_sources = jnp.transpose(source_grads, (1, 0, 2, 3))
    return (block_out, skip_out, grad_sources, totals[0], totals[1], totals[2], totals[3])
```

```python
import functools
import math

import jax
import jax.numpy as jnp
from jax import lax
from jax.experimental import pallas as pl
from jax.experimental.pallas import tpu as pltpu
from jax.sharding import PartitionSpec as P

DILATION = 128
LANES = 128
ROWS = 16
EPSILON = 1e-05
LN2 = math.log(2.0)
LOG2E = 1.0 / LN2
F32 = jnp.float32
BF16 = jnp.bfloat16
MESH = pl.DeviceIdType.MESH
NT = (((1,), (1,)), ((), ()))
NN = (((1,), (0,)), ((), ()))


def dot(a, b, dims=NN, precision=None):
    return lax.dot_general(a, b, dims, precision=precision, preferred_element_type=F32)


def remote(src, dst, send, recv, device):
    return pltpu.make_async_remote_copy(
        src_ref=src, dst_ref=dst, send_sem=send, recv_sem=recv, device_id=device, device_id_type=MESH
    )


def wide(v, width):
    return jnp.concatenate([v] * (width // LANES), axis=1)


def tall(v, rows):
    return jnp.concatenate([v] * (rows // v.shape[0]), axis=0)


def fold(v):
    parts = [v[:, at : at + LANES] for at in range(0, v.shape[1], LANES)]
    while len(parts) > 1:
        parts = [a + b for a, b in zip(parts[::2], parts[1::2])] + parts[len(parts) & ~1 :]
    return parts[0]


def fold_rows(v):
    parts = [v[at : at + 8] for at in range(0, v.shape[0], 8)]
    while len(parts) > 1:
        parts = [a + b for a, b in zip(parts[::2], parts[1::2])] + parts[len(parts) & ~1 :]
    return parts[0]


def column(table, j):
    return jnp.broadcast_to(table[:, j : j + 1], (table.shape[0], LANES))


def rows_at(t, count):
    return pl.ds(pl.multiple_of(t * count, count), count)


def kernel(
    dims,
    mix_h, gout_h, gskip_h, mask_ref, edge_mask_ref, invn_ref,
    wpre_h, wout_h, wg_h, win_h, chan_h, col_h,
    block_h, skip_h, gmix_h, gwi_h, gwo_h, gch_h, gb_h,
    x0, x1, skip0, out1, skip1, act1_0, act1_1, soft1, act2, soft2, buf, wide_s, dpre, dp, gacc,
    wpre, wout, wg, win, chan, col,
    gwi, gwo, gch, gb, rwi, rwo, rch, rb,
    stat, back, st_src, st_buf,
    edge_src, edge_in, x_edge, dp_edge, first_edge, act_edge, soft_edge, conv_edge,
    sem_w, sem_x, sem_xr, sem_g, sem_es, sem_er, sem_ss, sem_sr, sem_hs, sem_hr, sem_o, sem_or, sem_m, sem_mr,
    sem_k, sem_kr, sem_f,
):
    n_tm, NI, H, B, F = dims
    R = ROWS
    W = F + 2 * DILATION
    MID = slice(DILATION, DILATION + F)
    half = B // 2
    s = lax.axis_index("section")
    t = lax.axis_index("tm")
    o = 1 - s
    left = t - 1
    right = t + 1
    last = n_tm - 1
    first_item = s * NI
    lane = lax.broadcasted_iota(jnp.int32, (R, LANES), 1)
    lane8 = lax.broadcasted_iota(jnp.int32, (8, LANES), 1)

    edge_in[...] = jnp.zeros(edge_in.shape, BF16)

    barrier = pltpu.get_barrier_semaphore()
    pl.semaphore_signal(barrier, inc=1, device_id={"section": o}, device_id_type=MESH)

    def greet(d, c):
        to = lax.rem(t + d, n_tm)
        pl.semaphore_signal(barrier, inc=1, device_id={"tm": to}, device_id_type=MESH)
        pl.semaphore_signal(barrier, inc=1, device_id={"section": o, "tm": to}, device_id_type=MESH)
        return c

    lax.fori_loop(1, n_tm, greet, 0)
    pl.semaphore_wait(barrier, 2 * n_tm - 1)

    own_rows = pl.ds(pl.multiple_of(s * half, half), half)
    other_rows = pl.ds(pl.multiple_of(o * half, half), half)
    items_of = lambda core: pl.ds(core * NI, NI)
    centre = pl.ds(DILATION, F)
    head, tail = pl.ds(0, DILATION), pl.ds(F + DILATION, DILATION)

    main_local = pltpu.make_async_copy(mix_h.at[items_of(s)], x0.at[:, own_rows, centre], sem_x.at[0])
    main_send = remote(
        mix_h.at[items_of(o)], x0.at[:, own_rows, centre], sem_x.at[1], sem_xr.at[0], {"section": o}
    )
    main_recv = remote(
        mix_h.at[items_of(o)], x0.at[:, other_rows, centre], sem_x.at[1], sem_xr.at[0], {"section": o}
    )

    def halo_send(side, core):
        edge = pl.ds(0, DILATION) if side == 0 else pl.ds(F - DILATION, DILATION)
        place = tail if side == 0 else head
        return remote(
            mix_h.at[items_of(core), :, edge],
            x0.at[:, own_rows, place],
            sem_x.at[2 + 2 * side + core],
            sem_xr.at[1 + 2 * side + s],
            {"section": core, "tm": left if side == 0 else right},
        )

    def halo_recv(side, core):
        place = tail if side == 0 else head
        rows = pl.ds(core * half, half)
        return remote(
            x0.at[:, rows, place], x0.at[:, rows, place], sem_x.at[0], sem_xr.at[1 + 2 * side + core], {"section": o}
        )

    main_send.start()
    main_local.start()

    @pl.when(t > 0)
    def _():
        for core in (0, 1):
            halo_send(0, core).start()

    @pl.when(t < last)
    def _():
        for core in (0, 1):
            halo_send(1, core).start()

    weights = ((wpre_h, wpre), (wout_h, wout), (wg_h, wg), (win_h, win), (chan_h, chan), (col_h, col))

    def weight_copies(j):
        src, dst = weights[j]
        return (
            pltpu.make_async_copy(src, dst.at[s], sem_w.at[j, 0]),
            remote(src, dst.at[s], sem_w.at[j, 1], sem_w.at[j, 2], {"section": o}),
            remote(src, dst.at[o], sem_w.at[j, 1], sem_w.at[j, 2], {"section": o}),
        )

    for j in range(len(weights)):
        local, send, _ = weight_copies(j)
        send.start()
        local.start()
    load_out = pltpu.make_async_copy(gout_h.at[items_of(s)], dp.at[:, pl.ds(0, B)], sem_g.at[0])
    load_skip = pltpu.make_async_copy(gskip_h.at[items_of(s)], dp.at[:, pl.ds(B, B)], sem_g.at[1])
    load_out.start()
    load_skip.start()

    @pl.when(t == 0)
    def _():
        x0[:, :, 0:DILATION] = jnp.zeros((NI, B, DILATION), BF16)

    @pl.when(t == last)
    def _():
        x0[:, :, F + DILATION : W] = jnp.zeros((NI, B, DILATION), BF16)

    for j in range(2):
        gwi[j] = jnp.zeros((H, B), F32)
        gwo[j] = jnp.zeros((H, 2 * B), F32)
        gb[j] = jnp.zeros((8, 2 * B), F32)

    def stat_copy(ph, i, d, to):
        p = ph % 2
        return remote(
            st_src.at[p, i], st_buf.at[p, i, d - 1], sem_ss.at[p, i, d - 1], sem_sr.at[p, i, d - 1], {"tm": to}
        )

    def send_stats(ph, i, a, b):
        rows = [jnp.sum(a, axis=0, keepdims=True), jnp.sum(b, axis=0, keepdims=True)]
        st_src[ph % 2, i] = jnp.concatenate(rows + [jnp.zeros((6, LANES), F32)], axis=0)

        def one(d, c):
            stat_copy(ph, i, d, lax.rem(t + d, n_tm)).start()
            return c

        lax.fori_loop(1, n_tm, one, 0)

    def recv_stats(ph, i):
        def one(d, total):
            copy = stat_copy(ph, i, d, lax.rem(t + d, n_tm))
            copy.wait_send()
            copy.wait_recv()
            return total + st_buf[ph % 2, i, d - 1]

        total = lax.fori_loop(1, n_tm, one, st_src[ph % 2, i])
        sums = jnp.sum(total, axis=1, keepdims=True)
        return (
            jnp.broadcast_to(sums[0:1], (8, LANES)),
            jnp.broadcast_to(sums[1:2], (8, LANES)),
        )

    def finish_norm(ph, slot, i):
        a, b = recv_stats(ph, i)
        inv_n = invn_ref[i]
        mean = a * inv_n
        spread = jnp.maximum(b * inv_n - mean * mean, 0.0)
        stat[slot, i, 0] = mean
        stat[slot, i, 1] = lax.rsqrt(spread + EPSILON / (LN2 * LN2))

    def finish_back(ph, slot, i):
        a, b = recv_stats(ph, i)
        inv_n = invn_ref[i]
        mean, inv = stat[slot, i, 0], stat[slot, i, 1]
        q = b * inv_n * inv
        back[i, 0] = (mean * q - a * inv_n) * (inv * LOG2E)
        back[i, 1] = -q * (inv * LOG2E)

    def lanes_of(ref, j):
        out = ref[0, j]
        for i in range(1, NI):
            out = jnp.where(lane8 >= 32 * i, ref[i, j], out)
        return out

    def per_item(body):
        lax.fori_loop(0, NI, lambda i, c: (body(i), c)[1], 0)

    def per_tile(body, count=H, rows=R, init=0):
        return lax.fori_loop(0, count // rows, lambda j, c: body(rows_at(j, rows), c), init)

    def mask_row(i, rows, at=DILATION, width=F):
        return tall(mask_ref[i, :, at : at + width], rows)

    zero8 = jnp.zeros((8, LANES), F32)

    def pack_edges(src, channels, slot):
        def tile(r, c):
            to_left = to_right = own = jnp.zeros((R, LANES), F32)
            for i in range(NI):
                a = src[i, r, 0:LANES].astype(F32)
                z = src[i, r, F - LANES : F].astype(F32)
                base = 32 * i
                to_left += jnp.where(
                    (lane == base + 17) | (lane == base + 18), pltpu.roll(a, base + 17, 1), 0.0
                )
                to_right += jnp.where(
                    (lane == base) | (lane == base + 1), pltpu.roll(z, base + 2, 1), 0.0
                )
                own += jnp.where(lane == base + 2, pltpu.roll(a, base + 2, 1), 0.0)
                own += jnp.where(lane == base + 16, pltpu.roll(z, base + 17, 1), 0.0)
            edge_src[slot, 0, r, :] = to_left.astype(BF16)
            edge_src[slot, 1, r, :] = to_right.astype(BF16)
            edge_src[slot, 2, r, :] = own.astype(BF16)
            return c

        per_tile(tile, channels)

    def edge_copy(slot, side, channels):
        rows = pl.ds(0, channels)
        return remote(
            edge_src.at[slot, side, rows],
            edge_in.at[slot, side, rows],
            sem_es.at[slot, side],
            sem_er.at[slot, side],
            {"tm": left if side == 0 else right},
        )

    def send_edges(slot, channels):
        @pl.when(t > 0)
        def _():
            edge_copy(slot, 0, channels).start()

        @pl.when(t < last)
        def _():
            edge_copy(slot, 1, channels).start()

    def recv_edges(slot, channels, dst):
        @pl.when(t > 0)
        def _():
            edge_copy(slot, 0, channels).wait_send()
            edge_copy(slot, 1, channels).wait_recv()

        @pl.when(t < last)
        def _():
            edge_copy(slot, 1, channels).wait_send()
            edge_copy(slot, 0, channels).wait_recv()

        def tile(r, c):
            total = edge_src[slot, 2, r, :].astype(F32)
            for side in (0, 1):
                total += edge_in[slot, side, r, :].astype(F32)
            dst[r, :] = total.astype(BF16)
            return c

        per_tile(tile, channels)

    def rectify(neg, rest):
        soft = jnp.maximum(neg, jnp.log2(1.0 + jnp.exp2(jnp.minimum(neg, 100.0))))
        return rest * soft - neg, soft

    def masked_sums(a, m, sums):
        am = a * m
        return (sums[0] + fold_rows(fold(am)), sums[1] + fold_rows(fold(am * a)))

    def phase1(k):
        width = W if k == 0 else F
        x = x0 if k == 0 else x1
        act = act1_0 if k == 0 else act1_1
        mid = MID if k == 0 else slice(0, F)

        def item(i):
            wide_s[:, 0:width] = dot(wpre[k], x[i])
            m = mask_row(i, R)

            def tile(r, sums):
                table = chan[k, r, :]
                bias = column(table, 0) * -LOG2E
                rest = 1.0 - column(table, 1)
                neg = wide_s[r, 0:width] * -LOG2E + wide(bias, width)
                a, soft = rectify(neg, wide(rest, width))
                act[i, r, :] = a.astype(BF16)
                soft1[k, i, r, :] = soft[:, mid].astype(BF16)
                return masked_sums(a[:, mid], m, sums)

            a, b = per_tile(tile, init=(zero8, zero8))
            send_stats(4 * k, i, a, b)

        per_item(item)
        if k == 1:
            recv_edges(1, B, x_edge)
            wide_s[:, 0:LANES] = dot(wpre[1], x_edge[...])

            def tile(r, c):
                table = chan[1, r, :]
                neg = wide_s[r, 0:LANES] * -LOG2E + column(table, 0) * -LOG2E
                a, _ = rectify(neg, 1.0 - column(table, 1))
                wide_s[r, 0:LANES] = a
                return c

            per_tile(tile)

    def phase2(k):
        width = W if k == 0 else F
        at = 0 if k == 0 else DILATION
        act = act1_0 if k == 0 else act1_1

        def item(i):
            finish_norm(4 * k, 2 * k, i)
            mean, inv = tall(stat[2 * k, i, 0], R), tall(stat[2 * k, i, 1], R)
            m = mask_row(i, R, at, width)

            def tile(r, c):
                table = chan[k, r, :]
                scale = inv * column(table, 2)
                shift = column(table, 3) - mean * scale
                a = act[i, r, :].astype(F32)
                buf[i, r, at : at + width] = (
                    (a * wide(scale, width) + wide(shift, width)) * m
                ).astype(BF16)
                return c

            per_tile(tile)

        per_item(item)
        if k == 1:
            mean, inv = tall(lanes_of(stat.at[2], 0), R), tall(lanes_of(stat.at[2], 1), R)
            m = tall(edge_mask_ref[...], R)

            def tile(r, c):
                table = chan[1, r, :]
                scale = inv * column(table, 2)
                a = wide_s[r, 0:LANES]
                first_edge[r, :] = (((a - mean) * scale + column(table, 3)) * m).astype(BF16)
                return c

            per_tile(tile)

    def neighbours(f, edge, i):
        shifted_in = pltpu.roll(edge, lax.rem(127 - 32 * i + 256, 128), 1)
        before = pltpu.roll(f, 1, 1)
        lead = jnp.where(lane == 0, shifted_in, before[:, 0:LANES])
        before = jnp.concatenate([lead, before[:, LANES:]], axis=1)
        shifted_in = pltpu.roll(edge, lax.rem(110 - 32 * i + 256, 128), 1)
        after = pltpu.roll(f, F - 1, 1)
        trail = jnp.where(lane == LANES - 1, shifted_in, after[:, F - LANES :])
        after = jnp.concatenate([after[:, : F - LANES], trail], axis=1)
        return before, after

    def taps(k, i, r, edge):
        f = buf[i, r, MID].astype(F32)
        if k == 0:
            return buf[i, r, 0:F].astype(F32), f, buf[i, r, 2 * DILATION : W].astype(F32)
        before, after = neighbours(f, edge[r, :].astype(F32), i)
        return before, f, after

    def conv_coefs(table):
        return [column(table, j) * -LOG2E for j in (4, 5, 6, 7)], 1.0 - column(table, 8)

    def phase3(k):
        def item(i):
            m = mask_row(i, R)

            def tile(r, sums):
                c, rest = conv_coefs(chan[k, r, :])
                before, f, after = taps(k, i, r, first_edge)
                neg = wide(c[0], F) * before + wide(c[1], F) * f + wide(c[2], F) * after + wide(c[3], F)
                a, soft = rectify(neg, wide(rest, F))
                act2[k, i, r, :] = a.astype(BF16)
                soft2[k, i, r, :] = soft.astype(BF16)
                return masked_sums(a, m, sums)

            a, b = per_tile(tile, init=(zero8, zero8))
            send_stats(4 * k + 1, i, a, b)

        per_item(item)
        if k == 1:

            def tile(r, x):
                c, rest = conv_coefs(chan[1, r, :])
                f = first_edge[r, :].astype(F32)
                neg = c[0] * pltpu.roll(f, 1, 1) + c[1] * f + c[2] * pltpu.roll(f, LANES - 1, 1) + c[3]
                a, soft = rectify(neg, rest)
                act_edge[r, :] = a.astype(BF16)
                soft_edge[r, :] = soft.astype(BF16)
                return x

            per_tile(tile)

    def out_copy(kind, k, i, src):
        dst = (block_h, skip_h)[kind]
        row = first_item + i
        return (
            pltpu.make_async_copy(src.at[i], dst.at[row], sem_o.at[kind, k, i]),
            remote(src.at[i], dst.at[row], sem_o.at[kind, k, i], sem_or.at[kind, i], {"section": o}),
        )

    def phase4(k):
        x = x0 if k == 0 else x1
        mid = MID if k == 0 else slice(0, F)
        out = x1 if k == 0 else out1
        skip = skip0 if k == 0 else skip1

        def item(i):
            finish_norm(4 * k + 1, 2 * k + 1, i)
            mean, inv = tall(stat[2 * k + 1, i, 0], R), tall(stat[2 * k + 1, i, 1], R)
            m = mask_row(i, R)
            y = pl.ds(0, 2 * B)
            wide_s[y, 0:F] = dot(wg[k], act2[k, i])

            def project(r):
                table = col[k, r, :]
                shift = column(table, 0) - mean * inv * column(table, 1)
                return (wide_s[r, 0:F] * wide(inv, F) + wide(shift, F)) * m

            def residual(r, c):
                out[i, r, :] = (x[i, r, mid].astype(F32) + project(r)).astype(BF16)
                return c

            def skipped(j, c):
                r = rows_at(j, R)
                p = project(pl.ds(pl.multiple_of(B + j * R, R), R))
                if k == 1:
                    p += skip0[i, r, :].astype(F32)
                skip[i, r, :] = p.astype(BF16)
                return c

            per_tile(residual, B)
            lax.fori_loop(0, B // R, skipped, 0)
            for kind, src in ((0, out), (1, skip)):
                here, there = out_copy(kind, k, i, src)

                @pl.when(s == k)
                def _():
                    here.start()

                @pl.when(s != k)
                def _():
                    there.start()

        per_item(item)

    def phase5(k):
        R5 = 4 * R

        def item(i):
            mean, inv = tall(stat[2 * k + 1, i, 0], R5), tall(stat[2 * k + 1, i, 1], R5)
            wide_s[:, 0 : 2 * B] = dot(act2[k, i], dp[i], NT)
            total8 = dot(jnp.ones((8, F), BF16), dp[i], NT)
            gb[k] += total8
            total = tall(total8, R5)

            def tile(r, sums):
                table = chan[k, r, :]
                g, e = column(table, 9), column(table, 10)
                product = wide_s[r, 0 : 2 * B]
                w = wout[k, r, :].astype(F32)
                against = fold(w * product)
                plain = fold(w * total)
                normed = inv * (against - mean * plain)
                gacc[9, r, :] += normed
                gacc[10, r, :] += plain
                scale = inv * g
                shift = e - mean * scale
                gwo[k, r, :] += wide(scale, 2 * B) * product + wide(shift, 2 * B) * total
                return (sums[0] + fold_rows(g * plain), sums[1] + fold_rows(g * normed))

            a, b = per_tile(tile, rows=R5, init=(zero8, zero8))
            send_stats(4 * k + 2, i, a, b)

        per_item(item)

    def halo_copy(i, side):
        edge = pl.ds(DILATION, DILATION) if side == 0 else pl.ds(F, DILATION)
        return remote(
            buf.at[i, :, edge],
            buf.at[i, :, tail if side == 0 else head],
            sem_hs.at[side, i],
            sem_hr.at[side, i],
            {"tm": left if side == 0 else right},
        )

    def phase6(k):
        def item(i):
            finish_back(4 * k + 2, 2 * k + 1, i)
            inv = tall(stat[2 * k + 1, i, 1], R) * LOG2E
            p, q = wide(tall(back[i, 0], R), F), wide(tall(back[i, 1], R), F)
            m = mask_row(i, R)
            wide_s[:, 0:F] = dot(wout[k], dp[i])

            def tile(r, c):
                table = chan[k, r, :]
                slope = column(table, 8)
                g = inv * column(table, 9)
                d_act = wide_s[r, 0:F] * wide(g, F) + m * (p + q * act2[k, i, r, :].astype(F32))
                soft = soft2[k, i, r, :].astype(F32)
                d_conv = d_act * (wide(slope, F) + wide(1.0 - slope, F) * jnp.exp2(-soft))
                gacc[8, r, :] += fold(d_act * soft) * -LN2
                gacc[7, r, :] += fold(d_conv)
                buf[i, r, MID] = d_conv.astype(BF16)
                return c

            per_tile(tile)
            if k == 0:

                @pl.when(t > 0)
                def _():
                    halo_copy(i, 0).start()

                @pl.when(t < last)
                def _():
                    halo_copy(i, 1).start()

                @pl.when(t == 0)
                def _():
                    buf[i, :, 0:DILATION] = jnp.zeros((H, DILATION), BF16)

                @pl.when(t == last)
                def _():
                    buf[i, :, F + DILATION : W] = jnp.zeros((H, DILATION), BF16)

        per_item(item)
        if k == 1:
            wide_s[:, 0:LANES] = dot(wout[1], dp_edge[...])
            inv = tall(lanes_of(stat.at[3], 1), R) * LOG2E
            p, q = tall(lanes_of(back, 0), R), tall(lanes_of(back, 1), R)
            m = tall(edge_mask_ref[...], R)

            def tile(r, c):
                table = chan[1, r, :]
                slope = column(table, 8)
                d_act = wide_s[r, 0:LANES] * (inv * column(table, 9)) + m * (p + q * act_edge[r, :].astype(F32))
                d_conv = d_act * (slope + (1.0 - slope) * jnp.exp2(-soft_edge[r, :].astype(F32)))
                conv_edge[r, :] = d_conv.astype(BF16)
                return c

            per_tile(tile)

    def phase7(k):
        act = act1_0 if k == 0 else act1_1
        mid = MID if k == 0 else slice(0, F)

        def item(i):
            if k == 0:

                @pl.when(t > 0)
                def _():
                    halo_copy(i, 0).wait_send()
                    halo_copy(i, 1).wait_recv()

                @pl.when(t < last)
                def _():
                    halo_copy(i, 1).wait_send()
                    halo_copy(i, 0).wait_recv()

            mean, inv = tall(stat[2 * k, i, 0], R), tall(stat[2 * k, i, 1], R)
            m = mask_row(i, R)

            def tile(r, sums):
                table = chan[k, r, :]
                g = column(table, 2)
                scale = inv * g
                shift = column(table, 3) - mean * scale
                before, d, after = taps(k, i, r, conv_edge)
                u = (
                    wide(column(table, 4), F) * after
                    + wide(column(table, 5), F) * d
                    + wide(column(table, 6), F) * before
                ) * m
                a = act[i, r, mid].astype(F32)
                first = (a * wide(scale, F) + wide(shift, F)) * m
                plain = fold(u)
                normed = inv * (fold(u * a) - mean * plain)
                gacc[2, r, :] += normed
                gacc[3, r, :] += plain
                gacc[4, r, :] += fold(after * first)
                gacc[5, r, :] += fold(d * first)
                gacc[6, r, :] += fold(before * first)
                soft2[k, i, r, :] = u.astype(BF16)
                return (sums[0] + fold_rows(g * plain), sums[1] + fold_rows(g * normed))

            a, b = per_tile(tile, init=(zero8, zero8))
            send_stats(4 * k + 3, i, a, b)

        per_item(item)

    def mix_copy(i):
        row = first_item + i
        return (
            pltpu.make_async_copy(out1.at[i, own_rows], gmix_h.at[row], sem_m.at[0, i]),
            remote(out1.at[i, other_rows], gmix_h.at[row], sem_m.at[1, i], sem_mr.at[i], {"section": o}),
        )

    def phase8(k):
        act = act1_0 if k == 0 else act1_1
        x = x0 if k == 0 else x1
        mid = MID if k == 0 else slice(0, F)

        def item(i):
            finish_back(4 * k + 3, 2 * k, i)
            inv = tall(stat[2 * k, i, 1], R) * LOG2E
            p, q = wide(tall(back[i, 0], R), F), wide(tall(back[i, 1], R), F)
            m = mask_row(i, R)

            def tile(r, c):
                table = chan[k, r, :]
                slope = column(table, 1)
                g = inv * column(table, 2)
                d_act = soft2[k, i, r, :].astype(F32) * wide(g, F) + m * (p + q * act[i, r, mid].astype(F32))
                soft = soft1[k, i, r, :].astype(F32)
                d_pre = d_act * (wide(slope, F) + wide(1.0 - slope, F) * jnp.exp2(-soft))
                gacc[1, r, :] += fold(d_act * soft) * -LN2
                gacc[0, r, :] += fold(d_pre)
                dpre[r, :] = d_pre.astype(BF16)
                return c

            per_tile(tile)
            gwi[k] += dot(dpre[...], x[i, :, mid], NT)
            wide_s[0:B, 0:F] = dot(win[k], dpre[...])

            def add(r, c):
                d_input = wide_s[r, 0:F] + dp[i, r, :].astype(F32)
                if k == 1:
                    dp[i, r, :] = (d_input * m).astype(BF16)
                else:
                    out1[i, r, :] = (d_input * m).astype(BF16)
                return c

            per_tile(add, B)
            if k == 0:
                here, there = mix_copy(i)
                there.start()
                here.start()

        per_item(item)

    grads = ((gwi, rwi, gwi_h), (gwo, rwo, gwo_h), (gch, rch, gch_h), (gb, rb, gb_h))

    def grad_copy(j, k):
        own, there, _ = grads[j]
        return remote(own.at[k], there, sem_k.at[j], sem_kr.at[j], {"section": o})

    def finish_block(k):
        ones = jnp.ones((8, LANES), F32)
        gch[k] = jnp.concatenate(
            [dot(ones, gacc[j], NT, lax.Precision.HIGHEST)[0:1] for j in range(11)] + [jnp.zeros((5, H), F32)], axis=0
        )

        @pl.when(s != k)
        def _():
            for j in range(4):
                grad_copy(j, k).start()

    for j in range(len(weights)):
        local, send, recv = weight_copies(j)
        local.wait()
        recv.wait_recv()
        send.wait_send()
    main_local.wait()
    main_send.wait_send()
    main_recv.wait_recv()

    @pl.when(t > 0)
    def _():
        for core in (0, 1):
            halo_send(0, core).wait_send()
            halo_recv(1, core).wait_recv()

    @pl.when(t < last)
    def _():
        for core in (0, 1):
            halo_send(1, core).wait_send()
            halo_recv(0, core).wait_recv()

    phase1(0)
    load_out.wait()
    load_skip.wait()

    def mask_gradients(i):
        m = mask_row(i, R)

        def tile(r, c):
            dp[i, r, :] = (dp[i, r, :].astype(F32) * m).astype(BF16)
            return c

        per_tile(tile, 2 * B)

    per_item(mask_gradients)
    pack_edges(dp, 2 * B, 0)
    send_edges(0, 2 * B)
    phase2(0)
    phase3(0)
    phase4(0)
    pack_edges(x1, B, 1)
    send_edges(1, B)
    phase1(1)
    phase2(1)
    phase3(1)
    phase4(1)
    recv_edges(0, 2 * B, dp_edge)
    for k in (1, 0):
        gacc[...] = jnp.zeros(gacc.shape, F32)
        phase5(k)
        phase6(k)
        phase7(k)
        if k == 0:
            for i in range(NI):
                here, there = out_copy(0, 1, i, out1)

                @pl.when(s == 1)
                def _():
                    here.wait()

                @pl.when(s == 0)
                def _():
                    there.wait_send()

        phase8(k)
        finish_block(k)

    for k in (0, 1):

        @pl.when(s != k)
        def _():
            for j in range(4):
                grad_copy(j, k).wait_send()

        @pl.when(s == k)
        def _():
            for j in range(4):
                grad_copy(j, k).wait_recv()
                own, there, _ = grads[j]
                own[k] += there[...]
            for j in range(4):
                own, _, result = grads[j]
                pltpu.make_async_copy(own.at[k], result, sem_f.at[j]).start()
            for j in range(4):
                own, _, result = grads[j]
                pltpu.make_async_copy(own.at[k], result, sem_f.at[j]).wait()

    for i in range(NI):
        here, there = mix_copy(i)
        here.wait()
        there.wait_send()
        remote(
            out1.at[i, other_rows], gmix_h.at[o * NI + i], sem_m.at[1, i], sem_mr.at[i], {"section": o}
        ).wait_recv()
        for kind, srcs in ((0, (x1, out1)), (1, (skip0, skip1))):
            for k in (0, 1):
                here, there = out_copy(kind, k, i, srcs[k])

                if (kind, k) != (0, 1):

                    @pl.when(s == k)
                    def _():
                        here.wait()

                    @pl.when(s != k)
                    def _():
                        there.wait_send()

            dst = (block_h, skip_h)[kind]
            remote(
                srcs[0].at[i], dst.at[o * NI + i], sem_o.at[kind, 0, i], sem_or.at[kind, i], {"section": o}
            ).wait_recv()


def run(n_tm, mix, gout, gskip, masks, edge_mask, inv_n, wpre, wout, wg, win, chan, col):
    items, half, F = mix.shape
    NI = items // 2
    H, B = wpre.shape
    W = F + 2 * DILATION
    any_spec = pl.BlockSpec(memory_space=pl.ANY)
    vmem = pl.BlockSpec(memory_space=pltpu.VMEM)
    dma = pltpu.SemaphoreType.DMA
    shape = jax.ShapeDtypeStruct
    outs = (
        shape((items, B, F), BF16),
        shape((items, B, F), BF16),
        shape((items, half, F), BF16),
        shape((H, B), F32),
        shape((H, 2 * B), F32),
        shape((16, H), F32),
        shape((8, 2 * B), F32),
    )
    scratch = [
        pltpu.VMEM((NI, B, W), BF16),
        pltpu.VMEM((NI, B, F), BF16),
        pltpu.VMEM((NI, B, F), BF16),
        pltpu.VMEM((NI, B, F), BF16),
        pltpu.VMEM((NI, B, F), BF16),
        pltpu.VMEM((NI, H, W), BF16),
        pltpu.VMEM((NI, H, F), BF16),
        pltpu.VMEM((2, NI, H, F), BF16),
        pltpu.VMEM((2, NI, H, F), BF16),
        pltpu.VMEM((2, NI, H, F), BF16),
        pltpu.VMEM((NI, H, W), BF16),
        pltpu.VMEM((H, W), F32),
        pltpu.VMEM((H, F), BF16),
        pltpu.VMEM((NI, 2 * B, F), BF16),
        pltpu.VMEM((11, H, LANES), F32),
        pltpu.VMEM((2, H, B), BF16),
        pltpu.VMEM((2, H, 2 * B), BF16),
        pltpu.VMEM((2, 2 * B, H), BF16),
        pltpu.VMEM((2, B, H), BF16),
        pltpu.VMEM((2, H, LANES), F32),
        pltpu.VMEM((2, 2 * B, LANES), F32),
        pltpu.VMEM((2, H, B), F32),
        pltpu.VMEM((2, H, 2 * B), F32),
        pltpu.VMEM((2, 16, H), F32),
        pltpu.VMEM((2, 8, 2 * B), F32),
        pltpu.VMEM((H, B), F32),
        pltpu.VMEM((H, 2 * B), F32),
        pltpu.VMEM((16, H), F32),
        pltpu.VMEM((8, 2 * B), F32),
        pltpu.VMEM((4, NI, 2, 8, LANES), F32),
        pltpu.VMEM((NI, 2, 8, LANES), F32),
        pltpu.VMEM((2, NI, 8, LANES), F32),
        pltpu.VMEM((2, NI, n_tm - 1, 8, LANES), F32),
        pltpu.VMEM((2, 3, 2 * B, LANES), BF16),
        pltpu.VMEM((2, 2, 2 * B, LANES), BF16),
        pltpu.VMEM((B, LANES), BF16),
        pltpu.VMEM((2 * B, LANES), BF16),
        pltpu.VMEM((H, LANES), BF16),
        pltpu.VMEM((H, LANES), BF16),
        pltpu.VMEM((H, LANES), BF16),
        pltpu.VMEM((H, LANES), BF16),
        dma((6, 3)),
        dma((6,)),
        dma((5,)),
        dma((2,)),
        dma((2, 2)),
        dma((2, 2)),
        dma((2, NI, n_tm - 1)),
        dma((2, NI, n_tm - 1)),
        dma((2, NI)),
        dma((2, NI)),
        dma((2, 2, NI)),
        dma((2, NI)),
        dma((2, NI)),
        dma((NI,)),
        dma((4,)),
        dma((4,)),
        dma((4,)),
    ]
    return pl.pallas_call(
        functools.partial(kernel, (n_tm, NI, H, B, F)),
        out_shape=outs,
        in_specs=[any_spec] * 3 + [vmem] * 3 + [any_spec] * 6,
        out_specs=[any_spec] * len(outs),
        scratch_shapes=scratch,
        compiler_params=pltpu.CompilerParams(
            collective_id=0, has_side_effects=True, vmem_limit_bytes=63 * 1024 * 1024
        ),
        name="temporal_blocks",
    )(mix, gout, gskip, masks, edge_mask, inv_n, wpre, wout, wg, win, chan, col)


def local(sources, source_counts, valid_lengths, w_in, chan, w_out, b_out, grad_out, grad_skip):
    n_sources, per_device, half, F = sources.shape
    H, B = w_in.shape[1:]
    NI = per_device // 2
    n_tm = lax.axis_size("tm")
    s = lax.axis_index("section")
    start = lax.axis_index("tm") * F
    where = start + jnp.arange(F, dtype=jnp.int32)
    masks = (where[None, :] < valid_lengths[:, None]).astype(F32)
    chosen = (jnp.arange(n_sources, dtype=jnp.int32)[:, None] < source_counts[None, :]).astype(F32)
    mix = (jnp.sum(sources.astype(F32) * chosen[:, :, None, None], axis=0) * masks[:, None, :]).astype(BF16)
    own = lax.dynamic_slice_in_dim(valid_lengths, s * NI, NI, 0)
    wider = start - DILATION + jnp.arange(F + 2 * DILATION, dtype=jnp.int32)
    own_masks = ((wider[None, :] >= 0) & (wider[None, :] < own[:, None])).astype(F32)
    own_masks = jnp.broadcast_to(own_masks[:, None, :], (NI, 8, F + 2 * DILATION))
    lanes = jnp.arange(LANES, dtype=jnp.int32)
    within = lanes % 32
    frame = start + jnp.where(within < 16, within - 2, within - 17 + F)
    edge_mask = (
        ((within < 3) | ((within >= 16) & (within < 19))) & (frame >= 0) & (frame < jnp.repeat(own, 32)[:LANES])
    ).astype(F32)
    edge_mask = jnp.broadcast_to(edge_mask[None, :], (8, LANES))
    inv_n = jnp.broadcast_to((1.0 / (own.astype(F32) * H))[:, None, None], (NI, 8, LANES))
    table = chan[0]
    gained = (w_out[0].astype(F32) * table[9][None, :]).astype(BF16)
    col = jnp.stack(
        [
            b_out[0] + jnp.sum(w_out[0].astype(F32) * table[10][None, :], axis=1),
            jnp.sum(gained.astype(F32), axis=1),
        ],
        axis=1,
    )
    block_out, skip_out, gmix, gwi, gwo, gch, gb = run(
        n_tm,
        mix,
        grad_out,
        grad_skip,
        own_masks,
        edge_mask,
        inv_n,
        w_in[0],
        w_out[0].T,
        gained,
        w_in[0].T,
        jnp.pad(table.T, ((0, 0), (0, LANES - table.shape[0]))),
        jnp.pad(col, ((0, 0), (0, LANES - 2))),
    )
    gwi, gwo, gch, gb = lax.psum((gwi, gwo, gch[:11], gb[0]), ("tm", "item"))
    grad_sources = chosen[:, :, None, None] * gmix.astype(F32)[None]
    return (block_out[None], skip_out[None], grad_sources, gwi[None], gch[None], gwo.T[None], gb[None])


def solution(mesh):
    in_specs = (
        P(None, "item", "section", "tm"),
        P("item"),
        P("item"),
        P("section", None, None),
        P("section", None, None),
        P("section", None, None),
        P("section", None),
        P("item", None, "tm"),
        P("item", None, "tm"),
    )
    out_specs = (
        P("section", "item", None, "tm"),
        P("section", "item", None, "tm"),
        P(None, "item", "section", "tm"),
        P("section", None, None),
        P("section", None, None),
        P("section", None, None),
        P("section", None),
    )
    return jax.shard_map(local, mesh=mesh, in_specs=in_specs, out_specs=out_specs, check_vma=False)
```

```python
import functools
import math

import jax
import jax.numpy as jnp
from jax import lax
from jax.experimental import pallas as pl
from jax.experimental.pallas import tpu as pltpu
from jax.sharding import PartitionSpec as P

DILATION = 128
LANES = 128
ROWS = 128
EPSILON = 1e-05
LN2 = math.log(2.0)
LOG2E = 1.0 / LN2
F32 = jnp.float32
BF16 = jnp.bfloat16
MESH = pl.DeviceIdType.MESH
NT = (((1,), (1,)), ((), ()))
NN = (((1,), (0,)), ((), ()))


def dot(a, b, dims=NN, precision=None):
    return lax.dot_general(a, b, dims, precision=precision, preferred_element_type=F32)


def remote(src, dst, send, recv, device):
    return pltpu.make_async_remote_copy(
        src_ref=src, dst_ref=dst, send_sem=send, recv_sem=recv, device_id=device, device_id_type=MESH
    )


def wide(v, width):
    return jnp.concatenate([v] * (width // LANES), axis=1)


def tall(v, rows):
    return jnp.concatenate([v] * (rows // v.shape[0]), axis=0)


def fold(v):
    parts = [v[:, at : at + LANES] for at in range(0, v.shape[1], LANES)]
    while len(parts) > 1:
        parts = [a + b for a, b in zip(parts[::2], parts[1::2])] + parts[len(parts) & ~1 :]
    return parts[0]


def fold_rows(v):
    parts = [v[at : at + 8] for at in range(0, v.shape[0], 8)]
    while len(parts) > 1:
        parts = [a + b for a, b in zip(parts[::2], parts[1::2])] + parts[len(parts) & ~1 :]
    return parts[0]


def column(table, j):
    return jnp.broadcast_to(table[:, j : j + 1], (table.shape[0], LANES))


def rows_at(t, count):
    return pl.ds(pl.multiple_of(t * count, count), count)


def kernel(
    dims,
    mix_h, gout_h, gskip_h, mask_ref, edge_mask_ref, invn_ref,
    wpre_h, wout_h, wg_h, win_h, chan_h, col_h,
    block_h, skip_h, gmix_h, gwi_h, gwo_h, gch_h, gb_h,
    x0, x1, skip0, out1, skip1, act1_0, act1_1, soft1, act2, soft2, buf, wide_s, dpre, dp, gacc,
    wpre, wout, wg, win, chan, col,
    gwi, gwo, gch, gb, rwi, rwo, rch, rb,
    stat, back, st_src, st_buf,
    edge_src, edge_in, x_edge, dp_edge, first_edge, act_edge, soft_edge, conv_edge,
    sem_w, sem_x, sem_xr, sem_g, sem_es, sem_er, sem_ss, sem_sr, sem_hs, sem_hr, sem_o, sem_or, sem_m, sem_mr,
    sem_k, sem_kr, sem_f,
):
    n_tm, NI, H, B, F = dims
    R = ROWS
    W = F + 2 * DILATION
    MID = slice(DILATION, DILATION + F)
    half = B // 2
    s = lax.axis_index("section")
    t = lax.axis_index("tm")
    o = 1 - s
    left = t - 1
    right = t + 1
    last = n_tm - 1
    first_item = s * NI
    lane = lax.broadcasted_iota(jnp.int32, (R, LANES), 1)
    lane8 = lax.broadcasted_iota(jnp.int32, (8, LANES), 1)

    edge_in[...] = jnp.zeros(edge_in.shape, BF16)

    barrier = pltpu.get_barrier_semaphore()
    pl.semaphore_signal(barrier, inc=1, device_id={"section": o}, device_id_type=MESH)

    def greet(d, c):
        to = lax.rem(t + d, n_tm)
        pl.semaphore_signal(barrier, inc=1, device_id={"tm": to}, device_id_type=MESH)
        pl.semaphore_signal(barrier, inc=1, device_id={"section": o, "tm": to}, device_id_type=MESH)
        return c

    lax.fori_loop(1, n_tm, greet, 0)
    pl.semaphore_wait(barrier, 2 * n_tm - 1)

    own_rows = pl.ds(pl.multiple_of(s * half, half), half)
    other_rows = pl.ds(pl.multiple_of(o * half, half), half)
    items_of = lambda core: pl.ds(core * NI, NI)
    centre = pl.ds(DILATION, F)
    head, tail = pl.ds(0, DILATION), pl.ds(F + DILATION, DILATION)

    main_local = pltpu.make_async_copy(mix_h.at[items_of(s)], x0.at[:, own_rows, centre], sem_x.at[0])
    main_send = remote(
        mix_h.at[items_of(o)], x0.at[:, own_rows, centre], sem_x.at[1], sem_xr.at[0], {"section": o}
    )
    main_recv = remote(
        mix_h.at[items_of(o)], x0.at[:, other_rows, centre], sem_x.at[1], sem_xr.at[0], {"section": o}
    )

    def halo_send(side, core):
        edge = pl.ds(0, DILATION) if side == 0 else pl.ds(F - DILATION, DILATION)
        place = tail if side == 0 else head
        return remote(
            mix_h.at[items_of(core), :, edge],
            x0.at[:, own_rows, place],
            sem_x.at[2 + 2 * side + core],
            sem_xr.at[1 + 2 * side + s],
            {"section": core, "tm": left if side == 0 else right},
        )

    def halo_recv(side, core):
        place = tail if side == 0 else head
        rows = pl.ds(core * half, half)
        return remote(
            x0.at[:, rows, place], x0.at[:, rows, place], sem_x.at[0], sem_xr.at[1 + 2 * side + core], {"section": o}
        )

    main_send.start()
    main_local.start()

    @pl.when(t > 0)
    def _():
        for core in (0, 1):
            halo_send(0, core).start()

    @pl.when(t < last)
    def _():
        for core in (0, 1):
            halo_send(1, core).start()

    weights = ((wpre_h, wpre), (wout_h, wout), (wg_h, wg), (win_h, win), (chan_h, chan), (col_h, col))

    def weight_copies(j):
        src, dst = weights[j]
        return (
            pltpu.make_async_copy(src, dst.at[s], sem_w.at[j, 0]),
            remote(src, dst.at[s], sem_w.at[j, 1], sem_w.at[j, 2], {"section": o}),
            remote(src, dst.at[o], sem_w.at[j, 1], sem_w.at[j, 2], {"section": o}),
        )

    for j in range(len(weights)):
        local, send, _ = weight_copies(j)
        send.start()
        local.start()
    load_out = pltpu.make_async_copy(gout_h.at[items_of(s)], dp.at[:, pl.ds(0, B)], sem_g.at[0])
    load_skip = pltpu.make_async_copy(gskip_h.at[items_of(s)], dp.at[:, pl.ds(B, B)], sem_g.at[1])
    load_out.start()
    load_skip.start()

    @pl.when(t == 0)
    def _():
        x0[:, :, 0:DILATION] = jnp.zeros((NI, B, DILATION), BF16)

    @pl.when(t == last)
    def _():
        x0[:, :, F + DILATION : W] = jnp.zeros((NI, B, DILATION), BF16)

    for j in range(2):
        gwi[j] = jnp.zeros((H, B), F32)
        gwo[j] = jnp.zeros((H, 2 * B), F32)
        gb[j] = jnp.zeros((8, 2 * B), F32)

    def stat_copy(ph, i, d, to):
        p = ph % 2
        return remote(
            st_src.at[p, i], st_buf.at[p, i, d - 1], sem_ss.at[p, i, d - 1], sem_sr.at[p, i, d - 1], {"tm": to}
        )

    def send_stats(ph, i, a, b):
        rows = [jnp.sum(a, axis=0, keepdims=True), jnp.sum(b, axis=0, keepdims=True)]
        st_src[ph % 2, i] = jnp.concatenate(rows + [jnp.zeros((6, LANES), F32)], axis=0)

        def one(d, c):
            stat_copy(ph, i, d, lax.rem(t + d, n_tm)).start()
            return c

        lax.fori_loop(1, n_tm, one, 0)

    def recv_stats(ph, i):
        def one(d, total):
            copy = stat_copy(ph, i, d, lax.rem(t + d, n_tm))
            copy.wait_send()
            copy.wait_recv()
            return total + st_buf[ph % 2, i, d - 1]

        total = lax.fori_loop(1, n_tm, one, st_src[ph % 2, i])
        sums = jnp.sum(total, axis=1, keepdims=True)
        return (
            jnp.broadcast_to(sums[0:1], (8, LANES)),
            jnp.broadcast_to(sums[1:2], (8, LANES)),
        )

    def finish_norm(ph, slot, i):
        a, b = recv_stats(ph, i)
        inv_n = invn_ref[i]
        mean = a * inv_n
        spread = jnp.maximum(b * inv_n - mean * mean, 0.0)
        stat[slot, i, 0] = mean
        stat[slot, i, 1] = lax.rsqrt(spread + EPSILON / (LN2 * LN2))

    def finish_back(ph, slot, i):
        a, b = recv_stats(ph, i)
        inv_n = invn_ref[i]
        mean, inv = stat[slot, i, 0], stat[slot, i, 1]
        q = b * inv_n * inv
        back[i, 0] = (mean * q - a * inv_n) * (inv * LOG2E)
        back[i, 1] = -q * (inv * LOG2E)

    def lanes_of(ref, j):
        out = ref[0, j]
        for i in range(1, NI):
            out = jnp.where(lane8 >= 32 * i, ref[i, j], out)
        return out

    def per_item(body):
        lax.fori_loop(0, NI, lambda i, c: (body(i), c)[1], 0)

    def per_tile(body, count=H, rows=R, init=0):
        return lax.fori_loop(0, count // rows, lambda j, c: body(rows_at(j, rows), c), init)

    def mask_row(i, rows, at=DILATION, width=F):
        return tall(mask_ref[i, :, at : at + width], rows)

    zero8 = jnp.zeros((8, LANES), F32)

    def pack_edges(src, channels, slot):
        def tile(r, c):
            to_left = to_right = own = jnp.zeros((R, LANES), F32)
            for i in range(NI):
                a = src[i, r, 0:LANES].astype(F32)
                z = src[i, r, F - LANES : F].astype(F32)
                base = 32 * i
                to_left += jnp.where(
                    (lane == base + 17) | (lane == base + 18), pltpu.roll(a, base + 17, 1), 0.0
                )
                to_right += jnp.where(
                    (lane == base) | (lane == base + 1), pltpu.roll(z, base + 2, 1), 0.0
                )
                own += jnp.where(lane == base + 2, pltpu.roll(a, base + 2, 1), 0.0)
                own += jnp.where(lane == base + 16, pltpu.roll(z, base + 17, 1), 0.0)
            edge_src[slot, 0, r, :] = to_left.astype(BF16)
            edge_src[slot, 1, r, :] = to_right.astype(BF16)
            edge_src[slot, 2, r, :] = own.astype(BF16)
            return c

        per_tile(tile, channels)

    def edge_copy(slot, side, channels):
        rows = pl.ds(0, channels)
        return remote(
            edge_src.at[slot, side, rows],
            edge_in.at[slot, side, rows],
            sem_es.at[slot, side],
            sem_er.at[slot, side],
            {"tm": left if side == 0 else right},
        )

    def send_edges(slot, channels):
        @pl.when(t > 0)
        def _():
            edge_copy(slot, 0, channels).start()

        @pl.when(t < last)
        def _():
            edge_copy(slot, 1, channels).start()

    def recv_edges(slot, channels, dst):
        @pl.when(t > 0)
        def _():
            edge_copy(slot, 0, channels).wait_send()
            edge_copy(slot, 1, channels).wait_recv()

        @pl.when(t < last)
        def _():
            edge_copy(slot, 1, channels).wait_send()
            edge_copy(slot, 0, channels).wait_recv()

        def tile(r, c):
            total = edge_src[slot, 2, r, :].astype(F32)
            for side in (0, 1):
                total += edge_in[slot, side, r, :].astype(F32)
            dst[r, :] = total.astype(BF16)
            return c

        per_tile(tile, channels)

    def rectify(neg, rest):
        soft = jnp.maximum(neg, jnp.log2(1.0 + jnp.exp2(jnp.minimum(neg, 100.0))))
        return rest * soft - neg, soft

    def masked_sums(a, m, sums):
        am = a * m
        return (sums[0] + fold_rows(fold(am)), sums[1] + fold_rows(fold(am * a)))

    def phase1(k):
        width = W if k == 0 else F
        x = x0 if k == 0 else x1
        act = act1_0 if k == 0 else act1_1
        mid = MID if k == 0 else slice(0, F)

        def item(i):
            wide_s[:, 0:width] = dot(wpre[k], x[i])
            m = mask_row(i, R)

            def tile(r, sums):
                table = chan[k, r, :]
                bias = column(table, 0) * -LOG2E
                rest = 1.0 - column(table, 1)
                neg = wide_s[r, 0:width] * -LOG2E + wide(bias, width)
                a, soft = rectify(neg, wide(rest, width))
                act[i, r, :] = a.astype(BF16)
                soft1[k, i, r, :] = soft[:, mid].astype(BF16)
                return masked_sums(a[:, mid], m, sums)

            a, b = per_tile(tile, init=(zero8, zero8))
            send_stats(4 * k, i, a, b)

        per_item(item)
        if k == 1:
            recv_edges(1, B, x_edge)
            wide_s[:, 0:LANES] = dot(wpre[1], x_edge[...])

            def tile(r, c):
                table = chan[1, r, :]
                neg = wide_s[r, 0:LANES] * -LOG2E + column(table, 0) * -LOG2E
                a, _ = rectify(neg, 1.0 - column(table, 1))
                wide_s[r, 0:LANES] = a
                return c

            per_tile(tile)

    def phase2(k):
        width = W if k == 0 else F
        at = 0 if k == 0 else DILATION
        act = act1_0 if k == 0 else act1_1

        def item(i):
            finish_norm(4 * k, 2 * k, i)
            mean, inv = tall(stat[2 * k, i, 0], R), tall(stat[2 * k, i, 1], R)
            m = mask_row(i, R, at, width)

            def tile(r, c):
                table = chan[k, r, :]
                scale = inv * column(table, 2)
                shift = column(table, 3) - mean * scale
                a = act[i, r, :].astype(F32)
                buf[i, r, at : at + width] = (
                    (a * wide(scale, width) + wide(shift, width)) * m
                ).astype(BF16)
                return c

            per_tile(tile)

        per_item(item)
        if k == 1:
            mean, inv = tall(lanes_of(stat.at[2], 0), R), tall(lanes_of(stat.at[2], 1), R)
            m = tall(edge_mask_ref[...], R)

            def tile(r, c):
                table = chan[1, r, :]
                scale = inv * column(table, 2)
                a = wide_s[r, 0:LANES]
                first_edge[r, :] = (((a - mean) * scale + column(table, 3)) * m).astype(BF16)
                return c

            per_tile(tile)

    def neighbours(f, edge, i):
        shifted_in = pltpu.roll(edge, lax.rem(127 - 32 * i + 256, 128), 1)
        before = pltpu.roll(f, 1, 1)
        lead = jnp.where(lane == 0, shifted_in, before[:, 0:LANES])
        before = jnp.concatenate([lead, before[:, LANES:]], axis=1)
        shifted_in = pltpu.roll(edge, lax.rem(110 - 32 * i + 256, 128), 1)
        after = pltpu.roll(f, F - 1, 1)
        trail = jnp.where(lane == LANES - 1, shifted_in, after[:, F - LANES :])
        after = jnp.concatenate([after[:, : F - LANES], trail], axis=1)
        return before, after

    def taps(k, i, r, edge):
        f = buf[i, r, MID].astype(F32)
        if k == 0:
            return buf[i, r, 0:F].astype(F32), f, buf[i, r, 2 * DILATION : W].astype(F32)
        before, after = neighbours(f, edge[r, :].astype(F32), i)
        return before, f, after

    def conv_coefs(table):
        return [column(table, j) * -LOG2E for j in (4, 5, 6, 7)], 1.0 - column(table, 8)

    def phase3(k):
        def item(i):
            m = mask_row(i, R)

            def tile(r, sums):
                c, rest = conv_coefs(chan[k, r, :])
                before, f, after = taps(k, i, r, first_edge)
                neg = wide(c[0], F) * before + wide(c[1], F) * f + wide(c[2], F) * after + wide(c[3], F)
                a, soft = rectify(neg, wide(rest, F))
                act2[k, i, r, :] = a.astype(BF16)
                soft2[k, i, r, :] = soft.astype(BF16)
                return masked_sums(a, m, sums)

            a, b = per_tile(tile, init=(zero8, zero8))
            send_stats(4 * k + 1, i, a, b)

        per_item(item)
        if k == 1:

            def tile(r, x):
                c, rest = conv_coefs(chan[1, r, :])
                f = first_edge[r, :].astype(F32)
                neg = c[0] * pltpu.roll(f, 1, 1) + c[1] * f + c[2] * pltpu.roll(f, LANES - 1, 1) + c[3]
                a, soft = rectify(neg, rest)
                act_edge[r, :] = a.astype(BF16)
                soft_edge[r, :] = soft.astype(BF16)
                return x

            per_tile(tile)

    def out_copy(kind, k, i, src):
        dst = (block_h, skip_h)[kind]
        row = first_item + i
        return (
            pltpu.make_async_copy(src.at[i], dst.at[row], sem_o.at[kind, k, i]),
            remote(src.at[i], dst.at[row], sem_o.at[kind, k, i], sem_or.at[kind, i], {"section": o}),
        )

    def phase4(k):
        x = x0 if k == 0 else x1
        mid = MID if k == 0 else slice(0, F)
        out = x1 if k == 0 else out1
        skip = skip0 if k == 0 else skip1

        def item(i):
            finish_norm(4 * k + 1, 2 * k + 1, i)
            mean, inv = tall(stat[2 * k + 1, i, 0], R), tall(stat[2 * k + 1, i, 1], R)
            m = mask_row(i, R)
            y = pl.ds(0, 2 * B)
            wide_s[y, 0:F] = dot(wg[k], act2[k, i])

            def project(r):
                table = col[k, r, :]
                shift = column(table, 0) - mean * inv * column(table, 1)
                return (wide_s[r, 0:F] * wide(inv, F) + wide(shift, F)) * m

            def residual(r, c):
                out[i, r, :] = (x[i, r, mid].astype(F32) + project(r)).astype(BF16)
                return c

            def skipped(j, c):
                r = rows_at(j, R)
                p = project(pl.ds(pl.multiple_of(B + j * R, R), R))
                if k == 1:
                    p += skip0[i, r, :].astype(F32)
                skip[i, r, :] = p.astype(BF16)
                return c

            per_tile(residual, B)
            lax.fori_loop(0, B // R, skipped, 0)
            for kind, src in ((0, out), (1, skip)):
                here, there = out_copy(kind, k, i, src)

                @pl.when(s == k)
                def _():
                    here.start()

                @pl.when(s != k)
                def _():
                    there.start()

        per_item(item)

    def phase5(k):
        R5 = 4 * R

        def item(i):
            mean, inv = tall(stat[2 * k + 1, i, 0], R5), tall(stat[2 * k + 1, i, 1], R5)
            wide_s[:, 0 : 2 * B] = dot(act2[k, i], dp[i], NT)
            total8 = dot(jnp.ones((8, F), BF16), dp[i], NT)
            gb[k] += total8
            total = tall(total8, R5)

            def tile(r, sums):
                table = chan[k, r, :]
                g, e = column(table, 9), column(table, 10)
                product = wide_s[r, 0 : 2 * B]
                w = wout[k, r, :].astype(F32)
                against = fold(w * product)
                plain = fold(w * total)
                normed = inv * (against - mean * plain)
                gacc[9, r, :] += normed
                gacc[10, r, :] += plain
                scale = inv * g
                shift = e - mean * scale
                gwo[k, r, :] += wide(scale, 2 * B) * product + wide(shift, 2 * B) * total
                return (sums[0] + fold_rows(g * plain), sums[1] + fold_rows(g * normed))

            a, b = per_tile(tile, rows=R5, init=(zero8, zero8))
            send_stats(4 * k + 2, i, a, b)

        per_item(item)

    def halo_copy(i, side):
        edge = pl.ds(DILATION, DILATION) if side == 0 else pl.ds(F, DILATION)
        return remote(
            buf.at[i, :, edge],
            buf.at[i, :, tail if side == 0 else head],
            sem_hs.at[side, i],
            sem_hr.at[side, i],
            {"tm": left if side == 0 else right},
        )

    def phase6(k):
        def item(i):
            finish_back(4 * k + 2, 2 * k + 1, i)
            inv = tall(stat[2 * k + 1, i, 1], R) * LOG2E
            p, q = wide(tall(back[i, 0], R), F), wide(tall(back[i, 1], R), F)
            m = mask_row(i, R)
            wide_s[:, 0:F] = dot(wout[k], dp[i])

            def tile(r, c):
                table = chan[k, r, :]
                slope = column(table, 8)
                g = inv * column(table, 9)
                d_act = wide_s[r, 0:F] * wide(g, F) + m * (p + q * act2[k, i, r, :].astype(F32))
                soft = soft2[k, i, r, :].astype(F32)
                d_conv = d_act * (wide(slope, F) + wide(1.0 - slope, F) * jnp.exp2(-soft))
                gacc[8, r, :] += fold(d_act * soft) * -LN2
                gacc[7, r, :] += fold(d_conv)
                buf[i, r, MID] = d_conv.astype(BF16)
                return c

            per_tile(tile)
            if k == 0:

                @pl.when(t > 0)
                def _():
                    halo_copy(i, 0).start()

                @pl.when(t < last)
                def _():
                    halo_copy(i, 1).start()

                @pl.when(t == 0)
                def _():
                    buf[i, :, 0:DILATION] = jnp.zeros((H, DILATION), BF16)

                @pl.when(t == last)
                def _():
                    buf[i, :, F + DILATION : W] = jnp.zeros((H, DILATION), BF16)

        per_item(item)
        if k == 1:
            wide_s[:, 0:LANES] = dot(wout[1], dp_edge[...])
            inv = tall(lanes_of(stat.at[3], 1), R) * LOG2E
            p, q = tall(lanes_of(back, 0), R), tall(lanes_of(back, 1), R)
            m = tall(edge_mask_ref[...], R)

            def tile(r, c):
                table = chan[1, r, :]
                slope = column(table, 8)
                d_act = wide_s[r, 0:LANES] * (inv * column(table, 9)) + m * (p + q * act_edge[r, :].astype(F32))
                d_conv = d_act * (slope + (1.0 - slope) * jnp.exp2(-soft_edge[r, :].astype(F32)))
                conv_edge[r, :] = d_conv.astype(BF16)
                return c

            per_tile(tile)

    def phase7(k):
        act = act1_0 if k == 0 else act1_1
        mid = MID if k == 0 else slice(0, F)

        def item(i):
            if k == 0:

                @pl.when(t > 0)
                def _():
                    halo_copy(i, 0).wait_send()
                    halo_copy(i, 1).wait_recv()

                @pl.when(t < last)
                def _():
                    halo_copy(i, 1).wait_send()
                    halo_copy(i, 0).wait_recv()

            mean, inv = tall(stat[2 * k, i, 0], R), tall(stat[2 * k, i, 1], R)
            m = mask_row(i, R)

            def tile(r, sums):
                table = chan[k, r, :]
                g = column(table, 2)
                scale = inv * g
                shift = column(table, 3) - mean * scale
                before, d, after = taps(k, i, r, conv_edge)
                u = (
                    wide(column(table, 4), F) * after
                    + wide(column(table, 5), F) * d
                    + wide(column(table, 6), F) * before
                ) * m
                a = act[i, r, mid].astype(F32)
                first = (a * wide(scale, F) + wide(shift, F)) * m
                plain = fold(u)
                normed = inv * (fold(u * a) - mean * plain)
                gacc[2, r, :] += normed
                gacc[3, r, :] += plain
                gacc[4, r, :] += fold(after * first)
                gacc[5, r, :] += fold(d * first)
                gacc[6, r, :] += fold(before * first)
                soft2[k, i, r, :] = u.astype(BF16)
                return (sums[0] + fold_rows(g * plain), sums[1] + fold_rows(g * normed))

            a, b = per_tile(tile, init=(zero8, zero8))
            send_stats(4 * k + 3, i, a, b)

        per_item(item)

    def mix_copy(i):
        row = first_item + i
        return (
            pltpu.make_async_copy(out1.at[i, own_rows], gmix_h.at[row], sem_m.at[0, i]),
            remote(out1.at[i, other_rows], gmix_h.at[row], sem_m.at[1, i], sem_mr.at[i], {"section": o}),
        )

    def phase8(k):
        act = act1_0 if k == 0 else act1_1
        x = x0 if k == 0 else x1
        mid = MID if k == 0 else slice(0, F)

        def item(i):
            finish_back(4 * k + 3, 2 * k, i)
            inv = tall(stat[2 * k, i, 1], R) * LOG2E
            p, q = wide(tall(back[i, 0], R), F), wide(tall(back[i, 1], R), F)
            m = mask_row(i, R)

            def tile(r, c):
                table = chan[k, r, :]
                slope = column(table, 1)
                g = inv * column(table, 2)
                d_act = soft2[k, i, r, :].astype(F32) * wide(g, F) + m * (p + q * act[i, r, mid].astype(F32))
                soft = soft1[k, i, r, :].astype(F32)
                d_pre = d_act * (wide(slope, F) + wide(1.0 - slope, F) * jnp.exp2(-soft))
                gacc[1, r, :] += fold(d_act * soft) * -LN2
                gacc[0, r, :] += fold(d_pre)
                dpre[r, :] = d_pre.astype(BF16)
                return c

            per_tile(tile)
            gwi[k] += dot(dpre[...], x[i, :, mid], NT)
            wide_s[0:B, 0:F] = dot(win[k], dpre[...])

            def add(r, c):
                d_input = wide_s[r, 0:F] + dp[i, r, :].astype(F32)
                if k == 1:
                    dp[i, r, :] = (d_input * m).astype(BF16)
                else:
                    out1[i, r, :] = (d_input * m).astype(BF16)
                return c

            per_tile(add, B)
            if k == 0:
                here, there = mix_copy(i)
                there.start()
                here.start()

        per_item(item)

    grads = ((gwi, rwi, gwi_h), (gwo, rwo, gwo_h), (gch, rch, gch_h), (gb, rb, gb_h))

    def grad_copy(j, k):
        own, there, _ = grads[j]
        return remote(own.at[k], there, sem_k.at[j], sem_kr.at[j], {"section": o})

    def finish_block(k):
        ones = jnp.ones((8, LANES), F32)
        gch[k] = jnp.concatenate(
            [dot(ones, gacc[j], NT, lax.Precision.HIGHEST)[0:1] for j in range(11)] + [jnp.zeros((5, H), F32)], axis=0
        )

        @pl.when(s != k)
        def _():
            for j in range(4):
                grad_copy(j, k).start()

    for j in range(len(weights)):
        local, send, recv = weight_copies(j)
        local.wait()
        recv.wait_recv()
        send.wait_send()
    main_local.wait()
    main_send.wait_send()
    main_recv.wait_recv()

    @pl.when(t > 0)
    def _():
        for core in (0, 1):
            halo_send(0, core).wait_send()
            halo_recv(1, core).wait_recv()

    @pl.when(t < last)
    def _():
        for core in (0, 1):
            halo_send(1, core).wait_send()
            halo_recv(0, core).wait_recv()

    phase1(0)
    load_out.wait()
    load_skip.wait()

    def mask_gradients(i):
        m = mask_row(i, R)

        def tile(r, c):
            dp[i, r, :] = (dp[i, r, :].astype(F32) * m).astype(BF16)
            return c

        per_tile(tile, 2 * B)

    per_item(mask_gradients)
    pack_edges(dp, 2 * B, 0)
    send_edges(0, 2 * B)
    phase2(0)
    phase3(0)
    phase4(0)
    pack_edges(x1, B, 1)
    send_edges(1, B)
    phase1(1)
    phase2(1)
    phase3(1)
    phase4(1)
    recv_edges(0, 2 * B, dp_edge)
    for k in (1, 0):
        gacc[...] = jnp.zeros(gacc.shape, F32)
        phase5(k)
        phase6(k)
        phase7(k)
        if k == 0:
            for i in range(NI):
                here, there = out_copy(0, 1, i, out1)

                @pl.when(s == 1)
                def _():
                    here.wait()

                @pl.when(s == 0)
                def _():
                    there.wait_send()

        phase8(k)
        finish_block(k)

    for k in (0, 1):

        @pl.when(s != k)
        def _():
            for j in range(4):
                grad_copy(j, k).wait_send()

        @pl.when(s == k)
        def _():
            for j in range(4):
                grad_copy(j, k).wait_recv()
                own, there, _ = grads[j]
                own[k] += there[...]
            for j in range(4):
                own, _, result = grads[j]
                pltpu.make_async_copy(own.at[k], result, sem_f.at[j]).start()
            for j in range(4):
                own, _, result = grads[j]
                pltpu.make_async_copy(own.at[k], result, sem_f.at[j]).wait()

    for i in range(NI):
        here, there = mix_copy(i)
        here.wait()
        there.wait_send()
        remote(
            out1.at[i, other_rows], gmix_h.at[o * NI + i], sem_m.at[1, i], sem_mr.at[i], {"section": o}
        ).wait_recv()
        for kind, srcs in ((0, (x1, out1)), (1, (skip0, skip1))):
            for k in (0, 1):
                here, there = out_copy(kind, k, i, srcs[k])

                if (kind, k) != (0, 1):

                    @pl.when(s == k)
                    def _():
                        here.wait()

                    @pl.when(s != k)
                    def _():
                        there.wait_send()

            dst = (block_h, skip_h)[kind]
            remote(
                srcs[0].at[i], dst.at[o * NI + i], sem_o.at[kind, 0, i], sem_or.at[kind, i], {"section": o}
            ).wait_recv()


def run(n_tm, mix, gout, gskip, masks, edge_mask, inv_n, wpre, wout, wg, win, chan, col):
    items, half, F = mix.shape
    NI = items // 2
    H, B = wpre.shape
    W = F + 2 * DILATION
    any_spec = pl.BlockSpec(memory_space=pl.ANY)
    vmem = pl.BlockSpec(memory_space=pltpu.VMEM)
    dma = pltpu.SemaphoreType.DMA
    shape = jax.ShapeDtypeStruct
    outs = (
        shape((items, B, F), BF16),
        shape((items, B, F), BF16),
        shape((items, half, F), BF16),
        shape((H, B), F32),
        shape((H, 2 * B), F32),
        shape((16, H), F32),
        shape((8, 2 * B), F32),
    )
    scratch = [
        pltpu.VMEM((NI, B, W), BF16),
        pltpu.VMEM((NI, B, F), BF16),
        pltpu.VMEM((NI, B, F), BF16),
        pltpu.VMEM((NI, B, F), BF16),
        pltpu.VMEM((NI, B, F), BF16),
        pltpu.VMEM((NI, H, W), BF16),
        pltpu.VMEM((NI, H, F), BF16),
        pltpu.VMEM((2, NI, H, F), BF16),
        pltpu.VMEM((2, NI, H, F), BF16),
        pltpu.VMEM((2, NI, H, F), BF16),
        pltpu.VMEM((NI, H, W), BF16),
        pltpu.VMEM((H, W), F32),
        pltpu.VMEM((H, F), BF16),
        pltpu.VMEM((NI, 2 * B, F), BF16),
        pltpu.VMEM((11, H, LANES), F32),
        pltpu.VMEM((2, H, B), BF16),
        pltpu.VMEM((2, H, 2 * B), BF16),
        pltpu.VMEM((2, 2 * B, H), BF16),
        pltpu.VMEM((2, B, H), BF16),
        pltpu.VMEM((2, H, LANES), F32),
        pltpu.VMEM((2, 2 * B, LANES), F32),
        pltpu.VMEM((2, H, B), F32),
        pltpu.VMEM((2, H, 2 * B), F32),
        pltpu.VMEM((2, 16, H), F32),
        pltpu.VMEM((2, 8, 2 * B), F32),
        pltpu.VMEM((H, B), F32),
        pltpu.VMEM((H, 2 * B), F32),
        pltpu.VMEM((16, H), F32),
        pltpu.VMEM((8, 2 * B), F32),
        pltpu.VMEM((4, NI, 2, 8, LANES), F32),
        pltpu.VMEM((NI, 2, 8, LANES), F32),
        pltpu.VMEM((2, NI, 8, LANES), F32),
        pltpu.VMEM((2, NI, n_tm - 1, 8, LANES), F32),
        pltpu.VMEM((2, 3, 2 * B, LANES), BF16),
        pltpu.VMEM((2, 2, 2 * B, LANES), BF16),
        pltpu.VMEM((B, LANES), BF16),
        pltpu.VMEM((2 * B, LANES), BF16),
        pltpu.VMEM((H, LANES), BF16),
        pltpu.VMEM((H, LANES), BF16),
        pltpu.VMEM((H, LANES), BF16),
        pltpu.VMEM((H, LANES), BF16),
        dma((6, 3)),
        dma((6,)),
        dma((5,)),
        dma((2,)),
        dma((2, 2)),
        dma((2, 2)),
        dma((2, NI, n_tm - 1)),
        dma((2, NI, n_tm - 1)),
        dma((2, NI)),
        dma((2, NI)),
        dma((2, 2, NI)),
        dma((2, NI)),
        dma((2, NI)),
        dma((NI,)),
        dma((4,)),
        dma((4,)),
        dma((4,)),
    ]
    return pl.pallas_call(
        functools.partial(kernel, (n_tm, NI, H, B, F)),
        out_shape=outs,
        in_specs=[any_spec] * 3 + [vmem] * 3 + [any_spec] * 6,
        out_specs=[any_spec] * len(outs),
        scratch_shapes=scratch,
        compiler_params=pltpu.CompilerParams(
            collective_id=0, has_side_effects=True, vmem_limit_bytes=63 * 1024 * 1024
        ),
        name="temporal_blocks",
    )(mix, gout, gskip, masks, edge_mask, inv_n, wpre, wout, wg, win, chan, col)


def local(sources, source_counts, valid_lengths, w_in, chan, w_out, b_out, grad_out, grad_skip):
    n_sources, per_device, half, F = sources.shape
    H, B = w_in.shape[1:]
    NI = per_device // 2
    n_tm = lax.axis_size("tm")
    s = lax.axis_index("section")
    start = lax.axis_index("tm") * F
    where = start + jnp.arange(F, dtype=jnp.int32)
    masks = (where[None, :] < valid_lengths[:, None]).astype(F32)
    chosen = (jnp.arange(n_sources, dtype=jnp.int32)[:, None] < source_counts[None, :]).astype(F32)
    mix = (jnp.sum(sources.astype(F32) * chosen[:, :, None, None], axis=0) * masks[:, None, :]).astype(BF16)
    own = lax.dynamic_slice_in_dim(valid_lengths, s * NI, NI, 0)
    wider = start - DILATION + jnp.arange(F + 2 * DILATION, dtype=jnp.int32)
    own_masks = ((wider[None, :] >= 0) & (wider[None, :] < own[:, None])).astype(F32)
    own_masks = jnp.broadcast_to(own_masks[:, None, :], (NI, 8, F + 2 * DILATION))
    lanes = jnp.arange(LANES, dtype=jnp.int32)
    within = lanes % 32
    frame = start + jnp.where(within < 16, within - 2, within - 17 + F)
    edge_mask = (
        ((within < 3) | ((within >= 16) & (within < 19))) & (frame >= 0) & (frame < jnp.repeat(own, 32)[:LANES])
    ).astype(F32)
    edge_mask = jnp.broadcast_to(edge_mask[None, :], (8, LANES))
    inv_n = jnp.broadcast_to((1.0 / (own.astype(F32) * H))[:, None, None], (NI, 8, LANES))
    table = chan[0]
    gained = (w_out[0].astype(F32) * table[9][None, :]).astype(BF16)
    col = jnp.stack(
        [
            b_out[0] + jnp.sum(w_out[0].astype(F32) * table[10][None, :], axis=1),
            jnp.sum(gained.astype(F32), axis=1),
        ],
        axis=1,
    )
    block_out, skip_out, gmix, gwi, gwo, gch, gb = run(
        n_tm,
        mix,
        grad_out,
        grad_skip,
        own_masks,
        edge_mask,
        inv_n,
        w_in[0],
        w_out[0].T,
        gained,
        w_in[0].T,
        jnp.pad(table.T, ((0, 0), (0, LANES - table.shape[0]))),
        jnp.pad(col, ((0, 0), (0, LANES - 2))),
    )
    gwi, gwo, gch, gb = lax.psum((gwi, gwo, gch[:11], gb[0]), ("tm", "item"))
    grad_sources = chosen[:, :, None, None] * gmix.astype(F32)[None]
    return (block_out[None], skip_out[None], grad_sources, gwi[None], gch[None], gwo.T[None], gb[None])


def solution(mesh):
    in_specs = (
        P(None, "item", "section", "tm"),
        P("item"),
        P("item"),
        P("section", None, None),
        P("section", None, None),
        P("section", None, None),
        P("section", None),
        P("item", None, "tm"),
        P("item", None, "tm"),
    )
    out_specs = (
        P("section", "item", None, "tm"),
        P("section", "item", None, "tm"),
        P(None, "item", "section", "tm"),
        P("section", None, None),
        P("section", None, None),
        P("section", None, None),
        P("section", None),
    )
    return jax.shard_map(local, mesh=mesh, in_specs=in_specs, out_specs=out_specs, check_vma=False)
```

```python
import functools
import math

import jax
import jax.numpy as jnp
from jax import lax
from jax.experimental import pallas as pl
from jax.experimental.pallas import tpu as pltpu
from jax.sharding import PartitionSpec as P

DILATION = 128
LANES = 128
ROWS = 128
ROWS1 = 512
ROWS2 = 512
ROWS3 = 512
ROWS4 = 128
ROWS5 = 512
ROWS6 = 512
ROWS7 = 256
ROWS8 = 512
EPSILON = 1e-05
VMEM_LIMIT = 63 * 1024 * 1024 + 512 * 1024
LN2 = math.log(2.0)
LOG2E = 1.0 / LN2
F32 = jnp.float32
BF16 = jnp.bfloat16
MESH = pl.DeviceIdType.MESH
NT = (((1,), (1,)), ((), ()))
NN = (((1,), (0,)), ((), ()))


def dot(a, b, dims=NN, precision=None):
    return lax.dot_general(a, b, dims, precision=precision, preferred_element_type=F32)


def remote(src, dst, send, recv, device):
    return pltpu.make_async_remote_copy(
        src_ref=src, dst_ref=dst, send_sem=send, recv_sem=recv, device_id=device, device_id_type=MESH
    )


def wide(v, width):
    return jnp.concatenate([v] * (width // LANES), axis=1)


def tall(v, rows):
    return jnp.concatenate([v] * (rows // v.shape[0]), axis=0)


def fold(v):
    parts = [v[:, at : at + LANES] for at in range(0, v.shape[1], LANES)]
    while len(parts) > 1:
        parts = [a + b for a, b in zip(parts[::2], parts[1::2])] + parts[len(parts) & ~1 :]
    return parts[0]


def fold_rows(v):
    parts = [v[at : at + 8] for at in range(0, v.shape[0], 8)]
    while len(parts) > 1:
        parts = [a + b for a, b in zip(parts[::2], parts[1::2])] + parts[len(parts) & ~1 :]
    return parts[0]


def low(v):
    return v.astype(BF16)


def column(table, j):
    return jnp.broadcast_to(table[:, j : j + 1], (table.shape[0], LANES))


def rows_at(t, count):
    return pl.ds(pl.multiple_of(t * count, count), count)


def kernel(
    dims,
    sources_h, gout_h, gskip_h, w_in_ref, chan_ref, w_out_ref, b_out_ref, counts, lengths,
    block_h, skip_h, gmix_h, grad_h,
    stage, x0, x1, skips, act1_0, act1_1, soft1, act2, soft2, buf, wide_s, dp, gacc,
    wpre, wout, wg, win, chan, col,
    grad, bias_sum, came0, came1, from_item0, from_item1, from_tm0, from_tm1,
    mask_ref, edge_mask_ref, invn_ref, stat, back, st_src, st_buf,
    edge_src, edge_in, x_edge, dp_edge, first_edge, act_edge, soft_edge, conv_edge,
    sem_s, sem_w, sem_x, sem_xr, sem_g, sem_es, sem_er, sem_ss, sem_sr, sem_hs, sem_hr, sem_o, sem_or, sem_m, sem_mr,
    sem_k, sem_kr, sem_ri, sem_rir, sem_rt, sem_rtr, sem_at, sem_atr, sem_ai, sem_air, sem_f,
):
    n_tm, n_item, NI, H, B, F = dims
    R = ROWS
    W = F + 2 * DILATION
    MID = slice(DILATION, DILATION + F)
    half = B // 2
    s = lax.axis_index("section")
    t = lax.axis_index("tm")
    o = 1 - s
    left = t - 1
    right = t + 1
    last = n_tm - 1
    first_item = s * NI
    lane = lax.broadcasted_iota(jnp.int32, (R, LANES), 1)
    lane8 = lax.broadcasted_iota(jnp.int32, (8, LANES), 1)

    it = lax.axis_index("item")
    members = n_tm * n_item
    me = t * n_item + it
    n_src = sources_h.shape[0]

    def load_source(n):
        return pltpu.make_async_copy(sources_h.at[n], soft2.at[1, n], sem_s.at[n])

    for n in range(n_src):
        load_source(n).start()
    load_out = pltpu.make_async_copy(gout_h.at[pl.ds(first_item, NI)], dp.at[:, pl.ds(0, B)], sem_g.at[0])
    load_skip = pltpu.make_async_copy(gskip_h.at[pl.ds(first_item, NI)], dp.at[:, pl.ds(B, B)], sem_g.at[1])
    load_out.start()
    load_skip.start()
    edge_in[...] = jnp.zeros(edge_in.shape, BF16)

    barrier = pltpu.get_barrier_semaphore()

    def greet(d, c):
        peer = lax.rem(me + d, members)
        device = {"tm": peer // n_item, "item": lax.rem(peer, n_item)}
        pl.semaphore_signal(barrier, inc=1, device_id=device, device_id_type=MESH)
        return c

    def greet_other(d, c):
        device = {"section": o, "tm": lax.rem(t + d, n_tm)}
        pl.semaphore_signal(barrier, inc=1, device_id=device, device_id_type=MESH)
        return c

    lax.fori_loop(1, members, greet, 0)
    lax.fori_loop(0, n_tm, greet_other, 0)

    w_in = w_in_ref[...]
    w_out = w_out_ref[...].astype(F32)
    wpre[s] = w_in
    win[s] = w_in.astype(F32).T.astype(BF16)
    wout[s] = w_out.T.astype(BF16)
    gained = (w_out * chan_ref[9]).astype(BF16)
    wg[s] = gained
    wide_s[0:LANES, 0:H] = jnp.zeros((LANES, H), F32)
    for j in range(chan_ref.shape[0]):
        wide_s[j : j + 1, 0:H] = chan_ref[j]
    chan[s] = wide_s[0:LANES, 0:H].T
    bias = jnp.broadcast_to(b_out_ref[...], (LANES, 2 * B)).T
    bias += jnp.sum(w_out * chan_ref[10], axis=1, keepdims=True)
    gain = jnp.sum(gained.astype(F32), axis=1, keepdims=True)
    lane_w = lax.broadcasted_iota(jnp.int32, (2 * B, LANES), 1)
    col[s] = jnp.where(lane_w == 0, bias, gain)

    for i in range(NI):
        length = lengths[first_item + i]
        where = lax.broadcasted_iota(jnp.int32, (8, W), 1) + (t * F - DILATION)
        mask_ref[i] = jnp.where((where >= 0) & (where < length), 1.0, 0.0)
        invn_ref[i] = 1.0 / (jnp.full((8, LANES), length, jnp.int32).astype(F32) * H)
    within = lane8 % 32
    frame = t * F + jnp.where(within < 16, within - 2, within - 17 + F)
    length = jnp.full((8, LANES), lengths[first_item], jnp.int32)
    for i in range(1, NI):
        length = jnp.where(lane8 >= 32 * i, lengths[first_item + i], length)
    held = (within < 3) | ((within >= 16) & (within < 19))
    edge_mask_ref[...] = jnp.where(held & (frame >= 0) & (frame < length), 1.0, 0.0)

    for n in range(n_src):
        load_source(n).wait()

    def mix_item(i, c):
        rows = pl.ds(pl.multiple_of(i * half, half), half)
        where = lax.broadcasted_iota(jnp.int32, (8, F), 1) + t * F
        m = tall(jnp.where(where < lengths[i], 1.0, 0.0), half)
        total = jnp.zeros((half, F), F32)
        for n in range(n_src):
            total += soft2[1, n, rows, :].astype(F32) * jnp.where(n < counts[i], 1.0, 0.0)
        stage[i] = (total * m).astype(BF16)
        return c

    lax.fori_loop(0, 2 * NI, mix_item, 0)

    pl.semaphore_wait(barrier, members - 1 + n_tm)

    own_rows = pl.ds(pl.multiple_of(s * half, half), half)
    other_rows = pl.ds(pl.multiple_of(o * half, half), half)
    items_of = lambda core: pl.ds(core * NI, NI)
    centre = pl.ds(DILATION, F)
    head, tail = pl.ds(0, DILATION), pl.ds(F + DILATION, DILATION)

    main_local = pltpu.make_async_copy(stage.at[items_of(s)], x0.at[:, own_rows, centre], sem_x.at[0])
    main_send = remote(
        stage.at[items_of(o)], x0.at[:, own_rows, centre], sem_x.at[1], sem_xr.at[0], {"section": o}
    )
    main_recv = remote(
        stage.at[items_of(o)], x0.at[:, other_rows, centre], sem_x.at[1], sem_xr.at[0], {"section": o}
    )

    def halo_send(side, core):
        edge = pl.ds(0, DILATION) if side == 0 else pl.ds(F - DILATION, DILATION)
        place = tail if side == 0 else head
        return remote(
            stage.at[items_of(core), :, edge],
            x0.at[:, own_rows, place],
            sem_x.at[2 + 2 * side + core],
            sem_xr.at[1 + 2 * side + s],
            {"section": core, "tm": left if side == 0 else right},
        )

    def halo_recv(side, core):
        place = tail if side == 0 else head
        rows = pl.ds(core * half, half)
        return remote(
            x0.at[:, rows, place], x0.at[:, rows, place], sem_x.at[0], sem_xr.at[1 + 2 * side + core], {"section": o}
        )

    main_local.start()
    main_send.start()

    @pl.when(t > 0)
    def _():
        for core in (0, 1):
            halo_send(0, core).start()

    @pl.when(t < last)
    def _():
        for core in (0, 1):
            halo_send(1, core).start()

    weights = (wpre, chan, wg, col, wout, win)

    def weight_copies(j):
        ref = weights[j]
        return (
            remote(ref.at[s], ref.at[s], sem_w.at[j, 0], sem_w.at[j, 1], {"section": o}),
            remote(ref.at[o], ref.at[o], sem_w.at[j, 0], sem_w.at[j, 1], {"section": o}),
        )

    for j in range(len(weights)):
        weight_copies(j)[0].start()

    def wait_weights(*which):
        for j in which:
            send, recv = weight_copies(j)
            recv.wait_recv()
            send.wait_send()

    @pl.when(t == 0)
    def _():
        x0[:, :, 0:DILATION] = jnp.zeros((NI, B, DILATION), BF16)

    @pl.when(t == last)
    def _():
        x0[:, :, F + DILATION : W] = jnp.zeros((NI, B, DILATION), BF16)

    grad[...] = jnp.zeros(grad.shape, F32)
    bias_sum[...] = jnp.zeros(bias_sum.shape, F32)

    def stat_copy(ph, i, d, to):
        p = ph % 2
        return remote(
            st_src.at[p, i], st_buf.at[p, i, d - 1], sem_ss.at[p, i, d - 1], sem_sr.at[p, i, d - 1], {"tm": to}
        )

    def send_stats(ph, i, a, b):
        rows = [jnp.sum(a, axis=0, keepdims=True), jnp.sum(b, axis=0, keepdims=True)]
        st_src[ph % 2, i] = jnp.concatenate(rows + [jnp.zeros((6, LANES), F32)], axis=0)

        def one(d, c):
            stat_copy(ph, i, d, lax.rem(t + d, n_tm)).start()
            return c

        lax.fori_loop(1, n_tm, one, 0)

    def recv_stats(ph, i):
        def one(d, total):
            copy = stat_copy(ph, i, d, lax.rem(t + d, n_tm))
            copy.wait_send()
            copy.wait_recv()
            return total + st_buf[ph % 2, i, d - 1]

        total = lax.fori_loop(1, n_tm, one, st_src[ph % 2, i])
        sums = jnp.sum(total, axis=1, keepdims=True)
        return (
            jnp.broadcast_to(sums[0:1], (8, LANES)),
            jnp.broadcast_to(sums[1:2], (8, LANES)),
        )

    def finish_norm(ph, slot, i):
        a, b = recv_stats(ph, i)
        inv_n = invn_ref[i]
        mean = a * inv_n
        spread = jnp.maximum(b * inv_n - mean * mean, 0.0)
        stat[slot, i, 0] = mean
        stat[slot, i, 1] = lax.rsqrt(spread + EPSILON / (LN2 * LN2))

    def finish_back(ph, slot, i):
        a, b = recv_stats(ph, i)
        inv_n = invn_ref[i]
        mean, inv = stat[slot, i, 0], stat[slot, i, 1]
        q = b * inv_n * inv
        back[i, 0] = (mean * q - a * inv_n) * (inv * LOG2E)
        back[i, 1] = -q * (inv * LOG2E)

    def lanes_of(ref, j):
        out = ref[0, j]
        for i in range(1, NI):
            out = jnp.where(lane8 >= 32 * i, ref[i, j], out)
        return out

    def per_item(body):
        lax.fori_loop(0, NI, lambda i, c: (body(i), c)[1], 0)

    def per_tile(body, count=H, rows=R, init=0):
        return lax.fori_loop(0, count // rows, lambda j, c: body(rows_at(j, rows), c), init)

    def mask_row(i, rows, at=DILATION, width=F):
        return tall(mask_ref[i, :, at : at + width], rows)

    zero8 = jnp.zeros((8, LANES), F32)

    def pack_edges(src, channels, slot):
        def tile(r, c):
            to_left = to_right = own = jnp.zeros((R, LANES), F32)
            for i in range(NI):
                a = src[i, r, 0:LANES].astype(F32)
                z = src[i, r, F - LANES : F].astype(F32)
                base = 32 * i
                to_left += jnp.where(
                    (lane == base + 17) | (lane == base + 18), pltpu.roll(a, base + 17, 1), 0.0
                )
                to_right += jnp.where(
                    (lane == base) | (lane == base + 1), pltpu.roll(z, base + 2, 1), 0.0
                )
                own += jnp.where(lane == base + 2, pltpu.roll(a, base + 2, 1), 0.0)
                own += jnp.where(lane == base + 16, pltpu.roll(z, base + 17, 1), 0.0)
            edge_src[slot, 0, r, :] = to_left.astype(BF16)
            edge_src[slot, 1, r, :] = to_right.astype(BF16)
            edge_src[slot, 2, r, :] = own.astype(BF16)
            return c

        per_tile(tile, channels)

    def edge_copy(slot, side, channels):
        rows = pl.ds(0, channels)
        return remote(
            edge_src.at[slot, side, rows],
            edge_in.at[slot, side, rows],
            sem_es.at[slot, side],
            sem_er.at[slot, side],
            {"tm": left if side == 0 else right},
        )

    def send_edges(slot, channels):
        @pl.when(t > 0)
        def _():
            edge_copy(slot, 0, channels).start()

        @pl.when(t < last)
        def _():
            edge_copy(slot, 1, channels).start()

    def recv_edges(slot, channels, dst):
        @pl.when(t > 0)
        def _():
            edge_copy(slot, 0, channels).wait_send()
            edge_copy(slot, 1, channels).wait_recv()

        @pl.when(t < last)
        def _():
            edge_copy(slot, 1, channels).wait_send()
            edge_copy(slot, 0, channels).wait_recv()

        def tile(r, c):
            total = edge_src[slot, 2, r, :].astype(F32)
            for side in (0, 1):
                total += edge_in[slot, side, r, :].astype(F32)
            dst[r, :] = total.astype(BF16)
            return c

        per_tile(tile, channels)

    def rectify(neg, rest):
        soft = jnp.maximum(neg, jnp.log2(1.0 + jnp.exp2(jnp.minimum(neg, 100.0))))
        return rest * soft - neg, soft

    def masked_sums(a, m, sums):
        am = a * m
        return (sums[0] + fold_rows(fold(am)), sums[1] + fold_rows(fold(am * a)))

    def phase1(k):
        R = ROWS1
        width = W if k == 0 else F
        x = x0 if k == 0 else x1
        act = act1_0 if k == 0 else act1_1
        mid = MID if k == 0 else slice(0, F)

        def item(i):
            wide_s[:, 0:width] = dot(wpre[k], x[i])
            m = mask_row(i, R)

            def tile(r, sums):
                table = chan[k, r, :]
                bias = column(table, 0) * -LOG2E
                rest = 1.0 - column(table, 1)
                neg = wide_s[r, 0:width] * -LOG2E + wide(bias, width)
                a, soft = rectify(neg, wide(rest, width))
                act[i, r, :] = a.astype(BF16)
                soft1[k, i, r, :] = soft[:, mid].astype(BF16)
                return masked_sums(a[:, mid], m, sums)

            a, b = per_tile(tile, rows=R, init=(zero8, zero8))
            send_stats(4 * k, i, a, b)

        per_item(item)
        if k == 1:
            recv_edges(1, B, x_edge)
            wide_s[:, 0:LANES] = dot(wpre[1], x_edge[...])

            def tile(r, c):
                table = chan[1, r, :]
                neg = wide_s[r, 0:LANES] * -LOG2E + column(table, 0) * -LOG2E
                a, _ = rectify(neg, 1.0 - column(table, 1))
                wide_s[r, 0:LANES] = a
                return c

            per_tile(tile, rows=R)

    def phase2(k):
        R = ROWS2
        width = W if k == 0 else F
        at = 0 if k == 0 else DILATION
        act = act1_0 if k == 0 else act1_1

        def item(i):
            finish_norm(4 * k, 2 * k, i)
            mean, inv = tall(stat[2 * k, i, 0], R), tall(stat[2 * k, i, 1], R)
            m = mask_row(i, R, at, width)

            def tile(r, c):
                table = chan[k, r, :]
                scale = inv * column(table, 2)
                shift = column(table, 3) - mean * scale
                a = act[i, r, :].astype(F32)
                buf[i, r, at : at + width] = (
                    (a * wide(scale, width) + wide(shift, width)) * m
                ).astype(BF16)
                return c

            per_tile(tile, rows=R)

        per_item(item)
        if k == 1:
            mean, inv = tall(lanes_of(stat.at[2], 0), R), tall(lanes_of(stat.at[2], 1), R)
            m = tall(edge_mask_ref[...], R)

            def tile(r, c):
                table = chan[1, r, :]
                scale = inv * column(table, 2)
                a = wide_s[r, 0:LANES]
                first_edge[r, :] = (((a - mean) * scale + column(table, 3)) * m).astype(BF16)
                return c

            per_tile(tile, rows=R)

    def neighbours(f, edge, i):
        shifted_in = pltpu.roll(edge, lax.rem(127 - 32 * i + 256, 128), 1)
        before = pltpu.roll(f, 1, 1)
        lane = lax.broadcasted_iota(jnp.int32, edge.shape, 1)
        lead = jnp.where(lane == 0, shifted_in, before[:, 0:LANES])
        before = jnp.concatenate([lead, before[:, LANES:]], axis=1)
        shifted_in = pltpu.roll(edge, lax.rem(110 - 32 * i + 256, 128), 1)
        after = pltpu.roll(f, F - 1, 1)
        trail = jnp.where(lane == LANES - 1, shifted_in, after[:, F - LANES :])
        after = jnp.concatenate([after[:, : F - LANES], trail], axis=1)
        return before, after

    def taps(k, i, r, edge):
        f = buf[i, r, MID]
        if k == 0:
            return buf[i, r, 0:F], f, buf[i, r, 2 * DILATION : W]
        before, after = neighbours(f, edge[r, :], i)
        return before, f, after

    def conv_coefs(table):
        return [column(table, j) * -LOG2E for j in (4, 5, 6, 7)], 1.0 - column(table, 8)

    def phase3(k):
        R = ROWS3
        def item(i):
            m = mask_row(i, R)

            def tile(r, sums):
                c, rest = conv_coefs(chan[k, r, :])
                before, f, after = (v.astype(F32) for v in taps(k, i, r, first_edge))
                neg = wide(c[0], F) * before + wide(c[1], F) * f + wide(c[2], F) * after + wide(c[3], F)
                a, soft = rectify(neg, wide(rest, F))
                act2[k, i, r, :] = a.astype(BF16)
                soft2[k, i, r, :] = soft.astype(BF16)
                return masked_sums(a, m, sums)

            a, b = per_tile(tile, rows=R, init=(zero8, zero8))
            send_stats(4 * k + 1, i, a, b)

        per_item(item)
        if k == 1:

            def tile(r, x):
                c, rest = conv_coefs(chan[1, r, :])
                f = first_edge[r, :].astype(F32)
                neg = c[0] * pltpu.roll(f, 1, 1) + c[1] * f + c[2] * pltpu.roll(f, LANES - 1, 1) + c[3]
                a, soft = rectify(neg, rest)
                act_edge[r, :] = a.astype(BF16)
                soft_edge[r, :] = soft.astype(BF16)
                return x

            per_tile(tile, rows=R)

    def out_copies(kind, k, i):
        row = first_item + i
        if kind == 0 and k == 1:
            pairs = [
                (stage.at[2 * i + j], block_h.at[row, pl.ds(j * half, half)], sem_o.at[2 * j, 1, i], sem_or.at[2 * j, i])
                for j in (0, 1)
            ]
        else:
            src, dst = ((x1, block_h), (skips, skip_h))[kind]
            pairs = [(src.at[i], dst.at[row], sem_o.at[kind, k, i], sem_or.at[kind, i])]
        return [
            (pltpu.make_async_copy(a, b, sem), remote(a, b, sem, there, {"section": o})) for a, b, sem, there in pairs
        ]

    def start_out(kind, k, i):
        for here, there in out_copies(kind, k, i):
            pl.when(s == k)(lambda: here.start())
            pl.when(s != k)(lambda: there.start())

    def wait_out(kind, k, i):
        for here, there in out_copies(kind, k, i):
            pl.when(s == k)(lambda: here.wait())
            pl.when(s != k)(lambda: there.wait_send())

    def wait_came(i):
        row = o * NI + i
        skip_in = remote(skips.at[i], skip_h.at[row], sem_o.at[1, 0, i], sem_or.at[1, i], {"section": o})
        skip_in.wait_recv()

        @pl.when(s == 0)
        def _():
            remote(x1.at[i], block_h.at[row], sem_o.at[0, 0, i], sem_or.at[0, i], {"section": o}).wait_recv()

        @pl.when(s == 1)
        def _():
            for j in (0, 1):
                dst = block_h.at[row, pl.ds(j * half, half)]
                remote(stage.at[0], dst, sem_o.at[2 * j, 1, i], sem_or.at[2 * j, i], {"section": o}).wait_recv()

    def phase4(k):
        R = ROWS4
        x = x0 if k == 0 else x1
        mid = MID if k == 0 else slice(0, F)

        def item(i):
            finish_norm(4 * k + 1, 2 * k + 1, i)
            mean, inv = tall(stat[2 * k + 1, i, 0], B), tall(stat[2 * k + 1, i, 1], B)
            m = mask_row(i, B)
            y = pl.ds(0, 2 * B)
            wide_s[y, 0:F] = dot(wg[k], act2[k, i])

            def project(r):
                table = col[k, r, :]
                shift = column(table, 0) - mean * inv * column(table, 1)
                return (wide_s[r, 0:F] * wide(inv, F) + wide(shift, F)) * m

            total = (x[i, :, mid].astype(F32) + project(pl.ds(0, B))).astype(BF16)
            if k == 0:
                x1[i] = total
            else:
                stage[2 * i] = total[0:half]
                stage[2 * i + 1] = total[half:]

            p = project(pl.ds(B, B))
            if k == 1:
                wait_out(1, 0, i)
                p += skips[i].astype(F32)
            skips[i] = p.astype(BF16)
            start_out(0, k, i)
            start_out(1, k, i)

        per_item(item)

    def phase5(k):
        R = ROWS5
        R5 = ROWS5

        def item(i):
            mean, inv = tall(stat[2 * k + 1, i, 0], R5), tall(stat[2 * k + 1, i, 1], R5)
            wide_s[:, 0 : 2 * B] = dot(act2[k, i], dp[i], NT)
            total8 = dot(jnp.ones((8, F), BF16), dp[i], NT)
            bias_sum[k] += total8
            total = tall(total8, R5)

            def tile(r, sums):
                table = chan[k, r, :]
                g, e = column(table, 9), column(table, 10)
                product = wide_s[r, 0 : 2 * B]
                w = wout[k, r, :].astype(F32)
                against = fold(w * product)
                plain = fold(w * total)
                normed = inv * (against - mean * plain)
                gacc[9, r, :] += normed
                gacc[10, r, :] += plain
                scale = inv * g
                shift = e - mean * scale
                step = wide(scale, 2 * B) * product + wide(shift, 2 * B) * total
                grad[k, r, :] += step[:, :B]
                grad[k, pl.ds(H + r.start, R5), :] += step[:, B:]
                return (sums[0] + fold_rows(g * plain), sums[1] + fold_rows(g * normed))

            a, b = per_tile(tile, rows=R5, init=(zero8, zero8))
            send_stats(4 * k + 2, i, a, b)

        per_item(item)

    def halo_copy(i, side):
        edge = pl.ds(DILATION, DILATION) if side == 0 else pl.ds(F, DILATION)
        return remote(
            buf.at[i, :, edge],
            buf.at[i, :, tail if side == 0 else head],
            sem_hs.at[side, i],
            sem_hr.at[side, i],
            {"tm": left if side == 0 else right},
        )

    def phase6(k):
        R = ROWS6
        def item(i):
            finish_back(4 * k + 2, 2 * k + 1, i)
            inv = tall(stat[2 * k + 1, i, 1], R) * LOG2E
            p, q = wide(tall(back[i, 0], R), F), wide(tall(back[i, 1], R), F)
            m = mask_row(i, R)
            wide_s[:, 0:F] = dot(wout[k], dp[i])

            def tile(r, c):
                table = chan[k, r, :]
                slope = column(table, 8)
                g = inv * column(table, 9)
                d_act = low(wide_s[r, 0:F] * wide(g, F) + m * (p + q * act2[k, i, r, :].astype(F32)))
                soft = soft2[k, i, r, :]
                d_conv = d_act * (wide(low(slope), F) + wide(low(1.0 - slope), F) * jnp.exp2(-soft))
                gacc[8, r, :] += fold(d_act * soft).astype(F32) * -LN2
                gacc[7, r, :] += fold(d_conv).astype(F32)
                buf[i, r, MID] = d_conv
                return c

            per_tile(tile, rows=R)
            if k == 0:

                @pl.when(t > 0)
                def _():
                    halo_copy(i, 0).start()

                @pl.when(t < last)
                def _():
                    halo_copy(i, 1).start()

                @pl.when(t == 0)
                def _():
                    buf[i, :, 0:DILATION] = jnp.zeros((H, DILATION), BF16)

                @pl.when(t == last)
                def _():
                    buf[i, :, F + DILATION : W] = jnp.zeros((H, DILATION), BF16)

        per_item(item)
        if k == 1:
            wide_s[:, 0:LANES] = dot(wout[1], dp_edge[...])
            inv = tall(lanes_of(stat.at[3], 1), R) * LOG2E
            p, q = tall(lanes_of(back, 0), R), tall(lanes_of(back, 1), R)
            m = tall(edge_mask_ref[...], R)

            def tile(r, c):
                table = chan[1, r, :]
                slope = column(table, 8)
                d_act = wide_s[r, 0:LANES] * (inv * column(table, 9)) + m * (p + q * act_edge[r, :].astype(F32))
                d_conv = d_act * (slope + (1.0 - slope) * jnp.exp2(-soft_edge[r, :].astype(F32)))
                conv_edge[r, :] = d_conv.astype(BF16)
                return c

            per_tile(tile, rows=R)

    def phase7(k):
        R = ROWS7
        act = act1_0 if k == 0 else act1_1
        mid = MID if k == 0 else slice(0, F)

        def item(i):
            if k == 0:

                @pl.when(t > 0)
                def _():
                    halo_copy(i, 0).wait_send()
                    halo_copy(i, 1).wait_recv()

                @pl.when(t < last)
                def _():
                    halo_copy(i, 1).wait_send()
                    halo_copy(i, 0).wait_recv()

            mean, inv = tall(stat[2 * k, i, 0], R), tall(stat[2 * k, i, 1], R)
            m = low(mask_row(i, R))

            def tile(r, sums):
                table = chan[k, r, :]
                g = column(table, 2)
                scale = inv * g
                shift = column(table, 3) - mean * scale
                before, d, after = taps(k, i, r, conv_edge)
                u = (
                    wide(low(column(table, 4)), F) * after
                    + wide(low(column(table, 5)), F) * d
                    + wide(low(column(table, 6)), F) * before
                ) * m
                a = act[i, r, mid]
                first = (a * wide(low(scale), F) + wide(low(shift), F)) * m
                plain = fold(u).astype(F32)
                normed = inv * (fold(u * a).astype(F32) - mean * plain)
                gacc[2, r, :] += normed
                gacc[3, r, :] += plain
                gacc[4, r, :] += fold(after * first).astype(F32)
                gacc[5, r, :] += fold(d * first).astype(F32)
                gacc[6, r, :] += fold(before * first).astype(F32)
                soft2[k, i, r, :] = u
                return (sums[0] + fold_rows(g * plain), sums[1] + fold_rows(g * normed))

            a, b = per_tile(tile, rows=R, init=(zero8, zero8))
            send_stats(4 * k + 3, i, a, b)

        per_item(item)

    def mix_copy(i):
        row = first_item + i
        return (
            pltpu.make_async_copy(stage.at[2 * i + s], gmix_h.at[row], sem_m.at[0, i]),
            remote(stage.at[2 * i + o], gmix_h.at[row], sem_m.at[1, i], sem_mr.at[i], {"section": o}),
        )

    def phase8(k):
        R = ROWS8
        act = act1_0 if k == 0 else act1_1
        x = x0 if k == 0 else x1
        mid = MID if k == 0 else slice(0, F)

        def item(i):
            finish_back(4 * k + 3, 2 * k, i)
            inv = tall(stat[2 * k, i, 1], R) * LOG2E
            p, q = wide(tall(back[i, 0], R), F), wide(tall(back[i, 1], R), F)
            m = mask_row(i, R)

            def tile(r, c):
                table = chan[k, r, :]
                slope = column(table, 1)
                g = inv * column(table, 2)
                d_act = low(soft2[k, i, r, :].astype(F32) * wide(g, F) + m * (p + q * act[i, r, mid].astype(F32)))
                soft = soft1[k, i, r, :]
                d_pre = d_act * (wide(low(slope), F) + wide(low(1.0 - slope), F) * jnp.exp2(-soft))
                gacc[1, r, :] += fold(d_act * soft).astype(F32) * -LN2
                gacc[0, r, :] += fold(d_pre).astype(F32)
                buf[i, r, MID] = d_pre
                return c

            per_tile(tile, rows=R)
            grad[k, 2 * H : 3 * H] += dot(buf[i, :, MID], x[i, :, mid], NT)

            if k == 1:
                input_gradient(1, i)

        per_item(item)

    def input_gradient(k, i):
        wide_s[0:B, 0:F] = dot(win[k], buf[i, :, MID])
        m = mask_row(i, B)
        d_input = (wide_s[0:B, 0:F] + dp[i, 0:B, :].astype(F32)) * m
        if k == 1:
            dp[i, 0:B, :] = d_input.astype(BF16)
        else:
            stage[2 * i] = d_input[0:half].astype(BF16)
            stage[2 * i + 1] = d_input[half:].astype(BF16)
            here, there = mix_copy(i)
            there.start()
            here.start()

    rows_at_part = ((0, 2 * H), (2 * H, grad.shape[1]))
    came = (came0, came1)
    slots = ((from_item0, from_tm0), (from_item1, from_tm1))

    def sizes(part):
        big, chunk = slots[part][0].shape[1], slots[part][1].shape[1]
        return big, chunk, big // chunk

    def item_peer(d):
        return lax.rem(it + d, n_item)

    def tm_peer(d):
        return lax.rem(t + d, n_tm)

    def each(count, body):
        lax.fori_loop(1, count, lambda d, c: (body(d), c)[1], 0)

    def at_part(part, k, start, rows):
        return grad.at[k, pl.ds(rows_at_part[part][0] + start, rows)]

    def to_owner(part, k):
        a, b = rows_at_part[part]
        return remote(grad.at[k, pl.ds(a, b - a)], came[part], sem_k.at[part], sem_kr.at[part], {"section": o})

    def item_scatter(part, k, d):
        big = sizes(part)[0]
        src = at_part(part, k, item_peer(d) * big, big)
        return remote(
            src, slots[part][0].at[d - 1], sem_ri.at[part, d - 1], sem_rir.at[part, d - 1], {"item": item_peer(d)}
        )

    def tm_scatter(part, k, d):
        big, chunk, owners = sizes(part)
        src = at_part(part, k, it * big + lax.rem(tm_peer(d), owners) * chunk, chunk)
        return remote(
            src, slots[part][1].at[d - 1], sem_rt.at[part, d - 1], sem_rtr.at[part, d - 1], {"tm": tm_peer(d)}
        )

    def tm_gather(part, d, member):
        big, chunk, owners = sizes(part)
        rows = came[part].at[pl.ds(it * big + lax.rem(member, owners) * chunk, chunk)]
        return remote(rows, rows, sem_at.at[part, d - 1], sem_atr.at[part, d - 1], {"tm": tm_peer(d)})

    def item_gather(part, d, member):
        big = sizes(part)[0]
        rows = came[part].at[pl.ds(member * big, big)]
        return remote(rows, rows, sem_ai.at[part, d - 1], sem_air.at[part, d - 1], {"item": item_peer(d)})

    def sum_1(part, k):
        pl.when(s != k)(lambda: to_owner(part, k).start())

    def sum_2(part, k):
        pl.when(s != k)(lambda: to_owner(part, k).wait_send())

        @pl.when(s == k)
        def _():
            a, b = rows_at_part[part]
            to_owner(part, k).wait_recv()
            grad[k, a:b] += came[part][...]
            each(n_item, lambda d: item_scatter(part, k, d).start())

    def sum_3(part, k):
        big, chunk, owners = sizes(part)

        @pl.when(s == k)
        def _():
            each(n_item, lambda d: item_scatter(part, k, d).wait())
            mine = pl.ds(pl.multiple_of(rows_at_part[part][0] + it * big, 8), big)
            grad[k, mine] = lax.fori_loop(0, n_item - 1, lambda j, x: x + slots[part][0][j], grad[k, mine])
            each(n_tm, lambda d: pl.when(tm_peer(d) < owners)(lambda: tm_scatter(part, k, d).start()))

    def sum_4(part, k):
        big, chunk, owners = sizes(part)

        @pl.when(s == k)
        def _():
            def wait(d):
                pl.when(tm_peer(d) < owners)(lambda: tm_scatter(part, k, d).wait_send())
                pl.when(t < owners)(lambda: tm_scatter(part, k, d).wait_recv())

            each(n_tm, wait)

            @pl.when(t < owners)
            def _():
                start = it * big + t * chunk
                own = grad[k, pl.ds(pl.multiple_of(rows_at_part[part][0] + start, 8), chunk)]
                total = lax.fori_loop(0, n_tm - 1, lambda j, x: x + slots[part][1][j], own)
                came[part][pl.ds(pl.multiple_of(start, 8), chunk)] = total
                each(n_tm, lambda d: tm_gather(part, d, t).start())

    def sum_5(part, k):
        _, _, owners = sizes(part)

        @pl.when(s == k)
        def _():
            def wait(d):
                source = lax.rem(t - d + n_tm, n_tm)
                pl.when(t < owners)(lambda: tm_gather(part, d, t).wait_send())
                pl.when(source < owners)(lambda: tm_gather(part, d, source).wait_recv())

            each(n_tm, wait)
            each(n_item, lambda d: item_gather(part, d, it).start())

    def sum_6(part, k):
        @pl.when(s == k)
        def _():
            def wait(d):
                item_gather(part, d, it).wait_send()
                item_gather(part, d, lax.rem(it - d + n_item, n_item)).wait_recv()

            each(n_item, wait)

    def finish_block(k):
        group = H // 4
        lanes = lax.broadcasted_iota(jnp.int32, (group, LANES), 1)
        bias = jnp.broadcast_to(bias_sum[k, 0:1, :], (LANES, 2 * B)).T
        packed = jnp.zeros((group, LANES), F32)
        for g in range(4):
            for j in range(11):
                total = jnp.sum(gacc[j, g * group : (g + 1) * group, :], axis=1, keepdims=True)
                packed = jnp.where(lanes == 32 * g + j, total, packed)
            if (g + 1) * group <= 2 * B:
                packed = jnp.where(lanes == 32 * g + 11, bias[g * group : (g + 1) * group], packed)
        grad[k, 3 * H : 3 * H + group] = packed

    def mask_gradients(i):
        m = mask_row(i, R)

        def tile(r, c):
            dp[i, r, :] = (dp[i, r, :].astype(F32) * m).astype(BF16)
            return c

        per_tile(tile, 2 * B)

    wait_weights(0, 1)
    main_local.wait()
    main_send.wait_send()
    main_recv.wait_recv()

    @pl.when(t > 0)
    def _():
        for core in (0, 1):
            halo_send(0, core).wait_send()
            halo_recv(1, core).wait_recv()

    @pl.when(t < last)
    def _():
        for core in (0, 1):
            halo_send(1, core).wait_send()
            halo_recv(0, core).wait_recv()

    phase1(0)
    load_out.wait()
    load_skip.wait()

    per_item(mask_gradients)
    pack_edges(dp, 2 * B, 0)
    send_edges(0, 2 * B)
    phase2(0)
    phase3(0)
    wait_weights(2, 3)
    phase4(0)
    pack_edges(x1, B, 1)
    send_edges(1, B)
    phase1(1)
    phase2(1)
    phase3(1)
    phase4(1)
    recv_edges(0, 2 * B, dp_edge)
    wait_weights(4)
    gacc[...] = jnp.zeros(gacc.shape, F32)
    phase5(1)
    sum_1(0, 1)
    phase6(1)
    sum_2(0, 1)
    phase7(1)
    sum_3(0, 1)
    wait_weights(5)
    phase8(1)
    finish_block(1)
    sum_1(1, 1)
    sum_4(0, 1)
    gacc[...] = jnp.zeros(gacc.shape, F32)
    phase5(0)
    sum_1(0, 0)
    sum_2(1, 1)
    sum_5(0, 1)
    phase6(0)
    sum_2(0, 0)
    sum_3(1, 1)
    phase7(0)
    sum_3(0, 0)
    sum_4(1, 1)
    for i in range(NI):
        wait_out(0, 1, i)
    phase8(0)
    finish_block(0)
    sum_1(1, 0)
    sum_4(0, 0)
    sum_5(1, 1)
    per_item(lambda i: input_gradient(0, i))
    sum_2(1, 0)
    sum_5(0, 0)
    sum_3(1, 0)
    sum_4(1, 0)
    sum_5(1, 0)
    sum_6(0, 1)
    sum_6(1, 1)
    sum_6(0, 0)
    sum_6(1, 0)
    results = [
        pltpu.make_async_copy(came[part], grad_h.at[pl.ds(a, b - a)], sem_f.at[part])
        for part, (a, b) in enumerate(rows_at_part)
    ]
    for copy in results:
        copy.start()
    for copy in results:
        copy.wait()

    for i in range(NI):
        here, there = mix_copy(i)
        here.wait()
        there.wait_send()
        remote(
            stage.at[2 * i], gmix_h.at[o * NI + i], sem_m.at[1, i], sem_mr.at[i], {"section": o}
        ).wait_recv()
        wait_out(0, 0, i)
        wait_out(1, 1, i)
        wait_came(i)


def chunk_of(rows, members):
    chunk = -(-rows // members)
    chunk = -(-chunk // 8) * 8
    while rows % chunk:
        chunk += 8
    return chunk


def run(n_tm, n_item, sources, gout, gskip, w_in, chan, w_out, b_out, counts, lengths):
    n_src, flat, F = sources.shape
    items, B, _ = gout.shape
    NI = items // 2
    H = w_in.shape[0]
    W = F + 2 * DILATION
    half = B // 2
    rows0, rows1 = 2 * H, H + H // 4
    quarter0, quarter1 = rows0 // n_item, rows1 // n_item
    smem = pl.BlockSpec(memory_space=pltpu.SMEM)
    any_spec = pl.BlockSpec(memory_space=pl.ANY)
    vmem = pl.BlockSpec(memory_space=pltpu.VMEM)
    dma = pltpu.SemaphoreType.DMA
    shape = jax.ShapeDtypeStruct
    outs = (
        shape((items, B, F), BF16),
        shape((items, B, F), BF16),
        shape((items, half, F), BF16),
        shape((rows0 + rows1, LANES), F32),
    )
    scratch = [
        pltpu.VMEM((items, half, F), BF16),
        pltpu.VMEM((NI, B, W), BF16),
        pltpu.VMEM((NI, B, F), BF16),
        pltpu.VMEM((NI, B, F), BF16),
        pltpu.VMEM((NI, H, W), BF16),
        pltpu.VMEM((NI, H, F), BF16),
        pltpu.VMEM((2, NI, H, F), BF16),
        pltpu.VMEM((2, NI, H, F), BF16),
        pltpu.VMEM((2, NI, H, F), BF16),
        pltpu.VMEM((NI, H, W), BF16),
        pltpu.VMEM((H, W), F32),
        pltpu.VMEM((NI, 2 * B, F), BF16),
        pltpu.VMEM((11, H, LANES), F32),
        pltpu.VMEM((2, H, B), BF16),
        pltpu.VMEM((2, H, 2 * B), BF16),
        pltpu.VMEM((2, 2 * B, H), BF16),
        pltpu.VMEM((2, B, H), BF16),
        pltpu.VMEM((2, H, LANES), F32),
        pltpu.VMEM((2, 2 * B, LANES), F32),
        pltpu.VMEM((2, rows0 + rows1, LANES), F32),
        pltpu.VMEM((2, 8, 2 * B), F32),
        pltpu.VMEM((rows0, LANES), F32),
        pltpu.VMEM((rows1, LANES), F32),
        pltpu.VMEM((n_item - 1, quarter0, LANES), F32),
        pltpu.VMEM((n_item - 1, quarter1, LANES), F32),
        pltpu.VMEM((n_tm - 1, chunk_of(quarter0, n_tm), LANES), F32),
        pltpu.VMEM((n_tm - 1, chunk_of(quarter1, n_tm), LANES), F32),
        pltpu.VMEM((NI, 8, W), F32),
        pltpu.VMEM((8, LANES), F32),
        pltpu.VMEM((NI, 8, LANES), F32),
        pltpu.VMEM((4, NI, 2, 8, LANES), F32),
        pltpu.VMEM((NI, 2, 8, LANES), F32),
        pltpu.VMEM((2, NI, 8, LANES), F32),
        pltpu.VMEM((2, NI, n_tm - 1, 8, LANES), F32),
        pltpu.VMEM((2, 3, 2 * B, LANES), BF16),
        pltpu.VMEM((2, 2, 2 * B, LANES), BF16),
        pltpu.VMEM((B, LANES), BF16),
        pltpu.VMEM((2 * B, LANES), BF16),
        pltpu.VMEM((H, LANES), BF16),
        pltpu.VMEM((H, LANES), BF16),
        pltpu.VMEM((H, LANES), BF16),
        pltpu.VMEM((H, LANES), BF16),
        dma((n_src,)),
        dma((6, 2)),
        dma((6,)),
        dma((5,)),
        dma((2,)),
        dma((2, 2)),
        dma((2, 2)),
        dma((2, NI, n_tm - 1)),
        dma((2, NI, n_tm - 1)),
        dma((2, NI)),
        dma((2, NI)),
        dma((3, 2, NI)),
        dma((3, NI)),
        dma((2, NI)),
        dma((NI,)),
        dma((2,)),
        dma((2,)),
        dma((2, n_item - 1)),
        dma((2, n_item - 1)),
        dma((2, n_tm - 1)),
        dma((2, n_tm - 1)),
        dma((2, n_tm - 1)),
        dma((2, n_tm - 1)),
        dma((2, n_item - 1)),
        dma((2, n_item - 1)),
        dma((2,)),
    ]
    return pl.pallas_call(
        functools.partial(kernel, (n_tm, n_item, NI, H, B, F)),
        out_shape=outs,
        in_specs=[any_spec] * 3 + [vmem] * 4 + [smem] * 2,
        out_specs=[any_spec] * len(outs),
        scratch_shapes=scratch,
        compiler_params=pltpu.CompilerParams(
            collective_id=0, has_side_effects=True, vmem_limit_bytes=VMEM_LIMIT
        ),
        name="temporal_blocks",
    )(sources, gout, gskip, w_in, chan, w_out, b_out, counts, lengths)


def close_kernel(
    block_in, skip_in, gmix_in, grad_in, counts,
    block_h, skip_h, sources_h, w_in_out, chan_out, w_out_out, b_out_out,
    held, mixed, full, nothing, sem_a, sem_b, sem_g, sem_s,
):
    items = gmix_in.shape[0]
    H = w_in_out.shape[0]
    B = w_in_out.shape[1]
    n_src = sources_h.shape[0]
    plain = [(j, i) for i in range(items) for j in (0, 1)]

    def fetch(j, i):
        return pltpu.make_async_copy((block_in, skip_in)[j].at[i], held.at[j, i], sem_a.at[j, i])

    def store(j, i):
        return pltpu.make_async_copy(held.at[j, i], (block_h, skip_h)[j].at[i], sem_b.at[j, i])

    loads = [pltpu.make_async_copy(gmix_in.at[i], mixed.at[i], sem_g.at[i]) for i in range(items)]
    for copy in loads:
        copy.start()
    for j, i in plain:
        fetch(j, i).start()
    nothing[...] = jnp.zeros(nothing.shape, F32)
    for i in range(items):
        loads[i].wait()
        full[i] = mixed[i].astype(F32)
        for n in range(n_src):

            @pl.when(n < counts[i])
            def _():
                pltpu.make_async_copy(full.at[i], sources_h.at[n, i], sem_s.at[n, i]).start()

            @pl.when(n >= counts[i])
            def _():
                pltpu.make_async_copy(nothing, sources_h.at[n, i], sem_s.at[n, i]).start()

    for j, i in plain:
        fetch(j, i).wait()
        store(j, i).start()
    w_out_out[0:B, :] = grad_in[0:H, :].T
    w_out_out[B : 2 * B, :] = grad_in[H : 2 * H, :].T
    w_in_out[...] = grad_in[2 * H : 3 * H, :]
    rows = grad_in[3 * H : 3 * H + H // 4, :].T
    for j in range(chan_out.shape[0]):
        chan_out[j] = jnp.concatenate([rows[32 * g + j : 32 * g + j + 1] for g in range(4)], axis=1)
    b_out_out[...] = jnp.concatenate([rows[32 * g + 11 : 32 * g + 12] for g in range(2 * B * 4 // H)], axis=1)
    for j, i in plain:
        store(j, i).wait()
    for i in range(items):
        for n in range(n_src):
            pltpu.make_async_copy(full.at[i], sources_h.at[n, i], sem_s.at[n, i]).wait()


def close(n_src, n_rows, block, skip, gmix, grad, counts):
    items, half, F = gmix.shape
    B = 2 * half
    H = (grad.shape[0] * 4) // 13
    any_spec = pl.BlockSpec(memory_space=pl.ANY)
    vmem = pl.BlockSpec(memory_space=pltpu.VMEM)
    dma = pltpu.SemaphoreType.DMA
    shape = jax.ShapeDtypeStruct
    return pl.pallas_call(
        close_kernel,
        out_shape=(
            shape(block.shape, BF16),
            shape(skip.shape, BF16),
            shape((n_src, items, half, F), F32),
            shape((H, B), F32),
            shape((n_rows, 1, H), F32),
            shape((2 * B, H), F32),
            shape((1, 2 * B), F32),
        ),
        in_specs=[any_spec] * 3 + [vmem, pl.BlockSpec(memory_space=pltpu.SMEM)],
        out_specs=[any_spec] * 3 + [vmem] * 4,
        scratch_shapes=[
            pltpu.VMEM((2, items, B, F), BF16),
            pltpu.VMEM((items, half, F), BF16),
            pltpu.VMEM((items, half, F), F32),
            pltpu.VMEM((half, F), F32),
            dma((2, items)),
            dma((2, items)),
            dma((items,)),
            dma((n_src, items)),
        ],
        compiler_params=pltpu.CompilerParams(vmem_limit_bytes=VMEM_LIMIT),
        name="lay_out",
    )(block, skip, gmix, grad, counts)


def local(sources, source_counts, valid_lengths, w_in, chan, w_out, b_out, grad_out, grad_skip):
    n_sources, per_device, half, F = sources.shape
    block_out, skip_out, gmix, grad = run(
        lax.axis_size("tm"),
        lax.axis_size("item"),
        sources.reshape(n_sources, per_device * half, F),
        grad_out,
        grad_skip,
        w_in[0],
        chan.transpose(1, 0, 2),
        w_out[0],
        b_out,
        source_counts,
        valid_lengths,
    )
    block_out, skip_out, grad_sources, grad_w_in, grad_chan, grad_w_out, grad_b_out = close(
        n_sources, chan.shape[1], block_out, skip_out, gmix, grad, source_counts
    )
    return (
        block_out[None],
        skip_out[None],
        grad_sources,
        grad_w_in[None],
        grad_chan.transpose(1, 0, 2),
        grad_w_out[None],
        grad_b_out,
    )


def solution(mesh):
    in_specs = (
        P(None, "item", "section", "tm"),
        P("item"),
        P("item"),
        P("section", None, None),
        P("section", None, None),
        P("section", None, None),
        P("section", None),
        P("item", None, "tm"),
        P("item", None, "tm"),
    )
    out_specs = (
        P("section", "item", None, "tm"),
        P("section", "item", None, "tm"),
        P(None, "item", "section", "tm"),
        P("section", None, None),
        P("section", None, None),
        P("section", None, None),
        P("section", None),
    )
    return jax.shard_map(local, mesh=mesh, in_specs=in_specs, out_specs=out_specs, check_vma=False)
```

```python
import functools
import math

import jax
import jax.numpy as jnp
from jax import lax
from jax.experimental import pallas as pl
from jax.experimental.pallas import tpu as pltpu
from jax.sharding import PartitionSpec as P

DILATION = 128
LANES = 128
ROWS = 128
ROWS1 = 512
ROWS2 = 512
ROWS3 = 256
ROWS4 = 128
ROWS5 = 512
ROWS6 = 512
ROWS7 = 128
ROWS8 = 512
EPSILON = 1e-05
VMEM_LIMIT = 63 * 1024 * 1024 + 512 * 1024
LN2 = math.log(2.0)
LOG2E = 1.0 / LN2
F32 = jnp.float32
BF16 = jnp.bfloat16
MESH = pl.DeviceIdType.MESH
NT = (((1,), (1,)), ((), ()))
NN = (((1,), (0,)), ((), ()))


def dot(a, b, dims=NN, precision=None):
    return lax.dot_general(a, b, dims, precision=precision, preferred_element_type=F32)


def remote(src, dst, send, recv, device):
    return pltpu.make_async_remote_copy(
        src_ref=src, dst_ref=dst, send_sem=send, recv_sem=recv, device_id=device, device_id_type=MESH
    )


def wide(v, width):
    return jnp.concatenate([v] * (width // LANES), axis=1)


def tall(v, rows):
    return jnp.concatenate([v] * (rows // v.shape[0]), axis=0)


def fold(v):
    parts = [v[:, at : at + LANES] for at in range(0, v.shape[1], LANES)]
    while len(parts) > 1:
        parts = [a + b for a, b in zip(parts[::2], parts[1::2])] + parts[len(parts) & ~1 :]
    return parts[0]


def fold_rows(v):
    parts = [v[at : at + 8] for at in range(0, v.shape[0], 8)]
    while len(parts) > 1:
        parts = [a + b for a, b in zip(parts[::2], parts[1::2])] + parts[len(parts) & ~1 :]
    return parts[0]


def low(v):
    return v.astype(BF16)


def column(table, j):
    return jnp.broadcast_to(table[:, j : j + 1], (table.shape[0], LANES))


def rows_at(t, count):
    return pl.ds(pl.multiple_of(t * count, count), count)


def kernel(
    dims,
    sources_h, gout_h, gskip_h, w_in_ref, chan_ref, w_out_ref, b_out_ref, counts, lengths,
    block_h, skip_h, gmix_h, grad_h,
    stage, x0, x1, skips, act1_0, act1_1, soft1, act2, soft2, buf, wide_s, dp, gacc,
    wpre, wout, wg, win, chan, col,
    low_grad, low_total, to_owner_slots, grad, bias_sum, came0, came1, from_item0, from_item1, from_tm0, from_tm1,
    mask_ref, edge_mask_ref, invn_ref, stat, back, st_src, st_buf,
    edge_src, edge_in, x_edge, dp_edge, first_edge, act_edge, soft_edge, conv_edge,
    sem_s, sem_w, sem_x, sem_xr, sem_g, sem_es, sem_er, sem_ss, sem_sr, sem_hs, sem_hr, sem_o, sem_or, sem_m, sem_mr,
    sem_ls, sem_lr, sem_gs, sem_gr, sem_k, sem_kr, sem_ri, sem_rir, sem_rt, sem_rtr, sem_at, sem_atr, sem_ai, sem_air, sem_f,
):
    n_tm, n_item, NI, H, B, F = dims
    R = ROWS
    W = F + 2 * DILATION
    MID = slice(DILATION, DILATION + F)
    half = B // 2
    s = lax.axis_index("section")
    t = lax.axis_index("tm")
    o = 1 - s
    left = t - 1
    right = t + 1
    last = n_tm - 1
    first_item = s * NI
    lane = lax.broadcasted_iota(jnp.int32, (R, LANES), 1)
    lane8 = lax.broadcasted_iota(jnp.int32, (8, LANES), 1)

    it = lax.axis_index("item")
    members = n_tm * n_item
    me = t * n_item + it
    n_src = sources_h.shape[0]

    def load_source(n):
        return pltpu.make_async_copy(sources_h.at[n], soft2.at[1, n], sem_s.at[n])

    for n in range(n_src):
        load_source(n).start()
    load_out = pltpu.make_async_copy(gout_h.at[pl.ds(first_item, NI)], dp.at[:, pl.ds(0, B)], sem_g.at[0])
    load_skip = pltpu.make_async_copy(gskip_h.at[pl.ds(first_item, NI)], dp.at[:, pl.ds(B, B)], sem_g.at[1])
    load_out.start()
    load_skip.start()
    edge_in[...] = jnp.zeros(edge_in.shape, BF16)

    barrier = pltpu.get_barrier_semaphore()

    def greet(d, c):
        peer = lax.rem(me + d, members)
        device = {"tm": peer // n_item, "item": lax.rem(peer, n_item)}
        pl.semaphore_signal(barrier, inc=1, device_id=device, device_id_type=MESH)
        pl.semaphore_signal(barrier, inc=1, device_id={"section": o} | device, device_id_type=MESH)
        return c

    pl.semaphore_signal(barrier, inc=1, device_id={"section": o}, device_id_type=MESH)
    lax.fori_loop(1, members, greet, 0)

    w_in = w_in_ref[...]
    w_out = w_out_ref[...].astype(F32)
    wpre[s] = w_in
    win[s] = w_in.astype(F32).T.astype(BF16)
    wout[s] = w_out.T.astype(BF16)
    gained = (w_out * chan_ref[9]).astype(BF16)
    wg[s] = gained
    wide_s[0:LANES, 0:H] = jnp.zeros((LANES, H), F32)
    for j in range(chan_ref.shape[0]):
        wide_s[j : j + 1, 0:H] = chan_ref[j]
    chan[s] = wide_s[0:LANES, 0:H].T
    bias = jnp.broadcast_to(b_out_ref[...], (LANES, 2 * B)).T
    bias += jnp.sum(w_out * chan_ref[10], axis=1, keepdims=True)
    gain = jnp.sum(gained.astype(F32), axis=1, keepdims=True)
    lane_w = lax.broadcasted_iota(jnp.int32, (2 * B, LANES), 1)
    col[s] = jnp.where(lane_w == 0, bias, gain)

    for i in range(NI):
        length = lengths[first_item + i]
        where = lax.broadcasted_iota(jnp.int32, (8, W), 1) + (t * F - DILATION)
        mask_ref[i] = jnp.where((where >= 0) & (where < length), 1.0, 0.0)
        invn_ref[i] = 1.0 / (jnp.full((8, LANES), length, jnp.int32).astype(F32) * H)
    within = lane8 % 32
    frame = t * F + jnp.where(within < 16, within - 2, within - 17 + F)
    length = jnp.full((8, LANES), lengths[first_item], jnp.int32)
    for i in range(1, NI):
        length = jnp.where(lane8 >= 32 * i, lengths[first_item + i], length)
    held = (within < 3) | ((within >= 16) & (within < 19))
    edge_mask_ref[...] = jnp.where(held & (frame >= 0) & (frame < length), 1.0, 0.0)

    for n in range(n_src):
        load_source(n).wait()

    def mix_item(i, c):
        rows = pl.ds(pl.multiple_of(i * half, half), half)
        where = lax.broadcasted_iota(jnp.int32, (8, F), 1) + t * F
        m = tall(jnp.where(where < lengths[i], 1.0, 0.0), half)
        total = jnp.zeros((half, F), F32)
        for n in range(n_src):
            total += soft2[1, n, rows, :].astype(F32) * jnp.where(n < counts[i], 1.0, 0.0)
        stage[i] = (total * m).astype(BF16)
        return c

    lax.fori_loop(0, 2 * NI, mix_item, 0)

    pl.semaphore_wait(barrier, 2 * members - 1)

    own_rows = pl.ds(pl.multiple_of(s * half, half), half)
    other_rows = pl.ds(pl.multiple_of(o * half, half), half)
    items_of = lambda core: pl.ds(core * NI, NI)
    centre = pl.ds(DILATION, F)
    head, tail = pl.ds(0, DILATION), pl.ds(F + DILATION, DILATION)

    main_local = pltpu.make_async_copy(stage.at[items_of(s)], x0.at[:, own_rows, centre], sem_x.at[0])
    main_send = remote(
        stage.at[items_of(o)], x0.at[:, own_rows, centre], sem_x.at[1], sem_xr.at[0], {"section": o}
    )
    main_recv = remote(
        stage.at[items_of(o)], x0.at[:, other_rows, centre], sem_x.at[1], sem_xr.at[0], {"section": o}
    )

    def halo_send(side, core):
        edge = pl.ds(0, DILATION) if side == 0 else pl.ds(F - DILATION, DILATION)
        place = tail if side == 0 else head
        return remote(
            stage.at[items_of(core), :, edge],
            x0.at[:, own_rows, place],
            sem_x.at[2 + 2 * side + core],
            sem_xr.at[1 + 2 * side + s],
            {"section": core, "tm": left if side == 0 else right},
        )

    def halo_recv(side, core):
        place = tail if side == 0 else head
        rows = pl.ds(core * half, half)
        return remote(
            x0.at[:, rows, place], x0.at[:, rows, place], sem_x.at[0], sem_xr.at[1 + 2 * side + core], {"section": o}
        )

    main_local.start()
    main_send.start()

    @pl.when(t > 0)
    def _():
        for core in (0, 1):
            halo_send(0, core).start()

    @pl.when(t < last)
    def _():
        for core in (0, 1):
            halo_send(1, core).start()

    weights = (wpre, chan, wg, col, wout, win)

    def weight_copies(j):
        ref = weights[j]
        return (
            remote(ref.at[s], ref.at[s], sem_w.at[j, 0], sem_w.at[j, 1], {"section": o}),
            remote(ref.at[o], ref.at[o], sem_w.at[j, 0], sem_w.at[j, 1], {"section": o}),
        )

    for j in range(len(weights)):
        weight_copies(j)[0].start()

    def wait_weights(*which):
        for j in which:
            send, recv = weight_copies(j)
            recv.wait_recv()
            send.wait_send()

    @pl.when(t == 0)
    def _():
        x0[:, :, 0:DILATION] = jnp.zeros((NI, B, DILATION), BF16)

    @pl.when(t == last)
    def _():
        x0[:, :, F + DILATION : W] = jnp.zeros((NI, B, DILATION), BF16)

    grad[...] = jnp.zeros(grad.shape, F32)
    bias_sum[...] = jnp.zeros(bias_sum.shape, F32)

    def stat_copy(ph, i, d, to):
        p = ph % 2
        return remote(
            st_src.at[p, i], st_buf.at[p, i, d - 1], sem_ss.at[p, i, d - 1], sem_sr.at[p, i, d - 1], {"tm": to}
        )

    def send_stats(ph, i, a, b):
        rows = [jnp.sum(a, axis=0, keepdims=True), jnp.sum(b, axis=0, keepdims=True)]
        st_src[ph % 2, i] = jnp.concatenate(rows + [jnp.zeros((6, LANES), F32)], axis=0)

        def one(d, c):
            stat_copy(ph, i, d, lax.rem(t + d, n_tm)).start()
            return c

        lax.fori_loop(1, n_tm, one, 0)

    def recv_stats(ph, i):
        def one(d, total):
            copy = stat_copy(ph, i, d, lax.rem(t + d, n_tm))
            copy.wait_send()
            copy.wait_recv()
            return total + st_buf[ph % 2, i, d - 1]

        total = lax.fori_loop(1, n_tm, one, st_src[ph % 2, i])
        sums = jnp.sum(total, axis=1, keepdims=True)
        return (
            jnp.broadcast_to(sums[0:1], (8, LANES)),
            jnp.broadcast_to(sums[1:2], (8, LANES)),
        )

    def finish_norm(ph, slot, i):
        a, b = recv_stats(ph, i)
        inv_n = invn_ref[i]
        mean = a * inv_n
        spread = jnp.maximum(b * inv_n - mean * mean, 0.0)
        stat[slot, i, 0] = mean
        stat[slot, i, 1] = lax.rsqrt(spread + EPSILON / (LN2 * LN2))

    def finish_back(ph, slot, i):
        a, b = recv_stats(ph, i)
        inv_n = invn_ref[i]
        mean, inv = stat[slot, i, 0], stat[slot, i, 1]
        q = b * inv_n * inv
        back[i, 0] = (mean * q - a * inv_n) * (inv * LOG2E)
        back[i, 1] = -q * (inv * LOG2E)

    def lanes_of(ref, j):
        out = ref[0, j]
        for i in range(1, NI):
            out = jnp.where(lane8 >= 32 * i, ref[i, j], out)
        return out

    def per_item(body):
        lax.fori_loop(0, NI, lambda i, c: (body(i), c)[1], 0)

    def per_tile(body, count=H, rows=R, init=0):
        return lax.fori_loop(0, count // rows, lambda j, c: body(rows_at(j, rows), c), init)

    def mask_row(i, rows, at=DILATION, width=F):
        return tall(mask_ref[i, :, at : at + width], rows)

    zero8 = jnp.zeros((8, LANES), F32)
    zero8f = jnp.zeros((8, F), F32)

    def pack_edges(src, channels, slot):
        def tile(r, c):
            to_left = to_right = own = jnp.zeros((R, LANES), F32)
            for i in range(NI):
                a = src[i, r, 0:LANES].astype(F32)
                z = src[i, r, F - LANES : F].astype(F32)
                base = 32 * i
                to_left += jnp.where(
                    (lane == base + 17) | (lane == base + 18), pltpu.roll(a, base + 17, 1), 0.0
                )
                to_right += jnp.where(
                    (lane == base) | (lane == base + 1), pltpu.roll(z, base + 2, 1), 0.0
                )
                own += jnp.where(lane == base + 2, pltpu.roll(a, base + 2, 1), 0.0)
                own += jnp.where(lane == base + 16, pltpu.roll(z, base + 17, 1), 0.0)
            edge_src[slot, 0, r, :] = to_left.astype(BF16)
            edge_src[slot, 1, r, :] = to_right.astype(BF16)
            edge_src[slot, 2, r, :] = own.astype(BF16)
            return c

        per_tile(tile, channels)

    def edge_copy(slot, side, channels):
        rows = pl.ds(0, channels)
        return remote(
            edge_src.at[slot, side, rows],
            edge_in.at[slot, side, rows],
            sem_es.at[slot, side],
            sem_er.at[slot, side],
            {"tm": left if side == 0 else right},
        )

    def send_edges(slot, channels):
        @pl.when(t > 0)
        def _():
            edge_copy(slot, 0, channels).start()

        @pl.when(t < last)
        def _():
            edge_copy(slot, 1, channels).start()

    def recv_edges(slot, channels, dst):
        @pl.when(t > 0)
        def _():
            edge_copy(slot, 0, channels).wait_send()
            edge_copy(slot, 1, channels).wait_recv()

        @pl.when(t < last)
        def _():
            edge_copy(slot, 1, channels).wait_send()
            edge_copy(slot, 0, channels).wait_recv()

        def tile(r, c):
            total = edge_src[slot, 2, r, :].astype(F32)
            for side in (0, 1):
                total += edge_in[slot, side, r, :].astype(F32)
            dst[r, :] = total.astype(BF16)
            return c

        per_tile(tile, channels)

    def rectify(neg, rest):
        soft = jnp.maximum(neg, jnp.log2(1.0 + jnp.exp2(jnp.minimum(neg, 100.0))))
        return rest * soft - neg, soft

    def add_sums(a, sums):
        return (sums[0] + fold_rows(a), sums[1] + fold_rows(a * a))

    def send_sums(ph, i, sums):
        m = mask_ref[i, :, MID]
        send_stats(ph, i, fold(sums[0] * m), fold(sums[1] * m))

    def phase1(k):
        R = ROWS1
        width = W if k == 0 else F
        x = x0 if k == 0 else x1
        act = act1_0 if k == 0 else act1_1
        mid = MID if k == 0 else slice(0, F)

        def item(i):

            def tile(r, sums):
                table = chan[k, r, :]
                bias = column(table, 0) * -LOG2E
                rest = 1.0 - column(table, 1)
                neg = dot(wpre[k, r, :], x[i]) * -LOG2E + wide(bias, width)
                a, soft = rectify(neg, wide(rest, width))
                act[i, r, :] = a.astype(BF16)
                soft1[k, i, r, :] = soft[:, mid].astype(BF16)
                return add_sums(a[:, mid], sums)

            send_sums(4 * k, i, per_tile(tile, rows=R, init=(zero8f, zero8f)))

        return item

    def edge1():
        R = ROWS1
        recv_edges(1, B, x_edge)
        wide_s[:, 0:LANES] = dot(wpre[1], x_edge[...])

        def tile(r, c):
            table = chan[1, r, :]
            neg = wide_s[r, 0:LANES] * -LOG2E + column(table, 0) * -LOG2E
            a, _ = rectify(neg, 1.0 - column(table, 1))
            wide_s[r, 0:LANES] = a
            return c

        per_tile(tile, rows=R)

    def phase2(k):
        R = ROWS2
        width = W if k == 0 else F
        at = 0 if k == 0 else DILATION
        act = act1_0 if k == 0 else act1_1

        def item(i):
            finish_norm(4 * k, 2 * k, i)
            mean, inv = tall(stat[2 * k, i, 0], R), tall(stat[2 * k, i, 1], R)
            m = mask_row(i, R, at, width)

            def tile(r, c):
                table = chan[k, r, :]
                scale = inv * column(table, 2)
                shift = column(table, 3) - mean * scale
                a = act[i, r, :].astype(F32)
                buf[i, r, at : at + width] = (
                    (a * wide(scale, width) + wide(shift, width)) * m
                ).astype(BF16)
                return c

            per_tile(tile, rows=R)

        return item

    def edge2():
        R = ROWS2
        mean, inv = tall(lanes_of(stat.at[2], 0), R), tall(lanes_of(stat.at[2], 1), R)
        m = tall(edge_mask_ref[...], R)

        def tile(r, c):
            table = chan[1, r, :]
            scale = inv * column(table, 2)
            a = wide_s[r, 0:LANES]
            first_edge[r, :] = (((a - mean) * scale + column(table, 3)) * m).astype(BF16)
            return c

        per_tile(tile, rows=R)

    def neighbours(f, edge, i):
        shifted_in = pltpu.roll(edge, lax.rem(127 - 32 * i + 256, 128), 1)
        before = pltpu.roll(f, 1, 1)
        lane = lax.broadcasted_iota(jnp.int32, edge.shape, 1)
        lead = jnp.where(lane == 0, shifted_in, before[:, 0:LANES])
        before = jnp.concatenate([lead, before[:, LANES:]], axis=1)
        shifted_in = pltpu.roll(edge, lax.rem(110 - 32 * i + 256, 128), 1)
        after = pltpu.roll(f, F - 1, 1)
        trail = jnp.where(lane == LANES - 1, shifted_in, after[:, F - LANES :])
        after = jnp.concatenate([after[:, : F - LANES], trail], axis=1)
        return before, after

    def taps(k, i, r, edge):
        f = buf[i, r, MID]
        if k == 0:
            return buf[i, r, 0:F], f, buf[i, r, 2 * DILATION : W]
        before, after = neighbours(f, edge[r, :], i)
        return before, f, after

    def conv_coefs(table):
        return [column(table, j) * -LOG2E for j in (4, 5, 6, 7)], 1.0 - column(table, 8)

    def phase3(k):
        R = ROWS3
        def item(i):

            def tile(r, sums):
                c, rest = conv_coefs(chan[k, r, :])
                before, f, after = (v.astype(F32) for v in taps(k, i, r, first_edge))
                neg = wide(c[0], F) * before + wide(c[1], F) * f + wide(c[2], F) * after + wide(c[3], F)
                a, soft = rectify(neg, wide(rest, F))
                act2[k, i, r, :] = a.astype(BF16)
                soft2[k, i, r, :] = soft.astype(BF16)
                return add_sums(a, sums)

            send_sums(4 * k + 1, i, per_tile(tile, rows=R, init=(zero8f, zero8f)))

        return item

    def edge3():
        R = ROWS3
        def tile(r, x):
            c, rest = conv_coefs(chan[1, r, :])
            f = first_edge[r, :].astype(F32)
            neg = c[0] * pltpu.roll(f, 1, 1) + c[1] * f + c[2] * pltpu.roll(f, LANES - 1, 1) + c[3]
            a, soft = rectify(neg, rest)
            act_edge[r, :] = a.astype(BF16)
            soft_edge[r, :] = soft.astype(BF16)
            return x

        per_tile(tile, rows=R)

    def out_copy(kind, k, i):
        row = first_item + i
        src, dst = (((x1, x0)[k], block_h), (skips, skip_h))[kind]
        src = src.at[i, :, centre] if (kind, k) == (0, 1) else src.at[i]
        return (
            pltpu.make_async_copy(src, dst.at[row], sem_o.at[kind, k, i]),
            remote(src, dst.at[row], sem_o.at[kind, k, i], sem_or.at[kind, i], {"section": o}),
        )

    def start_out(kind, k, i):
        here, there = out_copy(kind, k, i)
        pl.when(s == k)(lambda: here.start())
        pl.when(s != k)(lambda: there.start())

    def wait_out(kind, k, i):
        here, there = out_copy(kind, k, i)
        pl.when(s == k)(lambda: here.wait())
        pl.when(s != k)(lambda: there.wait_send())

    def wait_came(kind, i):
        src, dst = ((x1, block_h), (skips, skip_h))[kind]
        remote(
            src.at[i], dst.at[o * NI + i], sem_o.at[kind, 0, i], sem_or.at[kind, i], {"section": o}
        ).wait_recv()

    def phase4(k):
        R = ROWS4
        x = x0 if k == 0 else x1
        mid = MID if k == 0 else slice(0, F)

        def item(i):
            if k == 0:
                finish_norm(1, 1, i)
            mean, inv = tall(stat[2 * k + 1, i, 0], B), tall(stat[2 * k + 1, i, 1], B)
            m = mask_row(i, B)
            y = pl.ds(0, 2 * B)
            wide_s[y, 0:F] = dot(wg[k], act2[k, i])

            def project(r):
                table = col[k, r, :]
                shift = column(table, 0) - mean * inv * column(table, 1)
                return (wide_s[r, 0:F] * wide(inv, F) + wide(shift, F)) * m

            total = (x[i, :, mid].astype(F32) + project(pl.ds(0, B))).astype(BF16)
            if k == 0:
                x1[i] = total
            else:
                x0[i, :, MID] = total
            p = project(pl.ds(B, B))
            if k == 1:
                wait_out(1, 0, i)
                p += skips[i].astype(F32)
            skips[i] = p.astype(BF16)
            start_out(0, k, i)
            start_out(1, k, i)

        return item

    def phase5(k):
        R = ROWS5
        R5 = ROWS5

        def item(i):
            if k == 1:
                finish_norm(5, 3, i)
            mean, inv = tall(stat[2 * k + 1, i, 0], R5), tall(stat[2 * k + 1, i, 1], R5)
            wide_s[:, 0 : 2 * B] = dot(act2[k, i], dp[i], NT)
            total8 = dot(jnp.ones((8, F), BF16), dp[i], NT)
            bias_sum[k] += total8
            total = tall(total8, R5)

            def tile(r, sums):
                table = chan[k, r, :]
                g, e = column(table, 9), column(table, 10)
                product = wide_s[r, 0 : 2 * B]
                w = wout[k, r, :].astype(F32)
                against = fold(w * product)
                plain = fold(w * total)
                normed = inv * (against - mean * plain)
                gacc[9, r, :] += normed
                gacc[10, r, :] += plain
                scale = inv * g
                shift = e - mean * scale
                step = wide(scale, 2 * B) * product + wide(shift, 2 * B) * total
                grad[k, r, :] += step[:, :B]
                grad[k, pl.ds(H + r.start, R5), :] += step[:, B:]
                return (sums[0] + fold_rows(g * plain), sums[1] + fold_rows(g * normed))

            a, b = per_tile(tile, rows=R5, init=(zero8, zero8))
            send_stats(4 * k + 2, i, a, b)

        return item

    def halo_copy(i, side):
        edge = pl.ds(DILATION, DILATION) if side == 0 else pl.ds(F, DILATION)
        return remote(
            buf.at[i, :, edge],
            buf.at[i, :, tail if side == 0 else head],
            sem_hs.at[side, i],
            sem_hr.at[side, i],
            {"tm": left if side == 0 else right},
        )

    def phase6(k):
        R = ROWS6
        def item(i):
            finish_back(4 * k + 2, 2 * k + 1, i)
            inv = tall(stat[2 * k + 1, i, 1], R) * LOG2E
            p, q = wide(tall(back[i, 0], R), F), wide(tall(back[i, 1], R), F)
            m = mask_row(i, R)

            def tile(r, c):
                table = chan[k, r, :]
                slope = column(table, 8)
                g = inv * column(table, 9)
                d_act = low(dot(wout[k, r, :], dp[i]) * wide(g, F) + m * (p + q * act2[k, i, r, :].astype(F32)))
                soft = soft2[k, i, r, :]
                d_conv = d_act * (wide(low(slope), F) + wide(low(1.0 - slope), F) * jnp.exp2(-soft))
                gacc[8, r, :] += fold(d_act * soft).astype(F32) * -LN2
                gacc[7, r, :] += fold(d_conv).astype(F32)
                buf[i, r, MID] = d_conv
                return c

            per_tile(tile, rows=R)
            if k == 0:

                @pl.when(t > 0)
                def _():
                    halo_copy(i, 0).start()

                @pl.when(t < last)
                def _():
                    halo_copy(i, 1).start()

                @pl.when(t == 0)
                def _():
                    buf[i, :, 0:DILATION] = jnp.zeros((H, DILATION), BF16)

                @pl.when(t == last)
                def _():
                    buf[i, :, F + DILATION : W] = jnp.zeros((H, DILATION), BF16)

        return item

    def edge6():
        R = ROWS6
        wide_s[:, 0:LANES] = dot(wout[1], dp_edge[...])
        inv = tall(lanes_of(stat.at[3], 1), R) * LOG2E
        p, q = tall(lanes_of(back, 0), R), tall(lanes_of(back, 1), R)
        m = tall(edge_mask_ref[...], R)

        def tile(r, c):
            table = chan[1, r, :]
            slope = column(table, 8)
            d_act = wide_s[r, 0:LANES] * (inv * column(table, 9)) + m * (p + q * act_edge[r, :].astype(F32))
            d_conv = d_act * (slope + (1.0 - slope) * jnp.exp2(-soft_edge[r, :].astype(F32)))
            conv_edge[r, :] = d_conv.astype(BF16)
            return c

        per_tile(tile, rows=R)

    def phase7(k):
        R = ROWS7
        act = act1_0 if k == 0 else act1_1
        mid = MID if k == 0 else slice(0, F)

        def item(i):
            if k == 0:

                @pl.when(t > 0)
                def _():
                    halo_copy(i, 0).wait_send()
                    halo_copy(i, 1).wait_recv()

                @pl.when(t < last)
                def _():
                    halo_copy(i, 1).wait_send()
                    halo_copy(i, 0).wait_recv()

            mean, inv = tall(stat[2 * k, i, 0], R), tall(stat[2 * k, i, 1], R)
            m = low(mask_row(i, R))

            def tile(r, sums):
                table = chan[k, r, :]
                g = column(table, 2)
                scale = inv * g
                shift = column(table, 3) - mean * scale
                before, d, after = taps(k, i, r, conv_edge)
                u = (
                    wide(low(column(table, 4)), F) * after
                    + wide(low(column(table, 5)), F) * d
                    + wide(low(column(table, 6)), F) * before
                ) * m
                a = act[i, r, mid]
                first = (a * wide(low(scale), F) + wide(low(shift), F)) * m
                plain = fold(u).astype(F32)
                normed = inv * (fold(u * a).astype(F32) - mean * plain)
                gacc[2, r, :] += normed
                gacc[3, r, :] += plain
                gacc[4, r, :] += fold(after * first).astype(F32)
                gacc[5, r, :] += fold(d * first).astype(F32)
                gacc[6, r, :] += fold(before * first).astype(F32)
                soft2[k, i, r, :] = u
                return (sums[0] + fold_rows(g * plain), sums[1] + fold_rows(g * normed))

            a, b = per_tile(tile, rows=R, init=(zero8, zero8))
            send_stats(4 * k + 3, i, a, b)

        return item

    def mix_copy(i):
        row = first_item + i
        return (
            pltpu.make_async_copy(stage.at[2 * i + s], gmix_h.at[row], sem_m.at[0, i]),
            remote(stage.at[2 * i + o], gmix_h.at[row], sem_m.at[1, i], sem_mr.at[i], {"section": o}),
        )

    def phase8(k):
        R = ROWS8
        act = act1_0 if k == 0 else act1_1
        x = x0 if k == 0 else x1
        mid = MID if k == 0 else slice(0, F)

        def item(i):
            finish_back(4 * k + 3, 2 * k, i)
            inv = tall(stat[2 * k, i, 1], R) * LOG2E
            p, q = wide(tall(back[i, 0], R), F), wide(tall(back[i, 1], R), F)
            m = mask_row(i, R)

            def tile(r, c):
                table = chan[k, r, :]
                slope = column(table, 1)
                g = inv * column(table, 2)
                d_act = low(soft2[k, i, r, :].astype(F32) * wide(g, F) + m * (p + q * act[i, r, mid].astype(F32)))
                soft = soft1[k, i, r, :]
                d_pre = d_act * (wide(low(slope), F) + wide(low(1.0 - slope), F) * jnp.exp2(-soft))
                gacc[1, r, :] += fold(d_act * soft).astype(F32) * -LN2
                gacc[0, r, :] += fold(d_pre).astype(F32)
                buf[i, r, MID] = d_pre
                grad[k, pl.ds(2 * H + r.start, R), :] += dot(d_pre, x[i, :, mid], NT)
                return c

            per_tile(tile, rows=R)

            if k == 1:
                input_gradient(1, i)

        return item

    def input_gradient(k, i):
        wide_s[0:B, 0:F] = dot(win[k], buf[i, :, MID])
        m = mask_row(i, B)
        d_input = (wide_s[0:B, 0:F] + dp[i, 0:B, :].astype(F32)) * m
        if k == 1:
            dp[i, 0:B, :] = d_input.astype(BF16)
        else:
            stage[2 * i] = d_input[0:half].astype(BF16)
            stage[2 * i + 1] = d_input[half:].astype(BF16)
            here, there = mix_copy(i)
            there.start()
            here.start()

    rows_at_part = ((0, 2 * H), (2 * H, grad.shape[1]))
    came = (came0, came1)
    slots = ((from_item0, from_tm0), (from_item1, from_tm1))

    def sizes(part):
        big, chunk = slots[part][0].shape[1], slots[part][1].shape[1]
        return big, chunk, big // chunk

    def item_peer(d):
        return lax.rem(it + d, n_item)

    def tm_peer(d):
        return lax.rem(t + d, n_tm)

    def each(count, body):
        lax.fori_loop(1, count, lambda d, c: (body(d), c)[1], 0)

    def at_part(part, k, start, rows):
        return grad.at[k, pl.ds(rows_at_part[part][0] + start, rows)]

    def to_owner(part, k):
        a, b = rows_at_part[part]
        return remote(grad.at[k, pl.ds(a, b - a)], came[part], sem_k.at[part], sem_kr.at[part], {"section": o})

    def item_scatter(part, k, d):
        big = sizes(part)[0]
        src = at_part(part, k, item_peer(d) * big, big)
        return remote(
            src, slots[part][0].at[d - 1], sem_ri.at[part, d - 1], sem_rir.at[part, d - 1], {"item": item_peer(d)}
        )

    def tm_scatter(part, k, d):
        big, chunk, owners = sizes(part)
        src = at_part(part, k, it * big + lax.rem(tm_peer(d), owners) * chunk, chunk)
        return remote(
            src, slots[part][1].at[d - 1], sem_rt.at[part, d - 1], sem_rtr.at[part, d - 1], {"tm": tm_peer(d)}
        )

    def tm_gather(part, d, member):
        big, chunk, owners = sizes(part)
        rows = came[part].at[pl.ds(it * big + lax.rem(member, owners) * chunk, chunk)]
        return remote(rows, rows, sem_at.at[part, d - 1], sem_atr.at[part, d - 1], {"tm": tm_peer(d)})

    def item_gather(part, d, member):
        big = sizes(part)[0]
        rows = came[part].at[pl.ds(member * big, big)]
        return remote(rows, rows, sem_ai.at[part, d - 1], sem_air.at[part, d - 1], {"item": item_peer(d)})

    def sum_1(part, k):
        pl.when(s != k)(lambda: to_owner(part, k).start())

    def sum_2(part, k):
        pl.when(s != k)(lambda: to_owner(part, k).wait_send())

        @pl.when(s == k)
        def _():
            a, b = rows_at_part[part]
            to_owner(part, k).wait_recv()
            grad[k, a:b] += came[part][...]
            each(n_item, lambda d: item_scatter(part, k, d).start())

    def sum_3(part, k):
        big, chunk, owners = sizes(part)

        @pl.when(s == k)
        def _():
            each(n_item, lambda d: item_scatter(part, k, d).wait())
            mine = pl.ds(pl.multiple_of(rows_at_part[part][0] + it * big, 8), big)
            grad[k, mine] = lax.fori_loop(0, n_item - 1, lambda j, x: x + slots[part][0][j], grad[k, mine])
            each(n_tm, lambda d: pl.when(tm_peer(d) < owners)(lambda: tm_scatter(part, k, d).start()))

    def sum_4(part, k):
        big, chunk, owners = sizes(part)

        @pl.when(s == k)
        def _():
            def wait(d):
                pl.when(tm_peer(d) < owners)(lambda: tm_scatter(part, k, d).wait_send())
                pl.when(t < owners)(lambda: tm_scatter(part, k, d).wait_recv())

            each(n_tm, wait)

            @pl.when(t < owners)
            def _():
                start = it * big + t * chunk
                own = grad[k, pl.ds(pl.multiple_of(rows_at_part[part][0] + start, 8), chunk)]
                total = lax.fori_loop(0, n_tm - 1, lambda j, x: x + slots[part][1][j], own)
                came[part][pl.ds(pl.multiple_of(start, 8), chunk)] = total
                each(n_tm, lambda d: tm_gather(part, d, t).start())

    def sum_5(part, k):
        _, _, owners = sizes(part)

        @pl.when(s == k)
        def _():
            def wait(d):
                source = lax.rem(t - d + n_tm, n_tm)
                pl.when(t < owners)(lambda: tm_gather(part, d, t).wait_send())
                pl.when(source < owners)(lambda: tm_gather(part, d, source).wait_recv())

            each(n_tm, wait)
            each(n_item, lambda d: item_gather(part, d, it).start())

    def sum_6(part, k):
        @pl.when(s == k)
        def _():
            def wait(d):
                item_gather(part, d, it).wait_send()
                item_gather(part, d, lax.rem(it - d + n_item, n_item)).wait_recv()

            each(n_item, wait)

    last_rows = grad.shape[1] - 2 * H
    last_chunk = to_owner_slots.shape[2]
    last_owners = low_grad.shape[0] // last_chunk
    first_core = jnp.int32(0)

    def member_at(d):
        peer = lax.rem(me + d, members)
        return peer, {"section": first_core, "tm": peer // n_item, "item": lax.rem(peer, n_item)}

    def chunk_rows(member):
        return pl.ds(pl.multiple_of(lax.rem(member, last_owners) * last_chunk, 16), last_chunk)

    def last_scatter(core, d):
        peer, device = member_at(d)
        return remote(
            low_grad.at[chunk_rows(peer)], to_owner_slots.at[core, d], sem_ls.at[d], sem_lr.at[core, d], device
        )

    def last_gather(d, member):
        rows = low_total.at[chunk_rows(member)]
        return remote(rows, rows, sem_gs.at[d], sem_gr.at[d], member_at(d)[1])

    def others(body, start=1):
        lax.fori_loop(start, members, lambda d, c: (body(d), c)[1], 0)

    def last_1():
        low_grad[0:last_rows] = low(grad[0, 2 * H :])
        if low_grad.shape[0] > last_rows:
            low_grad[last_rows:] = jnp.zeros((low_grad.shape[0] - last_rows, LANES), BF16)

        def send(core):
            def one(d):
                pl.when(member_at(d)[0] < last_owners)(lambda: last_scatter(core, d).start())

            others(one, 1 - core)

        pl.when(s == 0)(lambda: send(0))
        pl.when(s == 1)(lambda: send(1))

    def last_2():
        def sent(core):
            def one(d):
                pl.when(member_at(d)[0] < last_owners)(lambda: last_scatter(core, d).wait_send())

            others(one, 1 - core)

        pl.when(s == 1)(lambda: sent(1))

        @pl.when(s == 0)
        def _():
            sent(0)

            @pl.when(me < last_owners)
            def _():
                others(lambda d: last_scatter(0, d).wait_recv())
                others(lambda d: last_scatter(1, d).wait_recv(), 0)
                mine = chunk_rows(me)
                total = low_grad[mine].astype(F32) + to_owner_slots[1, 0].astype(F32)
                total = lax.fori_loop(
                    1,
                    members,
                    lambda d, x: x + (to_owner_slots[0, d].astype(F32) + to_owner_slots[1, d].astype(F32)),
                    total,
                )
                low_total[mine] = low(total)
                others(lambda d: last_gather(d, me).start())

    def last_3():
        @pl.when(s == 0)
        def _():
            def wait(d):
                source = lax.rem(me - d + members, members)
                pl.when(me < last_owners)(lambda: last_gather(d, me).wait_send())
                pl.when(source < last_owners)(lambda: last_gather(d, source).wait_recv())

            others(wait)
            came1[...] = low_total[0:last_rows].astype(F32)

    def finish_block(k):
        group = H // 4
        lanes = lax.broadcasted_iota(jnp.int32, (group, LANES), 1)
        bias = jnp.broadcast_to(bias_sum[k, 0:1, :], (LANES, 2 * B)).T
        packed = jnp.zeros((group, LANES), F32)
        for g in range(4):
            for j in range(11):
                total = jnp.sum(gacc[j, g * group : (g + 1) * group, :], axis=1, keepdims=True)
                packed = jnp.where(lanes == 32 * g + j, total, packed)
            if (g + 1) * group <= 2 * B:
                packed = jnp.where(lanes == 32 * g + 11, bias[g * group : (g + 1) * group], packed)
        grad[k, 3 * H : 3 * H + group] = packed

    def mask_gradients(i):
        m = mask_row(i, R)

        def tile(r, c):
            dp[i, r, :] = (dp[i, r, :].astype(F32) * m).astype(BF16)
            return c

        per_tile(tile, 2 * B)

    wait_weights(0, 1)
    main_local.wait()
    main_send.wait_send()
    main_recv.wait_recv()

    @pl.when(t > 0)
    def _():
        for core in (0, 1):
            halo_send(0, core).wait_send()
            halo_recv(1, core).wait_recv()

    @pl.when(t < last)
    def _():
        for core in (0, 1):
            halo_send(1, core).wait_send()
            halo_recv(0, core).wait_recv()

    def steps(count, *bodies):
        def step(j, c):
            for first, body in bodies:
                pl.when((j >= first) & (j < first + NI))(functools.partial(body, j - first))
            return c

        lax.fori_loop(0, count, step, 0)

    def send_x1_edges(i):
        @pl.when(i == NI - 1)
        def _():
            pack_edges(x1, B, 1)
            send_edges(1, B)

    per_item(phase1(0))
    p2, p3 = phase2(0), phase3(0)
    per_item(lambda i: (p2(i), p3(i)))
    wait_weights(2, 3)
    steps(NI + 2, (0, phase4(0)), (0, send_x1_edges), (2, phase1(1)))
    edge1()
    load_out.wait()
    load_skip.wait()
    per_item(mask_gradients)
    pack_edges(dp, 2 * B, 0)
    send_edges(0, 2 * B)
    per_item(phase2(1))
    edge2()
    per_item(phase3(1))
    edge3()
    recv_edges(0, 2 * B, dp_edge)
    wait_weights(4)
    gacc[...] = jnp.zeros(gacc.shape, F32)
    per_item(phase5(1))
    sum_1(0, 1)
    per_item(phase6(1))
    edge6()
    sum_2(0, 1)
    wait_weights(5)
    per_item(phase7(1))
    per_item(phase8(1))
    sum_3(0, 1)
    finish_block(1)
    sum_1(1, 1)
    gacc[...] = jnp.zeros(gacc.shape, F32)
    per_item(phase5(0))
    sum_1(0, 0)
    sum_4(0, 1)
    sum_2(1, 1)
    per_item(phase6(0))
    sum_5(0, 1)
    sum_2(0, 0)
    sum_3(1, 1)
    per_item(phase7(0))
    per_item(phase8(0))
    finish_block(0)
    last_1()
    sum_3(0, 0)
    sum_4(1, 1)
    per_item(phase4(1))
    sum_4(0, 0)
    sum_5(1, 1)
    per_item(lambda i: input_gradient(0, i))
    last_2()
    sum_5(0, 0)
    sum_6(0, 1)
    sum_6(1, 1)
    last_3()
    sum_6(0, 0)
    results = [
        pltpu.make_async_copy(came[part], grad_h.at[pl.ds(a, b - a)], sem_f.at[part])
        for part, (a, b) in enumerate(rows_at_part)
    ]
    for copy in results:
        copy.start()
    for copy in results:
        copy.wait()

    for i in range(NI):
        here, there = mix_copy(i)
        here.wait()
        there.wait_send()
        remote(
            stage.at[2 * i], gmix_h.at[o * NI + i], sem_m.at[1, i], sem_mr.at[i], {"section": o}
        ).wait_recv()
        for kind, k in ((0, 0), (0, 1), (1, 1)):
            wait_out(kind, k, i)
        wait_came(0, i)
        wait_came(1, i)


def chunk_of(rows, members):
    chunk = -(-rows // members)
    chunk = -(-chunk // 8) * 8
    while rows % chunk:
        chunk += 8
    return chunk


def run(n_tm, n_item, sources, gout, gskip, w_in, chan, w_out, b_out, counts, lengths):
    n_src, flat, F = sources.shape
    items, B, _ = gout.shape
    NI = items // 2
    H = w_in.shape[0]
    W = F + 2 * DILATION
    half = B // 2
    rows0, rows1 = 2 * H, H + H // 4
    quarter0, quarter1 = rows0 // n_item, rows1 // n_item
    members = n_tm * n_item
    low_chunk = -(-rows1 // (16 * members)) * 16
    low_owners = -(-rows1 // low_chunk)
    smem = pl.BlockSpec(memory_space=pltpu.SMEM)
    any_spec = pl.BlockSpec(memory_space=pl.ANY)
    vmem = pl.BlockSpec(memory_space=pltpu.VMEM)
    dma = pltpu.SemaphoreType.DMA
    shape = jax.ShapeDtypeStruct
    outs = (
        shape((items, B, F), BF16),
        shape((items, B, F), BF16),
        shape((items, half, F), BF16),
        shape((rows0 + rows1, LANES), F32),
    )
    scratch = [
        pltpu.VMEM((items, half, F), BF16),
        pltpu.VMEM((NI, B, W), BF16),
        pltpu.VMEM((NI, B, F), BF16),
        pltpu.VMEM((NI, B, F), BF16),
        pltpu.VMEM((NI, H, W), BF16),
        pltpu.VMEM((NI, H, F), BF16),
        pltpu.VMEM((2, NI, H, F), BF16),
        pltpu.VMEM((2, NI, H, F), BF16),
        pltpu.VMEM((2, NI, H, F), BF16),
        pltpu.VMEM((NI, H, W), BF16),
        pltpu.VMEM((H, W), F32),
        pltpu.VMEM((NI, 2 * B, F), BF16),
        pltpu.VMEM((11, H, LANES), F32),
        pltpu.VMEM((2, H, B), BF16),
        pltpu.VMEM((2, H, 2 * B), BF16),
        pltpu.VMEM((2, 2 * B, H), BF16),
        pltpu.VMEM((2, B, H), BF16),
        pltpu.VMEM((2, H, LANES), F32),
        pltpu.VMEM((2, 2 * B, LANES), F32),
        pltpu.VMEM((low_chunk * low_owners, LANES), BF16),
        pltpu.VMEM((low_chunk * low_owners, LANES), BF16),
        pltpu.VMEM((2, members, low_chunk, LANES), BF16),
        pltpu.VMEM((2, rows0 + rows1, LANES), F32),
        pltpu.VMEM((2, 8, 2 * B), F32),
        pltpu.VMEM((rows0, LANES), F32),
        pltpu.VMEM((rows1, LANES), F32),
        pltpu.VMEM((n_item - 1, quarter0, LANES), F32),
        pltpu.VMEM((n_item - 1, quarter1, LANES), F32),
        pltpu.VMEM((n_tm - 1, chunk_of(quarter0, n_tm), LANES), F32),
        pltpu.VMEM((n_tm - 1, chunk_of(quarter1, n_tm), LANES), F32),
        pltpu.VMEM((NI, 8, W), F32),
        pltpu.VMEM((8, LANES), F32),
        pltpu.VMEM((NI, 8, LANES), F32),
        pltpu.VMEM((4, NI, 2, 8, LANES), F32),
        pltpu.VMEM((NI, 2, 8, LANES), F32),
        pltpu.VMEM((2, NI, 8, LANES), F32),
        pltpu.VMEM((2, NI, n_tm - 1, 8, LANES), F32),
        pltpu.VMEM((2, 3, 2 * B, LANES), BF16),
        pltpu.VMEM((2, 2, 2 * B, LANES), BF16),
        pltpu.VMEM((B, LANES), BF16),
        pltpu.VMEM((2 * B, LANES), BF16),
        pltpu.VMEM((H, LANES), BF16),
        pltpu.VMEM((H, LANES), BF16),
        pltpu.VMEM((H, LANES), BF16),
        pltpu.VMEM((H, LANES), BF16),
        dma((n_src,)),
        dma((6, 2)),
        dma((6,)),
        dma((5,)),
        dma((2,)),
        dma((2, 2)),
        dma((2, 2)),
        dma((2, NI, n_tm - 1)),
        dma((2, NI, n_tm - 1)),
        dma((2, NI)),
        dma((2, NI)),
        dma((2, 2, NI)),
        dma((2, NI)),
        dma((2, NI)),
        dma((NI,)),
        dma((members,)),
        dma((2, members)),
        dma((members,)),
        dma((members,)),
        dma((2,)),
        dma((2,)),
        dma((2, n_item - 1)),
        dma((2, n_item - 1)),
        dma((2, n_tm - 1)),
        dma((2, n_tm - 1)),
        dma((2, n_tm - 1)),
        dma((2, n_tm - 1)),
        dma((2, n_item - 1)),
        dma((2, n_item - 1)),
        dma((2,)),
    ]
    return pl.pallas_call(
        functools.partial(kernel, (n_tm, n_item, NI, H, B, F)),
        out_shape=outs,
        in_specs=[any_spec] * 3 + [vmem] * 4 + [smem] * 2,
        out_specs=[any_spec] * len(outs),
        scratch_shapes=scratch,
        compiler_params=pltpu.CompilerParams(
            collective_id=0, has_side_effects=True, vmem_limit_bytes=VMEM_LIMIT
        ),
        name="temporal_blocks",
    )(sources, gout, gskip, w_in, chan, w_out, b_out, counts, lengths)


def close_kernel(
    block_in, skip_in, gmix_in, grad_in, counts,
    block_h, skip_h, sources_h, w_in_h, chan_h, w_out_h, b_out_h,
    held, mixed, full, nothing, sums, w_out, chan, bias, sem_a, sem_b, sem_g, sem_s, sem_w,
):
    items = gmix_in.shape[0]
    H, B = w_in_h.shape
    n_src = sources_h.shape[0]
    plain = [(j, i) for i in range(items) for j in (0, 1)]

    def fetch(j, i):
        return pltpu.make_async_copy((block_in, skip_in)[j].at[i], held.at[j, i], sem_a.at[j, i])

    def store(j, i):
        return pltpu.make_async_copy(held.at[j, i], (block_h, skip_h)[j].at[i], sem_b.at[j, i])

    loads = [pltpu.make_async_copy(gmix_in.at[i], mixed.at[i], sem_g.at[i]) for i in range(items)]
    load_sums = pltpu.make_async_copy(grad_in, sums, sem_w.at[0])
    for copy in loads:
        copy.start()
    load_sums.start()
    for j, i in plain:
        fetch(j, i).start()
    nothing[...] = jnp.zeros(nothing.shape, F32)
    for i in range(items):
        loads[i].wait()
        full[i] = mixed[i].astype(F32)
        for n in range(n_src):

            @pl.when(n < counts[i])
            def _():
                pltpu.make_async_copy(full.at[i], sources_h.at[n, i], sem_s.at[n, i]).start()

            @pl.when(n >= counts[i])
            def _():
                pltpu.make_async_copy(nothing, sources_h.at[n, i], sem_s.at[n, i]).start()

    load_sums.wait()
    store_w_in = pltpu.make_async_copy(sums.at[pl.ds(2 * H, H)], w_in_h, sem_w.at[1])
    store_w_in.start()
    for j, i in plain:
        fetch(j, i).wait()
        store(j, i).start()
    w_out[0:B, :] = sums[0:H, :].T
    w_out[B : 2 * B, :] = sums[H : 2 * H, :].T
    rows = sums[3 * H : 3 * H + H // 4, :].T
    for j in range(chan.shape[0]):
        chan[j] = jnp.concatenate([rows[32 * g + j : 32 * g + j + 1] for g in range(4)], axis=1)
    bias[...] = jnp.concatenate([rows[32 * g + 11 : 32 * g + 12] for g in range(2 * B * 4 // H)], axis=1)
    late = [
        pltpu.make_async_copy(src, dst, sem_w.at[2 + j])
        for j, (src, dst) in enumerate(((w_out, w_out_h), (chan, chan_h), (bias, b_out_h)))
    ]
    for copy in late:
        copy.start()
    for copy in late:
        copy.wait()
    store_w_in.wait()
    for j, i in plain:
        store(j, i).wait()
    for i in range(items):
        for n in range(n_src):
            pltpu.make_async_copy(full.at[i], sources_h.at[n, i], sem_s.at[n, i]).wait()


def close(n_src, n_rows, block, skip, gmix, grad, counts):
    items, half, F = gmix.shape
    B = 2 * half
    H = (grad.shape[0] * 4) // 13
    any_spec = pl.BlockSpec(memory_space=pl.ANY)
    dma = pltpu.SemaphoreType.DMA
    shape = jax.ShapeDtypeStruct
    return pl.pallas_call(
        close_kernel,
        out_shape=(
            shape(block.shape, BF16),
            shape(skip.shape, BF16),
            shape((n_src, items, half, F), F32),
            shape((H, B), F32),
            shape((n_rows, 1, H), F32),
            shape((2 * B, H), F32),
            shape((1, 2 * B), F32),
        ),
        in_specs=[any_spec] * 4 + [pl.BlockSpec(memory_space=pltpu.SMEM)],
        out_specs=[any_spec] * 7,
        scratch_shapes=[
            pltpu.VMEM((2, items, B, F), BF16),
            pltpu.VMEM((items, half, F), BF16),
            pltpu.VMEM((items, half, F), F32),
            pltpu.VMEM((half, F), F32),
            pltpu.VMEM(grad.shape, F32),
            pltpu.VMEM((2 * B, H), F32),
            pltpu.VMEM((n_rows, 1, H), F32),
            pltpu.VMEM((1, 2 * B), F32),
            dma((2, items)),
            dma((2, items)),
            dma((items,)),
            dma((n_src, items)),
            dma((5,)),
        ],
        compiler_params=pltpu.CompilerParams(vmem_limit_bytes=VMEM_LIMIT),
        name="lay_out",
    )(block, skip, gmix, grad, counts)


def local(sources, source_counts, valid_lengths, w_in, chan, w_out, b_out, grad_out, grad_skip):
    n_sources, per_device, half, F = sources.shape
    block_out, skip_out, gmix, grad = run(
        lax.axis_size("tm"),
        lax.axis_size("item"),
        sources.reshape(n_sources, per_device * half, F),
        grad_out,
        grad_skip,
        w_in[0],
        chan.transpose(1, 0, 2),
        w_out[0],
        b_out,
        source_counts,
        valid_lengths,
    )
    block_out, skip_out, grad_sources, grad_w_in, grad_chan, grad_w_out, grad_b_out = close(
        n_sources, chan.shape[1], block_out, skip_out, gmix, grad, source_counts
    )
    return (
        block_out[None],
        skip_out[None],
        grad_sources,
        grad_w_in[None],
        grad_chan.transpose(1, 0, 2),
        grad_w_out[None],
        grad_b_out,
    )


def solution(mesh):
    in_specs = (
        P(None, "item", "section", "tm"),
        P("item"),
        P("item"),
        P("section", None, None),
        P("section", None, None),
        P("section", None, None),
        P("section", None),
        P("item", None, "tm"),
        P("item", None, "tm"),
    )
    out_specs = (
        P("section", "item", None, "tm"),
        P("section", "item", None, "tm"),
        P(None, "item", "section", "tm"),
        P("section", None, None),
        P("section", None, None),
        P("section", None, None),
        P("section", None),
    )
    return jax.shard_map(local, mesh=mesh, in_specs=in_specs, out_specs=out_specs, check_vma=False)
```

```python
import functools
import math

import jax
import jax.numpy as jnp
from jax import lax
from jax.experimental import pallas as pl
from jax.experimental.pallas import tpu as pltpu
from jax.sharding import PartitionSpec as P

DILATION = 128
LANES = 128
ROWS = 128
ROWS1 = 512
ROWS2 = 512
ROWS3 = 256
ROWS4 = 128
ROWS5 = 512
ROWS6 = 512
ROWS7 = 256
ROWS7_ENDS = 512
ROWS8 = 512
EPSILON = 1e-05
VMEM_LIMIT = 63 * 1024 * 1024 + 512 * 1024
LN2 = math.log(2.0)
LOG2E = 1.0 / LN2
F32 = jnp.float32
BF16 = jnp.bfloat16
MESH = pl.DeviceIdType.MESH
NT = (((1,), (1,)), ((), ()))
NN = (((1,), (0,)), ((), ()))


def dot(a, b, dims=NN, precision=None):
    return lax.dot_general(a, b, dims, precision=precision, preferred_element_type=F32)


def remote(src, dst, send, recv, device):
    return pltpu.make_async_remote_copy(
        src_ref=src, dst_ref=dst, send_sem=send, recv_sem=recv, device_id=device, device_id_type=MESH
    )


def wide(v, width):
    return jnp.concatenate([v] * (width // LANES), axis=1)


def tall(v, rows):
    return jnp.concatenate([v] * (rows // v.shape[0]), axis=0)


def fold(v):
    parts = [v[:, at : at + LANES] for at in range(0, v.shape[1], LANES)]
    while len(parts) > 1:
        parts = [a + b for a, b in zip(parts[::2], parts[1::2])] + parts[len(parts) & ~1 :]
    return parts[0]


def fold_rows(v):
    parts = [v[at : at + 8] for at in range(0, v.shape[0], 8)]
    while len(parts) > 1:
        parts = [a + b for a, b in zip(parts[::2], parts[1::2])] + parts[len(parts) & ~1 :]
    return parts[0]


def low(v):
    return v.astype(BF16)


def column(table, j):
    return jnp.broadcast_to(table[:, j : j + 1], (table.shape[0], LANES))


def rows_at(t, count):
    return pl.ds(pl.multiple_of(t * count, count), count)


def kernel(
    dims,
    sources_h, gout_h, gskip_h, w_in_h, chan_h, w_out_h, b_out_h, counts, lengths,
    block_h, skip_h, gmix_h, grad_h,
    stage, x0, x1, skips, act1_0, act1_1, soft1, act2, soft2, buf, wide_s, dp, gacc,
    wpre, wout, wg, win, chan, col,
    low_grad, low_total, to_owner_slots, grad, bias_sum, came0, came1, from_item0, from_item1, from_tm0, from_tm1,
    mask_ref, edge_mask_ref, invn_ref, inner_sums, stat, back, st_src, st_buf,
    shifts, w_in_ref, chan_ref, w_out_ref, b_out_ref, edge_src, edge_in, x_edge, dp_edge, first_edge, act_edge, soft_edge, conv_edge,
    sem_s, sem_w, sem_x, sem_xr, sem_g, sem_es, sem_er, sem_ss, sem_sr, sem_hs, sem_hr, sem_o, sem_or, sem_m, sem_mr,
    sem_ls, sem_lr, sem_gs, sem_gr, sem_k, sem_kr, sem_ri, sem_rir, sem_rt, sem_rtr, sem_at, sem_atr, sem_ai, sem_air, sem_f,
):
    n_tm, n_item, NI, H, B, F = dims
    R = ROWS
    W = F + 2 * DILATION
    MID = slice(DILATION, DILATION + F)
    half = B // 2
    s = lax.axis_index("section")
    t = lax.axis_index("tm")
    o = 1 - s
    left = t - 1
    right = t + 1
    last = n_tm - 1
    first_item = s * NI
    lane = lax.broadcasted_iota(jnp.int32, (R, LANES), 1)
    lane8 = lax.broadcasted_iota(jnp.int32, (8, LANES), 1)

    it = lax.axis_index("item")
    members = n_tm * n_item
    me = t * n_item + it
    n_src = sources_h.shape[0]

    def load_source(n):
        return pltpu.make_async_copy(sources_h.at[n], soft2.at[1, n], sem_s.at[n])

    small = [
        pltpu.make_async_copy(src, dst, sem_s.at[n_src + j])
        for j, (src, dst) in enumerate(
            ((w_in_h, w_in_ref), (chan_h, chan_ref), (w_out_h, w_out_ref), (b_out_h, b_out_ref))
        )
    ]
    for copy in small:
        copy.start()
    for n in range(n_src):
        load_source(n).start()
    edge_in[...] = jnp.zeros(edge_in.shape, BF16)
    row = lax.broadcasted_iota(jnp.int32, (2 * LANES, 2 * LANES), 0)
    to = lax.broadcasted_iota(jnp.int32, (2 * LANES, 2 * LANES), 1)
    step = jnp.where(to < LANES, LANES - 1, 1 - LANES)
    shifts[...] = low(jnp.where(row - to == step, 1.0, 0.0))

    barrier = pltpu.get_barrier_semaphore()

    def greet(d, c):
        peer = lax.rem(me + d, members)
        device = {"tm": peer // n_item, "item": lax.rem(peer, n_item)}
        pl.semaphore_signal(barrier, inc=1, device_id=device, device_id_type=MESH)
        pl.semaphore_signal(barrier, inc=1, device_id={"section": o} | device, device_id_type=MESH)
        return c

    pl.semaphore_signal(barrier, inc=1, device_id={"section": o}, device_id_type=MESH)
    lax.fori_loop(1, members, greet, 0)
    for copy in small:
        copy.wait()

    w_in = w_in_ref[...]
    w_out = w_out_ref[...].astype(F32)
    wpre[s] = w_in
    win[s] = w_in.astype(F32).T.astype(BF16)
    wout[s] = w_out.T.astype(BF16)
    gained = (w_out * chan_ref[9]).astype(BF16)
    wg[s] = gained
    wide_s[0:LANES, 0:H] = jnp.zeros((LANES, H), F32)
    for j in range(chan_ref.shape[0]):
        wide_s[j : j + 1, 0:H] = chan_ref[j]
    chan[s] = wide_s[0:LANES, 0:H].T
    bias = jnp.broadcast_to(b_out_ref[...], (LANES, 2 * B)).T
    bias += jnp.sum(w_out * chan_ref[10], axis=1, keepdims=True)
    gain = jnp.sum(gained.astype(F32), axis=1, keepdims=True)
    lane_w = lax.broadcasted_iota(jnp.int32, (2 * B, LANES), 1)
    col[s] = jnp.where(lane_w == 0, bias, gain)

    for i in range(NI):
        length = lengths[first_item + i]
        where = lax.broadcasted_iota(jnp.int32, (8, W), 1) + (t * F - DILATION)
        mask_ref[i] = jnp.where((where >= 0) & (where < length), 1.0, 0.0)
        invn_ref[i] = 1.0 / (jnp.full((8, LANES), length, jnp.int32).astype(F32) * H)
    within = lane8 % 32
    frame = t * F + jnp.where(within < 16, within - 2, within - 17 + F)
    length = jnp.full((8, LANES), lengths[first_item], jnp.int32)
    for i in range(1, NI):
        length = jnp.where(lane8 >= 32 * i, lengths[first_item + i], length)
    held = (within < 3) | ((within >= 16) & (within < 19))
    edge_mask_ref[...] = jnp.where(held & (frame >= 0) & (frame < length), 1.0, 0.0)

    for n in range(n_src):
        load_source(n).wait()

    def mix_item(i, c):
        rows = pl.ds(pl.multiple_of(i * half, half), half)
        where = lax.broadcasted_iota(jnp.int32, (8, F), 1) + t * F
        m = tall(jnp.where(where < lengths[i], 1.0, 0.0), half)
        total = jnp.zeros((half, F), F32)
        for n in range(n_src):
            total += soft2[1, n, rows, :].astype(F32) * jnp.where(n < counts[i], 1.0, 0.0)
        stage[i] = (total * m).astype(BF16)
        return c

    lax.fori_loop(o * NI, o * NI + NI, mix_item, 0)
    pl.semaphore_wait(barrier, 2 * members - 1)

    own_rows = pl.ds(pl.multiple_of(s * half, half), half)
    other_rows = pl.ds(pl.multiple_of(o * half, half), half)
    items_of = lambda core: pl.ds(core * NI, NI)
    centre = pl.ds(DILATION, F)
    head, tail = pl.ds(0, DILATION), pl.ds(F + DILATION, DILATION)

    main_local = pltpu.make_async_copy(stage.at[items_of(s)], x0.at[:, own_rows, centre], sem_x.at[0])
    main_send = remote(
        stage.at[items_of(o)], x0.at[:, own_rows, centre], sem_x.at[1], sem_xr.at[0], {"section": o}
    )
    main_recv = remote(
        stage.at[items_of(o)], x0.at[:, other_rows, centre], sem_x.at[1], sem_xr.at[0], {"section": o}
    )

    def halo_send(side, core):
        edge = pl.ds(0, DILATION) if side == 0 else pl.ds(F - DILATION, DILATION)
        place = tail if side == 0 else head
        return remote(
            stage.at[items_of(core), :, edge],
            x0.at[:, own_rows, place],
            sem_x.at[2 + 2 * side + core],
            sem_xr.at[1 + 2 * side + s],
            {"section": core, "tm": left if side == 0 else right},
        )

    def halo_recv(side, core):
        place = tail if side == 0 else head
        rows = pl.ds(core * half, half)
        return remote(
            x0.at[:, rows, place], x0.at[:, rows, place], sem_x.at[0], sem_xr.at[1 + 2 * side + core], {"section": o}
        )

    def send_halos(core):
        pl.when(t > 0)(lambda: halo_send(0, core).start())
        pl.when(t < last)(lambda: halo_send(1, core).start())

    main_send.start()
    send_halos(o)
    lax.fori_loop(s * NI, s * NI + NI, mix_item, 0)
    main_local.start()
    send_halos(s)
    load_out = pltpu.make_async_copy(gout_h.at[pl.ds(first_item, NI)], dp.at[:, pl.ds(0, B)], sem_g.at[0])
    load_skip = pltpu.make_async_copy(gskip_h.at[pl.ds(first_item, NI)], dp.at[:, pl.ds(B, B)], sem_g.at[1])
    load_out.start()
    load_skip.start()

    weights = (wpre, chan, wg, col, wout, win)

    def weight_copies(j):
        ref = weights[j]
        return (
            remote(ref.at[s], ref.at[s], sem_w.at[j, 0], sem_w.at[j, 1], {"section": o}),
            remote(ref.at[o], ref.at[o], sem_w.at[j, 0], sem_w.at[j, 1], {"section": o}),
        )

    for j in range(len(weights)):
        weight_copies(j)[0].start()

    def wait_weights(*which):
        for j in which:
            send, recv = weight_copies(j)
            recv.wait_recv()
            send.wait_send()

    @pl.when(t == 0)
    def _():
        x0[:, :, 0:DILATION] = jnp.zeros((NI, B, DILATION), BF16)

    @pl.when(t == last)
    def _():
        x0[:, :, F + DILATION : W] = jnp.zeros((NI, B, DILATION), BF16)

    grad[...] = jnp.zeros(grad.shape, F32)
    bias_sum[...] = jnp.zeros(bias_sum.shape, F32)

    def stat_copy(ph, i, d, to):
        p = ph % 2
        return remote(
            st_src.at[p, i], st_buf.at[p, i, d - 1], sem_ss.at[p, i, d - 1], sem_sr.at[p, i, d - 1], {"tm": to}
        )

    def send_stats(ph, i, a, b):
        rows = [jnp.sum(a, axis=0, keepdims=True), jnp.sum(b, axis=0, keepdims=True)]
        st_src[ph % 2, i] = jnp.concatenate(rows + [jnp.zeros((6, LANES), F32)], axis=0)

        def one(d, c):
            stat_copy(ph, i, d, lax.rem(t + d, n_tm)).start()
            return c

        lax.fori_loop(1, n_tm, one, 0)

    def recv_stats(ph, i):
        def one(d, total):
            copy = stat_copy(ph, i, d, lax.rem(t + d, n_tm))
            copy.wait_send()
            copy.wait_recv()
            return total + st_buf[ph % 2, i, d - 1]

        total = lax.fori_loop(1, n_tm, one, st_src[ph % 2, i])
        sums = jnp.sum(total, axis=1, keepdims=True)
        return (
            jnp.broadcast_to(sums[0:1], (8, LANES)),
            jnp.broadcast_to(sums[1:2], (8, LANES)),
        )

    def finish_norm(ph, slot, i):
        a, b = recv_stats(ph, i)
        inv_n = invn_ref[i]
        mean = a * inv_n
        spread = jnp.maximum(b * inv_n - mean * mean, 0.0)
        stat[slot, i, 0] = mean
        stat[slot, i, 1] = lax.rsqrt(spread + EPSILON / (LN2 * LN2))

    def finish_back(ph, slot, i):
        a, b = recv_stats(ph, i)
        inv_n = invn_ref[i]
        mean, inv = stat[slot, i, 0], stat[slot, i, 1]
        q = b * inv_n * inv
        back[i, 0] = (mean * q - a * inv_n) * (inv * LOG2E)
        back[i, 1] = -q * (inv * LOG2E)

    def lanes_of(ref, j):
        out = ref[0, j]
        for i in range(1, NI):
            out = jnp.where(lane8 >= 32 * i, ref[i, j], out)
        return out

    def per_item(body):
        lax.fori_loop(0, NI, lambda i, c: (body(i), c)[1], 0)

    def per_tile(body, count=H, rows=R, init=0):
        return lax.fori_loop(0, count // rows, lambda j, c: body(rows_at(j, rows), c), init)

    def mask_row(i, rows, at=DILATION, width=F):
        return tall(mask_ref[i, :, at : at + width], rows)

    zero8 = jnp.zeros((8, LANES), F32)
    zero8f = jnp.zeros((8, F), F32)

    def pack_edges(src, channels, slot):
        def tile(r, c):
            to_left = to_right = own = jnp.zeros((R, LANES), F32)
            for i in range(NI):
                a = src[i, r, 0:LANES].astype(F32)
                z = src[i, r, F - LANES : F].astype(F32)
                base = 32 * i
                to_left += jnp.where(
                    (lane == base + 17) | (lane == base + 18), pltpu.roll(a, base + 17, 1), 0.0
                )
                to_right += jnp.where(
                    (lane == base) | (lane == base + 1), pltpu.roll(z, base + 2, 1), 0.0
                )
                own += jnp.where(lane == base + 2, pltpu.roll(a, base + 2, 1), 0.0)
                own += jnp.where(lane == base + 16, pltpu.roll(z, base + 17, 1), 0.0)
            edge_src[slot, 0, r, :] = to_left.astype(BF16)
            edge_src[slot, 1, r, :] = to_right.astype(BF16)
            edge_src[slot, 2, r, :] = own.astype(BF16)
            return c

        per_tile(tile, channels)

    def edge_copy(slot, side, channels):
        rows = pl.ds(0, channels)
        return remote(
            edge_src.at[slot, side, rows],
            edge_in.at[slot, side, rows],
            sem_es.at[slot, side],
            sem_er.at[slot, side],
            {"tm": left if side == 0 else right},
        )

    def send_edges(slot, channels):
        @pl.when(t > 0)
        def _():
            edge_copy(slot, 0, channels).start()

        @pl.when(t < last)
        def _():
            edge_copy(slot, 1, channels).start()

    def recv_edges(slot, channels, dst):
        @pl.when(t > 0)
        def _():
            edge_copy(slot, 0, channels).wait_send()
            edge_copy(slot, 1, channels).wait_recv()

        @pl.when(t < last)
        def _():
            edge_copy(slot, 1, channels).wait_send()
            edge_copy(slot, 0, channels).wait_recv()

        def tile(r, c):
            total = edge_src[slot, 2, r, :].astype(F32)
            for side in (0, 1):
                total += edge_in[slot, side, r, :].astype(F32)
            dst[r, :] = total.astype(BF16)
            return c

        per_tile(tile, channels)

    def rectify(neg, rest):
        soft = jnp.maximum(neg, jnp.log2(1.0 + jnp.exp2(jnp.minimum(neg, 100.0))))
        return rest * soft - neg, soft

    def add_sums(a, sums):
        return (sums[0] + fold_rows(a), sums[1] + fold_rows(a * a))

    def send_sums(ph, i, sums):
        m = mask_ref[i, :, MID]
        send_stats(ph, i, fold(sums[0] * m), fold(sums[1] * m))

    def phase1(k):
        R = ROWS1
        width = W if k == 0 else F
        x = x0 if k == 0 else x1
        act = act1_0 if k == 0 else act1_1
        mid = MID if k == 0 else slice(0, F)

        def item(i):

            def tile(r, sums):
                table = chan[k, r, :]
                bias = column(table, 0) * -LOG2E
                rest = 1.0 - column(table, 1)
                neg = dot(wpre[k, r, :], x[i]) * -LOG2E + wide(bias, width)
                a, soft = rectify(neg, wide(rest, width))
                act[i, r, :] = a.astype(BF16)
                soft1[k, i, r, :] = soft[:, mid].astype(BF16)
                return add_sums(a[:, mid], sums)

            send_sums(4 * k, i, per_tile(tile, rows=R, init=(zero8f, zero8f)))

        return item

    def edge1():
        R = ROWS1
        recv_edges(1, B, x_edge)
        wide_s[:, 0:LANES] = dot(wpre[1], x_edge[...])

        def tile(r, c):
            table = chan[1, r, :]
            neg = wide_s[r, 0:LANES] * -LOG2E + column(table, 0) * -LOG2E
            a, _ = rectify(neg, 1.0 - column(table, 1))
            wide_s[r, 0:LANES] = a
            return c

        per_tile(tile, rows=R)

    def phase2(k):
        R = ROWS2
        width = W if k == 0 else F
        at = 0 if k == 0 else DILATION
        act = act1_0 if k == 0 else act1_1

        def item(i):
            finish_norm(4 * k, 2 * k, i)
            mean, inv = tall(stat[2 * k, i, 0], R), tall(stat[2 * k, i, 1], R)
            m = mask_row(i, R, at, width)

            def tile(r, c):
                table = chan[k, r, :]
                scale = inv * column(table, 2)
                shift = column(table, 3) - mean * scale
                a = act[i, r, :].astype(F32)
                buf[i, r, at : at + width] = (
                    (a * wide(scale, width) + wide(shift, width)) * m
                ).astype(BF16)
                return c

            per_tile(tile, rows=R)

        return item

    def edge2():
        R = ROWS2
        mean, inv = tall(lanes_of(stat.at[2], 0), R), tall(lanes_of(stat.at[2], 1), R)
        m = tall(edge_mask_ref[...], R)

        def tile(r, c):
            table = chan[1, r, :]
            scale = inv * column(table, 2)
            a = wide_s[r, 0:LANES]
            first_edge[r, :] = (((a - mean) * scale + column(table, 3)) * m).astype(BF16)
            return c

        per_tile(tile, rows=R)

    def place_halos(edge):
        def item(i):
            wide_edge = edge[...].astype(F32)
            buf[i, :, 0:DILATION] = low(pltpu.roll(wide_edge, lax.rem(254 - 32 * i, 128), 1))
            buf[i, :, F + DILATION : W] = low(pltpu.roll(wide_edge, lax.rem(239 - 32 * i, 128), 1))

        per_item(item)

    def shifted(i, r):
        before, after = [], []
        for j in range(F // LANES + 1):
            v = dot(buf[i, r, j * LANES : (j + 2) * LANES], shifts[...])
            before.append(v[:, :LANES])
            after.append(v[:, LANES:])
        return jnp.concatenate(before[:-1], axis=1), jnp.concatenate(after[1:], axis=1)

    def taps(k, i, r):
        f = buf[i, r, MID]
        if k == 0:
            return buf[i, r, 0:F], f, buf[i, r, 2 * DILATION : W]
        before, after = shifted(i, r)
        return before, f, after

    def conv_coefs(table):
        return [column(table, j) * -LOG2E for j in (4, 5, 6, 7)], 1.0 - column(table, 8)

    def phase3(k):
        R = ROWS3
        def item(i):

            def tile(r, sums):
                c, rest = conv_coefs(chan[k, r, :])
                before, f, after = (v.astype(F32) for v in taps(k, i, r))
                neg = wide(c[0], F) * before + wide(c[1], F) * f + wide(c[2], F) * after + wide(c[3], F)
                a, soft = rectify(neg, wide(rest, F))
                act2[k, i, r, :] = a.astype(BF16)
                soft2[k, i, r, :] = soft.astype(BF16)
                return add_sums(a, sums)

            send_sums(4 * k + 1, i, per_tile(tile, rows=R, init=(zero8f, zero8f)))

        return item

    def edge3():
        R = ROWS3
        def tile(r, x):
            c, rest = conv_coefs(chan[1, r, :])
            f = first_edge[r, :].astype(F32)
            neg = c[0] * pltpu.roll(f, 1, 1) + c[1] * f + c[2] * pltpu.roll(f, LANES - 1, 1) + c[3]
            a, soft = rectify(neg, rest)
            act_edge[r, :] = a.astype(BF16)
            soft_edge[r, :] = soft.astype(BF16)
            return x

        per_tile(tile, rows=R)

    def out_copy(kind, k, i):
        row = first_item + i
        src, dst = (((x1, x0)[k], block_h), ((skips, x1)[k], skip_h))[kind]
        src = src.at[i, :, centre] if (kind, k) == (0, 1) else src.at[i]
        return (
            pltpu.make_async_copy(src, dst.at[row], sem_o.at[kind, k, i]),
            remote(src, dst.at[row], sem_o.at[kind, k, i], sem_or.at[kind, i], {"section": o}),
        )

    def start_out(kind, k, i):
        here, there = out_copy(kind, k, i)
        pl.when(s == k)(lambda: here.start())
        pl.when(s != k)(lambda: there.start())

    def wait_out(kind, k, i):
        here, there = out_copy(kind, k, i)
        pl.when(s == k)(lambda: here.wait())
        pl.when(s != k)(lambda: there.wait_send())

    def wait_came(kind, i):
        src, dst = ((x1, block_h), (skips, skip_h))[kind]
        remote(
            src.at[i], dst.at[o * NI + i], sem_o.at[kind, 0, i], sem_or.at[kind, i], {"section": o}
        ).wait_recv()

    def projected(k, i, first, rows):
        mean, inv = tall(stat[2 * k + 1, i, 0], rows), tall(stat[2 * k + 1, i, 1], rows)
        r = slice(first, first + rows)
        table = col[k, r, :]
        shift = column(table, 0) - mean * inv * column(table, 1)
        y = dot(wg[k, r, :], act2[k, i])
        return (y * wide(inv, F) + wide(shift, F)) * mask_row(i, rows)

    def phase4(k):
        def item(i):
            finish_norm(1, 1, i)
            x1[i] = low(x0[i, :, MID].astype(F32) + projected(0, i, 0, B))
            start_out(0, 0, i)

        return item

    def outputs(i):
        skips[i] = low(projected(0, i, B, B))
        start_out(1, 0, i)
        both = projected(1, i, 0, 2 * B)
        x0[i, :, MID] = low(x1[i].astype(F32) + both[:B])
        start_out(0, 1, i)
        wait_out(0, 0, i)
        x1[i] = low(skips[i].astype(F32) + both[B:])
        start_out(1, 1, i)

    def phase5(k):
        R = ROWS5
        R5 = ROWS5

        def item(i):
            if k == 1:
                finish_norm(5, 3, i)
            mean, inv = tall(stat[2 * k + 1, i, 0], R5), tall(stat[2 * k + 1, i, 1], R5)
            both = dot(jnp.concatenate([act2[k, i], jnp.ones((16, F), BF16)], axis=0), dp[i], NT)
            wide_s[:, 0 : 2 * B] = both[:H]
            total8 = both[H : H + 8]
            bias_sum[k] += total8
            total = tall(total8, R5)

            def tile(r, sums):
                table = chan[k, r, :]
                g, e = column(table, 9), column(table, 10)
                product = wide_s[r, 0 : 2 * B]
                w = wout[k, r, :].astype(F32)
                against = fold(w * product)
                plain = fold(w * total)
                normed = inv * (against - mean * plain)
                gacc[9, r, :] += normed
                gacc[10, r, :] += plain
                scale = inv * g
                shift = e - mean * scale
                step = wide(scale, 2 * B) * product + wide(shift, 2 * B) * total
                grad[k, r, :] += step[:, :B]
                grad[k, pl.ds(H + r.start, R5), :] += step[:, B:]
                return (sums[0] + fold_rows(g * plain), sums[1] + fold_rows(g * normed))

            a, b = per_tile(tile, rows=R5, init=(zero8, zero8))
            send_stats(4 * k + 2, i, a, b)

        return item

    def halo_copy(i, side):
        edge = pl.ds(DILATION, DILATION) if side == 0 else pl.ds(F, DILATION)
        return remote(
            buf.at[i, :, edge],
            buf.at[i, :, tail if side == 0 else head],
            sem_hs.at[side, i],
            sem_hr.at[side, i],
            {"tm": left if side == 0 else right},
        )

    def phase6(k):
        R = ROWS6
        def item(i):
            finish_back(4 * k + 2, 2 * k + 1, i)
            inv = tall(stat[2 * k + 1, i, 1], R) * LOG2E
            p, q = wide(tall(back[i, 0], R), F), wide(tall(back[i, 1], R), F)
            m = mask_row(i, R)

            def tile(r, c):
                table = chan[k, r, :]
                slope = column(table, 8)
                g = inv * column(table, 9)
                d_act = low(dot(wout[k, r, :], dp[i]) * wide(g, F) + m * (p + q * act2[k, i, r, :].astype(F32)))
                soft = soft2[k, i, r, :]
                d_conv = d_act * (wide(low(slope), F) + wide(low(1.0 - slope), F) * jnp.exp2(-soft))
                gacc[8, r, :] += fold(d_act * soft).astype(F32) * -LN2
                gacc[7, r, :] += fold(d_conv).astype(F32)
                buf[i, r, MID] = d_conv
                return c

            per_tile(tile, rows=R)
            if k == 0:

                @pl.when(t > 0)
                def _():
                    halo_copy(i, 0).start()

                @pl.when(t < last)
                def _():
                    halo_copy(i, 1).start()

                @pl.when(t == 0)
                def _():
                    buf[i, :, 0:DILATION] = jnp.zeros((H, DILATION), BF16)

                @pl.when(t == last)
                def _():
                    buf[i, :, F + DILATION : W] = jnp.zeros((H, DILATION), BF16)

        return item

    def edge6():
        R = ROWS6
        wide_s[:, 0:LANES] = dot(wout[1], dp_edge[...])
        inv = tall(lanes_of(stat.at[3], 1), R) * LOG2E
        p, q = tall(lanes_of(back, 0), R), tall(lanes_of(back, 1), R)
        m = tall(edge_mask_ref[...], R)

        def tile(r, c):
            table = chan[1, r, :]
            slope = column(table, 8)
            d_act = wide_s[r, 0:LANES] * (inv * column(table, 9)) + m * (p + q * act_edge[r, :].astype(F32))
            d_conv = d_act * (slope + (1.0 - slope) * jnp.exp2(-soft_edge[r, :].astype(F32)))
            conv_edge[r, :] = d_conv.astype(BF16)
            return c

        per_tile(tile, rows=R)

    def first_back(k, i, r, rows, before, d, after, a, m, sums, store):
        table = chan[k, r, :]
        g = column(table, 2)
        mean, inv = tall(stat[2 * k, i, 0], rows), tall(stat[2 * k, i, 1], rows)
        scale = inv * g
        shift = column(table, 3) - mean * scale
        spread = lambda v: wide(low(v), a.shape[1])
        u = (
            spread(column(table, 4)) * after + spread(column(table, 5)) * d + spread(column(table, 6)) * before
        ) * m
        first = (a * spread(scale) + spread(shift)) * m
        plain = fold(u).astype(F32)
        normed = inv * (fold(u * a).astype(F32) - mean * plain)
        gacc[2, r, :] += normed
        gacc[3, r, :] += plain
        gacc[4, r, :] += fold(after * first).astype(F32)
        gacc[5, r, :] += fold(d * first).astype(F32)
        gacc[6, r, :] += fold(before * first).astype(F32)
        store(u)
        return (sums[0] + fold_rows(g * plain), sums[1] + fold_rows(g * normed))

    def phase7(k):
        R = ROWS7

        def item(i):
            m = low(mask_row(i, R))

            def tile(r, sums):
                before, d, after = (low(v) for v in taps(1, i, r))

                def store(u):
                    soft2[1, i, r, :] = u

                return first_back(1, i, r, R, before, d, after, act1_1[i, r, :], m, sums, store)

            a, b = per_tile(tile, rows=R, init=(zero8, zero8))
            send_stats(7, i, a, b)

        def inner(i):
            lanes = slice(2 * DILATION, F)
            m = low(tall(mask_ref[i, :, lanes], R))

            def tile(r, sums):
                def store(u):
                    soft2[0, i, r, DILATION : F - DILATION] = u

                return first_back(
                    0, i, r, R,
                    buf[i, r, DILATION : F - DILATION], buf[i, r, lanes], buf[i, r, 3 * DILATION : F + DILATION],
                    act1_0[i, r, lanes], m, sums, store,
                )

            a, b = per_tile(tile, rows=R, init=(zero8, zero8))
            inner_sums[i, 0] = a
            inner_sums[i, 1] = b

        return item if k == 1 else inner

    def phase7_ends(i):
        R = ROWS7_ENDS

        @pl.when(t > 0)
        def _():
            halo_copy(i, 0).wait_send()
            halo_copy(i, 1).wait_recv()

        @pl.when(t < last)
        def _():
            halo_copy(i, 1).wait_send()
            halo_copy(i, 0).wait_recv()

        def ends(v, at):
            return jnp.concatenate([v(at, at + DILATION), v(at + F - DILATION, at + F)], axis=1)

        m = low(tall(ends(lambda x, y: mask_ref[i, :, x:y], DILATION), R))

        def tile(r, sums):
            def store(u):
                soft2[0, i, r, 0:DILATION] = u[:, :DILATION]
                soft2[0, i, r, F - DILATION : F] = u[:, DILATION:]

            before, d, after = (ends(lambda x, y: buf[i, r, x:y], at) for at in (0, DILATION, 2 * DILATION))
            a = ends(lambda x, y: act1_0[i, r, x:y], DILATION)
            return first_back(0, i, r, R, before, d, after, a, m, sums, store)

        a, b = per_tile(tile, rows=R, init=(inner_sums[i, 0], inner_sums[i, 1]))
        send_stats(3, i, a, b)

    def mix_copy(i):
        row = first_item + i
        return (
            pltpu.make_async_copy(stage.at[2 * i + s], gmix_h.at[row], sem_m.at[0, i]),
            remote(stage.at[2 * i + o], gmix_h.at[row], sem_m.at[1, i], sem_mr.at[i], {"section": o}),
        )

    def phase8(k):
        R = ROWS8
        act = act1_0 if k == 0 else act1_1
        x = x0 if k == 0 else x1
        mid = MID if k == 0 else slice(0, F)

        def item(i):
            finish_back(4 * k + 3, 2 * k, i)
            inv = tall(stat[2 * k, i, 1], R) * LOG2E
            p, q = wide(tall(back[i, 0], R), F), wide(tall(back[i, 1], R), F)
            m = mask_row(i, R)

            def tile(r, c):
                table = chan[k, r, :]
                slope = column(table, 1)
                g = inv * column(table, 2)
                d_act = low(soft2[k, i, r, :].astype(F32) * wide(g, F) + m * (p + q * act[i, r, mid].astype(F32)))
                soft = soft1[k, i, r, :]
                d_pre = d_act * (wide(low(slope), F) + wide(low(1.0 - slope), F) * jnp.exp2(-soft))
                gacc[1, r, :] += fold(d_act * soft).astype(F32) * -LN2
                gacc[0, r, :] += fold(d_pre).astype(F32)
                buf[i, r, MID] = d_pre
                grad[k, pl.ds(2 * H + r.start, R), :] += dot(d_pre, x[i, :, mid], NT)
                return c

            per_tile(tile, rows=R)

            if k == 1:
                input_gradient(1, i)

        return item

    def input_gradient(k, i):
        wide_s[0:B, 0:F] = dot(win[k], buf[i, :, MID])
        m = mask_row(i, B)
        d_input = (wide_s[0:B, 0:F] + dp[i, 0:B, :].astype(F32)) * m
        if k == 1:
            dp[i, 0:B, :] = d_input.astype(BF16)
        else:
            stage[2 * i] = d_input[0:half].astype(BF16)
            stage[2 * i + 1] = d_input[half:].astype(BF16)
            here, there = mix_copy(i)
            there.start()
            here.start()

    rows_at_part = ((0, 2 * H), (2 * H, grad.shape[1]))
    came = (came0, came1)
    slots = ((from_item0, from_tm0), (from_item1, from_tm1))

    def sizes(part):
        big, chunk = slots[part][0].shape[1], slots[part][1].shape[1]
        return big, chunk, big // chunk

    def item_peer(d):
        return lax.rem(it + d, n_item)

    def tm_peer(d):
        return lax.rem(t + d, n_tm)

    def each(count, body):
        lax.fori_loop(1, count, lambda d, c: (body(d), c)[1], 0)

    def at_part(part, k, start, rows):
        return grad.at[k, pl.ds(rows_at_part[part][0] + start, rows)]

    def to_owner(part, k):
        a, b = rows_at_part[part]
        return remote(grad.at[k, pl.ds(a, b - a)], came[part], sem_k.at[part], sem_kr.at[part], {"section": o})

    def item_scatter(part, k, d):
        big = sizes(part)[0]
        src = at_part(part, k, item_peer(d) * big, big)
        return remote(
            src, slots[part][0].at[d - 1], sem_ri.at[part, d - 1], sem_rir.at[part, d - 1], {"item": item_peer(d)}
        )

    def tm_scatter(part, k, d):
        big, chunk, owners = sizes(part)
        src = at_part(part, k, it * big + lax.rem(tm_peer(d), owners) * chunk, chunk)
        return remote(
            src, slots[part][1].at[d - 1], sem_rt.at[part, d - 1], sem_rtr.at[part, d - 1], {"tm": tm_peer(d)}
        )

    def tm_gather(part, d, member):
        big, chunk, owners = sizes(part)
        rows = came[part].at[pl.ds(it * big + lax.rem(member, owners) * chunk, chunk)]
        return remote(rows, rows, sem_at.at[part, d - 1], sem_atr.at[part, d - 1], {"tm": tm_peer(d)})

    def item_gather(part, d, member):
        big = sizes(part)[0]
        rows = came[part].at[pl.ds(member * big, big)]
        return remote(rows, rows, sem_ai.at[part, d - 1], sem_air.at[part, d - 1], {"item": item_peer(d)})

    def sum_1(part, k):
        pl.when(s != k)(lambda: to_owner(part, k).start())

    def sum_2(part, k):
        pl.when(s != k)(lambda: to_owner(part, k).wait_send())

        @pl.when(s == k)
        def _():
            a, b = rows_at_part[part]
            to_owner(part, k).wait_recv()
            grad[k, a:b] += came[part][...]
            each(n_item, lambda d: item_scatter(part, k, d).start())

    def sum_3(part, k):
        big, chunk, owners = sizes(part)

        @pl.when(s == k)
        def _():
            each(n_item, lambda d: item_scatter(part, k, d).wait())
            mine = pl.ds(pl.multiple_of(rows_at_part[part][0] + it * big, 8), big)
            grad[k, mine] = lax.fori_loop(0, n_item - 1, lambda j, x: x + slots[part][0][j], grad[k, mine])
            each(n_tm, lambda d: pl.when(tm_peer(d) < owners)(lambda: tm_scatter(part, k, d).start()))

    def sum_4(part, k):
        big, chunk, owners = sizes(part)

        @pl.when(s == k)
        def _():
            def wait(d):
                pl.when(tm_peer(d) < owners)(lambda: tm_scatter(part, k, d).wait_send())
                pl.when(t < owners)(lambda: tm_scatter(part, k, d).wait_recv())

            each(n_tm, wait)

            @pl.when(t < owners)
            def _():
                start = it * big + t * chunk
                own = grad[k, pl.ds(pl.multiple_of(rows_at_part[part][0] + start, 8), chunk)]
                total = lax.fori_loop(0, n_tm - 1, lambda j, x: x + slots[part][1][j], own)
                came[part][pl.ds(pl.multiple_of(start, 8), chunk)] = total
                each(n_tm, lambda d: tm_gather(part, d, t).start())

    def sum_5(part, k):
        _, _, owners = sizes(part)

        @pl.when(s == k)
        def _():
            def wait(d):
                source = lax.rem(t - d + n_tm, n_tm)
                pl.when(t < owners)(lambda: tm_gather(part, d, t).wait_send())
                pl.when(source < owners)(lambda: tm_gather(part, d, source).wait_recv())

            each(n_tm, wait)
            each(n_item, lambda d: item_gather(part, d, it).start())

    def sum_6(part, k):
        @pl.when(s == k)
        def _():
            def wait(d):
                item_gather(part, d, it).wait_send()
                item_gather(part, d, lax.rem(it - d + n_item, n_item)).wait_recv()

            each(n_item, wait)

    last_rows = grad.shape[1] - 2 * H
    last_chunk = to_owner_slots.shape[2]
    last_owners = low_grad.shape[0] // last_chunk
    first_core = jnp.int32(0)

    def member_at(d):
        peer = lax.rem(me + d, members)
        return peer, {"section": first_core, "tm": peer // n_item, "item": lax.rem(peer, n_item)}

    def chunk_rows(member):
        return pl.ds(pl.multiple_of(lax.rem(member, last_owners) * last_chunk, 16), last_chunk)

    def last_scatter(core, d):
        peer, device = member_at(d)
        return remote(
            low_grad.at[chunk_rows(peer)], to_owner_slots.at[core, d], sem_ls.at[d], sem_lr.at[core, d], device
        )

    def last_gather(d, member):
        rows = low_total.at[chunk_rows(member)]
        return remote(rows, rows, sem_gs.at[d], sem_gr.at[d], member_at(d)[1])

    def others(body, start=1):
        lax.fori_loop(start, members, lambda d, c: (body(d), c)[1], 0)

    def last_1():
        low_grad[0:last_rows] = low(grad[0, 2 * H :])
        if low_grad.shape[0] > last_rows:
            low_grad[last_rows:] = jnp.zeros((low_grad.shape[0] - last_rows, LANES), BF16)

        def send(core):
            def one(d):
                pl.when(member_at(d)[0] < last_owners)(lambda: last_scatter(core, d).start())

            others(one, 1 - core)

        pl.when(s == 0)(lambda: send(0))
        pl.when(s == 1)(lambda: send(1))

    def last_2():
        def sent(core):
            def one(d):
                pl.when(member_at(d)[0] < last_owners)(lambda: last_scatter(core, d).wait_send())

            others(one, 1 - core)

        pl.when(s == 1)(lambda: sent(1))

        @pl.when(s == 0)
        def _():
            sent(0)

            @pl.when(me < last_owners)
            def _():
                others(lambda d: last_scatter(0, d).wait_recv())
                others(lambda d: last_scatter(1, d).wait_recv(), 0)
                mine = chunk_rows(me)
                total = low_grad[mine].astype(F32) + to_owner_slots[1, 0].astype(F32)
                total = lax.fori_loop(
                    1,
                    members,
                    lambda d, x: x + (to_owner_slots[0, d].astype(F32) + to_owner_slots[1, d].astype(F32)),
                    total,
                )
                low_total[mine] = low(total)
                others(lambda d: last_gather(d, me).start())

    def last_3():
        @pl.when(s == 0)
        def _():
            def wait(d):
                source = lax.rem(me - d + members, members)
                pl.when(me < last_owners)(lambda: last_gather(d, me).wait_send())
                pl.when(source < last_owners)(lambda: last_gather(d, source).wait_recv())

            others(wait)
            came1[...] = low_total[0:last_rows].astype(F32)

    group = H // 4

    def pack_rows(packed, which):
        lanes = lax.broadcasted_iota(jnp.int32, (group, LANES), 1)
        for g in range(4):
            for j in which:
                total = jnp.sum(gacc[j, g * group : (g + 1) * group, :], axis=1, keepdims=True)
                packed = jnp.where(lanes == 32 * g + j, total, packed)
        return packed

    def finish_early(k):
        lanes = lax.broadcasted_iota(jnp.int32, (group, LANES), 1)
        bias = jnp.broadcast_to(bias_sum[k, 0:1, :], (LANES, 2 * B)).T
        packed = jnp.zeros((group, LANES), F32)
        for g in range(2 * B // group):
            packed = jnp.where(lanes == 32 * g + 11, bias[g * group : (g + 1) * group], packed)
        grad[k, 3 * H : 3 * H + group] = pack_rows(packed, range(2, 11))

    def finish_block(k):
        grad[k, 3 * H : 3 * H + group] = pack_rows(grad[k, 3 * H : 3 * H + group], (0, 1))

    def mask_gradients(i):
        m = mask_row(i, R)

        def tile(r, c):
            dp[i, r, :] = (dp[i, r, :].astype(F32) * m).astype(BF16)
            return c

        per_tile(tile, 2 * B)

    wait_weights(0, 1)
    main_local.wait()
    main_send.wait_send()
    main_recv.wait_recv()

    @pl.when(t > 0)
    def _():
        for core in (0, 1):
            halo_send(0, core).wait_send()
            halo_recv(1, core).wait_recv()

    @pl.when(t < last)
    def _():
        for core in (0, 1):
            halo_send(1, core).wait_send()
            halo_recv(0, core).wait_recv()

    def steps(count, *bodies):
        def step(j, c):
            for first, body in bodies:
                pl.when((j >= first) & (j < first + NI))(functools.partial(body, j - first))
            return c

        lax.fori_loop(0, count, step, 0)

    def at_item(j, body, *args):
        return lambda i: pl.when(i == j)(lambda: body(*args))

    def send_x1_edges(i):
        @pl.when(i == NI - 1)
        def _():
            pack_edges(x1, B, 1)
            send_edges(1, B)

    per_item(phase1(0))
    p2, p3 = phase2(0), phase3(0)
    per_item(lambda i: (p2(i), p3(i)))
    wait_weights(2, 3)
    steps(NI + 2, (0, phase4(0)), (0, send_x1_edges), (2, phase1(1)))
    edge1()
    load_out.wait()
    load_skip.wait()
    per_item(mask_gradients)
    pack_edges(dp, 2 * B, 0)
    send_edges(0, 2 * B)
    per_item(phase2(1))
    edge2()
    place_halos(first_edge)
    per_item(phase3(1))
    edge3()
    recv_edges(0, 2 * B, dp_edge)
    wait_weights(4)
    gacc[...] = jnp.zeros(gacc.shape, F32)
    per_item(phase5(1))
    sum_1(0, 1)
    per_item(phase6(1))
    edge6()
    place_halos(conv_edge)
    sum_2(0, 1)
    wait_weights(5)
    per_item(phase7(1))
    finish_early(1)
    per_item(phase8(1))
    sum_3(0, 1)
    finish_block(1)
    sum_1(1, 1)
    gacc[...] = jnp.zeros(gacc.shape, F32)
    per_item(phase5(0))
    sum_1(0, 0)
    sum_4(0, 1)
    sum_2(1, 1)
    steps(NI, (0, at_item(2, sum_2, 0, 0)), (0, phase6(0)))
    sum_5(0, 1)
    sum_3(1, 1)
    steps(NI, (0, at_item(2, sum_3, 0, 0)), (0, phase7(0)))
    per_item(phase7_ends)
    sum_4(1, 1)
    finish_early(0)
    steps(NI, (0, at_item(1, sum_4, 0, 0)), (0, phase8(0)))
    finish_block(0)
    last_1()
    sum_5(0, 0)
    sum_5(1, 1)
    steps(NI, (0, at_item(3, last_2)), (0, outputs))
    sum_6(0, 0)
    sum_6(0, 1)
    sum_6(1, 1)
    results = [
        pltpu.make_async_copy(came[part], grad_h.at[pl.ds(a, b - a)], sem_f.at[part])
        for part, (a, b) in enumerate(rows_at_part)
    ]
    results[0].start()
    per_item(lambda i: input_gradient(0, i))
    last_3()
    results[1].start()
    for copy in results:
        copy.wait()

    for i in range(NI):
        here, there = mix_copy(i)
        here.wait()
        there.wait_send()
        remote(
            stage.at[2 * i], gmix_h.at[o * NI + i], sem_m.at[1, i], sem_mr.at[i], {"section": o}
        ).wait_recv()
        for kind, k in ((1, 0), (0, 1), (1, 1)):
            wait_out(kind, k, i)
        wait_came(0, i)
        wait_came(1, i)


def chunk_of(rows, members):
    chunk = -(-rows // members)
    chunk = -(-chunk // 8) * 8
    while rows % chunk:
        chunk += 8
    return chunk


def run(n_tm, n_item, sources, gout, gskip, w_in, chan, w_out, b_out, counts, lengths):
    n_src, flat, F = sources.shape
    items, B, _ = gout.shape
    NI = items // 2
    H = w_in.shape[0]
    W = F + 2 * DILATION
    half = B // 2
    rows0, rows1 = 2 * H, H + H // 4
    quarter0, quarter1 = rows0 // n_item, rows1 // n_item
    members = n_tm * n_item
    low_chunk = -(-rows1 // (16 * members)) * 16
    low_owners = -(-rows1 // low_chunk)
    smem = pl.BlockSpec(memory_space=pltpu.SMEM)
    any_spec = pl.BlockSpec(memory_space=pl.ANY)
    dma = pltpu.SemaphoreType.DMA
    shape = jax.ShapeDtypeStruct
    outs = (
        shape((items, B, F), BF16),
        shape((items, B, F), BF16),
        shape((items, half, F), BF16),
        shape((rows0 + rows1, LANES), F32),
    )
    scratch = [
        pltpu.VMEM((items, half, F), BF16),
        pltpu.VMEM((NI, B, W), BF16),
        pltpu.VMEM((NI, B, F), BF16),
        pltpu.VMEM((NI, B, F), BF16),
        pltpu.VMEM((NI, H, W), BF16),
        pltpu.VMEM((NI, H, F), BF16),
        pltpu.VMEM((2, NI, H, F), BF16),
        pltpu.VMEM((2, NI, H, F), BF16),
        pltpu.VMEM((2, NI, H, F), BF16),
        pltpu.VMEM((NI, H, W), BF16),
        pltpu.VMEM((H, W), F32),
        pltpu.VMEM((NI, 2 * B, F), BF16),
        pltpu.VMEM((11, H, LANES), F32),
        pltpu.VMEM((2, H, B), BF16),
        pltpu.VMEM((2, H, 2 * B), BF16),
        pltpu.VMEM((2, 2 * B, H), BF16),
        pltpu.VMEM((2, B, H), BF16),
        pltpu.VMEM((2, H, LANES), F32),
        pltpu.VMEM((2, 2 * B, LANES), F32),
        pltpu.VMEM((low_chunk * low_owners, LANES), BF16),
        pltpu.VMEM((low_chunk * low_owners, LANES), BF16),
        pltpu.VMEM((2, members, low_chunk, LANES), BF16),
        pltpu.VMEM((2, rows0 + rows1, LANES), F32),
        pltpu.VMEM((2, 8, 2 * B), F32),
        pltpu.VMEM((rows0, LANES), F32),
        pltpu.VMEM((rows1, LANES), F32),
        pltpu.VMEM((n_item - 1, quarter0, LANES), F32),
        pltpu.VMEM((n_item - 1, quarter1, LANES), F32),
        pltpu.VMEM((n_tm - 1, chunk_of(quarter0, n_tm), LANES), F32),
        pltpu.VMEM((n_tm - 1, chunk_of(quarter1, n_tm), LANES), F32),
        pltpu.VMEM((NI, 8, W), F32),
        pltpu.VMEM((8, LANES), F32),
        pltpu.VMEM((NI, 8, LANES), F32),
        pltpu.VMEM((NI, 2, 8, LANES), F32),
        pltpu.VMEM((4, NI, 2, 8, LANES), F32),
        pltpu.VMEM((NI, 2, 8, LANES), F32),
        pltpu.VMEM((2, NI, 8, LANES), F32),
        pltpu.VMEM((2, NI, n_tm - 1, 8, LANES), F32),
        pltpu.VMEM((2 * LANES, 2 * LANES), BF16),
        pltpu.VMEM(w_in.shape, BF16),
        pltpu.VMEM(chan.shape, F32),
        pltpu.VMEM(w_out.shape, BF16),
        pltpu.VMEM(b_out.shape, F32),
        pltpu.VMEM((2, 3, 2 * B, LANES), BF16),
        pltpu.VMEM((2, 2, 2 * B, LANES), BF16),
        pltpu.VMEM((B, LANES), BF16),
        pltpu.VMEM((2 * B, LANES), BF16),
        pltpu.VMEM((H, LANES), BF16),
        pltpu.VMEM((H, LANES), BF16),
        pltpu.VMEM((H, LANES), BF16),
        pltpu.VMEM((H, LANES), BF16),
        dma((n_src + 4,)),
        dma((6, 2)),
        dma((6,)),
        dma((5,)),
        dma((2,)),
        dma((2, 2)),
        dma((2, 2)),
        dma((2, NI, n_tm - 1)),
        dma((2, NI, n_tm - 1)),
        dma((2, NI)),
        dma((2, NI)),
        dma((2, 2, NI)),
        dma((2, NI)),
        dma((2, NI)),
        dma((NI,)),
        dma((members,)),
        dma((2, members)),
        dma((members,)),
        dma((members,)),
        dma((2,)),
        dma((2,)),
        dma((2, n_item - 1)),
        dma((2, n_item - 1)),
        dma((2, n_tm - 1)),
        dma((2, n_tm - 1)),
        dma((2, n_tm - 1)),
        dma((2, n_tm - 1)),
        dma((2, n_item - 1)),
        dma((2, n_item - 1)),
        dma((2,)),
    ]
    return pl.pallas_call(
        functools.partial(kernel, (n_tm, n_item, NI, H, B, F)),
        out_shape=outs,
        in_specs=[any_spec] * 7 + [smem] * 2,
        out_specs=[any_spec] * len(outs),
        scratch_shapes=scratch,
        compiler_params=pltpu.CompilerParams(
            collective_id=0, has_side_effects=True, vmem_limit_bytes=VMEM_LIMIT
        ),
        name="temporal_blocks",
    )(sources, gout, gskip, w_in, chan, w_out, b_out, counts, lengths)


def close_kernel(
    block_in, skip_in, gmix_in, grad_in, counts,
    block_h, skip_h, sources_h, w_in_h, chan_h, w_out_h, b_out_h,
    held, mixed, full, nothing, sums, w_out, chan, bias, sem_a, sem_b, sem_g, sem_s, sem_w,
):
    items = gmix_in.shape[0]
    H, B = w_in_h.shape
    n_src = sources_h.shape[0]
    plain = [(j, i) for i in range(items) for j in (0, 1)]

    def fetch(j, i):
        return pltpu.make_async_copy((block_in, skip_in)[j].at[i], held.at[j, i], sem_a.at[j, i])

    def store(j, i):
        return pltpu.make_async_copy(held.at[j, i], (block_h, skip_h)[j].at[i], sem_b.at[j, i])

    loads = [pltpu.make_async_copy(gmix_in.at[i], mixed.at[i], sem_g.at[i]) for i in range(items)]
    load_sums = pltpu.make_async_copy(grad_in, sums, sem_w.at[0])
    for copy in loads:
        copy.start()
    load_sums.start()
    for j, i in plain:
        fetch(j, i).start()
    nothing[...] = jnp.zeros(nothing.shape, F32)
    for i in range(items):
        loads[i].wait()
        full[i] = mixed[i].astype(F32)
        for n in range(n_src):

            @pl.when(n < counts[i])
            def _():
                pltpu.make_async_copy(full.at[i], sources_h.at[n, i], sem_s.at[n, i]).start()

            @pl.when(n >= counts[i])
            def _():
                pltpu.make_async_copy(nothing, sources_h.at[n, i], sem_s.at[n, i]).start()

    load_sums.wait()
    store_w_in = pltpu.make_async_copy(sums.at[pl.ds(2 * H, H)], w_in_h, sem_w.at[1])
    store_w_in.start()
    for j, i in plain:
        fetch(j, i).wait()
        store(j, i).start()
    w_out[0:B, :] = sums[0:H, :].T
    w_out[B : 2 * B, :] = sums[H : 2 * H, :].T
    rows = sums[3 * H : 3 * H + H // 4, :].T
    for j in range(chan.shape[0]):
        chan[j] = jnp.concatenate([rows[32 * g + j : 32 * g + j + 1] for g in range(4)], axis=1)
    bias[...] = jnp.concatenate([rows[32 * g + 11 : 32 * g + 12] for g in range(2 * B * 4 // H)], axis=1)
    late = [
        pltpu.make_async_copy(src, dst, sem_w.at[2 + j])
        for j, (src, dst) in enumerate(((w_out, w_out_h), (chan, chan_h), (bias, b_out_h)))
    ]
    for copy in late:
        copy.start()
    for copy in late:
        copy.wait()
    store_w_in.wait()
    for j, i in plain:
        store(j, i).wait()
    for i in range(items):
        for n in range(n_src):
            pltpu.make_async_copy(full.at[i], sources_h.at[n, i], sem_s.at[n, i]).wait()


def close(n_src, n_rows, block, skip, gmix, grad, counts):
    items, half, F = gmix.shape
    B = 2 * half
    H = (grad.shape[0] * 4) // 13
    any_spec = pl.BlockSpec(memory_space=pl.ANY)
    dma = pltpu.SemaphoreType.DMA
    shape = jax.ShapeDtypeStruct
    return pl.pallas_call(
        close_kernel,
        out_shape=(
            shape(block.shape, BF16),
            shape(skip.shape, BF16),
            shape((n_src, items, half, F), F32),
            shape((H, B), F32),
            shape((n_rows, 1, H), F32),
            shape((2 * B, H), F32),
            shape((1, 2 * B), F32),
        ),
        in_specs=[any_spec] * 4 + [pl.BlockSpec(memory_space=pltpu.SMEM)],
        out_specs=[any_spec] * 7,
        scratch_shapes=[
            pltpu.VMEM((2, items, B, F), BF16),
            pltpu.VMEM((items, half, F), BF16),
            pltpu.VMEM((items, half, F), F32),
            pltpu.VMEM((half, F), F32),
            pltpu.VMEM(grad.shape, F32),
            pltpu.VMEM((2 * B, H), F32),
            pltpu.VMEM((n_rows, 1, H), F32),
            pltpu.VMEM((1, 2 * B), F32),
            dma((2, items)),
            dma((2, items)),
            dma((items,)),
            dma((n_src, items)),
            dma((5,)),
        ],
        compiler_params=pltpu.CompilerParams(vmem_limit_bytes=VMEM_LIMIT),
        name="lay_out",
    )(block, skip, gmix, grad, counts)


def local(sources, source_counts, valid_lengths, w_in, chan, w_out, b_out, grad_out, grad_skip):
    n_sources, per_device, half, F = sources.shape
    block_out, skip_out, gmix, grad = run(
        lax.axis_size("tm"),
        lax.axis_size("item"),
        sources.reshape(n_sources, per_device * half, F),
        grad_out,
        grad_skip,
        w_in[0],
        chan.transpose(1, 0, 2),
        w_out[0],
        b_out,
        source_counts,
        valid_lengths,
    )
    block_out, skip_out, grad_sources, grad_w_in, grad_chan, grad_w_out, grad_b_out = close(
        n_sources, chan.shape[1], block_out, skip_out, gmix, grad, source_counts
    )
    return (
        block_out[None],
        skip_out[None],
        grad_sources,
        grad_w_in[None],
        grad_chan.transpose(1, 0, 2),
        grad_w_out[None],
        grad_b_out,
    )


def solution(mesh):
    in_specs = (
        P(None, "item", "section", "tm"),
        P("item"),
        P("item"),
        P("section", None, None),
        P("section", None, None),
        P("section", None, None),
        P("section", None),
        P("item", None, "tm"),
        P("item", None, "tm"),
    )
    out_specs = (
        P("section", "item", None, "tm"),
        P("section", "item", None, "tm"),
        P(None, "item", "section", "tm"),
        P("section", None, None),
        P("section", None, None),
        P("section", None, None),
        P("section", None),
    )
    return jax.shard_map(local, mesh=mesh, in_specs=in_specs, out_specs=out_specs, check_vma=False)
```

```python
import functools
import math

import jax
import jax.numpy as jnp
from jax import lax
from jax.experimental import pallas as pl
from jax.experimental.pallas import tpu as pltpu
from jax.sharding import PartitionSpec as P

DILATION = 128
LANES = 128
ROWS = 128
ROWS1 = 512
ROWS2 = 512
ROWS3 = 256
ROWS4 = 128
ROWS5 = 512
ROWS6 = 512
ROWS7 = 256
ROWS7_ENDS = 512
ROWS8 = 512
EPSILON = 1e-05
VMEM_LIMIT = 63 * 1024 * 1024 + 512 * 1024
LN2 = math.log(2.0)
LOG2E = 1.0 / LN2
F32 = jnp.float32
BF16 = jnp.bfloat16
MESH = pl.DeviceIdType.MESH
NT = (((1,), (1,)), ((), ()))
NN = (((1,), (0,)), ((), ()))


def dot(a, b, dims=NN, precision=None):
    return lax.dot_general(a, b, dims, precision=precision, preferred_element_type=F32)


def remote(src, dst, send, recv, device):
    return pltpu.make_async_remote_copy(
        src_ref=src, dst_ref=dst, send_sem=send, recv_sem=recv, device_id=device, device_id_type=MESH
    )


def wide(v, width):
    return jnp.concatenate([v] * (width // LANES), axis=1)


def tall(v, rows):
    return jnp.concatenate([v] * (rows // v.shape[0]), axis=0)


def fold(v):
    parts = [v[:, at : at + LANES] for at in range(0, v.shape[1], LANES)]
    while len(parts) > 1:
        parts = [a + b for a, b in zip(parts[::2], parts[1::2])] + parts[len(parts) & ~1 :]
    return parts[0]


def fold_rows(v, count=8):
    parts = [v[at : at + count] for at in range(0, v.shape[0], count)]
    while len(parts) > 1:
        parts = [a + b for a, b in zip(parts[::2], parts[1::2])] + parts[len(parts) & ~1 :]
    return parts[0]


def low(v):
    return v.astype(BF16)


def column(table, j):
    return jnp.broadcast_to(table[:, j : j + 1], (table.shape[0], LANES))


def rows_at(t, count):
    return pl.ds(pl.multiple_of(t * count, count), count)


def kernel(
    dims,
    sources_h, gout_h, gskip_h, w_in_h, chan_h, w_out_h, b_out_h, counts, lengths,
    block_h, skip_h, gmix_h, grad_h,
    stage, x0, x1, skips, act1_0, act1_1, soft1, act2, soft2, buf, wide_s, dp, gacc,
    wpre, wout, wg, win, chan, col,
    low_grad, low_total, to_owner_slots, grad, bias_sum, came0, came1, from_item0, from_item1, from_tm0, from_tm1,
    mask_ref, edge_mask_ref, invn_ref, inner_sums, stat, back, st_src, st_buf,
    shifts, w_in_ref, chan_ref, w_out_ref, b_out_ref, edge_src, edge_in, x_edge, dp_edge, first_edge, act_edge, soft_edge, conv_edge,
    sem_s, sem_w, sem_x, sem_xr, sem_g, sem_es, sem_er, sem_ss, sem_sr, sem_hs, sem_hr, sem_o, sem_or, sem_m, sem_mr,
    sem_ls, sem_lr, sem_gs, sem_gr, sem_k, sem_kr, sem_ri, sem_rir, sem_rt, sem_rtr, sem_at, sem_atr, sem_ai, sem_air, sem_f,
):
    n_tm, n_item, NI, H, B, F = dims
    R = ROWS
    W = F + 2 * DILATION
    MID = slice(DILATION, DILATION + F)
    half = B // 2
    s = lax.axis_index("section")
    t = lax.axis_index("tm")
    o = 1 - s
    left = t - 1
    right = t + 1
    last = n_tm - 1
    first_item = s * NI
    lane = lax.broadcasted_iota(jnp.int32, (R, LANES), 1)
    lane8 = lax.broadcasted_iota(jnp.int32, (8, LANES), 1)

    it = lax.axis_index("item")
    members = n_tm * n_item
    me = t * n_item + it
    n_src = sources_h.shape[0]

    def load_source(n):
        return pltpu.make_async_copy(sources_h.at[n], soft2.at[1, n], sem_s.at[n])

    small = [
        pltpu.make_async_copy(src, dst, sem_s.at[n_src + j])
        for j, (src, dst) in enumerate(
            ((w_in_h, w_in_ref), (chan_h, chan_ref), (w_out_h, w_out_ref), (b_out_h, b_out_ref))
        )
    ]
    for copy in small:
        copy.start()
    for n in range(n_src):
        load_source(n).start()
    edge_in[...] = jnp.zeros(edge_in.shape, BF16)
    row = lax.broadcasted_iota(jnp.int32, (2 * LANES, 2 * LANES), 0)
    to = lax.broadcasted_iota(jnp.int32, (2 * LANES, 2 * LANES), 1)
    step = jnp.where(to < LANES, LANES - 1, 1 - LANES)
    shifts[...] = low(jnp.where(row - to == step, 1.0, 0.0))

    barrier = pltpu.get_barrier_semaphore()

    def greet(d, c):
        peer = lax.rem(me + d, members)
        device = {"tm": peer // n_item, "item": lax.rem(peer, n_item)}
        pl.semaphore_signal(barrier, inc=1, device_id=device, device_id_type=MESH)
        pl.semaphore_signal(barrier, inc=1, device_id={"section": o} | device, device_id_type=MESH)
        return c

    pl.semaphore_signal(barrier, inc=1, device_id={"section": o}, device_id_type=MESH)
    lax.fori_loop(1, members, greet, 0)
    for copy in small:
        copy.wait()

    wpre[s] = w_in_ref[...]
    wide_s[0:LANES, 0:H] = jnp.zeros((LANES, H), F32)
    for j in range(chan_ref.shape[0]):
        wide_s[j : j + 1, 0:H] = chan_ref[j]
    chan[s] = wide_s[0:LANES, 0:H].T
    weights = (wpre, chan, wg, col, wout, win)

    def weight_copies(j):
        ref = weights[j]
        return (
            remote(ref.at[s], ref.at[s], sem_w.at[j, 0], sem_w.at[j, 1], {"section": o}),
            remote(ref.at[o], ref.at[o], sem_w.at[j, 0], sem_w.at[j, 1], {"section": o}),
        )

    def wait_weights(*which):
        for j in which:
            send, recv = weight_copies(j)
            recv.wait_recv()
            send.wait_send()

    pl.semaphore_wait(barrier, 2 * members - 1)
    for j in (0, 1):
        weight_copies(j)[0].start()

    for n in range(n_src):
        load_source(n).wait()

    def mix_item(i, c):
        rows = pl.ds(pl.multiple_of(i * half, half), half)
        where = lax.broadcasted_iota(jnp.int32, (8, F), 1) + t * F
        m = tall(jnp.where(where < lengths[i], 1.0, 0.0), half)
        total = jnp.zeros((half, F), F32)
        for n in range(n_src):
            total += soft2[1, n, rows, :].astype(F32) * jnp.where(n < counts[i], 1.0, 0.0)
        stage[i] = (total * m).astype(BF16)
        return c

    lax.fori_loop(o * NI, o * NI + NI, mix_item, 0)

    own_rows = pl.ds(pl.multiple_of(s * half, half), half)
    other_rows = pl.ds(pl.multiple_of(o * half, half), half)
    items_of = lambda core: pl.ds(core * NI, NI)
    centre = pl.ds(DILATION, F)
    head, tail = pl.ds(0, DILATION), pl.ds(F + DILATION, DILATION)

    main_local = pltpu.make_async_copy(stage.at[items_of(s)], x0.at[:, own_rows, centre], sem_x.at[0])
    main_send = remote(
        stage.at[items_of(o)], x0.at[:, own_rows, centre], sem_x.at[1], sem_xr.at[0], {"section": o}
    )
    main_recv = remote(
        stage.at[items_of(o)], x0.at[:, other_rows, centre], sem_x.at[1], sem_xr.at[0], {"section": o}
    )

    def halo_send(side, core):
        edge = pl.ds(0, DILATION) if side == 0 else pl.ds(F - DILATION, DILATION)
        place = tail if side == 0 else head
        return remote(
            stage.at[items_of(core), :, edge],
            x0.at[:, own_rows, place],
            sem_x.at[2 + 2 * side + core],
            sem_xr.at[1 + 2 * side + s],
            {"section": core, "tm": left if side == 0 else right},
        )

    def halo_recv(side, core):
        place = tail if side == 0 else head
        rows = pl.ds(core * half, half)
        return remote(
            x0.at[:, rows, place], x0.at[:, rows, place], sem_x.at[0], sem_xr.at[1 + 2 * side + core], {"section": o}
        )

    def send_halos(core):
        pl.when(t > 0)(lambda: halo_send(0, core).start())
        pl.when(t < last)(lambda: halo_send(1, core).start())

    main_send.start()
    send_halos(o)
    lax.fori_loop(s * NI, s * NI + NI, mix_item, 0)
    main_local.start()
    send_halos(s)
    load_out = pltpu.make_async_copy(gout_h.at[pl.ds(first_item, NI)], dp.at[:, pl.ds(0, B)], sem_g.at[0])
    load_skip = pltpu.make_async_copy(gskip_h.at[pl.ds(first_item, NI)], dp.at[:, pl.ds(B, B)], sem_g.at[1])
    load_out.start()
    load_skip.start()

    w_out = w_out_ref[...].astype(F32)
    win[s] = w_in_ref[...].astype(F32).T.astype(BF16)
    wout[s] = w_out.T.astype(BF16)
    gained = (w_out * chan_ref[9]).astype(BF16)
    wg[s] = gained
    bias = jnp.broadcast_to(b_out_ref[...], (LANES, 2 * B)).T
    bias += jnp.sum(w_out * chan_ref[10], axis=1, keepdims=True)
    gain = jnp.sum(gained.astype(F32), axis=1, keepdims=True)
    lane_w = lax.broadcasted_iota(jnp.int32, (2 * B, LANES), 1)
    col[s] = jnp.where(lane_w == 0, bias, gain)
    for j in range(2, len(weights)):
        weight_copies(j)[0].start()

    for i in range(NI):
        length = lengths[first_item + i]
        where = lax.broadcasted_iota(jnp.int32, (8, W), 1) + (t * F - DILATION)
        mask_ref[i] = jnp.where((where >= 0) & (where < length), 1.0, 0.0)
        invn_ref[i] = 1.0 / (jnp.full((8, LANES), length, jnp.int32).astype(F32) * H)
    within = lane8 % 32
    frame = t * F + jnp.where(within < 16, within - 2, within - 17 + F)
    length = jnp.full((8, LANES), lengths[first_item], jnp.int32)
    for i in range(1, NI):
        length = jnp.where(lane8 >= 32 * i, lengths[first_item + i], length)
    held = (within < 3) | ((within >= 16) & (within < 19))
    edge_mask_ref[...] = jnp.where(held & (frame >= 0) & (frame < length), 1.0, 0.0)

    @pl.when(t == 0)
    def _():
        x0[:, :, 0:DILATION] = jnp.zeros((NI, B, DILATION), BF16)

    @pl.when(t == last)
    def _():
        x0[:, :, F + DILATION : W] = jnp.zeros((NI, B, DILATION), BF16)

    grad[...] = jnp.zeros(grad.shape, F32)
    bias_sum[...] = jnp.zeros(bias_sum.shape, F32)

    def each(count, body, first=1):
        if count <= 8:
            for d in range(first, count):
                body(d)
        else:
            lax.fori_loop(first, count, lambda d, c: (body(d), c)[1], 0)

    def stat_copy(ph, i, d, to):
        p = ph % 2
        return remote(
            st_src.at[p, i], st_buf.at[p, i, d - 1], sem_ss.at[p, i, d - 1], sem_sr.at[p, i, d - 1], {"tm": to}
        )

    def send_stats(ph, i, a, b):
        rows = [jnp.sum(a, axis=0, keepdims=True), jnp.sum(b, axis=0, keepdims=True)]
        st_src[ph % 2, i] = jnp.concatenate(rows + [jnp.zeros((6, LANES), F32)], axis=0)

        each(n_tm, lambda d: stat_copy(ph, i, d, lax.rem(t + d, n_tm)).start())

    def recv_stats(ph, i):
        def one(d, total):
            copy = stat_copy(ph, i, d, lax.rem(t + d, n_tm))
            copy.wait_send()
            copy.wait_recv()
            return total + st_buf[ph % 2, i, d - 1]

        total = st_src[ph % 2, i]
        if n_tm <= 8:
            for d in range(1, n_tm):
                total = one(d, total)
        else:
            total = lax.fori_loop(1, n_tm, one, total)
        sums = jnp.sum(total, axis=1, keepdims=True)
        return (
            jnp.broadcast_to(sums[0:1], (8, LANES)),
            jnp.broadcast_to(sums[1:2], (8, LANES)),
        )

    def finish_norm(ph, slot, i):
        a, b = recv_stats(ph, i)
        inv_n = invn_ref[i]
        mean = a * inv_n
        spread = jnp.maximum(b * inv_n - mean * mean, 0.0)
        stat[slot, i, 0] = mean
        stat[slot, i, 1] = lax.rsqrt(spread + EPSILON / (LN2 * LN2))

    def finish_back(ph, slot, i):
        a, b = recv_stats(ph, i)
        inv_n = invn_ref[i]
        mean, inv = stat[slot, i, 0], stat[slot, i, 1]
        q = b * inv_n * inv
        back[i, 0] = (mean * q - a * inv_n) * (inv * LOG2E)
        back[i, 1] = -q * (inv * LOG2E)

    def correction(i, rows):
        m = mask_ref[i, :, MID]
        return [tall(m * wide(back[i, j], F), rows) for j in (0, 1)]

    def lanes_of(ref, j):
        out = ref[0, j]
        for i in range(1, NI):
            out = jnp.where(lane8 >= 32 * i, ref[i, j], out)
        return out

    def per_item(body):
        lax.fori_loop(0, NI, lambda i, c: (body(i), c)[1], 0)

    def per_tile(body, count=H, rows=R, init=0):
        return lax.fori_loop(0, count // rows, lambda j, c: body(rows_at(j, rows), c), init)

    def mask_row(i, rows, at=DILATION, width=F):
        return tall(mask_ref[i, :, at : at + width], rows)

    zero8 = jnp.zeros((8, LANES), F32)
    zero8f = jnp.zeros((8, F), F32)

    def pack_edges(src, channels, slot):
        def tile(r, c):
            to_left = to_right = own = jnp.zeros((R, LANES), F32)
            for i in range(NI):
                a = src[i, r, 0:LANES].astype(F32)
                z = src[i, r, F - LANES : F].astype(F32)
                base = 32 * i
                to_left += jnp.where(
                    (lane == base + 17) | (lane == base + 18), pltpu.roll(a, base + 17, 1), 0.0
                )
                to_right += jnp.where(
                    (lane == base) | (lane == base + 1), pltpu.roll(z, base + 2, 1), 0.0
                )
                own += jnp.where(lane == base + 2, pltpu.roll(a, base + 2, 1), 0.0)
                own += jnp.where(lane == base + 16, pltpu.roll(z, base + 17, 1), 0.0)
            edge_src[slot, 0, r, :] = to_left.astype(BF16)
            edge_src[slot, 1, r, :] = to_right.astype(BF16)
            edge_src[slot, 2, r, :] = own.astype(BF16)
            return c

        per_tile(tile, channels)

    def edge_copy(slot, side, channels):
        rows = pl.ds(0, channels)
        return remote(
            edge_src.at[slot, side, rows],
            edge_in.at[slot, side, rows],
            sem_es.at[slot, side],
            sem_er.at[slot, side],
            {"tm": left if side == 0 else right},
        )

    def send_edges(slot, channels):
        @pl.when(t > 0)
        def _():
            edge_copy(slot, 0, channels).start()

        @pl.when(t < last)
        def _():
            edge_copy(slot, 1, channels).start()

    def recv_edges(slot, channels, dst):
        @pl.when(t > 0)
        def _():
            edge_copy(slot, 0, channels).wait_send()
            edge_copy(slot, 1, channels).wait_recv()

        @pl.when(t < last)
        def _():
            edge_copy(slot, 1, channels).wait_send()
            edge_copy(slot, 0, channels).wait_recv()

        def tile(r, c):
            total = edge_src[slot, 2, r, :].astype(F32)
            for side in (0, 1):
                total += edge_in[slot, side, r, :].astype(F32)
            dst[r, :] = total.astype(BF16)
            return c

        per_tile(tile, channels)

    def rectify(neg, rest):
        soft = jnp.maximum(neg, jnp.log2(1.0 + jnp.exp2(jnp.minimum(neg, 100.0))))
        return rest * soft - neg, soft

    def add_sums(a, sums):
        return tuple(x + fold_rows(fold_rows(v, 16).astype(F32)) for x, v in zip(sums, (a, a * a)))

    def send_sums(ph, i, sums):
        m = mask_ref[i, :, MID]
        send_stats(ph, i, fold(sums[0] * m), fold(sums[1] * m))

    def phase1(k):
        R = ROWS1
        width = W if k == 0 else F
        x = x0 if k == 0 else x1
        act = act1_0 if k == 0 else act1_1
        mid = MID if k == 0 else slice(0, F)

        def item(i):

            def tile(r, sums):
                table = chan[k, r, :]
                bias = column(table, 0) * -LOG2E
                rest = 1.0 - column(table, 1)
                neg = dot(wpre[k, r, :], x[i]) * -LOG2E + wide(bias, width)
                a, soft = rectify(neg, wide(rest, width))
                a = low(a)
                act[i, r, :] = a
                soft1[k, i, r, :] = soft[:, mid].astype(BF16)
                return add_sums(a[:, mid], sums)

            send_sums(4 * k, i, per_tile(tile, rows=R, init=(zero8f, zero8f)))

        return item

    def edge1():
        R = ROWS1
        recv_edges(1, B, x_edge)
        wide_s[:, 0:LANES] = dot(wpre[1], x_edge[...])

        def tile(r, c):
            table = chan[1, r, :]
            neg = wide_s[r, 0:LANES] * -LOG2E + column(table, 0) * -LOG2E
            a, _ = rectify(neg, 1.0 - column(table, 1))
            wide_s[r, 0:LANES] = a
            return c

        per_tile(tile, rows=R)

    def phase2(k):
        R = ROWS2
        width = W if k == 0 else F
        at = 0 if k == 0 else DILATION
        act = act1_0 if k == 0 else act1_1

        def item(i):
            finish_norm(4 * k, 2 * k, i)
            mean, inv = tall(stat[2 * k, i, 0], R), tall(stat[2 * k, i, 1], R)
            m = low(mask_row(i, R, at, width))

            def tile(r, c):
                table = chan[k, r, :]
                scale = inv * column(table, 2)
                shift = column(table, 3) - mean * scale
                a = act[i, r, :].astype(F32)
                buf[i, r, at : at + width] = low(a * wide(scale, width) + wide(shift, width)) * m
                return c

            per_tile(tile, rows=R)

        return item

    def edge2():
        R = ROWS2
        mean, inv = tall(lanes_of(stat.at[2], 0), R), tall(lanes_of(stat.at[2], 1), R)
        m = tall(edge_mask_ref[...], R)

        def tile(r, c):
            table = chan[1, r, :]
            scale = inv * column(table, 2)
            a = wide_s[r, 0:LANES]
            first_edge[r, :] = (((a - mean) * scale + column(table, 3)) * m).astype(BF16)
            return c

        per_tile(tile, rows=R)

    def place_halos(edge):
        for i in range(NI):
            buf[i, :, 0:DILATION] = pltpu.roll(edge[...], (254 - 32 * i) % 128, 1)
            buf[i, :, F + DILATION : W] = pltpu.roll(edge[...], (239 - 32 * i) % 128, 1)

    def shifted(i, r):
        before, after = [], []
        for j in range(F // LANES + 1):
            v = dot(buf[i, r, j * LANES : (j + 2) * LANES], shifts[...])
            before.append(v[:, :LANES])
            after.append(v[:, LANES:])
        return jnp.concatenate(before[:-1], axis=1), jnp.concatenate(after[1:], axis=1)

    def taps(k, i, r):
        f = buf[i, r, MID]
        if k == 0:
            return buf[i, r, 0:F], f, buf[i, r, 2 * DILATION : W]
        before, after = shifted(i, r)
        return before, f, after

    def conv_coefs(table):
        return [column(table, j) * -LOG2E for j in (4, 5, 6, 7)], 1.0 - column(table, 8)

    def phase3(k):
        R = ROWS3
        def item(i):

            def tile(r, sums):
                c, rest = conv_coefs(chan[k, r, :])
                before, f, after = (v.astype(F32) for v in taps(k, i, r))
                neg = wide(c[0], F) * before + wide(c[1], F) * f + wide(c[2], F) * after + wide(c[3], F)
                a, soft = rectify(neg, wide(rest, F))
                a = low(a)
                act2[k, i, r, :] = a
                soft2[k, i, r, :] = soft.astype(BF16)
                return add_sums(a, sums)

            send_sums(4 * k + 1, i, per_tile(tile, rows=R, init=(zero8f, zero8f)))

        return item

    def edge3():
        R = ROWS3
        def tile(r, x):
            c, rest = conv_coefs(chan[1, r, :])
            f = first_edge[r, :].astype(F32)
            neg = c[0] * pltpu.roll(f, 1, 1) + c[1] * f + c[2] * pltpu.roll(f, LANES - 1, 1) + c[3]
            a, soft = rectify(neg, rest)
            act_edge[r, :] = a.astype(BF16)
            soft_edge[r, :] = soft.astype(BF16)
            return x

        per_tile(tile, rows=R)

    def out_copy(kind, k, i):
        row = first_item + i
        src, dst = (((x1, x0)[k], block_h), ((skips, x1)[k], skip_h))[kind]
        src = src.at[i, :, centre] if (kind, k) == (0, 1) else src.at[i]
        return (
            pltpu.make_async_copy(src, dst.at[row], sem_o.at[kind, k, i]),
            remote(src, dst.at[row], sem_o.at[kind, k, i], sem_or.at[kind, i], {"section": o}),
        )

    def start_out(kind, k, i):
        here, there = out_copy(kind, k, i)
        pl.when(s == k)(lambda: here.start())
        pl.when(s != k)(lambda: there.start())

    def wait_out(kind, k, i):
        here, there = out_copy(kind, k, i)
        pl.when(s == k)(lambda: here.wait())
        pl.when(s != k)(lambda: there.wait_send())

    def wait_came(kind, i):
        src, dst = ((x1, block_h), (skips, skip_h))[kind]
        remote(
            src.at[i], dst.at[o * NI + i], sem_o.at[kind, 0, i], sem_or.at[kind, i], {"section": o}
        ).wait_recv()

    def projected(k, i, first, rows):
        mean, inv = tall(stat[2 * k + 1, i, 0], rows), tall(stat[2 * k + 1, i, 1], rows)
        r = slice(first, first + rows)
        table = col[k, r, :]
        shift = column(table, 0) - mean * inv * column(table, 1)
        y = dot(wg[k, r, :], act2[k, i])
        return (y * wide(inv, F) + wide(shift, F)) * mask_row(i, rows)

    def phase4(k):
        def item(i):
            finish_norm(1, 1, i)
            x1[i] = low(x0[i, :, MID].astype(F32) + projected(0, i, 0, B))
            start_out(0, 0, i)

        return item

    def outputs(i):
        skips[i] = low(projected(0, i, B, B))
        start_out(1, 0, i)
        both = projected(1, i, 0, 2 * B)
        x0[i, :, MID] = low(x1[i].astype(F32) + both[:B])
        start_out(0, 1, i)
        wait_out(0, 0, i)
        x1[i] = low(skips[i].astype(F32) + both[B:])
        start_out(1, 1, i)

    def phase5(k):
        R = ROWS5
        R5 = ROWS5

        def item(i):
            if k == 1:
                finish_norm(5, 3, i)
            mean, inv = tall(stat[2 * k + 1, i, 0], R5), tall(stat[2 * k + 1, i, 1], R5)
            both = dot(jnp.concatenate([act2[k, i], jnp.ones((16, F), BF16)], axis=0), dp[i], NT)
            wide_s[:, 0 : 2 * B] = both[:H]
            total8 = both[H : H + 8]
            bias_sum[k] += total8
            total = tall(total8, R5)

            def tile(r, sums):
                table = chan[k, r, :]
                g, e = column(table, 9), column(table, 10)
                product = wide_s[r, 0 : 2 * B]
                w = wout[k, r, :].astype(F32)
                against = fold(w * product)
                plain = fold(w * total)
                normed = inv * (against - mean * plain)
                gacc[9, r, :] += normed
                gacc[10, r, :] += plain
                scale = inv * g
                shift = e - mean * scale
                step = wide(scale, 2 * B) * product + wide(shift, 2 * B) * total
                grad[k, r, :] += step[:, :B]
                grad[k, pl.ds(H + r.start, R5), :] += step[:, B:]
                return (sums[0] + fold_rows(g * plain), sums[1] + fold_rows(g * normed))

            a, b = per_tile(tile, rows=R5, init=(zero8, zero8))
            send_stats(4 * k + 2, i, a, b)

        return item

    def halo_copy(i, side):
        edge = pl.ds(DILATION, DILATION) if side == 0 else pl.ds(F, DILATION)
        return remote(
            buf.at[i, :, edge],
            buf.at[i, :, tail if side == 0 else head],
            sem_hs.at[side, i],
            sem_hr.at[side, i],
            {"tm": left if side == 0 else right},
        )

    def phase6(k):
        R = ROWS6
        def item(i):
            finish_back(4 * k + 2, 2 * k + 1, i)
            inv = tall(stat[2 * k + 1, i, 1], R) * LOG2E
            p, q = correction(i, R)

            def tile(r, c):
                table = chan[k, r, :]
                slope = column(table, 8)
                g = inv * column(table, 9)
                d_act = low(dot(wout[k, r, :], dp[i]) * wide(g, F) + (p + q * act2[k, i, r, :].astype(F32)))
                soft = soft2[k, i, r, :]
                d_conv = d_act * (wide(low(slope), F) + wide(low(1.0 - slope), F) * jnp.exp2(-soft))
                gacc[8, r, :] += fold(d_act * soft).astype(F32) * -LN2
                gacc[7, r, :] += fold(d_conv).astype(F32)
                buf[i, r, MID] = d_conv
                return c

            per_tile(tile, rows=R)
            if k == 0:

                @pl.when(t > 0)
                def _():
                    halo_copy(i, 0).start()

                @pl.when(t < last)
                def _():
                    halo_copy(i, 1).start()

                @pl.when(t == 0)
                def _():
                    buf[i, :, 0:DILATION] = jnp.zeros((H, DILATION), BF16)

                @pl.when(t == last)
                def _():
                    buf[i, :, F + DILATION : W] = jnp.zeros((H, DILATION), BF16)

        return item

    def edge6():
        R = ROWS6
        wide_s[:, 0:LANES] = dot(wout[1], dp_edge[...])
        inv = tall(lanes_of(stat.at[3], 1), R) * LOG2E
        p, q = tall(lanes_of(back, 0), R), tall(lanes_of(back, 1), R)
        m = tall(edge_mask_ref[...], R)

        def tile(r, c):
            table = chan[1, r, :]
            slope = column(table, 8)
            d_act = wide_s[r, 0:LANES] * (inv * column(table, 9)) + m * (p + q * act_edge[r, :].astype(F32))
            d_conv = d_act * (slope + (1.0 - slope) * jnp.exp2(-soft_edge[r, :].astype(F32)))
            conv_edge[r, :] = d_conv.astype(BF16)
            return c

        per_tile(tile, rows=R)

    def first_back(k, i, r, rows, before, d, after, a, m, sums, store):
        table = chan[k, r, :]
        g = column(table, 2)
        mean, inv = tall(stat[2 * k, i, 0], rows), tall(stat[2 * k, i, 1], rows)
        scale = inv * g
        shift = column(table, 3) - mean * scale
        spread = lambda v: wide(low(v), a.shape[1])
        u = (
            spread(column(table, 4)) * after + spread(column(table, 5)) * d + spread(column(table, 6)) * before
        ) * m
        first = (a * spread(scale) + spread(shift)) * m
        plain = fold(u).astype(F32)
        normed = inv * (fold(u * a).astype(F32) - mean * plain)
        gacc[2, r, :] += normed
        gacc[3, r, :] += plain
        gacc[4, r, :] += fold(after * first).astype(F32)
        gacc[5, r, :] += fold(d * first).astype(F32)
        gacc[6, r, :] += fold(before * first).astype(F32)
        store(u)
        return (sums[0] + fold_rows(g * plain), sums[1] + fold_rows(g * normed))

    def phase7(k):
        R = ROWS7

        def item(i):
            m = low(mask_row(i, R))

            def tile(r, sums):
                before, d, after = (low(v) for v in taps(1, i, r))

                def store(u):
                    soft2[1, i, r, :] = u

                return first_back(1, i, r, R, before, d, after, act1_1[i, r, :], m, sums, store)

            a, b = per_tile(tile, rows=R, init=(zero8, zero8))
            send_stats(7, i, a, b)

        def inner(i):
            lanes = slice(2 * DILATION, F)
            m = low(tall(mask_ref[i, :, lanes], R))

            def tile(r, sums):
                def store(u):
                    soft2[0, i, r, DILATION : F - DILATION] = u

                return first_back(
                    0, i, r, R,
                    buf[i, r, DILATION : F - DILATION], buf[i, r, lanes], buf[i, r, 3 * DILATION : F + DILATION],
                    act1_0[i, r, lanes], m, sums, store,
                )

            a, b = per_tile(tile, rows=R, init=(zero8, zero8))
            inner_sums[i, 0] = a
            inner_sums[i, 1] = b

        return item if k == 1 else inner

    def phase7_ends(i):
        R = ROWS7_ENDS

        @pl.when(t > 0)
        def _():
            halo_copy(i, 0).wait_send()
            halo_copy(i, 1).wait_recv()

        @pl.when(t < last)
        def _():
            halo_copy(i, 1).wait_send()
            halo_copy(i, 0).wait_recv()

        def ends(v, at):
            return jnp.concatenate([v(at, at + DILATION), v(at + F - DILATION, at + F)], axis=1)

        m = low(tall(ends(lambda x, y: mask_ref[i, :, x:y], DILATION), R))

        def tile(r, sums):
            def store(u):
                soft2[0, i, r, 0:DILATION] = u[:, :DILATION]
                soft2[0, i, r, F - DILATION : F] = u[:, DILATION:]

            before, d, after = (ends(lambda x, y: buf[i, r, x:y], at) for at in (0, DILATION, 2 * DILATION))
            a = ends(lambda x, y: act1_0[i, r, x:y], DILATION)
            return first_back(0, i, r, R, before, d, after, a, m, sums, store)

        a, b = per_tile(tile, rows=R, init=(inner_sums[i, 0], inner_sums[i, 1]))
        send_stats(3, i, a, b)

    def mix_copy(i):
        row = first_item + i
        return (
            pltpu.make_async_copy(stage.at[2 * i + s], gmix_h.at[row], sem_m.at[0, i]),
            remote(stage.at[2 * i + o], gmix_h.at[row], sem_m.at[1, i], sem_mr.at[i], {"section": o}),
        )

    def phase8(k):
        R = ROWS8
        act = act1_0 if k == 0 else act1_1
        x = x0 if k == 0 else x1
        mid = MID if k == 0 else slice(0, F)

        def item(i):
            finish_back(4 * k + 3, 2 * k, i)
            inv = tall(stat[2 * k, i, 1], R) * LOG2E
            p, q = correction(i, R)

            def tile(r, c):
                table = chan[k, r, :]
                slope = column(table, 1)
                g = inv * column(table, 2)
                d_act = low(soft2[k, i, r, :].astype(F32) * wide(g, F) + (p + q * act[i, r, mid].astype(F32)))
                soft = soft1[k, i, r, :]
                d_pre = d_act * (wide(low(slope), F) + wide(low(1.0 - slope), F) * jnp.exp2(-soft))
                gacc[1, r, :] += fold(d_act * soft).astype(F32) * -LN2
                gacc[0, r, :] += fold(d_pre).astype(F32)
                buf[i, r, MID] = d_pre
                grad[k, pl.ds(2 * H + r.start, R), :] += dot(d_pre, x[i, :, mid], NT)
                return c

            per_tile(tile, rows=R)

            if k == 1:
                input_gradient(1, i)

        return item

    def input_gradient(k, i):
        m = mask_row(i, B)
        d_input = (dot(win[k], buf[i, :, MID]) + dp[i, 0:B, :].astype(F32)) * m
        if k == 1:
            dp[i, 0:B, :] = d_input.astype(BF16)
        else:
            stage[2 * i] = d_input[0:half].astype(BF16)
            stage[2 * i + 1] = d_input[half:].astype(BF16)
            here, there = mix_copy(i)
            there.start()
            here.start()

    rows_at_part = ((0, 2 * H), (2 * H, grad.shape[1]))
    came = (came0, came1)
    slots = ((from_item0, from_tm0), (from_item1, from_tm1))

    def sizes(part):
        big, chunk = slots[part][0].shape[1], slots[part][1].shape[1]
        return big, chunk, big // chunk

    def item_peer(d):
        return lax.rem(it + d, n_item)

    def tm_peer(d):
        return lax.rem(t + d, n_tm)

    def at_part(part, k, start, rows):
        return grad.at[k, pl.ds(rows_at_part[part][0] + start, rows)]

    def to_owner(part, k):
        a, b = rows_at_part[part]
        return remote(grad.at[k, pl.ds(a, b - a)], came[part], sem_k.at[part], sem_kr.at[part], {"section": o})

    def item_scatter(part, k, d):
        big = sizes(part)[0]
        src = at_part(part, k, item_peer(d) * big, big)
        return remote(
            src, slots[part][0].at[d - 1], sem_ri.at[part, d - 1], sem_rir.at[part, d - 1], {"item": item_peer(d)}
        )

    def tm_scatter(part, k, d):
        big, chunk, owners = sizes(part)
        src = at_part(part, k, it * big + lax.rem(tm_peer(d), owners) * chunk, chunk)
        return remote(
            src, slots[part][1].at[d - 1], sem_rt.at[part, d - 1], sem_rtr.at[part, d - 1], {"tm": tm_peer(d)}
        )

    def tm_gather(part, d, member):
        big, chunk, owners = sizes(part)
        rows = came[part].at[pl.ds(it * big + lax.rem(member, owners) * chunk, chunk)]
        return remote(rows, rows, sem_at.at[part, d - 1], sem_atr.at[part, d - 1], {"tm": tm_peer(d)})

    def item_gather(part, d, member):
        big = sizes(part)[0]
        rows = came[part].at[pl.ds(member * big, big)]
        return remote(rows, rows, sem_ai.at[part, d - 1], sem_air.at[part, d - 1], {"item": item_peer(d)})

    def sum_1(part, k):
        pl.when(s != k)(lambda: to_owner(part, k).start())

    def sum_2(part, k):
        pl.when(s != k)(lambda: to_owner(part, k).wait_send())

        @pl.when(s == k)
        def _():
            a, b = rows_at_part[part]
            to_owner(part, k).wait_recv()
            grad[k, a:b] += came[part][...]
            each(n_item, lambda d: item_scatter(part, k, d).start())

    def sum_3(part, k):
        big, chunk, owners = sizes(part)

        @pl.when(s == k)
        def _():
            each(n_item, lambda d: item_scatter(part, k, d).wait())
            mine = pl.ds(pl.multiple_of(rows_at_part[part][0] + it * big, 8), big)
            grad[k, mine] = lax.fori_loop(0, n_item - 1, lambda j, x: x + slots[part][0][j], grad[k, mine])
            each(n_tm, lambda d: pl.when(tm_peer(d) < owners)(lambda: tm_scatter(part, k, d).start()))

    def sum_4(part, k):
        big, chunk, owners = sizes(part)

        @pl.when(s == k)
        def _():
            def wait(d):
                pl.when(tm_peer(d) < owners)(lambda: tm_scatter(part, k, d).wait_send())
                pl.when(t < owners)(lambda: tm_scatter(part, k, d).wait_recv())

            each(n_tm, wait)

            @pl.when(t < owners)
            def _():
                start = it * big + t * chunk
                own = grad[k, pl.ds(pl.multiple_of(rows_at_part[part][0] + start, 8), chunk)]
                total = lax.fori_loop(0, n_tm - 1, lambda j, x: x + slots[part][1][j], own)
                came[part][pl.ds(pl.multiple_of(start, 8), chunk)] = total
                each(n_tm, lambda d: tm_gather(part, d, t).start())

    def sum_5(part, k):
        _, _, owners = sizes(part)

        @pl.when(s == k)
        def _():
            def wait(d):
                source = lax.rem(t - d + n_tm, n_tm)
                pl.when(t < owners)(lambda: tm_gather(part, d, t).wait_send())
                pl.when(source < owners)(lambda: tm_gather(part, d, source).wait_recv())

            each(n_tm, wait)
            each(n_item, lambda d: item_gather(part, d, it).start())

    def sum_6(part, k):
        @pl.when(s == k)
        def _():
            def wait(d):
                item_gather(part, d, it).wait_send()
                item_gather(part, d, lax.rem(it - d + n_item, n_item)).wait_recv()

            each(n_item, wait)

    last_rows = grad.shape[1] - 2 * H
    last_chunk = to_owner_slots.shape[2]
    last_owners = low_grad.shape[0] // last_chunk
    first_core = jnp.int32(0)

    def member_at(d):
        peer = lax.rem(me + d, members)
        return peer, {"section": first_core, "tm": peer // n_item, "item": lax.rem(peer, n_item)}

    def chunk_rows(member):
        return pl.ds(pl.multiple_of(lax.rem(member, last_owners) * last_chunk, 16), last_chunk)

    def last_scatter(core, d):
        peer, device = member_at(d)
        return remote(
            low_grad.at[chunk_rows(peer)], to_owner_slots.at[core, d], sem_ls.at[d], sem_lr.at[core, d], device
        )

    def last_gather(d, member):
        rows = low_total.at[chunk_rows(member)]
        return remote(rows, rows, sem_gs.at[d], sem_gr.at[d], member_at(d)[1])

    def others(body, start=1):
        lax.fori_loop(start, members, lambda d, c: (body(d), c)[1], 0)

    def last_1():
        low_grad[0:last_rows] = low(grad[0, 2 * H :])
        if low_grad.shape[0] > last_rows:
            low_grad[last_rows:] = jnp.zeros((low_grad.shape[0] - last_rows, LANES), BF16)

        def send(core):
            def one(d):
                pl.when(member_at(d)[0] < last_owners)(lambda: last_scatter(core, d).start())

            others(one, 1 - core)

        pl.when(s == 0)(lambda: send(0))
        pl.when(s == 1)(lambda: send(1))

    def last_2():
        def sent(core):
            def one(d):
                pl.when(member_at(d)[0] < last_owners)(lambda: last_scatter(core, d).wait_send())

            others(one, 1 - core)

        pl.when(s == 1)(lambda: sent(1))

        @pl.when(s == 0)
        def _():
            sent(0)

            @pl.when(me < last_owners)
            def _():
                others(lambda d: last_scatter(0, d).wait_recv())
                others(lambda d: last_scatter(1, d).wait_recv(), 0)
                mine = chunk_rows(me)
                total = low_grad[mine].astype(F32) + to_owner_slots[1, 0].astype(F32)
                total = lax.fori_loop(
                    1,
                    members,
                    lambda d, x: x + (to_owner_slots[0, d].astype(F32) + to_owner_slots[1, d].astype(F32)),
                    total,
                )
                low_total[mine] = low(total)
                others(lambda d: last_gather(d, me).start())

    def last_3():
        @pl.when(s == 0)
        def _():
            def wait(d):
                source = lax.rem(me - d + members, members)
                pl.when(me < last_owners)(lambda: last_gather(d, me).wait_send())
                pl.when(source < last_owners)(lambda: last_gather(d, source).wait_recv())

            others(wait)
            came1[...] = low_total[0:last_rows].astype(F32)

    group = H // 4

    def pack_rows(packed, which):
        lanes = lax.broadcasted_iota(jnp.int32, (group, LANES), 1)
        for g in range(4):
            for j in which:
                total = jnp.sum(gacc[j, g * group : (g + 1) * group, :], axis=1, keepdims=True)
                packed = jnp.where(lanes == 32 * g + j, total, packed)
        return packed

    def finish_early(k):
        lanes = lax.broadcasted_iota(jnp.int32, (group, LANES), 1)
        bias = jnp.broadcast_to(bias_sum[k, 0:1, :], (LANES, 2 * B)).T
        packed = jnp.zeros((group, LANES), F32)
        for g in range(2 * B // group):
            packed = jnp.where(lanes == 32 * g + 11, bias[g * group : (g + 1) * group], packed)
        grad[k, 3 * H : 3 * H + group] = pack_rows(packed, range(2, 11))

    def finish_block(k):
        grad[k, 3 * H : 3 * H + group] = pack_rows(grad[k, 3 * H : 3 * H + group], (0, 1))

    def mask_gradients(i):
        m = mask_row(i, R)

        def tile(r, c):
            dp[i, r, :] = (dp[i, r, :].astype(F32) * m).astype(BF16)
            return c

        per_tile(tile, 2 * B)

    wait_weights(0, 1)
    main_local.wait()
    main_send.wait_send()
    main_recv.wait_recv()

    @pl.when(t > 0)
    def _():
        for core in (0, 1):
            halo_send(0, core).wait_send()
            halo_recv(1, core).wait_recv()

    @pl.when(t < last)
    def _():
        for core in (0, 1):
            halo_send(1, core).wait_send()
            halo_recv(0, core).wait_recv()

    def steps(count, *bodies):
        def step(j, c):
            for first, body in bodies:
                pl.when((j >= first) & (j < first + NI))(functools.partial(body, j - first))
            return c

        lax.fori_loop(0, count, step, 0)

    def at_item(j, body, *args):
        return lambda i: pl.when(i == j)(lambda: body(*args))

    def send_x1_edges(i):
        @pl.when(i == NI - 1)
        def _():
            pack_edges(x1, B, 1)
            send_edges(1, B)

    per_item(phase1(0))
    p2, p3 = phase2(0), phase3(0)
    per_item(lambda i: (p2(i), p3(i)))
    wait_weights(2, 3)
    steps(NI + 2, (0, phase4(0)), (0, send_x1_edges), (2, phase1(1)))
    edge1()
    load_out.wait()
    load_skip.wait()
    per_item(mask_gradients)
    pack_edges(dp, 2 * B, 0)
    send_edges(0, 2 * B)
    per_item(phase2(1))
    edge2()
    place_halos(first_edge)
    per_item(phase3(1))
    edge3()
    recv_edges(0, 2 * B, dp_edge)
    wait_weights(4)
    gacc[...] = jnp.zeros(gacc.shape, F32)
    per_item(phase5(1))
    sum_1(0, 1)
    per_item(phase6(1))
    edge6()
    place_halos(conv_edge)
    sum_2(0, 1)
    wait_weights(5)
    per_item(phase7(1))
    finish_early(1)
    per_item(phase8(1))
    sum_3(0, 1)
    finish_block(1)
    sum_1(1, 1)
    gacc[...] = jnp.zeros(gacc.shape, F32)
    per_item(phase5(0))
    sum_1(0, 0)
    sum_4(0, 1)
    sum_2(1, 1)
    steps(NI, (0, at_item(2, sum_2, 0, 0)), (0, phase6(0)))
    sum_5(0, 1)
    sum_3(1, 1)
    steps(NI, (0, at_item(2, sum_3, 0, 0)), (0, phase7(0)))
    per_item(phase7_ends)
    sum_4(1, 1)
    finish_early(0)
    steps(NI, (0, at_item(1, sum_4, 0, 0)), (0, phase8(0)))
    finish_block(0)
    last_1()
    sum_5(0, 0)
    sum_5(1, 1)
    steps(NI, (0, at_item(3, last_2)), (0, outputs))
    sum_6(0, 0)
    sum_6(0, 1)
    sum_6(1, 1)
    results = [
        pltpu.make_async_copy(came[part], grad_h.at[pl.ds(a, b - a)], sem_f.at[part])
        for part, (a, b) in enumerate(rows_at_part)
    ]
    results[0].start()
    per_item(lambda i: input_gradient(0, i))
    last_3()
    results[1].start()
    for copy in results:
        copy.wait()

    for i in range(NI):
        here, there = mix_copy(i)
        here.wait()
        there.wait_send()
        remote(
            stage.at[2 * i], gmix_h.at[o * NI + i], sem_m.at[1, i], sem_mr.at[i], {"section": o}
        ).wait_recv()
        for kind, k in ((1, 0), (0, 1), (1, 1)):
            wait_out(kind, k, i)
        wait_came(0, i)
        wait_came(1, i)


def chunk_of(rows, members):
    chunk = -(-rows // members)
    chunk = -(-chunk // 8) * 8
    while rows % chunk:
        chunk += 8
    return chunk


def run(n_tm, n_item, sources, gout, gskip, w_in, chan, w_out, b_out, counts, lengths):
    n_src, flat, F = sources.shape
    items, B, _ = gout.shape
    NI = items // 2
    H = w_in.shape[0]
    W = F + 2 * DILATION
    half = B // 2
    rows0, rows1 = 2 * H, H + H // 4
    quarter0, quarter1 = rows0 // n_item, rows1 // n_item
    members = n_tm * n_item
    low_chunk = -(-rows1 // (16 * members)) * 16
    low_owners = -(-rows1 // low_chunk)
    smem = pl.BlockSpec(memory_space=pltpu.SMEM)
    any_spec = pl.BlockSpec(memory_space=pl.ANY)
    dma = pltpu.SemaphoreType.DMA
    shape = jax.ShapeDtypeStruct
    outs = (
        shape((items, B, F), BF16),
        shape((items, B, F), BF16),
        shape((items, half, F), BF16),
        shape((rows0 + rows1, LANES), F32),
    )
    scratch = [
        pltpu.VMEM((items, half, F), BF16),
        pltpu.VMEM((NI, B, W), BF16),
        pltpu.VMEM((NI, B, F), BF16),
        pltpu.VMEM((NI, B, F), BF16),
        pltpu.VMEM((NI, H, W), BF16),
        pltpu.VMEM((NI, H, F), BF16),
        pltpu.VMEM((2, NI, H, F), BF16),
        pltpu.VMEM((2, NI, H, F), BF16),
        pltpu.VMEM((2, NI, H, F), BF16),
        pltpu.VMEM((NI, H, W), BF16),
        pltpu.VMEM((H, H), F32),
        pltpu.VMEM((NI, 2 * B, F), BF16),
        pltpu.VMEM((11, H, LANES), F32),
        pltpu.VMEM((2, H, B), BF16),
        pltpu.VMEM((2, H, 2 * B), BF16),
        pltpu.VMEM((2, 2 * B, H), BF16),
        pltpu.VMEM((2, B, H), BF16),
        pltpu.VMEM((2, H, LANES), F32),
        pltpu.VMEM((2, 2 * B, LANES), F32),
        pltpu.VMEM((low_chunk * low_owners, LANES), BF16),
        pltpu.VMEM((low_chunk * low_owners, LANES), BF16),
        pltpu.VMEM((2, members, low_chunk, LANES), BF16),
        pltpu.VMEM((2, rows0 + rows1, LANES), F32),
        pltpu.VMEM((2, 8, 2 * B), F32),
        pltpu.VMEM((rows0, LANES), F32),
        pltpu.VMEM((rows1, LANES), F32),
        pltpu.VMEM((n_item - 1, quarter0, LANES), F32),
        pltpu.VMEM((n_item - 1, quarter1, LANES), F32),
        pltpu.VMEM((n_tm - 1, chunk_of(quarter0, n_tm), LANES), F32),
        pltpu.VMEM((n_tm - 1, chunk_of(quarter1, n_tm), LANES), F32),
        pltpu.VMEM((NI, 8, W), F32),
        pltpu.VMEM((8, LANES), F32),
        pltpu.VMEM((NI, 8, LANES), F32),
        pltpu.VMEM((NI, 2, 8, LANES), F32),
        pltpu.VMEM((4, NI, 2, 8, LANES), F32),
        pltpu.VMEM((NI, 2, 8, LANES), F32),
        pltpu.VMEM((2, NI, 8, LANES), F32),
        pltpu.VMEM((2, NI, n_tm - 1, 8, LANES), F32),
        pltpu.VMEM((2 * LANES, 2 * LANES), BF16),
        pltpu.VMEM(w_in.shape, BF16),
        pltpu.VMEM(chan.shape, F32),
        pltpu.VMEM(w_out.shape, BF16),
        pltpu.VMEM(b_out.shape, F32),
        pltpu.VMEM((2, 3, 2 * B, LANES), BF16),
        pltpu.VMEM((2, 2, 2 * B, LANES), BF16),
        pltpu.VMEM((B, LANES), BF16),
        pltpu.VMEM((2 * B, LANES), BF16),
        pltpu.VMEM((H, LANES), BF16),
        pltpu.VMEM((H, LANES), BF16),
        pltpu.VMEM((H, LANES), BF16),
        pltpu.VMEM((H, LANES), BF16),
        dma((n_src + 4,)),
        dma((6, 2)),
        dma((6,)),
        dma((5,)),
        dma((2,)),
        dma((2, 2)),
        dma((2, 2)),
        dma((2, NI, n_tm - 1)),
        dma((2, NI, n_tm - 1)),
        dma((2, NI)),
        dma((2, NI)),
        dma((2, 2, NI)),
        dma((2, NI)),
        dma((2, NI)),
        dma((NI,)),
        dma((members,)),
        dma((2, members)),
        dma((members,)),
        dma((members,)),
        dma((2,)),
        dma((2,)),
        dma((2, n_item - 1)),
        dma((2, n_item - 1)),
        dma((2, n_tm - 1)),
        dma((2, n_tm - 1)),
        dma((2, n_tm - 1)),
        dma((2, n_tm - 1)),
        dma((2, n_item - 1)),
        dma((2, n_item - 1)),
        dma((2,)),
    ]
    return pl.pallas_call(
        functools.partial(kernel, (n_tm, n_item, NI, H, B, F)),
        out_shape=outs,
        in_specs=[any_spec] * 7 + [smem] * 2,
        out_specs=[any_spec] * len(outs),
        scratch_shapes=scratch,
        compiler_params=pltpu.CompilerParams(
            collective_id=0, has_side_effects=True, vmem_limit_bytes=VMEM_LIMIT
        ),
        name="temporal_blocks",
    )(sources, gout, gskip, w_in, chan, w_out, b_out, counts, lengths)


def close_kernel(
    block_in, skip_in, gmix_in, grad_in, counts,
    block_h, skip_h, sources_h, w_in_h, chan_h, w_out_h, b_out_h,
    held, mixed, full, nothing, sums, w_out, chan, bias, sem_a, sem_b, sem_g, sem_s, sem_w,
):
    items = gmix_in.shape[0]
    H, B = w_in_h.shape
    n_src = sources_h.shape[0]
    part = items // 2
    plain = [(j, i) for i in (0, 1) for j in (0, 1)]

    def some(i):
        return pl.ds(i * part, part)

    def fetch(j, i):
        return pltpu.make_async_copy((block_in, skip_in)[j].at[some(i)], held.at[j, some(i)], sem_a.at[j, i])

    def store(j, i):
        return pltpu.make_async_copy(held.at[j, some(i)], (block_h, skip_h)[j].at[some(i)], sem_b.at[j, i])

    loads = [pltpu.make_async_copy(gmix_in.at[some(i)], mixed.at[some(i)], sem_g.at[i]) for i in (0, 1)]
    load_sums = pltpu.make_async_copy(grad_in, sums, sem_w.at[0])
    for copy in loads:
        copy.start()
    load_sums.start()
    for j, i in plain:
        fetch(j, i).start()
    nothing[...] = jnp.zeros(nothing.shape, F32)
    for i in range(items):
        if i % part == 0:
            loads[i // part].wait()
        full[i] = mixed[i].astype(F32)
        for n in range(n_src):

            @pl.when(n < counts[i])
            def _():
                pltpu.make_async_copy(full.at[i], sources_h.at[n, i], sem_s.at[n, i]).start()

            @pl.when(n >= counts[i])
            def _():
                pltpu.make_async_copy(nothing, sources_h.at[n, i], sem_s.at[n, i]).start()

    load_sums.wait()
    store_w_in = pltpu.make_async_copy(sums.at[pl.ds(2 * H, H)], w_in_h, sem_w.at[1])
    store_w_in.start()
    for j, i in plain:
        fetch(j, i).wait()
        store(j, i).start()
    w_out[0:B, :] = sums[0:H, :].T
    w_out[B : 2 * B, :] = sums[H : 2 * H, :].T
    rows = sums[3 * H : 3 * H + H // 4, :].T
    for j in range(chan.shape[0]):
        chan[j] = jnp.concatenate([rows[32 * g + j : 32 * g + j + 1] for g in range(4)], axis=1)
    bias[...] = jnp.concatenate([rows[32 * g + 11 : 32 * g + 12] for g in range(2 * B * 4 // H)], axis=1)
    late = [
        pltpu.make_async_copy(src, dst, sem_w.at[2 + j])
        for j, (src, dst) in enumerate(((w_out, w_out_h), (chan, chan_h), (bias, b_out_h)))
    ]
    for copy in late:
        copy.start()
    for copy in late:
        copy.wait()
    store_w_in.wait()
    for j, i in plain:
        store(j, i).wait()
    for i in range(items):
        for n in range(n_src):
            pltpu.make_async_copy(full.at[i], sources_h.at[n, i], sem_s.at[n, i]).wait()


def close(n_src, n_rows, block, skip, gmix, grad, counts):
    items, half, F = gmix.shape
    B = 2 * half
    H = (grad.shape[0] * 4) // 13
    any_spec = pl.BlockSpec(memory_space=pl.ANY)
    dma = pltpu.SemaphoreType.DMA
    shape = jax.ShapeDtypeStruct
    return pl.pallas_call(
        close_kernel,
        out_shape=(
            shape(block.shape, BF16),
            shape(skip.shape, BF16),
            shape((n_src, items, half, F), F32),
            shape((H, B), F32),
            shape((n_rows, 1, H), F32),
            shape((2 * B, H), F32),
            shape((1, 2 * B), F32),
        ),
        in_specs=[any_spec] * 4 + [pl.BlockSpec(memory_space=pltpu.SMEM)],
        out_specs=[any_spec] * 7,
        scratch_shapes=[
            pltpu.VMEM((2, items, B, F), BF16),
            pltpu.VMEM((items, half, F), BF16),
            pltpu.VMEM((items, half, F), F32),
            pltpu.VMEM((half, F), F32),
            pltpu.VMEM(grad.shape, F32),
            pltpu.VMEM((2 * B, H), F32),
            pltpu.VMEM((n_rows, 1, H), F32),
            pltpu.VMEM((1, 2 * B), F32),
            dma((2, 2)),
            dma((2, 2)),
            dma((2,)),
            dma((n_src, items)),
            dma((5,)),
        ],
        compiler_params=pltpu.CompilerParams(vmem_limit_bytes=VMEM_LIMIT),
        name="lay_out",
    )(block, skip, gmix, grad, counts)


def local(sources, source_counts, valid_lengths, w_in, chan, w_out, b_out, grad_out, grad_skip):
    n_sources, per_device, half, F = sources.shape
    block_out, skip_out, gmix, grad = run(
        lax.axis_size("tm"),
        lax.axis_size("item"),
        sources.reshape(n_sources, per_device * half, F),
        grad_out,
        grad_skip,
        w_in[0],
        chan.transpose(1, 0, 2),
        w_out[0],
        b_out,
        source_counts,
        valid_lengths,
    )
    block_out, skip_out, grad_sources, grad_w_in, grad_chan, grad_w_out, grad_b_out = close(
        n_sources, chan.shape[1], block_out, skip_out, gmix, grad, source_counts
    )
    return (
        block_out[None],
        skip_out[None],
        grad_sources,
        grad_w_in[None],
        grad_chan.transpose(1, 0, 2),
        grad_w_out[None],
        grad_b_out,
    )


def solution(mesh):
    in_specs = (
        P(None, "item", "section", "tm"),
        P("item"),
        P("item"),
        P("section", None, None),
        P("section", None, None),
        P("section", None, None),
        P("section", None),
        P("item", None, "tm"),
        P("item", None, "tm"),
    )
    out_specs = (
        P("section", "item", None, "tm"),
        P("section", "item", None, "tm"),
        P(None, "item", "section", "tm"),
        P("section", None, None),
        P("section", None, None),
        P("section", None, None),
        P("section", None),
    )
    return jax.shard_map(local, mesh=mesh, in_specs=in_specs, out_specs=out_specs, check_vma=False)
```

```python
import functools
import math

import jax
import jax.numpy as jnp
from jax import lax
from jax.experimental import pallas as pl
from jax.experimental.pallas import tpu as pltpu
from jax.sharding import PartitionSpec as P

DILATION = 128
LANES = 128
ROWS = 128
ROWS1 = 512
ROWS2 = 512
ROWS3 = 512
ROWS4 = 128
ROWS5 = 512
ROWS6 = 512
ROWS7 = 512
ROWS7_ENDS = 512
ROWS8 = 512
EPSILON = 1e-05
VMEM_LIMIT = 63 * 1024 * 1024 + 512 * 1024
LN2 = math.log(2.0)
LOG2E = 1.0 / LN2
F32 = jnp.float32
BF16 = jnp.bfloat16
MESH = pl.DeviceIdType.MESH
NT = (((1,), (1,)), ((), ()))
NN = (((1,), (0,)), ((), ()))


def dot(a, b, dims=NN, precision=None):
    return lax.dot_general(a, b, dims, precision=precision, preferred_element_type=F32)


def remote(src, dst, send, recv, device):
    return pltpu.make_async_remote_copy(
        src_ref=src, dst_ref=dst, send_sem=send, recv_sem=recv, device_id=device, device_id_type=MESH
    )


def wide(v, width):
    return jnp.concatenate([v] * (width // LANES), axis=1)


def tall(v, rows):
    return jnp.concatenate([v] * (rows // v.shape[0]), axis=0)


def fold(v):
    parts = [v[:, at : at + LANES] for at in range(0, v.shape[1], LANES)]
    while len(parts) > 1:
        parts = [a + b for a, b in zip(parts[::2], parts[1::2])] + parts[len(parts) & ~1 :]
    return parts[0]


def fold_rows(v, count=8):
    parts = [v[at : at + count] for at in range(0, v.shape[0], count)]
    while len(parts) > 1:
        parts = [a + b for a, b in zip(parts[::2], parts[1::2])] + parts[len(parts) & ~1 :]
    return parts[0]


def low(v):
    return v.astype(BF16)


def column(table, j):
    return jnp.broadcast_to(table[:, j : j + 1], (table.shape[0], LANES))


def rows_at(t, count):
    return pl.ds(pl.multiple_of(t * count, count), count)


def kernel(
    dims,
    sources_h, gout_h, gskip_h, w_in_h, chan_h, w_out_h, b_out_h, counts, lengths,
    block_h, skip_h, gmix_h, grad_h,
    stage, x0, x1, skips, act1_0, act1_1, soft1, act2, soft2, buf, wide_s, dp, gacc,
    wpre, wout, wg, win, chan, col,
    low_grad, low_total, to_owner_slots, grad, bias_sum, came0, came1, from_item0, from_item1, from_tm0, from_tm1,
    mask_ref, edge_mask_ref, invn_ref, inner_sums, stat, back, st_src, st_buf,
    shifts, w_in_ref, chan_ref, w_out_ref, b_out_ref, edge_src, edge_in, x_edge, dp_edge, first_edge, act_edge, soft_edge, conv_edge,
    sem_s, sem_w, sem_x, sem_xr, sem_g, sem_es, sem_er, sem_ss, sem_sr, sem_hs, sem_hr, sem_o, sem_or, sem_m, sem_mr,
    sem_ls, sem_lr, sem_gs, sem_gr, sem_k, sem_kr, sem_ri, sem_rir, sem_rt, sem_rtr, sem_at, sem_atr, sem_ai, sem_air, sem_f,
):
    n_tm, n_item, NI, H, B, F = dims
    R = ROWS
    W = F + 2 * DILATION
    MID = slice(DILATION, DILATION + F)
    half = B // 2
    s = lax.axis_index("section")
    t = lax.axis_index("tm")
    o = 1 - s
    left = t - 1
    right = t + 1
    last = n_tm - 1
    first_item = s * NI
    lane = lax.broadcasted_iota(jnp.int32, (R, LANES), 1)
    lane8 = lax.broadcasted_iota(jnp.int32, (8, LANES), 1)

    it = lax.axis_index("item")
    members = n_tm * n_item
    me = t * n_item + it
    n_src = sources_h.shape[0]

    def load_source(n):
        return pltpu.make_async_copy(sources_h.at[n], soft2.at[1, n], sem_s.at[n])

    small = [
        pltpu.make_async_copy(src, dst, sem_s.at[n_src + j])
        for j, (src, dst) in enumerate(
            ((w_in_h, w_in_ref), (chan_h, chan_ref), (w_out_h, w_out_ref), (b_out_h, b_out_ref))
        )
    ]
    for copy in small:
        copy.start()
    for n in range(n_src):
        load_source(n).start()
    edge_in[...] = jnp.zeros(edge_in.shape, BF16)
    row = lax.broadcasted_iota(jnp.int32, (2 * LANES, 2 * LANES), 0)
    to = lax.broadcasted_iota(jnp.int32, (2 * LANES, 2 * LANES), 1)
    step = jnp.where(to < LANES, LANES - 1, 1 - LANES)
    shifts[...] = low(jnp.where(row - to == step, 1.0, 0.0))

    barrier = pltpu.get_barrier_semaphore()

    def greet(d, c):
        peer = lax.rem(me + d, members)
        device = {"tm": peer // n_item, "item": lax.rem(peer, n_item)}
        pl.semaphore_signal(barrier, inc=1, device_id=device, device_id_type=MESH)
        pl.semaphore_signal(barrier, inc=1, device_id={"section": o} | device, device_id_type=MESH)
        return c

    pl.semaphore_signal(barrier, inc=1, device_id={"section": o}, device_id_type=MESH)
    lax.fori_loop(1, members, greet, 0)
    for copy in small:
        copy.wait()

    wpre[s] = w_in_ref[...]
    wide_s[0:LANES, 0:H] = jnp.zeros((LANES, H), F32)
    for j in range(chan_ref.shape[0]):
        wide_s[j : j + 1, 0:H] = chan_ref[j]
    chan[s] = wide_s[0:LANES, 0:H].T
    weights = (wpre, chan, wg, col, wout, win)

    def weight_copies(j):
        ref = weights[j]
        return (
            remote(ref.at[s], ref.at[s], sem_w.at[j, 0], sem_w.at[j, 1], {"section": o}),
            remote(ref.at[o], ref.at[o], sem_w.at[j, 0], sem_w.at[j, 1], {"section": o}),
        )

    def wait_weights(*which):
        for j in which:
            send, recv = weight_copies(j)
            recv.wait_recv()
            send.wait_send()

    pl.semaphore_wait(barrier, 2 * members - 1)
    for j in (0, 1):
        weight_copies(j)[0].start()

    for n in range(n_src):
        load_source(n).wait()

    def mix_item(i, c):
        rows = pl.ds(pl.multiple_of(i * half, half), half)
        where = lax.broadcasted_iota(jnp.int32, (8, F), 1) + t * F
        m = tall(jnp.where(where < lengths[i], 1.0, 0.0), half)
        total = jnp.zeros((half, F), F32)
        for n in range(n_src):
            total += soft2[1, n, rows, :].astype(F32) * jnp.where(n < counts[i], 1.0, 0.0)
        stage[i] = (total * m).astype(BF16)
        return c

    lax.fori_loop(o * NI, o * NI + NI, mix_item, 0)

    own_rows = pl.ds(pl.multiple_of(s * half, half), half)
    other_rows = pl.ds(pl.multiple_of(o * half, half), half)
    items_of = lambda core: pl.ds(core * NI, NI)
    centre = pl.ds(DILATION, F)
    head, tail = pl.ds(0, DILATION), pl.ds(F + DILATION, DILATION)

    main_local = pltpu.make_async_copy(stage.at[items_of(s)], x0.at[:, own_rows, centre], sem_x.at[0])
    main_send = remote(
        stage.at[items_of(o)], x0.at[:, own_rows, centre], sem_x.at[1], sem_xr.at[0], {"section": o}
    )
    main_recv = remote(
        stage.at[items_of(o)], x0.at[:, other_rows, centre], sem_x.at[1], sem_xr.at[0], {"section": o}
    )

    def halo_send(side, core):
        edge = pl.ds(0, DILATION) if side == 0 else pl.ds(F - DILATION, DILATION)
        place = tail if side == 0 else head
        return remote(
            stage.at[items_of(core), :, edge],
            x0.at[:, own_rows, place],
            sem_x.at[2 + 2 * side + core],
            sem_xr.at[1 + 2 * side + s],
            {"section": core, "tm": left if side == 0 else right},
        )

    def halo_recv(side, core):
        place = tail if side == 0 else head
        rows = pl.ds(core * half, half)
        return remote(
            x0.at[:, rows, place], x0.at[:, rows, place], sem_x.at[0], sem_xr.at[1 + 2 * side + core], {"section": o}
        )

    def send_halos(core):
        pl.when(t > 0)(lambda: halo_send(0, core).start())
        pl.when(t < last)(lambda: halo_send(1, core).start())

    main_send.start()
    send_halos(o)
    lax.fori_loop(s * NI, s * NI + NI, mix_item, 0)
    main_local.start()
    send_halos(s)
    load_out = pltpu.make_async_copy(gout_h.at[pl.ds(first_item, NI)], dp.at[:, pl.ds(0, B)], sem_g.at[0])
    load_skip = pltpu.make_async_copy(gskip_h.at[pl.ds(first_item, NI)], dp.at[:, pl.ds(B, B)], sem_g.at[1])
    load_out.start()
    load_skip.start()

    w_out = w_out_ref[...].astype(F32)
    win[s] = w_in_ref[...].astype(F32).T.astype(BF16)
    wout[s] = w_out.T.astype(BF16)
    gained = (w_out * chan_ref[9]).astype(BF16)
    wg[s] = gained
    bias = jnp.broadcast_to(b_out_ref[...], (LANES, 2 * B)).T
    bias += jnp.sum(w_out * chan_ref[10], axis=1, keepdims=True)
    gain = jnp.sum(gained.astype(F32), axis=1, keepdims=True)
    lane_w = lax.broadcasted_iota(jnp.int32, (2 * B, LANES), 1)
    col[s] = jnp.where(lane_w == 0, bias, gain)
    for j in range(2, len(weights)):
        weight_copies(j)[0].start()

    for i in range(NI):
        length = lengths[first_item + i]
        where = lax.broadcasted_iota(jnp.int32, (8, W), 1) + (t * F - DILATION)
        mask_ref[i] = jnp.where((where >= 0) & (where < length), 1.0, 0.0)
        invn_ref[i] = 1.0 / (jnp.full((8, LANES), length, jnp.int32).astype(F32) * H)
    within = lane8 % 32
    frame = t * F + jnp.where(within < 16, within - 2, within - 17 + F)
    length = jnp.full((8, LANES), lengths[first_item], jnp.int32)
    for i in range(1, NI):
        length = jnp.where(lane8 >= 32 * i, lengths[first_item + i], length)
    held = (within < 3) | ((within >= 16) & (within < 19))
    edge_mask_ref[...] = jnp.where(held & (frame >= 0) & (frame < length), 1.0, 0.0)

    @pl.when(t == 0)
    def _():
        x0[:, :, 0:DILATION] = jnp.zeros((NI, B, DILATION), BF16)

    @pl.when(t == last)
    def _():
        x0[:, :, F + DILATION : W] = jnp.zeros((NI, B, DILATION), BF16)

    grad[...] = jnp.zeros(grad.shape, F32)
    bias_sum[...] = jnp.zeros(bias_sum.shape, F32)

    def each(count, body, first=1):
        if count <= 8:
            for d in range(first, count):
                body(d)
        else:
            lax.fori_loop(first, count, lambda d, c: (body(d), c)[1], 0)

    def stat_copy(ph, i, d, to):
        p = ph % 2
        return remote(
            st_src.at[p, i], st_buf.at[p, i, d - 1], sem_ss.at[p, i, d - 1], sem_sr.at[p, i, d - 1], {"tm": to}
        )

    def send_stats(ph, i, a, b):
        rows = [jnp.sum(a, axis=0, keepdims=True), jnp.sum(b, axis=0, keepdims=True)]
        st_src[ph % 2, i] = jnp.concatenate(rows + [jnp.zeros((6, LANES), F32)], axis=0)

        each(n_tm, lambda d: stat_copy(ph, i, d, lax.rem(t + d, n_tm)).start())

    def recv_stats(ph, i):
        def one(d, total):
            copy = stat_copy(ph, i, d, lax.rem(t + d, n_tm))
            copy.wait_send()
            copy.wait_recv()
            return total + st_buf[ph % 2, i, d - 1]

        total = st_src[ph % 2, i]
        if n_tm <= 8:
            for d in range(1, n_tm):
                total = one(d, total)
        else:
            total = lax.fori_loop(1, n_tm, one, total)
        sums = jnp.sum(total, axis=1, keepdims=True)
        return (
            jnp.broadcast_to(sums[0:1], (8, LANES)),
            jnp.broadcast_to(sums[1:2], (8, LANES)),
        )

    def finish_norm(ph, slot, i):
        a, b = recv_stats(ph, i)
        inv_n = invn_ref[i]
        mean = a * inv_n
        spread = jnp.maximum(b * inv_n - mean * mean, 0.0)
        stat[slot, i, 0] = mean
        stat[slot, i, 1] = lax.rsqrt(spread + EPSILON / (LN2 * LN2))

    def finish_back(ph, slot, i):
        a, b = recv_stats(ph, i)
        inv_n = invn_ref[i]
        mean, inv = stat[slot, i, 0], stat[slot, i, 1]
        q = b * inv_n * inv
        back[i, 0] = (mean * q - a * inv_n) * (inv * LOG2E)
        back[i, 1] = -q * (inv * LOG2E)

    def correction(i, rows):
        m = mask_ref[i, :, MID]
        return [tall(m * wide(back[i, j], F), rows) for j in (0, 1)]

    def lanes_of(ref, j):
        out = ref[0, j]
        for i in range(1, NI):
            out = jnp.where(lane8 >= 32 * i, ref[i, j], out)
        return out

    def per_item(body):
        lax.fori_loop(0, NI, lambda i, c: (body(i), c)[1], 0)

    def per_tile(body, count=H, rows=R, init=0):
        return lax.fori_loop(0, count // rows, lambda j, c: body(rows_at(j, rows), c), init)

    def mask_row(i, rows, at=DILATION, width=F):
        return tall(mask_ref[i, :, at : at + width], rows)

    zero8 = jnp.zeros((8, LANES), F32)
    zero8f = jnp.zeros((8, F), F32)

    def pack_edges(src, channels, slot):
        def tile(r, c):
            to_left = to_right = own = jnp.zeros((R, LANES), F32)
            for i in range(NI):
                a = src[i, r, 0:LANES].astype(F32)
                z = src[i, r, F - LANES : F].astype(F32)
                base = 32 * i
                to_left += jnp.where(
                    (lane == base + 17) | (lane == base + 18), pltpu.roll(a, base + 17, 1), 0.0
                )
                to_right += jnp.where(
                    (lane == base) | (lane == base + 1), pltpu.roll(z, base + 2, 1), 0.0
                )
                own += jnp.where(lane == base + 2, pltpu.roll(a, base + 2, 1), 0.0)
                own += jnp.where(lane == base + 16, pltpu.roll(z, base + 17, 1), 0.0)
            edge_src[slot, 0, r, :] = to_left.astype(BF16)
            edge_src[slot, 1, r, :] = to_right.astype(BF16)
            edge_src[slot, 2, r, :] = own.astype(BF16)
            return c

        per_tile(tile, channels)

    def edge_copy(slot, side, channels):
        rows = pl.ds(0, channels)
        return remote(
            edge_src.at[slot, side, rows],
            edge_in.at[slot, side, rows],
            sem_es.at[slot, side],
            sem_er.at[slot, side],
            {"tm": left if side == 0 else right},
        )

    def send_edges(slot, channels):
        @pl.when(t > 0)
        def _():
            edge_copy(slot, 0, channels).start()

        @pl.when(t < last)
        def _():
            edge_copy(slot, 1, channels).start()

    def recv_edges(slot, channels, dst):
        @pl.when(t > 0)
        def _():
            edge_copy(slot, 0, channels).wait_send()
            edge_copy(slot, 1, channels).wait_recv()

        @pl.when(t < last)
        def _():
            edge_copy(slot, 1, channels).wait_send()
            edge_copy(slot, 0, channels).wait_recv()

        def tile(r, c):
            total = edge_src[slot, 2, r, :].astype(F32)
            for side in (0, 1):
                total += edge_in[slot, side, r, :].astype(F32)
            dst[r, :] = total.astype(BF16)
            return c

        per_tile(tile, channels)

    def rectify(neg, rest):
        soft = jnp.maximum(neg, jnp.log2(1.0 + jnp.exp2(jnp.minimum(neg, 100.0))))
        return rest * soft - neg, soft

    def add_sums(a, sums):
        return tuple(x + fold_rows(fold_rows(v, 16).astype(F32)) for x, v in zip(sums, (a, a * a)))

    def send_sums(ph, i, sums):
        m = mask_ref[i, :, MID]
        send_stats(ph, i, fold(sums[0] * m), fold(sums[1] * m))

    def phase1(k):
        R = ROWS1
        width = W if k == 0 else F
        x = x0 if k == 0 else x1
        act = act1_0 if k == 0 else act1_1
        mid = MID if k == 0 else slice(0, F)

        def item(i):

            def tile(r, sums):
                table = chan[k, r, :]
                bias = column(table, 0) * -LOG2E
                rest = 1.0 - column(table, 1)
                neg = dot(wpre[k, r, :], x[i]) * -LOG2E + wide(bias, width)
                a, soft = rectify(neg, wide(rest, width))
                a = low(a)
                act[i, r, :] = a
                soft1[k, i, r, :] = soft[:, mid].astype(BF16)
                return add_sums(a[:, mid], sums)

            send_sums(4 * k, i, per_tile(tile, rows=R, init=(zero8f, zero8f)))

        return item

    def edge1():
        R = ROWS1
        recv_edges(1, B, x_edge)
        wide_s[:, 0:LANES] = dot(wpre[1], x_edge[...])

        def tile(r, c):
            table = chan[1, r, :]
            neg = wide_s[r, 0:LANES] * -LOG2E + column(table, 0) * -LOG2E
            a, _ = rectify(neg, 1.0 - column(table, 1))
            wide_s[r, 0:LANES] = a
            return c

        per_tile(tile, rows=R)

    def phase2(k):
        R = ROWS2
        width = W if k == 0 else F
        at = 0 if k == 0 else DILATION
        act = act1_0 if k == 0 else act1_1

        def item(i):
            finish_norm(4 * k, 2 * k, i)
            mean, inv = tall(stat[2 * k, i, 0], R), tall(stat[2 * k, i, 1], R)
            m = low(mask_row(i, R, at, width))

            def tile(r, c):
                table = chan[k, r, :]
                scale = inv * column(table, 2)
                shift = column(table, 3) - mean * scale
                a = act[i, r, :].astype(F32)
                buf[i, r, at : at + width] = low(a * wide(scale, width) + wide(shift, width)) * m
                return c

            per_tile(tile, rows=R)

        return item

    def edge2():
        R = ROWS2
        mean, inv = tall(lanes_of(stat.at[2], 0), R), tall(lanes_of(stat.at[2], 1), R)
        m = tall(edge_mask_ref[...], R)

        def tile(r, c):
            table = chan[1, r, :]
            scale = inv * column(table, 2)
            a = wide_s[r, 0:LANES]
            first_edge[r, :] = (((a - mean) * scale + column(table, 3)) * m).astype(BF16)
            return c

        per_tile(tile, rows=R)

    def place_halos(edge):
        for i in range(NI):
            buf[i, :, 0:DILATION] = pltpu.roll(edge[...], (254 - 32 * i) % 128, 1)
            buf[i, :, F + DILATION : W] = pltpu.roll(edge[...], (239 - 32 * i) % 128, 1)

    def shifted(i, r):
        before, after = [], []
        for j in range(F // LANES + 1):
            v = dot(buf[i, r, j * LANES : (j + 2) * LANES], shifts[...])
            before.append(v[:, :LANES])
            after.append(v[:, LANES:])
        return jnp.concatenate(before[:-1], axis=1), jnp.concatenate(after[1:], axis=1)

    def taps(k, i, r):
        f = buf[i, r, MID]
        if k == 0:
            return buf[i, r, 0:F], f, buf[i, r, 2 * DILATION : W]
        before, after = shifted(i, r)
        return before, f, after

    def conv_coefs(table):
        return [column(table, j) * -LOG2E for j in (4, 5, 6, 7)], 1.0 - column(table, 8)

    def phase3(k):
        R = ROWS3
        def item(i):

            def tile(r, sums):
                c, rest = conv_coefs(chan[k, r, :])
                before, f, after = (v.astype(F32) for v in taps(k, i, r))
                neg = wide(c[0], F) * before + wide(c[1], F) * f + wide(c[2], F) * after + wide(c[3], F)
                a, soft = rectify(neg, wide(rest, F))
                a = low(a)
                act2[k, i, r, :] = a
                soft2[k, i, r, :] = soft.astype(BF16)
                return add_sums(a, sums)

            send_sums(4 * k + 1, i, per_tile(tile, rows=R, init=(zero8f, zero8f)))

        return item

    def edge3():
        R = ROWS3
        def tile(r, x):
            c, rest = conv_coefs(chan[1, r, :])
            f = first_edge[r, :].astype(F32)
            neg = c[0] * pltpu.roll(f, 1, 1) + c[1] * f + c[2] * pltpu.roll(f, LANES - 1, 1) + c[3]
            a, soft = rectify(neg, rest)
            act_edge[r, :] = a.astype(BF16)
            soft_edge[r, :] = soft.astype(BF16)
            return x

        per_tile(tile, rows=R)

    def out_copy(kind, k, i):
        row = first_item + i
        src, dst = (((x1, x0)[k], block_h), ((skips, x1)[k], skip_h))[kind]
        src = src.at[i, :, centre] if (kind, k) == (0, 1) else src.at[i]
        return (
            pltpu.make_async_copy(src, dst.at[row], sem_o.at[kind, k, i]),
            remote(src, dst.at[row], sem_o.at[kind, k, i], sem_or.at[kind, i], {"section": o}),
        )

    def start_out(kind, k, i):
        here, there = out_copy(kind, k, i)
        pl.when(s == k)(lambda: here.start())
        pl.when(s != k)(lambda: there.start())

    def wait_out(kind, k, i):
        here, there = out_copy(kind, k, i)
        pl.when(s == k)(lambda: here.wait())
        pl.when(s != k)(lambda: there.wait_send())

    def wait_came(kind, i):
        src, dst = ((x1, block_h), (skips, skip_h))[kind]
        remote(
            src.at[i], dst.at[o * NI + i], sem_o.at[kind, 0, i], sem_or.at[kind, i], {"section": o}
        ).wait_recv()

    def projected(k, i, first, rows):
        mean, inv = tall(stat[2 * k + 1, i, 0], rows), tall(stat[2 * k + 1, i, 1], rows)
        r = slice(first, first + rows)
        table = col[k, r, :]
        shift = column(table, 0) - mean * inv * column(table, 1)
        y = dot(wg[k, r, :], act2[k, i])
        return (y * wide(inv, F) + wide(shift, F)) * mask_row(i, rows)

    def phase4(k):
        def item(i):
            finish_norm(1, 1, i)
            x1[i] = low(x0[i, :, MID].astype(F32) + projected(0, i, 0, B))
            start_out(0, 0, i)

        return item

    def outputs(i):
        skips[i] = low(projected(0, i, B, B))
        start_out(1, 0, i)
        both = projected(1, i, 0, 2 * B)
        x0[i, :, MID] = low(x1[i].astype(F32) + both[:B])
        start_out(0, 1, i)
        wait_out(0, 0, i)
        x1[i] = low(skips[i].astype(F32) + both[B:])
        start_out(1, 1, i)

    def phase5(k):
        R = ROWS5
        R5 = ROWS5

        def item(i):
            if k == 1:
                finish_norm(5, 3, i)
            mean, inv = tall(stat[2 * k + 1, i, 0], R5), tall(stat[2 * k + 1, i, 1], R5)
            both = dot(jnp.concatenate([act2[k, i], jnp.ones((16, F), BF16)], axis=0), dp[i], NT)
            wide_s[:, 0 : 2 * B] = both[:H]
            total8 = both[H : H + 8]
            bias_sum[k] += total8
            total = tall(total8, R5)

            def tile(r, sums):
                table = chan[k, r, :]
                g, e = column(table, 9), column(table, 10)
                product = wide_s[r, 0 : 2 * B]
                w = wout[k, r, :].astype(F32)
                against = fold(w * product)
                plain = fold(w * total)
                normed = inv * (against - mean * plain)
                gacc[9, r, :] += normed
                gacc[10, r, :] += plain
                scale = inv * g
                shift = e - mean * scale
                step = wide(scale, 2 * B) * product + wide(shift, 2 * B) * total
                grad[k, r, :] += step[:, :B]
                grad[k, pl.ds(H + r.start, R5), :] += step[:, B:]
                return (sums[0] + fold_rows(g * plain), sums[1] + fold_rows(g * normed))

            a, b = per_tile(tile, rows=R5, init=(zero8, zero8))
            send_stats(4 * k + 2, i, a, b)

        return item

    def halo_copy(i, side):
        edge = pl.ds(DILATION, DILATION) if side == 0 else pl.ds(F, DILATION)
        return remote(
            buf.at[i, :, edge],
            buf.at[i, :, tail if side == 0 else head],
            sem_hs.at[side, i],
            sem_hr.at[side, i],
            {"tm": left if side == 0 else right},
        )

    def phase6(k):
        R = ROWS6
        def item(i):
            finish_back(4 * k + 2, 2 * k + 1, i)
            inv = tall(stat[2 * k + 1, i, 1], R) * LOG2E
            p, q = correction(i, R)

            def tile(r, c):
                table = chan[k, r, :]
                slope = column(table, 8)
                g = inv * column(table, 9)
                d_act = low(dot(wout[k, r, :], dp[i]) * wide(g, F) + (p + q * act2[k, i, r, :].astype(F32)))
                soft = soft2[k, i, r, :]
                d_conv = d_act * (wide(low(slope), F) + wide(low(1.0 - slope), F) * jnp.exp2(-soft))
                gacc[8, r, :] += fold(d_act * soft).astype(F32) * -LN2
                gacc[7, r, :] += fold(d_conv).astype(F32)
                buf[i, r, MID] = d_conv
                return c

            per_tile(tile, rows=R)
            if k == 0:

                @pl.when(t > 0)
                def _():
                    halo_copy(i, 0).start()

                @pl.when(t < last)
                def _():
                    halo_copy(i, 1).start()

                @pl.when(t == 0)
                def _():
                    buf[i, :, 0:DILATION] = jnp.zeros((H, DILATION), BF16)

                @pl.when(t == last)
                def _():
                    buf[i, :, F + DILATION : W] = jnp.zeros((H, DILATION), BF16)

        return item

    def edge6():
        R = ROWS6
        wide_s[:, 0:LANES] = dot(wout[1], dp_edge[...])
        inv = tall(lanes_of(stat.at[3], 1), R) * LOG2E
        p, q = tall(lanes_of(back, 0), R), tall(lanes_of(back, 1), R)
        m = tall(edge_mask_ref[...], R)

        def tile(r, c):
            table = chan[1, r, :]
            slope = column(table, 8)
            d_act = wide_s[r, 0:LANES] * (inv * column(table, 9)) + m * (p + q * act_edge[r, :].astype(F32))
            d_conv = d_act * (slope + (1.0 - slope) * jnp.exp2(-soft_edge[r, :].astype(F32)))
            conv_edge[r, :] = d_conv.astype(BF16)
            return c

        per_tile(tile, rows=R)

    def first_back(k, i, r, rows, before, d, after, a, m, sums, store):
        table = chan[k, r, :]
        g = column(table, 2)
        mean, inv = tall(stat[2 * k, i, 0], rows), tall(stat[2 * k, i, 1], rows)
        scale = inv * g
        shift = column(table, 3) - mean * scale
        spread = lambda v: wide(low(v), a.shape[1])
        u = (
            spread(column(table, 4)) * after + spread(column(table, 5)) * d + spread(column(table, 6)) * before
        ) * m
        first = (a * spread(scale) + spread(shift)) * m
        plain = fold(u).astype(F32)
        normed = inv * (fold(u * a).astype(F32) - mean * plain)
        gacc[2, r, :] += normed
        gacc[3, r, :] += plain
        gacc[4, r, :] += fold(after * first).astype(F32)
        gacc[5, r, :] += fold(d * first).astype(F32)
        gacc[6, r, :] += fold(before * first).astype(F32)
        store(u)
        return (sums[0] + fold_rows(g * plain), sums[1] + fold_rows(g * normed))

    def phase7(k):
        R = ROWS7

        def item(i):
            m = low(mask_row(i, R))

            def tile(r, sums):
                before, d, after = (low(v) for v in taps(1, i, r))

                def store(u):
                    soft2[1, i, r, :] = u

                return first_back(1, i, r, R, before, d, after, act1_1[i, r, :], m, sums, store)

            a, b = per_tile(tile, rows=R, init=(zero8, zero8))
            send_stats(7, i, a, b)

        def inner(i):
            lanes = slice(2 * DILATION, F)
            m = low(tall(mask_ref[i, :, lanes], R))

            def tile(r, sums):
                def store(u):
                    soft2[0, i, r, DILATION : F - DILATION] = u

                return first_back(
                    0, i, r, R,
                    buf[i, r, DILATION : F - DILATION], buf[i, r, lanes], buf[i, r, 3 * DILATION : F + DILATION],
                    act1_0[i, r, lanes], m, sums, store,
                )

            a, b = per_tile(tile, rows=R, init=(zero8, zero8))
            inner_sums[i, 0] = a
            inner_sums[i, 1] = b

        return item if k == 1 else inner

    def phase7_ends(i):
        R = ROWS7_ENDS

        @pl.when(t > 0)
        def _():
            halo_copy(i, 0).wait_send()
            halo_copy(i, 1).wait_recv()

        @pl.when(t < last)
        def _():
            halo_copy(i, 1).wait_send()
            halo_copy(i, 0).wait_recv()

        def ends(v, at):
            return jnp.concatenate([v(at, at + DILATION), v(at + F - DILATION, at + F)], axis=1)

        m = low(tall(ends(lambda x, y: mask_ref[i, :, x:y], DILATION), R))

        def tile(r, sums):
            def store(u):
                soft2[0, i, r, 0:DILATION] = u[:, :DILATION]
                soft2[0, i, r, F - DILATION : F] = u[:, DILATION:]

            before, d, after = (ends(lambda x, y: buf[i, r, x:y], at) for at in (0, DILATION, 2 * DILATION))
            a = ends(lambda x, y: act1_0[i, r, x:y], DILATION)
            return first_back(0, i, r, R, before, d, after, a, m, sums, store)

        a, b = per_tile(tile, rows=R, init=(inner_sums[i, 0], inner_sums[i, 1]))
        send_stats(3, i, a, b)

    def mix_copy(i):
        row = first_item + i
        return (
            pltpu.make_async_copy(stage.at[2 * i + s], gmix_h.at[row], sem_m.at[0, i]),
            remote(stage.at[2 * i + o], gmix_h.at[row], sem_m.at[1, i], sem_mr.at[i], {"section": o}),
        )

    def phase8(k):
        R = ROWS8
        act = act1_0 if k == 0 else act1_1
        x = x0 if k == 0 else x1
        mid = MID if k == 0 else slice(0, F)

        def item(i):
            finish_back(4 * k + 3, 2 * k, i)
            inv = tall(stat[2 * k, i, 1], R) * LOG2E
            p, q = correction(i, R)

            def tile(r, c):
                table = chan[k, r, :]
                slope = column(table, 1)
                g = inv * column(table, 2)
                d_act = low(soft2[k, i, r, :].astype(F32) * wide(g, F) + (p + q * act[i, r, mid].astype(F32)))
                soft = soft1[k, i, r, :]
                d_pre = d_act * (wide(low(slope), F) + wide(low(1.0 - slope), F) * jnp.exp2(-soft))
                gacc[1, r, :] += fold(d_act * soft).astype(F32) * -LN2
                gacc[0, r, :] += fold(d_pre).astype(F32)
                buf[i, r, MID] = d_pre
                grad[k, pl.ds(2 * H + r.start, R), :] += dot(d_pre, x[i, :, mid], NT)
                return c

            per_tile(tile, rows=R)

            if k == 1:
                input_gradient(1, i)

        return item

    def input_gradient(k, i):
        m = mask_row(i, B)
        d_input = (dot(win[k], buf[i, :, MID]) + dp[i, 0:B, :].astype(F32)) * m
        if k == 1:
            dp[i, 0:B, :] = d_input.astype(BF16)
        else:
            stage[2 * i] = d_input[0:half].astype(BF16)
            stage[2 * i + 1] = d_input[half:].astype(BF16)
            here, there = mix_copy(i)
            there.start()
            here.start()

    rows_at_part = ((0, 2 * H), (2 * H, grad.shape[1]))
    came = (came0, came1)
    slots = ((from_item0, from_tm0), (from_item1, from_tm1))

    def sizes(part):
        big, chunk = slots[part][0].shape[1], slots[part][1].shape[1]
        return big, chunk, big // chunk

    def item_peer(d):
        return lax.rem(it + d, n_item)

    def tm_peer(d):
        return lax.rem(t + d, n_tm)

    def at_part(part, k, start, rows):
        return grad.at[k, pl.ds(rows_at_part[part][0] + start, rows)]

    def to_owner(part, k):
        a, b = rows_at_part[part]
        return remote(grad.at[k, pl.ds(a, b - a)], came[part], sem_k.at[part], sem_kr.at[part], {"section": o})

    def item_scatter(part, k, d):
        big = sizes(part)[0]
        src = at_part(part, k, item_peer(d) * big, big)
        return remote(
            src, slots[part][0].at[d - 1], sem_ri.at[part, d - 1], sem_rir.at[part, d - 1], {"item": item_peer(d)}
        )

    def tm_scatter(part, k, d):
        big, chunk, owners = sizes(part)
        src = at_part(part, k, it * big + lax.rem(tm_peer(d), owners) * chunk, chunk)
        return remote(
            src, slots[part][1].at[d - 1], sem_rt.at[part, d - 1], sem_rtr.at[part, d - 1], {"tm": tm_peer(d)}
        )

    def tm_gather(part, d, member):
        big, chunk, owners = sizes(part)
        rows = came[part].at[pl.ds(it * big + lax.rem(member, owners) * chunk, chunk)]
        return remote(rows, rows, sem_at.at[part, d - 1], sem_atr.at[part, d - 1], {"tm": tm_peer(d)})

    def item_gather(part, d, member):
        big = sizes(part)[0]
        rows = came[part].at[pl.ds(member * big, big)]
        return remote(rows, rows, sem_ai.at[part, d - 1], sem_air.at[part, d - 1], {"item": item_peer(d)})

    def sum_1(part, k):
        pl.when(s != k)(lambda: to_owner(part, k).start())

    def sum_2(part, k):
        pl.when(s != k)(lambda: to_owner(part, k).wait_send())

        @pl.when(s == k)
        def _():
            a, b = rows_at_part[part]
            to_owner(part, k).wait_recv()
            grad[k, a:b] += came[part][...]
            each(n_item, lambda d: item_scatter(part, k, d).start())

    def sum_3(part, k):
        big, chunk, owners = sizes(part)

        @pl.when(s == k)
        def _():
            each(n_item, lambda d: item_scatter(part, k, d).wait())
            mine = pl.ds(pl.multiple_of(rows_at_part[part][0] + it * big, 8), big)
            grad[k, mine] = lax.fori_loop(0, n_item - 1, lambda j, x: x + slots[part][0][j], grad[k, mine])
            each(n_tm, lambda d: pl.when(tm_peer(d) < owners)(lambda: tm_scatter(part, k, d).start()))

    def sum_4(part, k):
        big, chunk, owners = sizes(part)

        @pl.when(s == k)
        def _():
            def wait(d):
                pl.when(tm_peer(d) < owners)(lambda: tm_scatter(part, k, d).wait_send())
                pl.when(t < owners)(lambda: tm_scatter(part, k, d).wait_recv())

            each(n_tm, wait)

            @pl.when(t < owners)
            def _():
                start = it * big + t * chunk
                own = grad[k, pl.ds(pl.multiple_of(rows_at_part[part][0] + start, 8), chunk)]
                total = lax.fori_loop(0, n_tm - 1, lambda j, x: x + slots[part][1][j], own)
                came[part][pl.ds(pl.multiple_of(start, 8), chunk)] = total
                each(n_tm, lambda d: tm_gather(part, d, t).start())

    def sum_5(part, k):
        _, _, owners = sizes(part)

        @pl.when(s == k)
        def _():
            def wait(d):
                source = lax.rem(t - d + n_tm, n_tm)
                pl.when(t < owners)(lambda: tm_gather(part, d, t).wait_send())
                pl.when(source < owners)(lambda: tm_gather(part, d, source).wait_recv())

            each(n_tm, wait)
            each(n_item, lambda d: item_gather(part, d, it).start())

    def sum_6(part, k):
        @pl.when(s == k)
        def _():
            def wait(d):
                item_gather(part, d, it).wait_send()
                item_gather(part, d, lax.rem(it - d + n_item, n_item)).wait_recv()

            each(n_item, wait)

    last_rows = grad.shape[1] - 2 * H
    last_chunk = to_owner_slots.shape[2]
    last_owners = low_grad.shape[0] // last_chunk
    first_core = jnp.int32(0)

    def member_at(d):
        peer = lax.rem(me + d, members)
        return peer, {"section": first_core, "tm": peer // n_item, "item": lax.rem(peer, n_item)}

    def chunk_rows(member):
        return pl.ds(pl.multiple_of(lax.rem(member, last_owners) * last_chunk, 16), last_chunk)

    def last_scatter(core, d):
        peer, device = member_at(d)
        return remote(
            low_grad.at[chunk_rows(peer)], to_owner_slots.at[core, d], sem_ls.at[d], sem_lr.at[core, d], device
        )

    def last_gather(d, member):
        rows = low_total.at[chunk_rows(member)]
        return remote(rows, rows, sem_gs.at[d], sem_gr.at[d], member_at(d)[1])

    def others(body, start=1):
        lax.fori_loop(start, members, lambda d, c: (body(d), c)[1], 0)

    def last_1():
        low_grad[0:last_rows] = low(grad[0, 2 * H :])
        if low_grad.shape[0] > last_rows:
            low_grad[last_rows:] = jnp.zeros((low_grad.shape[0] - last_rows, LANES), BF16)

        def send(core):
            def one(d):
                pl.when(member_at(d)[0] < last_owners)(lambda: last_scatter(core, d).start())

            others(one, 1 - core)

        pl.when(s == 0)(lambda: send(0))
        pl.when(s == 1)(lambda: send(1))

    def last_2():
        def sent(core):
            def one(d):
                pl.when(member_at(d)[0] < last_owners)(lambda: last_scatter(core, d).wait_send())

            others(one, 1 - core)

        pl.when(s == 1)(lambda: sent(1))

        @pl.when(s == 0)
        def _():
            sent(0)

            @pl.when(me < last_owners)
            def _():
                others(lambda d: last_scatter(0, d).wait_recv())
                others(lambda d: last_scatter(1, d).wait_recv(), 0)
                mine = chunk_rows(me)
                total = low_grad[mine].astype(F32) + to_owner_slots[1, 0].astype(F32)
                total = lax.fori_loop(
                    1,
                    members,
                    lambda d, x: x + (to_owner_slots[0, d].astype(F32) + to_owner_slots[1, d].astype(F32)),
                    total,
                )
                low_total[mine] = low(total)
                others(lambda d: last_gather(d, me).start())

    def last_3():
        @pl.when(s == 0)
        def _():
            def wait(d):
                source = lax.rem(me - d + members, members)
                pl.when(me < last_owners)(lambda: last_gather(d, me).wait_send())
                pl.when(source < last_owners)(lambda: last_gather(d, source).wait_recv())

            others(wait)
            came1[...] = low_total[0:last_rows].astype(F32)

    group = H // 4

    def pack_rows(packed, which):
        lanes = lax.broadcasted_iota(jnp.int32, (group, LANES), 1)
        for g in range(4):
            for j in which:
                total = jnp.sum(gacc[j, g * group : (g + 1) * group, :], axis=1, keepdims=True)
                packed = jnp.where(lanes == 32 * g + j, total, packed)
        return packed

    def finish_early(k):
        lanes = lax.broadcasted_iota(jnp.int32, (group, LANES), 1)
        bias = jnp.broadcast_to(bias_sum[k, 0:1, :], (LANES, 2 * B)).T
        packed = jnp.zeros((group, LANES), F32)
        for g in range(2 * B // group):
            packed = jnp.where(lanes == 32 * g + 11, bias[g * group : (g + 1) * group], packed)
        grad[k, 3 * H : 3 * H + group] = pack_rows(packed, range(2, 11))

    def finish_block(k):
        grad[k, 3 * H : 3 * H + group] = pack_rows(grad[k, 3 * H : 3 * H + group], (0, 1))

    def mask_gradients(i):
        m = mask_row(i, R)

        def tile(r, c):
            dp[i, r, :] = (dp[i, r, :].astype(F32) * m).astype(BF16)
            return c

        per_tile(tile, 2 * B)

    wait_weights(0, 1)
    main_local.wait()
    main_send.wait_send()
    main_recv.wait_recv()

    @pl.when(t > 0)
    def _():
        for core in (0, 1):
            halo_send(0, core).wait_send()
            halo_recv(1, core).wait_recv()

    @pl.when(t < last)
    def _():
        for core in (0, 1):
            halo_send(1, core).wait_send()
            halo_recv(0, core).wait_recv()

    def steps(count, *bodies):
        def step(j, c):
            for first, body in bodies:
                pl.when((j >= first) & (j < first + NI))(functools.partial(body, j - first))
            return c

        lax.fori_loop(0, count, step, 0)

    def at_item(j, body, *args):
        return lambda i: pl.when(i == j)(lambda: body(*args))

    def send_x1_edges(i):
        @pl.when(i == NI - 1)
        def _():
            pack_edges(x1, B, 1)
            send_edges(1, B)

    per_item(phase1(0))
    p2, p3 = phase2(0), phase3(0)
    per_item(lambda i: (p2(i), p3(i)))
    wait_weights(2, 3)
    steps(NI + 1, (0, phase4(0)), (0, send_x1_edges), (1, phase1(1)))
    load_out.wait()
    load_skip.wait()
    per_item(mask_gradients)
    pack_edges(dp, 2 * B, 0)
    send_edges(0, 2 * B)
    edge1()
    gacc[...] = jnp.zeros(gacc.shape, F32)
    per_item(phase2(1))
    edge2()
    place_halos(first_edge)
    per_item(phase3(1))
    edge3()
    recv_edges(0, 2 * B, dp_edge)
    wait_weights(4)
    per_item(phase5(1))
    sum_1(0, 1)
    per_item(phase6(1))
    edge6()
    place_halos(conv_edge)
    sum_2(0, 1)
    wait_weights(5)
    per_item(phase7(1))
    finish_early(1)
    per_item(phase8(1))
    sum_3(0, 1)
    finish_block(1)
    sum_1(1, 1)
    gacc[...] = jnp.zeros(gacc.shape, F32)
    per_item(phase5(0))
    sum_1(0, 0)
    sum_4(0, 1)
    sum_2(1, 1)
    steps(NI, (0, at_item(2, sum_2, 0, 0)), (0, phase6(0)))
    sum_5(0, 1)
    sum_3(1, 1)
    steps(NI, (0, at_item(2, sum_3, 0, 0)), (0, phase7(0)))
    per_item(phase7_ends)
    sum_4(1, 1)
    finish_early(0)
    steps(NI, (0, at_item(1, sum_4, 0, 0)), (0, phase8(0)))
    finish_block(0)
    last_1()
    sum_5(0, 0)
    sum_5(1, 1)
    steps(NI, (0, at_item(3, last_2)), (0, outputs))
    sum_6(0, 1)
    sum_6(1, 1)
    results = [
        pltpu.make_async_copy(came[part], grad_h.at[pl.ds(a, b - a)], sem_f.at[part])
        for part, (a, b) in enumerate(rows_at_part)
    ]
    per_item(lambda i: input_gradient(0, i))
    sum_6(0, 0)
    results[0].start()
    last_3()
    results[1].start()
    for copy in results:
        copy.wait()

    for i in range(NI):
        here, there = mix_copy(i)
        here.wait()
        there.wait_send()
        remote(
            stage.at[2 * i], gmix_h.at[o * NI + i], sem_m.at[1, i], sem_mr.at[i], {"section": o}
        ).wait_recv()
        for kind, k in ((1, 0), (0, 1), (1, 1)):
            wait_out(kind, k, i)
        wait_came(0, i)
        wait_came(1, i)


def chunk_of(rows, members):
    chunk = -(-rows // members)
    chunk = -(-chunk // 8) * 8
    while rows % chunk:
        chunk += 8
    return chunk


def run(n_tm, n_item, sources, gout, gskip, w_in, chan, w_out, b_out, counts, lengths):
    n_src, flat, F = sources.shape
    items, B, _ = gout.shape
    NI = items // 2
    H = w_in.shape[0]
    W = F + 2 * DILATION
    half = B // 2
    rows0, rows1 = 2 * H, H + H // 4
    quarter0, quarter1 = rows0 // n_item, rows1 // n_item
    members = n_tm * n_item
    low_chunk = -(-rows1 // (16 * members)) * 16
    low_owners = -(-rows1 // low_chunk)
    smem = pl.BlockSpec(memory_space=pltpu.SMEM)
    any_spec = pl.BlockSpec(memory_space=pl.ANY)
    dma = pltpu.SemaphoreType.DMA
    shape = jax.ShapeDtypeStruct
    outs = (
        shape((items, B, F), BF16),
        shape((items, B, F), BF16),
        shape((items, half, F), BF16),
        shape((rows0 + rows1, LANES), F32),
    )
    scratch = [
        pltpu.VMEM((items, half, F), BF16),
        pltpu.VMEM((NI, B, W), BF16),
        pltpu.VMEM((NI, B, F), BF16),
        pltpu.VMEM((NI, B, F), BF16),
        pltpu.VMEM((NI, H, W), BF16),
        pltpu.VMEM((NI, H, F), BF16),
        pltpu.VMEM((2, NI, H, F), BF16),
        pltpu.VMEM((2, NI, H, F), BF16),
        pltpu.VMEM((2, NI, H, F), BF16),
        pltpu.VMEM((NI, H, W), BF16),
        pltpu.VMEM((H, H), F32),
        pltpu.VMEM((NI, 2 * B, F), BF16),
        pltpu.VMEM((11, H, LANES), F32),
        pltpu.VMEM((2, H, B), BF16),
        pltpu.VMEM((2, H, 2 * B), BF16),
        pltpu.VMEM((2, 2 * B, H), BF16),
        pltpu.VMEM((2, B, H), BF16),
        pltpu.VMEM((2, H, LANES), F32),
        pltpu.VMEM((2, 2 * B, LANES), F32),
        pltpu.VMEM((low_chunk * low_owners, LANES), BF16),
        pltpu.VMEM((low_chunk * low_owners, LANES), BF16),
        pltpu.VMEM((2, members, low_chunk, LANES), BF16),
        pltpu.VMEM((2, rows0 + rows1, LANES), F32),
        pltpu.VMEM((2, 8, 2 * B), F32),
        pltpu.VMEM((rows0, LANES), F32),
        pltpu.VMEM((rows1, LANES), F32),
        pltpu.VMEM((n_item - 1, quarter0, LANES), F32),
        pltpu.VMEM((n_item - 1, quarter1, LANES), F32),
        pltpu.VMEM((n_tm - 1, chunk_of(quarter0, n_tm), LANES), F32),
        pltpu.VMEM((n_tm - 1, chunk_of(quarter1, n_tm), LANES), F32),
        pltpu.VMEM((NI, 8, W), F32),
        pltpu.VMEM((8, LANES), F32),
        pltpu.VMEM((NI, 8, LANES), F32),
        pltpu.VMEM((NI, 2, 8, LANES), F32),
        pltpu.VMEM((4, NI, 2, 8, LANES), F32),
        pltpu.VMEM((NI, 2, 8, LANES), F32),
        pltpu.VMEM((2, NI, 8, LANES), F32),
        pltpu.VMEM((2, NI, n_tm - 1, 8, LANES), F32),
        pltpu.VMEM((2 * LANES, 2 * LANES), BF16),
        pltpu.VMEM(w_in.shape, BF16),
        pltpu.VMEM(chan.shape, F32),
        pltpu.VMEM(w_out.shape, BF16),
        pltpu.VMEM(b_out.shape, F32),
        pltpu.VMEM((2, 3, 2 * B, LANES), BF16),
        pltpu.VMEM((2, 2, 2 * B, LANES), BF16),
        pltpu.VMEM((B, LANES), BF16),
        pltpu.VMEM((2 * B, LANES), BF16),
        pltpu.VMEM((H, LANES), BF16),
        pltpu.VMEM((H, LANES), BF16),
        pltpu.VMEM((H, LANES), BF16),
        pltpu.VMEM((H, LANES), BF16),
        dma((n_src + 4,)),
        dma((6, 2)),
        dma((6,)),
        dma((5,)),
        dma((2,)),
        dma((2, 2)),
        dma((2, 2)),
        dma((2, NI, n_tm - 1)),
        dma((2, NI, n_tm - 1)),
        dma((2, NI)),
        dma((2, NI)),
        dma((2, 2, NI)),
        dma((2, NI)),
        dma((2, NI)),
        dma((NI,)),
        dma((members,)),
        dma((2, members)),
        dma((members,)),
        dma((members,)),
        dma((2,)),
        dma((2,)),
        dma((2, n_item - 1)),
        dma((2, n_item - 1)),
        dma((2, n_tm - 1)),
        dma((2, n_tm - 1)),
        dma((2, n_tm - 1)),
        dma((2, n_tm - 1)),
        dma((2, n_item - 1)),
        dma((2, n_item - 1)),
        dma((2,)),
    ]
    return pl.pallas_call(
        functools.partial(kernel, (n_tm, n_item, NI, H, B, F)),
        out_shape=outs,
        in_specs=[any_spec] * 7 + [smem] * 2,
        out_specs=[any_spec] * len(outs),
        scratch_shapes=scratch,
        compiler_params=pltpu.CompilerParams(
            collective_id=0, has_side_effects=True, vmem_limit_bytes=VMEM_LIMIT
        ),
        name="temporal_blocks",
    )(sources, gout, gskip, w_in, chan, w_out, b_out, counts, lengths)


def close_kernel(
    block_in, skip_in, gmix_in, grad_in, counts,
    block_h, skip_h, sources_h, w_in_h, chan_h, w_out_h, b_out_h,
    held, mixed, full, nothing, sums, w_out, chan, bias, sem_a, sem_b, sem_g, sem_s, sem_w,
):
    items = gmix_in.shape[0]
    H, B = w_in_h.shape
    n_src = sources_h.shape[0]
    part = items // 2
    plain = [(j, i) for i in (0, 1) for j in (0, 1)]

    def some(i):
        return pl.ds(i * part, part)

    def fetch(j, i):
        return pltpu.make_async_copy((block_in, skip_in)[j].at[some(i)], held.at[j, some(i)], sem_a.at[j, i])

    def store(j, i):
        return pltpu.make_async_copy(held.at[j, some(i)], (block_h, skip_h)[j].at[some(i)], sem_b.at[j, i])

    loads = [pltpu.make_async_copy(gmix_in.at[some(i)], mixed.at[some(i)], sem_g.at[i]) for i in (0, 1)]
    load_sums = pltpu.make_async_copy(grad_in, sums, sem_w.at[0])
    for copy in loads:
        copy.start()
    load_sums.start()
    for j, i in plain:
        fetch(j, i).start()
    nothing[...] = jnp.zeros(nothing.shape, F32)
    for i in range(items):
        if i % part == 0:
            loads[i // part].wait()
        full[i] = mixed[i].astype(F32)
        for n in range(n_src):

            @pl.when(n < counts[i])
            def _():
                pltpu.make_async_copy(full.at[i], sources_h.at[n, i], sem_s.at[n, i]).start()

            @pl.when(n >= counts[i])
            def _():
                pltpu.make_async_copy(nothing, sources_h.at[n, i], sem_s.at[n, i]).start()

    load_sums.wait()
    store_w_in = pltpu.make_async_copy(sums.at[pl.ds(2 * H, H)], w_in_h, sem_w.at[1])
    store_w_in.start()
    for j, i in plain:
        fetch(j, i).wait()
        store(j, i).start()
    w_out[0:B, :] = sums[0:H, :].T
    w_out[B : 2 * B, :] = sums[H : 2 * H, :].T
    rows = sums[3 * H : 3 * H + H // 4, :].T
    for j in range(chan.shape[0]):
        chan[j] = jnp.concatenate([rows[32 * g + j : 32 * g + j + 1] for g in range(4)], axis=1)
    bias[...] = jnp.concatenate([rows[32 * g + 11 : 32 * g + 12] for g in range(2 * B * 4 // H)], axis=1)
    late = [
        pltpu.make_async_copy(src, dst, sem_w.at[2 + j])
        for j, (src, dst) in enumerate(((w_out, w_out_h), (chan, chan_h), (bias, b_out_h)))
    ]
    for copy in late:
        copy.start()
    for copy in late:
        copy.wait()
    store_w_in.wait()
    for j, i in plain:
        store(j, i).wait()
    for i in range(items):
        for n in range(n_src):
            pltpu.make_async_copy(full.at[i], sources_h.at[n, i], sem_s.at[n, i]).wait()


def close(n_src, n_rows, block, skip, gmix, grad, counts):
    items, half, F = gmix.shape
    B = 2 * half
    H = (grad.shape[0] * 4) // 13
    any_spec = pl.BlockSpec(memory_space=pl.ANY)
    dma = pltpu.SemaphoreType.DMA
    shape = jax.ShapeDtypeStruct
    return pl.pallas_call(
        close_kernel,
        out_shape=(
            shape(block.shape, BF16),
            shape(skip.shape, BF16),
            shape((n_src, items, half, F), F32),
            shape((H, B), F32),
            shape((n_rows, 1, H), F32),
            shape((2 * B, H), F32),
            shape((1, 2 * B), F32),
        ),
        in_specs=[any_spec] * 4 + [pl.BlockSpec(memory_space=pltpu.SMEM)],
        out_specs=[any_spec] * 7,
        scratch_shapes=[
            pltpu.VMEM((2, items, B, F), BF16),
            pltpu.VMEM((items, half, F), BF16),
            pltpu.VMEM((items, half, F), F32),
            pltpu.VMEM((half, F), F32),
            pltpu.VMEM(grad.shape, F32),
            pltpu.VMEM((2 * B, H), F32),
            pltpu.VMEM((n_rows, 1, H), F32),
            pltpu.VMEM((1, 2 * B), F32),
            dma((2, 2)),
            dma((2, 2)),
            dma((2,)),
            dma((n_src, items)),
            dma((5,)),
        ],
        compiler_params=pltpu.CompilerParams(vmem_limit_bytes=VMEM_LIMIT),
        name="lay_out",
    )(block, skip, gmix, grad, counts)


def local(sources, source_counts, valid_lengths, w_in, chan, w_out, b_out, grad_out, grad_skip):
    n_sources, per_device, half, F = sources.shape
    block_out, skip_out, gmix, grad = run(
        lax.axis_size("tm"),
        lax.axis_size("item"),
        sources.reshape(n_sources, per_device * half, F),
        grad_out,
        grad_skip,
        w_in[0],
        chan.transpose(1, 0, 2),
        w_out[0],
        b_out,
        source_counts,
        valid_lengths,
    )
    block_out, skip_out, grad_sources, grad_w_in, grad_chan, grad_w_out, grad_b_out = close(
        n_sources, chan.shape[1], block_out, skip_out, gmix, grad, source_counts
    )
    return (
        block_out[None],
        skip_out[None],
        grad_sources,
        grad_w_in[None],
        grad_chan.transpose(1, 0, 2),
        grad_w_out[None],
        grad_b_out,
    )


def solution(mesh):
    in_specs = (
        P(None, "item", "section", "tm"),
        P("item"),
        P("item"),
        P("section", None, None),
        P("section", None, None),
        P("section", None, None),
        P("section", None),
        P("item", None, "tm"),
        P("item", None, "tm"),
    )
    out_specs = (
        P("section", "item", None, "tm"),
        P("section", "item", None, "tm"),
        P(None, "item", "section", "tm"),
        P("section", None, None),
        P("section", None, None),
        P("section", None, None),
        P("section", None),
    )
    return jax.shard_map(local, mesh=mesh, in_specs=in_specs, out_specs=out_specs, check_vma=False)
```

```python
import functools
import math

import jax
import jax.numpy as jnp
from jax import lax
from jax.experimental import pallas as pl
from jax.experimental.pallas import tpu as pltpu
from jax.sharding import PartitionSpec as P

DILATION = 128
LANES = 128
ROWS = 128
ROWS1 = 512
ROWS2 = 512
ROWS3 = 512
ROWS4 = 128
ROWS5 = 512
ROWS6 = 512
ROWS7 = 512
ROWS7_ENDS = 512
ROWS8 = 512
EPSILON = 1e-05
VMEM_LIMIT = 63 * 1024 * 1024 + 512 * 1024
LN2 = math.log(2.0)
LOG2E = 1.0 / LN2
F32 = jnp.float32
BF16 = jnp.bfloat16
MESH = pl.DeviceIdType.MESH
NT = (((1,), (1,)), ((), ()))
NN = (((1,), (0,)), ((), ()))


def dot(a, b, dims=NN, precision=None):
    return lax.dot_general(a, b, dims, precision=precision, preferred_element_type=F32)


def remote(src, dst, send, recv, device):
    return pltpu.make_async_remote_copy(
        src_ref=src, dst_ref=dst, send_sem=send, recv_sem=recv, device_id=device, device_id_type=MESH
    )


def wide(v, width):
    return jnp.concatenate([v] * (width // LANES), axis=1)


def tall(v, rows):
    return jnp.concatenate([v] * (rows // v.shape[0]), axis=0)


def fold(v):
    parts = [v[:, at : at + LANES] for at in range(0, v.shape[1], LANES)]
    while len(parts) > 1:
        parts = [a + b for a, b in zip(parts[::2], parts[1::2])] + parts[len(parts) & ~1 :]
    return parts[0]


def fold_rows(v, count=8):
    parts = [v[at : at + count] for at in range(0, v.shape[0], count)]
    while len(parts) > 1:
        parts = [a + b for a, b in zip(parts[::2], parts[1::2])] + parts[len(parts) & ~1 :]
    return parts[0]


def low(v):
    return v.astype(BF16)


def column(table, j):
    return jnp.broadcast_to(table[:, j : j + 1], (table.shape[0], LANES))


def rows_at(t, count):
    return pl.ds(pl.multiple_of(t * count, count), count)


def kernel(
    dims,
    sources_h, gout_h, gskip_h, w_in_h, chan_h, w_out_h, b_out_h, counts, lengths,
    block_h, skip_h, gmix_h, grad_h,
    stage, x0, x1, skips, act1_0, act1_1, soft1, act2, soft2, buf, wide_s, dp, gacc,
    wpre, wout, wg, win, chan, col,
    low_grad, low_total, to_owner_slots, grad, bias_sum, came0, came1, from_item0, from_item1, from_tm0, from_tm1,
    mask_ref, edge_mask_ref, invn_ref, inner_sums, stat, back, st_src, st_buf,
    shifts, w_in_ref, chan_ref, w_out_ref, b_out_ref, edge_src, edge_in, x_edge, dp_edge, first_edge, act_edge, soft_edge, conv_edge,
    sem_s, sem_w, sem_x, sem_xr, sem_g, sem_es, sem_er, sem_ss, sem_sr, sem_hs, sem_hr, sem_o, sem_or, sem_m, sem_mr,
    sem_ls, sem_lr, sem_gs, sem_gr, sem_k, sem_kr, sem_ri, sem_rir, sem_rt, sem_rtr, sem_at, sem_atr, sem_ai, sem_air, sem_f,
):
    n_tm, n_item, NI, H, B, F = dims
    R = ROWS
    W = F + 2 * DILATION
    MID = slice(DILATION, DILATION + F)
    half = B // 2
    s = lax.axis_index("section")
    t = lax.axis_index("tm")
    o = 1 - s
    left = t - 1
    right = t + 1
    last = n_tm - 1
    first_item = s * NI
    lane = lax.broadcasted_iota(jnp.int32, (R, LANES), 1)
    lane8 = lax.broadcasted_iota(jnp.int32, (8, LANES), 1)

    it = lax.axis_index("item")
    members = n_tm * n_item
    me = t * n_item + it
    n_src = sources_h.shape[0]

    def load_source(n):
        return pltpu.make_async_copy(sources_h.at[n], soft2.at[1, n], sem_s.at[n])

    small = [
        pltpu.make_async_copy(src, dst, sem_s.at[n_src + j])
        for j, (src, dst) in enumerate(
            ((w_in_h, w_in_ref), (chan_h, chan_ref), (w_out_h, w_out_ref), (b_out_h, b_out_ref))
        )
    ]
    for copy in small:
        copy.start()
    for n in range(n_src):
        load_source(n).start()
    edge_in[...] = jnp.zeros(edge_in.shape, BF16)
    row = lax.broadcasted_iota(jnp.int32, (2 * LANES, 2 * LANES), 0)
    to = lax.broadcasted_iota(jnp.int32, (2 * LANES, 2 * LANES), 1)
    step = jnp.where(to < LANES, LANES - 1, 1 - LANES)
    shifts[...] = low(jnp.where(row - to == step, 1.0, 0.0))

    barrier = pltpu.get_barrier_semaphore()

    def greet(d, c):
        peer = lax.rem(me + d, members)
        device = {"tm": peer // n_item, "item": lax.rem(peer, n_item)}
        pl.semaphore_signal(barrier, inc=1, device_id=device, device_id_type=MESH)
        pl.semaphore_signal(barrier, inc=1, device_id={"section": o} | device, device_id_type=MESH)
        return c

    pl.semaphore_signal(barrier, inc=1, device_id={"section": o}, device_id_type=MESH)
    lax.fori_loop(1, members, greet, 0)
    for copy in small:
        copy.wait()

    wpre[s] = w_in_ref[...]
    wide_s[0:LANES, 0:H] = jnp.zeros((LANES, H), F32)
    for j in range(chan_ref.shape[0]):
        wide_s[j : j + 1, 0:H] = chan_ref[j]
    chan[s] = wide_s[0:LANES, 0:H].T
    weights = (wpre, chan, wg, col, wout, win)

    def weight_copies(j):
        ref = weights[j]
        return (
            remote(ref.at[s], ref.at[s], sem_w.at[j, 0], sem_w.at[j, 1], {"section": o}),
            remote(ref.at[o], ref.at[o], sem_w.at[j, 0], sem_w.at[j, 1], {"section": o}),
        )

    def wait_weights(*which):
        for j in which:
            send, recv = weight_copies(j)
            recv.wait_recv()
            send.wait_send()

    pl.semaphore_wait(barrier, 2 * members - 1)
    for j in (0, 1):
        weight_copies(j)[0].start()

    for n in range(n_src):
        load_source(n).wait()

    def mix_item(i, c):
        rows = pl.ds(pl.multiple_of(i * half, half), half)
        where = lax.broadcasted_iota(jnp.int32, (8, F), 1) + t * F
        m = tall(jnp.where(where < lengths[i], 1.0, 0.0), half)
        total = jnp.zeros((half, F), F32)
        for n in range(n_src):
            total += soft2[1, n, rows, :].astype(F32) * jnp.where(n < counts[i], 1.0, 0.0)
        stage[i] = (total * m).astype(BF16)
        return c

    lax.fori_loop(o * NI, o * NI + NI, mix_item, 0)

    own_rows = pl.ds(pl.multiple_of(s * half, half), half)
    other_rows = pl.ds(pl.multiple_of(o * half, half), half)
    items_of = lambda core: pl.ds(core * NI, NI)
    centre = pl.ds(DILATION, F)
    head, tail = pl.ds(0, DILATION), pl.ds(F + DILATION, DILATION)

    main_local = pltpu.make_async_copy(stage.at[items_of(s)], x0.at[:, own_rows, centre], sem_x.at[0])
    main_send = remote(
        stage.at[items_of(o)], x0.at[:, own_rows, centre], sem_x.at[1], sem_xr.at[0], {"section": o}
    )
    main_recv = remote(
        stage.at[items_of(o)], x0.at[:, other_rows, centre], sem_x.at[1], sem_xr.at[0], {"section": o}
    )

    def halo_send(side, core):
        edge = pl.ds(0, DILATION) if side == 0 else pl.ds(F - DILATION, DILATION)
        place = tail if side == 0 else head
        return remote(
            stage.at[items_of(core), :, edge],
            x0.at[:, own_rows, place],
            sem_x.at[2 + 2 * side + core],
            sem_xr.at[1 + 2 * side + s],
            {"section": core, "tm": left if side == 0 else right},
        )

    def halo_recv(side, core):
        place = tail if side == 0 else head
        rows = pl.ds(core * half, half)
        return remote(
            x0.at[:, rows, place], x0.at[:, rows, place], sem_x.at[0], sem_xr.at[1 + 2 * side + core], {"section": o}
        )

    def send_halos(core):
        pl.when(t > 0)(lambda: halo_send(0, core).start())
        pl.when(t < last)(lambda: halo_send(1, core).start())

    main_send.start()
    send_halos(o)
    lax.fori_loop(s * NI, s * NI + NI, mix_item, 0)
    main_local.start()
    send_halos(s)
    load_out = pltpu.make_async_copy(gout_h.at[pl.ds(first_item, NI)], dp.at[:, pl.ds(0, B)], sem_g.at[0])
    load_skip = pltpu.make_async_copy(gskip_h.at[pl.ds(first_item, NI)], dp.at[:, pl.ds(B, B)], sem_g.at[1])
    load_out.start()
    load_skip.start()

    w_out = w_out_ref[...].astype(F32)
    win[s] = w_in_ref[...].astype(F32).T.astype(BF16)
    wout[s] = w_out.T.astype(BF16)
    gained = (w_out * chan_ref[9]).astype(BF16)
    wg[s] = gained
    bias = jnp.broadcast_to(b_out_ref[...], (LANES, 2 * B)).T
    bias += jnp.sum(w_out * chan_ref[10], axis=1, keepdims=True)
    gain = jnp.sum(gained.astype(F32), axis=1, keepdims=True)
    lane_w = lax.broadcasted_iota(jnp.int32, (2 * B, LANES), 1)
    col[s] = jnp.where(lane_w == 0, bias, gain)
    for j in range(2, len(weights)):
        weight_copies(j)[0].start()

    for i in range(NI):
        length = lengths[first_item + i]
        where = lax.broadcasted_iota(jnp.int32, (8, W), 1) + (t * F - DILATION)
        mask_ref[i] = jnp.where((where >= 0) & (where < length), 1.0, 0.0)
        invn_ref[i] = 1.0 / (jnp.full((8, LANES), length, jnp.int32).astype(F32) * H)
    within = lane8 % 32
    frame = t * F + jnp.where(within < 16, within - 2, within - 17 + F)
    length = jnp.full((8, LANES), lengths[first_item], jnp.int32)
    for i in range(1, NI):
        length = jnp.where(lane8 >= 32 * i, lengths[first_item + i], length)
    held = (within < 3) | ((within >= 16) & (within < 19))
    edge_mask_ref[...] = jnp.where(held & (frame >= 0) & (frame < length), 1.0, 0.0)

    @pl.when(t == 0)
    def _():
        x0[:, :, 0:DILATION] = jnp.zeros((NI, B, DILATION), BF16)

    @pl.when(t == last)
    def _():
        x0[:, :, F + DILATION : W] = jnp.zeros((NI, B, DILATION), BF16)

    grad[...] = jnp.zeros(grad.shape, F32)
    bias_sum[...] = jnp.zeros(bias_sum.shape, F32)

    def each(count, body, first=1):
        if count <= 8:
            for d in range(first, count):
                body(d)
        else:
            lax.fori_loop(first, count, lambda d, c: (body(d), c)[1], 0)

    def stat_copy(ph, i, d, to):
        p = ph % 2
        return remote(
            st_src.at[p, i], st_buf.at[p, i, d - 1], sem_ss.at[p, i, d - 1], sem_sr.at[p, i, d - 1], {"tm": to}
        )

    def send_stats(ph, i, a, b):
        rows = [jnp.sum(a, axis=0, keepdims=True), jnp.sum(b, axis=0, keepdims=True)]
        st_src[ph % 2, i] = jnp.concatenate(rows + [jnp.zeros((6, LANES), F32)], axis=0)

        each(n_tm, lambda d: stat_copy(ph, i, d, lax.rem(t + d, n_tm)).start())

    def recv_stats(ph, i):
        def one(d, total):
            copy = stat_copy(ph, i, d, lax.rem(t + d, n_tm))
            copy.wait_send()
            copy.wait_recv()
            return total + st_buf[ph % 2, i, d - 1]

        total = st_src[ph % 2, i]
        if n_tm <= 8:
            for d in range(1, n_tm):
                total = one(d, total)
        else:
            total = lax.fori_loop(1, n_tm, one, total)
        sums = jnp.sum(total, axis=1, keepdims=True)
        return (
            jnp.broadcast_to(sums[0:1], (8, LANES)),
            jnp.broadcast_to(sums[1:2], (8, LANES)),
        )

    def finish_norm(ph, slot, i):
        a, b = recv_stats(ph, i)
        inv_n = invn_ref[i]
        mean = a * inv_n
        spread = jnp.maximum(b * inv_n - mean * mean, 0.0)
        stat[slot, i, 0] = mean
        stat[slot, i, 1] = lax.rsqrt(spread + EPSILON / (LN2 * LN2))

    def finish_back(ph, slot, i):
        a, b = recv_stats(ph, i)
        inv_n = invn_ref[i]
        mean, inv = stat[slot, i, 0], stat[slot, i, 1]
        q = b * inv_n * inv
        back[i, 0] = (mean * q - a * inv_n) * (inv * LOG2E)
        back[i, 1] = -q * (inv * LOG2E)

    def correction(i, rows):
        m = mask_ref[i, :, MID]
        return [tall(m * wide(back[i, j], F), rows) for j in (0, 1)]

    def lanes_of(ref, j):
        out = ref[0, j]
        for i in range(1, NI):
            out = jnp.where(lane8 >= 32 * i, ref[i, j], out)
        return out

    def per_item(body):
        lax.fori_loop(0, NI, lambda i, c: (body(i), c)[1], 0)

    def per_tile(body, count=H, rows=R, init=0):
        return lax.fori_loop(0, count // rows, lambda j, c: body(rows_at(j, rows), c), init)

    def mask_row(i, rows, at=DILATION, width=F):
        return tall(mask_ref[i, :, at : at + width], rows)

    zero8 = jnp.zeros((8, LANES), F32)
    zero8f = jnp.zeros((8, F), F32)

    def pack_edges(src, channels, slot):
        def tile(r, c):
            to_left = to_right = own = jnp.zeros((R, LANES), F32)
            for i in range(NI):
                a = src[i, r, 0:LANES].astype(F32)
                z = src[i, r, F - LANES : F].astype(F32)
                base = 32 * i
                to_left += jnp.where(
                    (lane == base + 17) | (lane == base + 18), pltpu.roll(a, base + 17, 1), 0.0
                )
                to_right += jnp.where(
                    (lane == base) | (lane == base + 1), pltpu.roll(z, base + 2, 1), 0.0
                )
                own += jnp.where(lane == base + 2, pltpu.roll(a, base + 2, 1), 0.0)
                own += jnp.where(lane == base + 16, pltpu.roll(z, base + 17, 1), 0.0)
            edge_src[slot, 0, r, :] = to_left.astype(BF16)
            edge_src[slot, 1, r, :] = to_right.astype(BF16)
            edge_src[slot, 2, r, :] = own.astype(BF16)
            return c

        per_tile(tile, channels)

    def edge_copy(slot, side, channels):
        rows = pl.ds(0, channels)
        return remote(
            edge_src.at[slot, side, rows],
            edge_in.at[slot, side, rows],
            sem_es.at[slot, side],
            sem_er.at[slot, side],
            {"tm": left if side == 0 else right},
        )

    def send_edges(slot, channels):
        @pl.when(t > 0)
        def _():
            edge_copy(slot, 0, channels).start()

        @pl.when(t < last)
        def _():
            edge_copy(slot, 1, channels).start()

    def recv_edges(slot, channels, dst):
        @pl.when(t > 0)
        def _():
            edge_copy(slot, 0, channels).wait_send()
            edge_copy(slot, 1, channels).wait_recv()

        @pl.when(t < last)
        def _():
            edge_copy(slot, 1, channels).wait_send()
            edge_copy(slot, 0, channels).wait_recv()

        def tile(r, c):
            total = edge_src[slot, 2, r, :].astype(F32)
            for side in (0, 1):
                total += edge_in[slot, side, r, :].astype(F32)
            dst[r, :] = total.astype(BF16)
            return c

        per_tile(tile, channels)

    def rectify(neg, rest):
        soft = jnp.maximum(neg, jnp.log2(1.0 + jnp.exp2(jnp.minimum(neg, 100.0))))
        return rest * soft - neg, soft

    def add_sums(a, sums):
        return tuple(x + fold_rows(fold_rows(v, 16).astype(F32)) for x, v in zip(sums, (a, a * a)))

    def send_sums(ph, i, sums):
        m = mask_ref[i, :, MID]
        send_stats(ph, i, fold(sums[0] * m), fold(sums[1] * m))

    def phase1(k):
        R = ROWS1
        width = W if k == 0 else F
        x = x0 if k == 0 else x1
        act = act1_0 if k == 0 else act1_1
        mid = MID if k == 0 else slice(0, F)

        def item(i):

            def tile(r, sums):
                table = chan[k, r, :]
                bias = column(table, 0) * -LOG2E
                rest = 1.0 - column(table, 1)
                neg = dot(wpre[k, r, :], x[i]) * -LOG2E + wide(bias, width)
                a, soft = rectify(neg, wide(rest, width))
                a = low(a)
                act[i, r, :] = a
                soft1[k, i, r, :] = soft[:, mid].astype(BF16)
                return add_sums(a[:, mid], sums)

            send_sums(4 * k, i, per_tile(tile, rows=R, init=(zero8f, zero8f)))

        return item

    def edge1():
        R = ROWS1
        recv_edges(1, B, x_edge)
        wide_s[:, 0:LANES] = dot(wpre[1], x_edge[...])

        def tile(r, c):
            table = chan[1, r, :]
            neg = wide_s[r, 0:LANES] * -LOG2E + column(table, 0) * -LOG2E
            a, _ = rectify(neg, 1.0 - column(table, 1))
            wide_s[r, 0:LANES] = a
            return c

        per_tile(tile, rows=R)

    def phase2(k):
        R = ROWS2
        width = W if k == 0 else F
        at = 0 if k == 0 else DILATION
        act = act1_0 if k == 0 else act1_1

        def item(i):
            finish_norm(4 * k, 2 * k, i)
            mean, inv = tall(stat[2 * k, i, 0], R), tall(stat[2 * k, i, 1], R)
            m = low(mask_row(i, R, at, width))

            def tile(r, c):
                table = chan[k, r, :]
                scale = inv * column(table, 2)
                shift = column(table, 3) - mean * scale
                a = act[i, r, :].astype(F32)
                buf[i, r, at : at + width] = low(a * wide(scale, width) + wide(shift, width)) * m
                return c

            per_tile(tile, rows=R)

        return item

    def edge2():
        R = ROWS2
        mean, inv = tall(lanes_of(stat.at[2], 0), R), tall(lanes_of(stat.at[2], 1), R)
        m = tall(edge_mask_ref[...], R)

        def tile(r, c):
            table = chan[1, r, :]
            scale = inv * column(table, 2)
            a = wide_s[r, 0:LANES]
            first_edge[r, :] = (((a - mean) * scale + column(table, 3)) * m).astype(BF16)
            return c

        per_tile(tile, rows=R)

    def place_halos(edge):
        for i in range(NI):
            buf[i, :, 0:DILATION] = pltpu.roll(edge[...], (254 - 32 * i) % 128, 1)
            buf[i, :, F + DILATION : W] = pltpu.roll(edge[...], (239 - 32 * i) % 128, 1)

    def shifted(i, r):
        before, after = [], []
        for j in range(F // LANES + 1):
            v = dot(buf[i, r, j * LANES : (j + 2) * LANES], shifts[...])
            before.append(v[:, :LANES])
            after.append(v[:, LANES:])
        return jnp.concatenate(before[:-1], axis=1), jnp.concatenate(after[1:], axis=1)

    def taps(k, i, r):
        f = buf[i, r, MID]
        if k == 0:
            return buf[i, r, 0:F], f, buf[i, r, 2 * DILATION : W]
        before, after = shifted(i, r)
        return before, f, after

    def conv_coefs(table):
        return [column(table, j) * -LOG2E for j in (4, 5, 6, 7)], 1.0 - column(table, 8)

    def phase3(k):
        R = ROWS3
        def item(i):

            def tile(r, sums):
                c, rest = conv_coefs(chan[k, r, :])
                before, f, after = (v.astype(F32) for v in taps(k, i, r))
                neg = wide(c[0], F) * before + wide(c[1], F) * f + wide(c[2], F) * after + wide(c[3], F)
                a, soft = rectify(neg, wide(rest, F))
                a = low(a)
                act2[k, i, r, :] = a
                soft2[k, i, r, :] = soft.astype(BF16)
                return add_sums(a, sums)

            send_sums(4 * k + 1, i, per_tile(tile, rows=R, init=(zero8f, zero8f)))

        return item

    def edge3():
        R = ROWS3
        def tile(r, x):
            c, rest = conv_coefs(chan[1, r, :])
            f = first_edge[r, :].astype(F32)
            neg = c[0] * pltpu.roll(f, 1, 1) + c[1] * f + c[2] * pltpu.roll(f, LANES - 1, 1) + c[3]
            a, soft = rectify(neg, rest)
            act_edge[r, :] = a.astype(BF16)
            soft_edge[r, :] = soft.astype(BF16)
            return x

        per_tile(tile, rows=R)

    def out_copy(kind, k, i):
        row = first_item + i
        src, dst = (((x1, x0)[k], block_h), ((skips, x1)[k], skip_h))[kind]
        src = src.at[i, :, centre] if (kind, k) == (0, 1) else src.at[i]
        return (
            pltpu.make_async_copy(src, dst.at[row], sem_o.at[kind, k, i]),
            remote(src, dst.at[row], sem_o.at[kind, k, i], sem_or.at[kind, i], {"section": o}),
        )

    def start_out(kind, k, i):
        here, there = out_copy(kind, k, i)
        pl.when(s == k)(lambda: here.start())
        pl.when(s != k)(lambda: there.start())

    def wait_out(kind, k, i):
        here, there = out_copy(kind, k, i)
        pl.when(s == k)(lambda: here.wait())
        pl.when(s != k)(lambda: there.wait_send())

    def wait_came(kind, i):
        src, dst = ((x1, block_h), (skips, skip_h))[kind]
        remote(
            src.at[i], dst.at[o * NI + i], sem_o.at[kind, 0, i], sem_or.at[kind, i], {"section": o}
        ).wait_recv()

    def projected(k, i, first, rows):
        mean, inv = tall(stat[2 * k + 1, i, 0], rows), tall(stat[2 * k + 1, i, 1], rows)
        r = slice(first, first + rows)
        table = col[k, r, :]
        shift = column(table, 0) - mean * inv * column(table, 1)
        y = dot(wg[k, r, :], act2[k, i])
        return (y * wide(inv, F) + wide(shift, F)) * mask_row(i, rows)

    def phase4(k):
        def item(i):
            finish_norm(1, 1, i)
            x1[i] = low(x0[i, :, MID].astype(F32) + projected(0, i, 0, B))
            start_out(0, 0, i)

        return item

    def outputs(i):
        skips[i] = low(projected(0, i, B, B))
        start_out(1, 0, i)
        both = projected(1, i, 0, 2 * B)
        x0[i, :, MID] = low(x1[i].astype(F32) + both[:B])
        start_out(0, 1, i)
        wait_out(0, 0, i)
        x1[i] = low(skips[i].astype(F32) + both[B:])
        start_out(1, 1, i)

    def phase5(k):
        R = ROWS5
        R5 = ROWS5

        def item(i):
            if k == 1:
                finish_norm(5, 3, i)
            mean, inv = tall(stat[2 * k + 1, i, 0], R5), tall(stat[2 * k + 1, i, 1], R5)
            both = dot(jnp.concatenate([act2[k, i], jnp.ones((16, F), BF16)], axis=0), dp[i], NT)
            wide_s[:, 0 : 2 * B] = both[:H]
            total8 = both[H : H + 8]
            bias_sum[k] += total8
            total = tall(total8, R5)

            def tile(r, sums):
                table = chan[k, r, :]
                g, e = column(table, 9), column(table, 10)
                product = wide_s[r, 0 : 2 * B]
                w = wout[k, r, :].astype(F32)
                against = fold(w * product)
                plain = fold(w * total)
                normed = inv * (against - mean * plain)
                gacc[9, r, :] += normed
                gacc[10, r, :] += plain
                scale = inv * g
                shift = e - mean * scale
                step = wide(scale, 2 * B) * product + wide(shift, 2 * B) * total
                grad[k, r, :] += step[:, :B]
                grad[k, pl.ds(H + r.start, R5), :] += step[:, B:]
                return (sums[0] + fold_rows(g * plain), sums[1] + fold_rows(g * normed))

            a, b = per_tile(tile, rows=R5, init=(zero8, zero8))
            send_stats(4 * k + 2, i, a, b)

        return item

    def halo_copy(i, side):
        edge = pl.ds(DILATION, DILATION) if side == 0 else pl.ds(F, DILATION)
        return remote(
            buf.at[i, :, edge],
            buf.at[i, :, tail if side == 0 else head],
            sem_hs.at[side, i],
            sem_hr.at[side, i],
            {"tm": left if side == 0 else right},
        )

    def phase6(k):
        R = ROWS6
        def item(i):
            finish_back(4 * k + 2, 2 * k + 1, i)
            inv = tall(stat[2 * k + 1, i, 1], R) * LOG2E
            p, q = correction(i, R)

            def tile(r, c):
                table = chan[k, r, :]
                slope = column(table, 8)
                g = inv * column(table, 9)
                d_act = low(dot(wout[k, r, :], dp[i]) * wide(g, F) + (p + q * act2[k, i, r, :].astype(F32)))
                soft = soft2[k, i, r, :]
                d_conv = d_act * (wide(low(slope), F) + wide(low(1.0 - slope), F) * jnp.exp2(-soft))
                gacc[8, r, :] += fold(d_act * soft).astype(F32) * -LN2
                gacc[7, r, :] += fold(d_conv).astype(F32)
                buf[i, r, MID] = d_conv
                return c

            per_tile(tile, rows=R)
            if k == 0:

                @pl.when(t > 0)
                def _():
                    halo_copy(i, 0).start()

                @pl.when(t < last)
                def _():
                    halo_copy(i, 1).start()

                @pl.when(t == 0)
                def _():
                    buf[i, :, 0:DILATION] = jnp.zeros((H, DILATION), BF16)

                @pl.when(t == last)
                def _():
                    buf[i, :, F + DILATION : W] = jnp.zeros((H, DILATION), BF16)

        return item

    def edge6():
        R = ROWS6
        wide_s[:, 0:LANES] = dot(wout[1], dp_edge[...])
        inv = tall(lanes_of(stat.at[3], 1), R) * LOG2E
        p, q = tall(lanes_of(back, 0), R), tall(lanes_of(back, 1), R)
        m = tall(edge_mask_ref[...], R)

        def tile(r, c):
            table = chan[1, r, :]
            slope = column(table, 8)
            d_act = wide_s[r, 0:LANES] * (inv * column(table, 9)) + m * (p + q * act_edge[r, :].astype(F32))
            d_conv = d_act * (slope + (1.0 - slope) * jnp.exp2(-soft_edge[r, :].astype(F32)))
            conv_edge[r, :] = d_conv.astype(BF16)
            return c

        per_tile(tile, rows=R)

    def first_back(k, i, r, rows, before, d, after, a, m, sums, store):
        table = chan[k, r, :]
        g = column(table, 2)
        mean, inv = tall(stat[2 * k, i, 0], rows), tall(stat[2 * k, i, 1], rows)
        scale = inv * g
        shift = column(table, 3) - mean * scale
        spread = lambda v: wide(low(v), a.shape[1])
        u = (
            spread(column(table, 4)) * after + spread(column(table, 5)) * d + spread(column(table, 6)) * before
        ) * m
        first = (a * spread(scale) + spread(shift)) * m
        plain = fold(u).astype(F32)
        normed = inv * (fold(u * a).astype(F32) - mean * plain)
        gacc[2, r, :] += normed
        gacc[3, r, :] += plain
        gacc[4, r, :] += fold(after * first).astype(F32)
        gacc[5, r, :] += fold(d * first).astype(F32)
        gacc[6, r, :] += fold(before * first).astype(F32)
        store(u)
        return (sums[0] + fold_rows(g * plain), sums[1] + fold_rows(g * normed))

    def phase7(k):
        R = ROWS7

        def item(i):
            m = low(mask_row(i, R))

            def tile(r, sums):
                before, d, after = (low(v) for v in taps(1, i, r))

                def store(u):
                    soft2[1, i, r, :] = u

                return first_back(1, i, r, R, before, d, after, act1_1[i, r, :], m, sums, store)

            a, b = per_tile(tile, rows=R, init=(zero8, zero8))
            send_stats(7, i, a, b)

        def inner(i):
            lanes = slice(2 * DILATION, F)
            m = low(tall(mask_ref[i, :, lanes], R))

            def tile(r, sums):
                def store(u):
                    soft2[0, i, r, DILATION : F - DILATION] = u

                return first_back(
                    0, i, r, R,
                    buf[i, r, DILATION : F - DILATION], buf[i, r, lanes], buf[i, r, 3 * DILATION : F + DILATION],
                    act1_0[i, r, lanes], m, sums, store,
                )

            a, b = per_tile(tile, rows=R, init=(zero8, zero8))
            inner_sums[i, 0] = a
            inner_sums[i, 1] = b

        return item if k == 1 else inner

    def phase7_ends(i):
        R = ROWS7_ENDS

        @pl.when(t > 0)
        def _():
            halo_copy(i, 0).wait_send()
            halo_copy(i, 1).wait_recv()

        @pl.when(t < last)
        def _():
            halo_copy(i, 1).wait_send()
            halo_copy(i, 0).wait_recv()

        def ends(v, at):
            return jnp.concatenate([v(at, at + DILATION), v(at + F - DILATION, at + F)], axis=1)

        m = low(tall(ends(lambda x, y: mask_ref[i, :, x:y], DILATION), R))

        def tile(r, sums):
            def store(u):
                soft2[0, i, r, 0:DILATION] = u[:, :DILATION]
                soft2[0, i, r, F - DILATION : F] = u[:, DILATION:]

            before, d, after = (ends(lambda x, y: buf[i, r, x:y], at) for at in (0, DILATION, 2 * DILATION))
            a = ends(lambda x, y: act1_0[i, r, x:y], DILATION)
            return first_back(0, i, r, R, before, d, after, a, m, sums, store)

        a, b = per_tile(tile, rows=R, init=(inner_sums[i, 0], inner_sums[i, 1]))
        send_stats(3, i, a, b)

    def mix_copy(i):
        row = first_item + i
        return (
            pltpu.make_async_copy(stage.at[2 * i + s], gmix_h.at[row], sem_m.at[0, i]),
            remote(stage.at[2 * i + o], gmix_h.at[row], sem_m.at[1, i], sem_mr.at[i], {"section": o}),
        )

    def phase8(k):
        R = ROWS8
        act = act1_0 if k == 0 else act1_1
        x = x0 if k == 0 else x1
        mid = MID if k == 0 else slice(0, F)

        def item(i):
            finish_back(4 * k + 3, 2 * k, i)
            inv = tall(stat[2 * k, i, 1], R) * LOG2E
            p, q = correction(i, R)

            def tile(r, c):
                table = chan[k, r, :]
                slope = column(table, 1)
                g = inv * column(table, 2)
                d_act = low(soft2[k, i, r, :].astype(F32) * wide(g, F) + (p + q * act[i, r, mid].astype(F32)))
                soft = soft1[k, i, r, :]
                d_pre = d_act * (wide(low(slope), F) + wide(low(1.0 - slope), F) * jnp.exp2(-soft))
                gacc[1, r, :] += fold(d_act * soft).astype(F32) * -LN2
                gacc[0, r, :] += fold(d_pre).astype(F32)
                buf[i, r, MID] = d_pre
                grad[k, pl.ds(2 * H + r.start, R), :] += dot(d_pre, x[i, :, mid], NT)
                return c

            per_tile(tile, rows=R)

            if k == 1:
                input_gradient(1, i)

        return item

    def input_gradient(k, i):
        m = mask_row(i, B)
        d_input = (dot(win[k], buf[i, :, MID]) + dp[i, 0:B, :].astype(F32)) * m
        if k == 1:
            dp[i, 0:B, :] = d_input.astype(BF16)
        else:
            stage[2 * i] = d_input[0:half].astype(BF16)
            stage[2 * i + 1] = d_input[half:].astype(BF16)
            here, there = mix_copy(i)
            there.start()
            here.start()

    rows_at_part = ((0, 2 * H), (2 * H, grad.shape[1]))
    came = (came0, came1)
    slots = ((from_item0, from_tm0), (from_item1, from_tm1))

    def sizes(part):
        big, chunk = slots[part][0].shape[1], slots[part][1].shape[1]
        return big, chunk, big // chunk

    def item_peer(d):
        return lax.rem(it + d, n_item)

    def tm_peer(d):
        return lax.rem(t + d, n_tm)

    def at_part(part, k, start, rows):
        return grad.at[k, pl.ds(rows_at_part[part][0] + start, rows)]

    def to_owner(part, k):
        a, b = rows_at_part[part]
        return remote(grad.at[k, pl.ds(a, b - a)], came[part], sem_k.at[part], sem_kr.at[part], {"section": o})

    def item_scatter(part, k, d):
        big = sizes(part)[0]
        src = at_part(part, k, item_peer(d) * big, big)
        return remote(
            src, slots[part][0].at[d - 1], sem_ri.at[part, d - 1], sem_rir.at[part, d - 1], {"item": item_peer(d)}
        )

    def tm_scatter(part, k, d):
        big, chunk, owners = sizes(part)
        src = at_part(part, k, it * big + lax.rem(tm_peer(d), owners) * chunk, chunk)
        return remote(
            src, slots[part][1].at[d - 1], sem_rt.at[part, d - 1], sem_rtr.at[part, d - 1], {"tm": tm_peer(d)}
        )

    def tm_gather(part, d, member):
        big, chunk, owners = sizes(part)
        rows = came[part].at[pl.ds(it * big + lax.rem(member, owners) * chunk, chunk)]
        return remote(rows, rows, sem_at.at[part, d - 1], sem_atr.at[part, d - 1], {"tm": tm_peer(d)})

    def item_gather(part, d, member):
        big = sizes(part)[0]
        rows = came[part].at[pl.ds(member * big, big)]
        return remote(rows, rows, sem_ai.at[part, d - 1], sem_air.at[part, d - 1], {"item": item_peer(d)})

    def sum_1(part, k):
        pl.when(s != k)(lambda: to_owner(part, k).start())

    def sum_2(part, k):
        pl.when(s != k)(lambda: to_owner(part, k).wait_send())

        @pl.when(s == k)
        def _():
            a, b = rows_at_part[part]
            to_owner(part, k).wait_recv()
            grad[k, a:b] += came[part][...]
            each(n_item, lambda d: item_scatter(part, k, d).start())

    def sum_3(part, k):
        big, chunk, owners = sizes(part)

        @pl.when(s == k)
        def _():
            each(n_item, lambda d: item_scatter(part, k, d).wait())
            mine = pl.ds(pl.multiple_of(rows_at_part[part][0] + it * big, 8), big)
            grad[k, mine] = lax.fori_loop(0, n_item - 1, lambda j, x: x + slots[part][0][j], grad[k, mine])
            each(n_tm, lambda d: pl.when(tm_peer(d) < owners)(lambda: tm_scatter(part, k, d).start()))

    def sum_4(part, k):
        big, chunk, owners = sizes(part)

        @pl.when(s == k)
        def _():
            def wait(d):
                pl.when(tm_peer(d) < owners)(lambda: tm_scatter(part, k, d).wait_send())
                pl.when(t < owners)(lambda: tm_scatter(part, k, d).wait_recv())

            each(n_tm, wait)

            @pl.when(t < owners)
            def _():
                start = it * big + t * chunk
                own = grad[k, pl.ds(pl.multiple_of(rows_at_part[part][0] + start, 8), chunk)]
                total = lax.fori_loop(0, n_tm - 1, lambda j, x: x + slots[part][1][j], own)
                came[part][pl.ds(pl.multiple_of(start, 8), chunk)] = total
                each(n_tm, lambda d: tm_gather(part, d, t).start())

    def sum_5(part, k):
        _, _, owners = sizes(part)

        @pl.when(s == k)
        def _():
            def wait(d):
                source = lax.rem(t - d + n_tm, n_tm)
                pl.when(t < owners)(lambda: tm_gather(part, d, t).wait_send())
                pl.when(source < owners)(lambda: tm_gather(part, d, source).wait_recv())

            each(n_tm, wait)
            each(n_item, lambda d: item_gather(part, d, it).start())

    def sum_6(part, k):
        @pl.when(s == k)
        def _():
            def wait(d):
                item_gather(part, d, it).wait_send()
                item_gather(part, d, lax.rem(it - d + n_item, n_item)).wait_recv()

            each(n_item, wait)

    last_rows = grad.shape[1] - 2 * H
    last_chunk = to_owner_slots.shape[2]
    last_owners = low_grad.shape[0] // last_chunk
    first_core = jnp.int32(0)

    def member_at(d):
        peer = lax.rem(me + d, members)
        return peer, {"section": first_core, "tm": peer // n_item, "item": lax.rem(peer, n_item)}

    def chunk_rows(member):
        return pl.ds(pl.multiple_of(lax.rem(member, last_owners) * last_chunk, 16), last_chunk)

    def last_scatter(core, d):
        peer, device = member_at(d)
        return remote(
            low_grad.at[chunk_rows(peer)], to_owner_slots.at[core, d], sem_ls.at[d], sem_lr.at[core, d], device
        )

    def last_gather(d, member):
        rows = low_total.at[chunk_rows(member)]
        return remote(rows, rows, sem_gs.at[d], sem_gr.at[d], member_at(d)[1])

    def others(body, start=1):
        if members <= 16:
            for d in range(start, members):
                body(d)
        else:
            lax.fori_loop(start, members, lambda d, c: (body(d), c)[1], 0)

    def last_1():
        low_grad[0:last_rows] = low(grad[0, 2 * H :])
        if low_grad.shape[0] > last_rows:
            low_grad[last_rows:] = jnp.zeros((low_grad.shape[0] - last_rows, LANES), BF16)

        def send(core):
            def one(d):
                pl.when(member_at(d)[0] < last_owners)(lambda: last_scatter(core, d).start())

            others(one, 1 - core)

        pl.when(s == 0)(lambda: send(0))
        pl.when(s == 1)(lambda: send(1))

    def last_2():
        def sent(core):
            def one(d):
                pl.when(member_at(d)[0] < last_owners)(lambda: last_scatter(core, d).wait_send())

            others(one, 1 - core)

        pl.when(s == 1)(lambda: sent(1))

        @pl.when(s == 0)
        def _():
            sent(0)

            @pl.when(me < last_owners)
            def _():
                others(lambda d: last_scatter(0, d).wait_recv())
                others(lambda d: last_scatter(1, d).wait_recv(), 0)
                mine = chunk_rows(me)
                total = low_grad[mine].astype(F32) + to_owner_slots[1, 0].astype(F32)
                total = lax.fori_loop(
                    1,
                    members,
                    lambda d, x: x + (to_owner_slots[0, d].astype(F32) + to_owner_slots[1, d].astype(F32)),
                    total,
                )
                low_total[mine] = low(total)
                others(lambda d: last_gather(d, me).start())

    def last_3():
        @pl.when(s == 0)
        def _():
            def wait(d):
                source = lax.rem(me - d + members, members)
                pl.when(me < last_owners)(lambda: last_gather(d, me).wait_send())
                pl.when(source < last_owners)(lambda: last_gather(d, source).wait_recv())

            others(wait)
            came1[...] = low_total[0:last_rows].astype(F32)

    group = H // 4

    def pack_rows(packed, which):
        lanes = lax.broadcasted_iota(jnp.int32, (group, LANES), 1)
        for g in range(4):
            for j in which:
                total = jnp.sum(gacc[j, g * group : (g + 1) * group, :], axis=1, keepdims=True)
                packed = jnp.where(lanes == 32 * g + j, total, packed)
        return packed

    def finish_early(k):
        lanes = lax.broadcasted_iota(jnp.int32, (group, LANES), 1)
        bias = jnp.broadcast_to(bias_sum[k, 0:1, :], (LANES, 2 * B)).T
        packed = jnp.zeros((group, LANES), F32)
        for g in range(2 * B // group):
            packed = jnp.where(lanes == 32 * g + 11, bias[g * group : (g + 1) * group], packed)
        grad[k, 3 * H : 3 * H + group] = pack_rows(packed, range(2, 11))

    def finish_block(k):
        grad[k, 3 * H : 3 * H + group] = pack_rows(grad[k, 3 * H : 3 * H + group], (0, 1))

    def mask_gradients(i):
        m = mask_row(i, R)

        def tile(r, c):
            dp[i, r, :] = (dp[i, r, :].astype(F32) * m).astype(BF16)
            return c

        per_tile(tile, 2 * B)

    wait_weights(0, 1)
    main_local.wait()
    main_send.wait_send()
    main_recv.wait_recv()

    @pl.when(t > 0)
    def _():
        for core in (0, 1):
            halo_send(0, core).wait_send()
            halo_recv(1, core).wait_recv()

    @pl.when(t < last)
    def _():
        for core in (0, 1):
            halo_send(1, core).wait_send()
            halo_recv(0, core).wait_recv()

    def steps(count, *bodies):
        def step(j, c):
            for first, body in bodies:
                pl.when((j >= first) & (j < first + NI))(functools.partial(body, j - first))
            return c

        lax.fori_loop(0, count, step, 0)

    def at_item(j, body, *args):
        return lambda i: pl.when(i == j)(lambda: body(*args))

    def send_x1_edges(i):
        @pl.when(i == NI - 1)
        def _():
            pack_edges(x1, B, 1)
            send_edges(1, B)

    per_item(phase1(0))
    p2, p3 = phase2(0), phase3(0)
    per_item(lambda i: (p2(i), p3(i)))
    wait_weights(2, 3)
    steps(NI + 1, (0, phase4(0)), (0, send_x1_edges), (1, phase1(1)))
    load_out.wait()
    load_skip.wait()
    per_item(mask_gradients)
    pack_edges(dp, 2 * B, 0)
    send_edges(0, 2 * B)
    edge1()
    gacc[...] = jnp.zeros(gacc.shape, F32)
    per_item(phase2(1))
    edge2()
    place_halos(first_edge)
    per_item(phase3(1))
    edge3()
    recv_edges(0, 2 * B, dp_edge)
    wait_weights(4)
    per_item(phase5(1))
    sum_1(0, 1)
    per_item(phase6(1))
    edge6()
    place_halos(conv_edge)
    sum_2(0, 1)
    wait_weights(5)
    per_item(phase7(1))
    finish_early(1)
    per_item(phase8(1))
    sum_3(0, 1)
    finish_block(1)
    sum_1(1, 1)
    gacc[...] = jnp.zeros(gacc.shape, F32)
    per_item(phase5(0))
    sum_1(0, 0)
    sum_4(0, 1)
    sum_2(1, 1)
    steps(NI, (0, at_item(2, sum_2, 0, 0)), (0, phase6(0)))
    sum_5(0, 1)
    sum_3(1, 1)
    steps(NI, (0, at_item(2, sum_3, 0, 0)), (0, phase7(0)))
    per_item(phase7_ends)
    sum_4(1, 1)
    finish_early(0)
    steps(NI, (0, at_item(1, sum_4, 0, 0)), (0, phase8(0)))
    finish_block(0)
    last_1()
    sum_5(0, 0)
    sum_5(1, 1)
    steps(NI, (0, at_item(3, last_2)), (0, outputs))
    sum_6(0, 1)
    sum_6(1, 1)
    results = [
        pltpu.make_async_copy(came[part], grad_h.at[pl.ds(a, b - a)], sem_f.at[part])
        for part, (a, b) in enumerate(rows_at_part)
    ]
    per_item(lambda i: input_gradient(0, i))
    sum_6(0, 0)
    results[0].start()
    last_3()
    results[1].start()
    for copy in results:
        copy.wait()

    for i in range(NI):
        here, there = mix_copy(i)
        here.wait()
        there.wait_send()
        remote(
            stage.at[2 * i], gmix_h.at[o * NI + i], sem_m.at[1, i], sem_mr.at[i], {"section": o}
        ).wait_recv()
        for kind, k in ((1, 0), (0, 1), (1, 1)):
            wait_out(kind, k, i)
        wait_came(0, i)
        wait_came(1, i)


def chunk_of(rows, members):
    chunk = -(-rows // members)
    chunk = -(-chunk // 8) * 8
    while rows % chunk:
        chunk += 8
    return chunk


def run(n_tm, n_item, sources, gout, gskip, w_in, chan, w_out, b_out, counts, lengths):
    n_src, flat, F = sources.shape
    items, B, _ = gout.shape
    NI = items // 2
    H = w_in.shape[0]
    W = F + 2 * DILATION
    half = B // 2
    rows0, rows1 = 2 * H, H + H // 4
    quarter0, quarter1 = rows0 // n_item, rows1 // n_item
    members = n_tm * n_item
    low_chunk = -(-rows1 // (16 * members)) * 16
    low_owners = -(-rows1 // low_chunk)
    smem = pl.BlockSpec(memory_space=pltpu.SMEM)
    any_spec = pl.BlockSpec(memory_space=pl.ANY)
    dma = pltpu.SemaphoreType.DMA
    shape = jax.ShapeDtypeStruct
    outs = (
        shape((items, B, F), BF16),
        shape((items, B, F), BF16),
        shape((items, half, F), BF16),
        shape((rows0 + rows1, LANES), F32),
    )
    scratch = [
        pltpu.VMEM((items, half, F), BF16),
        pltpu.VMEM((NI, B, W), BF16),
        pltpu.VMEM((NI, B, F), BF16),
        pltpu.VMEM((NI, B, F), BF16),
        pltpu.VMEM((NI, H, W), BF16),
        pltpu.VMEM((NI, H, F), BF16),
        pltpu.VMEM((2, NI, H, F), BF16),
        pltpu.VMEM((2, NI, H, F), BF16),
        pltpu.VMEM((2, NI, H, F), BF16),
        pltpu.VMEM((NI, H, W), BF16),
        pltpu.VMEM((H, H), F32),
        pltpu.VMEM((NI, 2 * B, F), BF16),
        pltpu.VMEM((11, H, LANES), F32),
        pltpu.VMEM((2, H, B), BF16),
        pltpu.VMEM((2, H, 2 * B), BF16),
        pltpu.VMEM((2, 2 * B, H), BF16),
        pltpu.VMEM((2, B, H), BF16),
        pltpu.VMEM((2, H, LANES), F32),
        pltpu.VMEM((2, 2 * B, LANES), F32),
        pltpu.VMEM((low_chunk * low_owners, LANES), BF16),
        pltpu.VMEM((low_chunk * low_owners, LANES), BF16),
        pltpu.VMEM((2, members, low_chunk, LANES), BF16),
        pltpu.VMEM((2, rows0 + rows1, LANES), F32),
        pltpu.VMEM((2, 8, 2 * B), F32),
        pltpu.VMEM((rows0, LANES), F32),
        pltpu.VMEM((rows1, LANES), F32),
        pltpu.VMEM((n_item - 1, quarter0, LANES), F32),
        pltpu.VMEM((n_item - 1, quarter1, LANES), F32),
        pltpu.VMEM((n_tm - 1, chunk_of(quarter0, n_tm), LANES), F32),
        pltpu.VMEM((n_tm - 1, chunk_of(quarter1, n_tm), LANES), F32),
        pltpu.VMEM((NI, 8, W), F32),
        pltpu.VMEM((8, LANES), F32),
        pltpu.VMEM((NI, 8, LANES), F32),
        pltpu.VMEM((NI, 2, 8, LANES), F32),
        pltpu.VMEM((4, NI, 2, 8, LANES), F32),
        pltpu.VMEM((NI, 2, 8, LANES), F32),
        pltpu.VMEM((2, NI, 8, LANES), F32),
        pltpu.VMEM((2, NI, n_tm - 1, 8, LANES), F32),
        pltpu.VMEM((2 * LANES, 2 * LANES), BF16),
        pltpu.VMEM(w_in.shape, BF16),
        pltpu.VMEM(chan.shape, F32),
        pltpu.VMEM(w_out.shape, BF16),
        pltpu.VMEM(b_out.shape, F32),
        pltpu.VMEM((2, 3, 2 * B, LANES), BF16),
        pltpu.VMEM((2, 2, 2 * B, LANES), BF16),
        pltpu.VMEM((B, LANES), BF16),
        pltpu.VMEM((2 * B, LANES), BF16),
        pltpu.VMEM((H, LANES), BF16),
        pltpu.VMEM((H, LANES), BF16),
        pltpu.VMEM((H, LANES), BF16),
        pltpu.VMEM((H, LANES), BF16),
        dma((n_src + 4,)),
        dma((6, 2)),
        dma((6,)),
        dma((5,)),
        dma((2,)),
        dma((2, 2)),
        dma((2, 2)),
        dma((2, NI, n_tm - 1)),
        dma((2, NI, n_tm - 1)),
        dma((2, NI)),
        dma((2, NI)),
        dma((2, 2, NI)),
        dma((2, NI)),
        dma((2, NI)),
        dma((NI,)),
        dma((members,)),
        dma((2, members)),
        dma((members,)),
        dma((members,)),
        dma((2,)),
        dma((2,)),
        dma((2, n_item - 1)),
        dma((2, n_item - 1)),
        dma((2, n_tm - 1)),
        dma((2, n_tm - 1)),
        dma((2, n_tm - 1)),
        dma((2, n_tm - 1)),
        dma((2, n_item - 1)),
        dma((2, n_item - 1)),
        dma((2,)),
    ]
    return pl.pallas_call(
        functools.partial(kernel, (n_tm, n_item, NI, H, B, F)),
        out_shape=outs,
        in_specs=[any_spec] * 7 + [smem] * 2,
        out_specs=[any_spec] * len(outs),
        scratch_shapes=scratch,
        compiler_params=pltpu.CompilerParams(
            collective_id=0, has_side_effects=True, vmem_limit_bytes=VMEM_LIMIT
        ),
        name="temporal_blocks",
    )(sources, gout, gskip, w_in, chan, w_out, b_out, counts, lengths)


def close_kernel(
    block_in, skip_in, gmix_in, grad_in, counts,
    block_h, skip_h, sources_h, w_in_h, chan_h, w_out_h, b_out_h,
    held, mixed, full, nothing, sums, w_out, chan, bias, sem_a, sem_b, sem_g, sem_s, sem_w,
):
    items = gmix_in.shape[0]
    H, B = w_in_h.shape
    n_src = sources_h.shape[0]
    part = items // 2
    plain = [(j, i) for i in (0, 1) for j in (0, 1)]

    def some(i):
        return pl.ds(i * part, part)

    def fetch(j, i):
        return pltpu.make_async_copy((block_in, skip_in)[j].at[some(i)], held.at[j, some(i)], sem_a.at[j, i])

    def store(j, i):
        return pltpu.make_async_copy(held.at[j, some(i)], (block_h, skip_h)[j].at[some(i)], sem_b.at[j, i])

    loads = [pltpu.make_async_copy(gmix_in.at[some(i)], mixed.at[some(i)], sem_g.at[i]) for i in (0, 1)]
    load_sums = pltpu.make_async_copy(grad_in, sums, sem_w.at[0])
    for copy in loads:
        copy.start()
    load_sums.start()
    for j, i in plain:
        fetch(j, i).start()
    nothing[...] = jnp.zeros(nothing.shape, F32)
    for i in range(items):
        if i % part == 0:
            loads[i // part].wait()
        full[i] = mixed[i].astype(F32)
        for n in range(n_src):

            @pl.when(n < counts[i])
            def _():
                pltpu.make_async_copy(full.at[i], sources_h.at[n, i], sem_s.at[n, i]).start()

            @pl.when(n >= counts[i])
            def _():
                pltpu.make_async_copy(nothing, sources_h.at[n, i], sem_s.at[n, i]).start()

    load_sums.wait()
    store_w_in = pltpu.make_async_copy(sums.at[pl.ds(2 * H, H)], w_in_h, sem_w.at[1])
    store_w_in.start()
    for j, i in plain:
        fetch(j, i).wait()
        store(j, i).start()
    w_out[0:B, :] = sums[0:H, :].T
    w_out[B : 2 * B, :] = sums[H : 2 * H, :].T
    rows = sums[3 * H : 3 * H + H // 4, :].T
    for j in range(chan.shape[0]):
        chan[j] = jnp.concatenate([rows[32 * g + j : 32 * g + j + 1] for g in range(4)], axis=1)
    bias[...] = jnp.concatenate([rows[32 * g + 11 : 32 * g + 12] for g in range(2 * B * 4 // H)], axis=1)
    late = [
        pltpu.make_async_copy(src, dst, sem_w.at[2 + j])
        for j, (src, dst) in enumerate(((w_out, w_out_h), (chan, chan_h), (bias, b_out_h)))
    ]
    for copy in late:
        copy.start()
    for copy in late:
        copy.wait()
    store_w_in.wait()
    for j, i in plain:
        store(j, i).wait()
    for i in range(items):
        for n in range(n_src):
            pltpu.make_async_copy(full.at[i], sources_h.at[n, i], sem_s.at[n, i]).wait()


def close(n_src, n_rows, block, skip, gmix, grad, counts):
    items, half, F = gmix.shape
    B = 2 * half
    H = (grad.shape[0] * 4) // 13
    any_spec = pl.BlockSpec(memory_space=pl.ANY)
    dma = pltpu.SemaphoreType.DMA
    shape = jax.ShapeDtypeStruct
    return pl.pallas_call(
        close_kernel,
        out_shape=(
            shape(block.shape, BF16),
            shape(skip.shape, BF16),
            shape((n_src, items, half, F), F32),
            shape((H, B), F32),
            shape((n_rows, 1, H), F32),
            shape((2 * B, H), F32),
            shape((1, 2 * B), F32),
        ),
        in_specs=[any_spec] * 4 + [pl.BlockSpec(memory_space=pltpu.SMEM)],
        out_specs=[any_spec] * 7,
        scratch_shapes=[
            pltpu.VMEM((2, items, B, F), BF16),
            pltpu.VMEM((items, half, F), BF16),
            pltpu.VMEM((items, half, F), F32),
            pltpu.VMEM((half, F), F32),
            pltpu.VMEM(grad.shape, F32),
            pltpu.VMEM((2 * B, H), F32),
            pltpu.VMEM((n_rows, 1, H), F32),
            pltpu.VMEM((1, 2 * B), F32),
            dma((2, 2)),
            dma((2, 2)),
            dma((2,)),
            dma((n_src, items)),
            dma((5,)),
        ],
        compiler_params=pltpu.CompilerParams(vmem_limit_bytes=VMEM_LIMIT),
        name="lay_out",
    )(block, skip, gmix, grad, counts)


def local(sources, source_counts, valid_lengths, w_in, chan, w_out, b_out, grad_out, grad_skip):
    n_sources, per_device, half, F = sources.shape
    block_out, skip_out, gmix, grad = run(
        lax.axis_size("tm"),
        lax.axis_size("item"),
        sources.reshape(n_sources, per_device * half, F),
        grad_out,
        grad_skip,
        w_in[0],
        chan.transpose(1, 0, 2),
        w_out[0],
        b_out,
        source_counts,
        valid_lengths,
    )
    block_out, skip_out, grad_sources, grad_w_in, grad_chan, grad_w_out, grad_b_out = close(
        n_sources, chan.shape[1], block_out, skip_out, gmix, grad, source_counts
    )
    return (
        block_out[None],
        skip_out[None],
        grad_sources,
        grad_w_in[None],
        grad_chan.transpose(1, 0, 2),
        grad_w_out[None],
        grad_b_out,
    )


def solution(mesh):
    in_specs = (
        P(None, "item", "section", "tm"),
        P("item"),
        P("item"),
        P("section", None, None),
        P("section", None, None),
        P("section", None, None),
        P("section", None),
        P("item", None, "tm"),
        P("item", None, "tm"),
    )
    out_specs = (
        P("section", "item", None, "tm"),
        P("section", "item", None, "tm"),
        P(None, "item", "section", "tm"),
        P("section", None, None),
        P("section", None, None),
        P("section", None, None),
        P("section", None),
    )
    return jax.shard_map(local, mesh=mesh, in_specs=in_specs, out_specs=out_specs, check_vma=False)
```
